32 devices in a mesh: dp: 4 (over z), own: 8 (over y, x, core).
Axes of the slice: x: 2, y: 2, z: 4, core: 2. Of those that a mesh axis runs over, the one named last changes fastest.
Arguments:
- signals: bfloat16 [8192, 384], P(('dp', 'own')), may hold values from -6 to 6
- cotangent: bfloat16 [8192, 384], P(('dp', 'own')), may hold values from -6 to 6
- row_insertion: int32 [8192], P(('dp', 'own')), may hold values from 0 to 15, as said below
- touched: int32 [32, 4], replicated, may hold values from 0 to 15, as said below
- slot_map: int32 [16], replicated, may hold values from 0 to 15, each once
- weights: bfloat16 [16, 2, 384, 1024], P(None, None, 'own'), may hold values from -0.3125 to 0.3125
- moment1: float32 [16, 2, 384, 1024], P(None, None, 'own', 'dp'), may hold values from -18.101934 to 18.101934
- moment2: float32 [16, 2, 384, 1024], P(None, None, 'own', 'dp'), may hold values from 0.1024 to 3.072
Outputs:
- predicted: bfloat16 [8192, 384], P(('dp', 'own'))
- new_weights: bfloat16 [16, 2, 384, 1024], P(None, None, 'own')
- new_moment1: float32 [16, 2, 384, 1024], P(None, None, 'own', 'dp')
- new_moment2: float32 [16, 2, 384, 1024], P(None, None, 'own', 'dp')
The draws below stay inside these ranges and needn't reach their ends.
Inputs may be any that keep to these rules, and one draw needn't show every extreme that they name: `row_insertion`: device d (dp index times the size of own plus own index) holds rows d * 256 to (d + 1) * 256 - 1; their insertions are all in row d of touched; at most 128 rows of one device name the same insertion, and on every device one insertion is named by exactly 128 rows. `touched`: each row lists 4 different insertions.
All inputs are finite; a program needn't handle non-finite values.
Results may differ from the reference program's by a relative error of at most 0.0049.
Values may be sent and summed in bfloat16 or wider, within the bound.
No kernel may reach another device: no remote copies, remote signals or barrier semaphores. Data moves between devices by JAX's collectives and lax.ppermute only.
A program may use at most 128 MiB of HBM per device.

```python
import math
import jax
import jax.numpy as jnp
from jax import lax

SITES = 384
WIDTH = 1024
ROWS_DEV = 256
TOUCH = 4
CAP = 128
INSERTIONS = 16
ROWS = 8192
ROWS_INS = 512


def listed_insertions(key):
    base = jax.random.fold_in(key, 11)
    number = ROWS // ROWS_DEV
    subkeys = jax.random.split(base, number)

    def pick(subkey):
        return jax.random.permutation(subkey, INSERTIONS)[:TOUCH]
    return jax.vmap(pick)(subkeys).astype(jnp.int32)


def draw_touched(key, part):
    return listed_insertions(key)


def draw_row_insertion(key, part):
    listed = listed_insertions(key)
    number = listed.shape[0]
    subkeys = jax.random.split(jax.random.fold_in(key, 23), number)

    def device_rows(subkey, picks):
        key_cut, key_rot, key_mix = jax.random.split(subkey, 3)
        cut_points = jax.random.randint(key_cut, (2,), 1, CAP)
        lower = jnp.min(cut_points)
        upper = jnp.max(cut_points)
        counts = jnp.stack([jnp.array(CAP, jnp.int32), lower, upper - lower, CAP - upper]).astype(jnp.int32)
        rotation = jax.random.randint(key_rot, (), 0, 4)
        counts = counts[(jnp.arange(4) - rotation) % 4]
        bounds = jnp.cumsum(counts)
        slot_rows = jnp.sum((jnp.arange(ROWS_DEV)[:, None] >= bounds[None, :]).astype(jnp.int32), axis=1)
        shuffle = jax.random.permutation(key_mix, ROWS_DEV)
        return picks[slot_rows[shuffle]]
    return jax.vmap(device_rows)(subkeys, listed).reshape(-1).astype(jnp.int32)


def block_scale(rng, dims, pieces, least, top_value):
    loudness, own = 1.0, jax.random.fold_in(rng, 6)
    for position, shards_of in pieces:
        steps = jnp.exp(jax.random.uniform(jax.random.fold_in(own, position), (shards_of,), jnp.float32, least / len(pieces), top_value / len(pieces)))
        loudness = loudness * jnp.repeat(steps, dims[position] // shards_of).reshape([-1 if axis == position else 1 for axis in range(len(dims))])
    return loudness


def noise(rng, extent, scale, limit, cuts=(), kind=jnp.bfloat16):
    loudness = block_scale(rng, extent, cuts, -0.22, 0.18) if cuts else 1.0
    values = jax.random.normal(rng, extent, jnp.float32) * scale * loudness
    return jnp.minimum(jnp.maximum(values, -limit), limit).astype(kind)


def setup_inputs(seed: int = 0) -> dict:
    streams_of = jax.random.split(jax.random.key(seed), 9)
    return {
        "signals": noise(streams_of[0], (ROWS, SITES), 1.0, 6.0, ((0, 32),)),
        "cotangent": noise(streams_of[1], (ROWS, SITES), 1.0, 6.0, ((0, 32),)),
        "row_insertion": draw_row_insertion(jax.random.fold_in(streams_of[8], 71), 0),
        "touched": draw_touched(jax.random.fold_in(streams_of[8], 71), 0),
        "slot_map": jax.random.permutation(streams_of[4], INSERTIONS).astype(jnp.int32),
        "weights": noise(streams_of[5], (INSERTIONS, 2, SITES, WIDTH), SITES ** -0.5, 0.3125, ((2, 8),)),
        "moment1": noise(streams_of[6], (INSERTIONS, 2, SITES, WIDTH), (0.2 * ROWS_INS ** 0.5), 18.101934, ((2, 8), (3, 4)), jnp.float32),
        "moment2": jnp.clip(jnp.exp(math.log(3.072) - 3.4011974 * jax.random.uniform(streams_of[7], (INSERTIONS, 2, SITES, WIDTH), jnp.float32) ** block_scale(streams_of[7], (INSERTIONS, 2, SITES, WIDTH), ((2, 8), (3, 4)), -0.2, 0.2)), 0.1024, 3.072),
    }


gelu_coef = math.sqrt(2.0 / math.pi)
cubic_coef = 0.044715
learn_rate = 0.01
highest = lax.Precision.HIGHEST

def gelu_parts(preact):
    tanh_input = gelu_coef * (preact + cubic_coef * preact * preact * preact)
    tangent = jnp.tanh(tanh_input)
    gelu_val = 0.5 * preact * (1.0 + tangent)
    slopes = 0.5 * (1.0 + tangent) + 0.5 * preact * (1.0 - tangent * tangent) * gelu_coef * (1.0 + 3.0 * cubic_coef * preact * preact)
    return (gelu_val, slopes)

def dispatch(row_ids, listed):
    match_table = (row_ids[:, None] == listed[None, :]).astype(jnp.int32)
    running = jnp.cumsum(match_table, axis=0) - 1
    slot_of = lax.optimization_barrier(jnp.sum(match_table * jnp.arange(listed.shape[0], dtype=jnp.int32)[None, :], axis=1))
    within = lax.optimization_barrier(jnp.sum(match_table * running, axis=1))
    return (slot_of * CAP + within).astype(jnp.int32)

def adam_step(params, moment_one, moment_two, gradient):
    moment_one = 0.9 * moment_one + 0.1 * gradient
    moment_two = 0.999 * moment_two + 0.001 * gradient * gradient
    correct_one = 1.0 - 0.9 ** 10
    correct_two = 1.0 - 0.999 ** 10
    updated = params - learn_rate * (moment_one / correct_one) / (jnp.sqrt(moment_two / correct_two) + 1e-08)
    return (updated.astype(jnp.bfloat16), moment_one, moment_two)

def reference(signals, cotangent, row_insertion, touched, slot_map, weights, moment1, moment2):
    blocks = weights[slot_map]
    number = touched.shape[0]
    sig_dev = signals.reshape(number, ROWS_DEV, SITES)
    cot_dev = cotangent.reshape(number, ROWS_DEV, SITES)
    ids_dev = row_insertion.reshape(number, ROWS_DEV)

    def device_step(totals, inputs):
        sig_rows, cot_rows, row_ids, listed = inputs
        places = dispatch(row_ids, listed)
        stacked = jnp.zeros((TOUCH * CAP, 2 * SITES), signals.dtype).at[places].set(jnp.concatenate([sig_rows, cot_rows], axis=1))
        stacked = stacked.reshape(TOUCH, CAP, 2 * SITES).astype(jnp.float32)
        sig_slots = stacked[:, :, :SITES]
        cot_slots = stacked[:, :, SITES:]
        chosen = blocks[listed].astype(jnp.float32)
        read_in = chosen[:, 0]
        read_out = chosen[:, 1]
        preact = jnp.einsum('kcs,ksw->kcw', sig_slots, read_in, precision=highest)
        gelu_val, slopes = gelu_parts(preact)
        hidden = lax.optimization_barrier(gelu_val.astype(jnp.bfloat16)).astype(jnp.float32)
        pred_slots = jnp.einsum('kcw,ksw->kcs', hidden, read_out, precision=highest).astype(jnp.bfloat16)
        back_hidden = jnp.einsum('kcs,ksw->kcw', cot_slots, read_out, precision=highest)
        back_pre = lax.optimization_barrier((back_hidden * slopes).astype(jnp.bfloat16)).astype(jnp.float32)
        grad_in = jnp.einsum('kcs,kcw->ksw', sig_slots, back_pre, precision=highest)
        grad_out = jnp.einsum('kcs,kcw->ksw', cot_slots, hidden, precision=highest)
        totals = totals.at[listed].add(jnp.stack([grad_in, grad_out], axis=1))
        predicted = pred_slots.reshape(TOUCH * CAP, SITES)[places]
        return (totals, predicted)
    totals, predicted = lax.scan(device_step, jnp.zeros(weights.shape, jnp.float32), (sig_dev, cot_dev, ids_dev, touched))
    gradient = jnp.zeros(weights.shape, jnp.float32).at[slot_map].set(totals)
    new_weights, new_moment1, new_moment2 = adam_step(weights.astype(jnp.float32), moment1, moment2, gradient)
    return (predicted.reshape(-1, SITES), new_weights, new_moment1, new_moment2)
```

```python
import math

import jax
import jax.numpy as jnp
from jax import lax
from jax.experimental import pallas as pl
from jax.experimental.pallas import tpu as pltpu
from jax.sharding import PartitionSpec as P

SITES = 384
CAP = 128
CHUNKS = 1
ID_ROWS = 16
VMEM_BYTES = 56 * 2**20

gelu_coef = math.sqrt(2.0 / math.pi)
cubic_coef = 0.044715
learn_rate = 0.01


def gelu_parts(preact):
    tanh_input = gelu_coef * (preact + cubic_coef * preact * preact * preact)
    tangent = jnp.tanh(tanh_input)
    gelu_val = 0.5 * preact * (1.0 + tangent)
    slopes = 0.5 * (1.0 + tangent) + 0.5 * preact * (1.0 - tangent * tangent) * gelu_coef * (
        1.0 + 3.0 * cubic_coef * preact * preact
    )
    return (gelu_val, slopes)


def params():
    return pltpu.CompilerParams(vmem_limit_bytes=VMEM_BYTES)


def vmem():
    return pl.BlockSpec(memory_space=pltpu.VMEM)


def smem():
    return pl.BlockSpec(memory_space=pltpu.SMEM)


def pack_rows(ids, signals, cotangent):
    rows = signals.shape[0]

    def body(ids_ref, sig_ref, cot_ref, out_ref, perm_ref):
        ids_row = ids_ref[...].astype(jnp.float32)
        lane_ids = jnp.broadcast_to(ids_row, (rows, rows))
        same = lane_ids == lane_ids.T
        count = jnp.sum(same.astype(jnp.float32), axis=0, keepdims=True)
        full = jnp.max(jnp.where(count == CAP, ids_row, -1.0), axis=1, keepdims=True)
        chosen = ids_row == full
        from_row = lax.broadcasted_iota(jnp.int32, (rows, rows), 0)
        to_lane = lax.broadcasted_iota(jnp.int32, (rows, rows), 1)
        upto = (from_row <= to_lane).astype(jnp.bfloat16)
        ahead = jnp.dot(
            jnp.broadcast_to(chosen.astype(jnp.float32), (8, rows)).astype(jnp.bfloat16),
            upto,
            preferred_element_type=jnp.float32,
        )[:1].astype(jnp.int32)
        place = jnp.where(chosen, ahead - 1, CAP + to_lane[:1] - ahead)
        perm = (from_row == place).astype(jnp.float32).astype(jnp.bfloat16)
        perm_ref[...] = perm
        out_ref[:rows] = jnp.dot(perm, sig_ref[...], preferred_element_type=jnp.float32).astype(
            jnp.bfloat16
        )
        out_ref[rows : 2 * rows] = jnp.dot(
            perm, cot_ref[...], preferred_element_type=jnp.float32
        ).astype(jnp.bfloat16)
        sorted_ids = lax.dot_general(
            jnp.broadcast_to(ids_row, (ID_ROWS, rows)).astype(jnp.bfloat16),
            perm,
            (((1,), (1,)), ((), ())),
            preferred_element_type=jnp.float32,
        ).astype(jnp.bfloat16)
        out_ref[2 * rows :, :rows] = sorted_ids
        out_ref[2 * rows :, rows:] = jnp.zeros((ID_ROWS, SITES - rows), jnp.bfloat16)

    return pl.pallas_call(
        body,
        out_shape=(
            jax.ShapeDtypeStruct((2 * rows + ID_ROWS, SITES), jnp.bfloat16),
            jax.ShapeDtypeStruct((rows, rows), jnp.bfloat16),
        ),
        in_specs=[vmem(), vmem(), vmem()],
        out_specs=(vmem(), vmem()),
        compiler_params=params(),
        name="pack_rows",
    )(ids, signals, cotangent)


def local_grads(pos, touched, slot_map, mine, other, blocks, n_own, half, piece, width):
    planes = mine.shape[0]
    rows = (mine.shape[1] - ID_ROWS) // 2
    touch = touched.shape[1]
    aligned = piece % 16 == 0
    part = half // CHUNKS

    def body(pos_ref, touched_ref, slot_ref, mine_ref, other_ref, blocks_ref, *rest):
        pred_mine, pred_other = rest[:2]
        grad_refs = rest[2 : 2 + CHUNKS]
        rest = rest[2 + CHUNKS :]
        if aligned:
            acc, id_cols, held, sems = rest
            copies = [
                pltpu.make_async_copy(
                    blocks_ref.at[s], held.at[:, :, pl.ds(s * piece, piece), :], sems.at[s]
                )
                for s in range(n_own)
            ]
            for copy in copies:
                copy.start()
        else:
            acc, id_cols = rest
            held = blocks_ref

        def clear(e, _):
            acc[e] = jnp.zeros(acc.shape[1:], jnp.float32)
            return 0

        lax.fori_loop(0, half, clear, 0)
        pred_mine[...] = jnp.zeros_like(pred_mine)
        pred_other[...] = jnp.zeros_like(pred_other)
        own_at = pos_ref[1]
        core = lax.rem(own_at, 2)
        partner = own_at + 1 - 2 * core
        for which, ref in enumerate((mine_ref, other_ref)):
            for p in range(planes):
                ids_row = ref[p, 2 * rows :, :rows][:1].astype(jnp.float32)
                id_cols[which, p] = jnp.broadcast_to(ids_row, (128, rows)).T
        if aligned:
            for copy in copies:
                copy.wait()
        for which, (ref, pred) in enumerate(((mine_ref, pred_mine), (other_ref, pred_other))):
            source = own_at if which == 0 else partner

            def plane(p, _, which=which, ref=ref, pred=pred, source=source):
                full = jnp.max(id_cols[which, p, :8, :]).astype(jnp.int32)

                def task(j, _):
                    insertion = jnp.where(
                        j == 0, full, touched_ref[p * n_own + source, jnp.maximum(j - 1, 0)]
                    )
                    stored = slot_ref[insertion]
                    here = stored // half == core
                    here = here & ((j == 0) | (insertion != full))
                    first = pl.multiple_of(jnp.where(j == 0, 0, CAP), CAP)

                    @pl.when(here)
                    def _():
                        e = lax.rem(stored, half)
                        keep = (
                            (id_cols[which, p, pl.ds(first, CAP), :] == insertion.astype(jnp.float32))
                            .astype(jnp.float32)
                            .astype(jnp.bfloat16)
                        )
                        keep = jnp.concatenate([keep] * (SITES // 128), axis=1)
                        sig = ref[p, pl.ds(first, CAP), :] * keep
                        cot = ref[p, pl.ds(rows + first, CAP), :] * keep
                        read_in = held[e, 0]
                        read_out = held[e, 1]
                        preact = jnp.dot(sig, read_in, preferred_element_type=jnp.float32)
                        back_hidden = jnp.dot(cot, read_out, preferred_element_type=jnp.float32)
                        gelu_val, slopes = gelu_parts(preact)
                        hidden = gelu_val.astype(jnp.bfloat16)
                        back_pre = (back_hidden * slopes).astype(jnp.bfloat16)
                        pred[p, pl.ds(first, CAP), :] += lax.dot_general(
                            hidden,
                            read_out,
                            (((1,), (1,)), ((), ())),
                            preferred_element_type=jnp.float32,
                        ).astype(jnp.bfloat16)
                        acc[e, 0] += lax.dot_general(
                            sig,
                            back_pre,
                            (((0,), (0,)), ((), ())),
                            preferred_element_type=jnp.float32,
                        )
                        acc[e, 1] += lax.dot_general(
                            cot,
                            hidden,
                            (((0,), (0,)), ((), ())),
                            preferred_element_type=jnp.float32,
                        )

                    return 0

                return lax.fori_loop(0, touch + 1, task, 0)

            lax.fori_loop(0, planes, plane, 0)

        for chunk, grad_ref in enumerate(grad_refs):

            def write(e, _, chunk=chunk, grad_ref=grad_ref):
                if aligned:
                    for s in range(n_own):
                        grad_ref[s, e] = acc[
                            chunk * part + e, :, s * piece : (s + 1) * piece, :
                        ].astype(jnp.bfloat16)
                else:
                    grad_ref[e] = acc[chunk * part + e].astype(jnp.bfloat16)
                return 0

            lax.fori_loop(0, part, write, 0)

    grad_shape = (n_own, part, 2, piece, width) if aligned else (part, 2, SITES, width)
    pred_shape = jax.ShapeDtypeStruct((planes, rows, SITES), jnp.bfloat16)
    scratch = [
        pltpu.VMEM((half, 2, SITES, width), jnp.float32),
        pltpu.VMEM((2, planes, rows, 128), jnp.float32),
    ]
    if aligned:
        scratch += [
            pltpu.VMEM((half, 2, SITES, width), jnp.bfloat16),
            pltpu.SemaphoreType.DMA((n_own,)),
        ]
    else:
        blocks = blocks.transpose(1, 2, 0, 3, 4).reshape(half, 2, SITES, width)
    found = pl.pallas_call(
        body,
        out_shape=(pred_shape, pred_shape)
        + (jax.ShapeDtypeStruct(grad_shape, jnp.bfloat16),) * CHUNKS,
        in_specs=[smem(), smem(), smem(), vmem(), vmem()]
        + [pl.BlockSpec(memory_space=pl.ANY) if aligned else vmem()],
        out_specs=(vmem(),) * (2 + CHUNKS),
        scratch_shapes=scratch,
        compiler_params=params(),
        name="local_grads",
    )(pos, touched, slot_map, mine, other, blocks)
    grads = found[2:]
    if not aligned:
        grads = [
            g.reshape(part, 2, n_own, piece, width).transpose(2, 0, 1, 3, 4) for g in grads
        ]
    return found[0], found[1], grads


def adam(pos, arrived, weights, moment1, moment2, half):
    n_own, part, _, piece, width = arrived.shape
    chips = n_own // 2
    blocks = arrived.reshape(chips, 2, part, 2, piece, width)
    correct_one = 1.0 - 0.9**10
    correct_two = 1.0 - 0.999**10

    def body(pos_ref, arrived_ref, w_ref, m1_ref, m2_ref, new_w, new_m1, new_m2):
        gradient = arrived_ref[0, 0].astype(jnp.float32)
        for s in range(1, chips):
            gradient = gradient + arrived_ref[s, 0].astype(jnp.float32)
        one = 0.9 * m1_ref[...] + 0.1 * gradient
        two = 0.999 * m2_ref[...] + 0.001 * gradient * gradient
        new_m1[...] = one
        new_m2[...] = two
        updated = w_ref[...].astype(jnp.float32) - learn_rate * (one / correct_one) / (
            jnp.sqrt(two / correct_two) + 1e-08
        )
        new_w[...] = updated.astype(jnp.bfloat16)

    def plain(c, i, pos_ref):
        return (c * half + i, 0, 0, 0)

    small = pl.BlockSpec((1, 2, piece, width), plain)
    grid_spec = pltpu.PrefetchScalarGridSpec(
        num_scalar_prefetch=1,
        grid=(2, part),
        in_specs=[
            pl.BlockSpec((chips, 1, 1, 2, piece, width), lambda c, i, pos_ref: (0, c, i, 0, 0, 0)),
            pl.BlockSpec(
                (1, 2, piece, width), lambda c, i, pos_ref: (c * half + i, 0, 0, pos_ref[0])
            ),
            small,
            small,
        ],
        out_specs=(small, small, small),
    )

    def wrapped(pos_ref, arrived_ref, *refs):
        body(pos_ref, arrived_ref.at[:, :, 0], *[r.at[0] for r in refs])

    return pl.pallas_call(
        wrapped,
        out_shape=(
            jax.ShapeDtypeStruct(moment1.shape, jnp.bfloat16),
            jax.ShapeDtypeStruct(moment1.shape, jnp.float32),
            jax.ShapeDtypeStruct(moment1.shape, jnp.float32),
        ),
        grid_spec=grid_spec,
        compiler_params=params(),
        name="adam_step",
    )(pos, blocks, weights, moment1, moment2)


def finish_predicted(perm, parts):
    def body(perm_ref, *refs):
        total = refs[0][...].astype(jnp.float32)
        for ref in refs[1:-1]:
            total = total + ref[...].astype(jnp.float32)
        refs[-1][...] = lax.dot_general(
            perm_ref[...],
            total.astype(jnp.bfloat16),
            (((0,), (0,)), ((), ())),
            preferred_element_type=jnp.float32,
        ).astype(jnp.bfloat16)

    return pl.pallas_call(
        body,
        out_shape=jax.ShapeDtypeStruct(parts[0].shape, jnp.bfloat16),
        in_specs=[vmem()] * (1 + len(parts)),
        out_specs=vmem(),
        compiler_params=params(),
        name="finish_predicted",
    )(perm, *parts)


def shards(signals, cotangent, row_insertion, touched, slot_map, weights, moment1, moment2):
    n_own = lax.axis_size("own")
    n_dp = lax.axis_size("dp")
    dp_at = lax.axis_index("dp")
    own_at = lax.axis_index("own")
    number, _, piece, _ = weights.shape
    width = moment1.shape[3]
    half = number // 2
    rows = signals.shape[0]
    pos = jnp.stack([dp_at, own_at]).astype(jnp.int32)
    swap = [(o, o ^ 1) for o in range(n_own)]

    column = lax.dynamic_slice_in_dim(weights, dp_at * width, width, 3)
    outgoing = jnp.broadcast_to(
        column.reshape(1, 2, half, 2, piece, width), (n_own // 2, 2, half, 2, piece, width)
    ).reshape(n_own, half, 2, piece, width)
    blocks = lax.all_to_all(outgoing, "own", split_axis=0, concat_axis=0, tiled=True)

    packed, perm = pack_rows(row_insertion.reshape(1, rows), signals, cotangent)
    mine = lax.all_gather(packed, "dp", axis=0)
    other = lax.ppermute(mine, "own", swap)

    pred_mine, pred_other, grads = local_grads(
        pos, touched, slot_map, mine, other, blocks, n_own, half, piece, width
    )
    arrived = lax.all_to_all(grads[0], "own", split_axis=0, concat_axis=0, tiled=True)
    fresh, new_moment1, new_moment2 = adam(pos, arrived, weights, moment1, moment2, half)
    new_weights = lax.all_gather(fresh, "dp", axis=3, tiled=True)

    pred_part = pred_mine + lax.ppermute(pred_other, "own", swap)
    parts = [lax.dynamic_index_in_dim(pred_part, dp_at, 0, keepdims=False)]
    for shift in range(1, n_dp):
        block = lax.dynamic_index_in_dim(pred_part, lax.rem(dp_at + shift, n_dp), 0, keepdims=False)
        parts.append(lax.ppermute(block, "dp", [(d, (d + shift) % n_dp) for d in range(n_dp)]))
    predicted = finish_predicted(perm, parts)
    return (predicted, new_weights, new_moment1, new_moment2)


def solution(mesh):
    in_specs = (
        P(("dp", "own"), None),
        P(("dp", "own"), None),
        P(("dp", "own")),
        P(),
        P(),
        P(None, None, "own", None),
        P(None, None, "own", "dp"),
        P(None, None, "own", "dp"),
    )
    out_specs = (
        P(("dp", "own"), None),
        P(None, None, "own", None),
        P(None, None, "own", "dp"),
        P(None, None, "own", "dp"),
    )
    return jax.shard_map(shards, mesh=mesh, in_specs=in_specs, out_specs=out_specs, check_vma=False)
```

```python
import math

import jax
import jax.numpy as jnp
from jax import lax
from jax.experimental import pallas as pl
from jax.experimental.pallas import tpu as pltpu
from jax.sharding import PartitionSpec as P

SITES = 384
CAP = 128
CHUNK_PARTS = (2, 2, 2, 2)
ID_ROWS = 16
VMEM_BYTES = 56 * 2**20

gelu_coef = math.sqrt(2.0 / math.pi)
cubic_coef = 0.044715
learn_rate = 0.01


def gelu_parts(preact):
    tanh_input = gelu_coef * (preact + cubic_coef * preact * preact * preact)
    tangent = jnp.tanh(tanh_input)
    gelu_val = 0.5 * preact * (1.0 + tangent)
    slopes = 0.5 * (1.0 + tangent) + 0.5 * preact * (1.0 - tangent * tangent) * gelu_coef * (
        1.0 + 3.0 * cubic_coef * preact * preact
    )
    return (gelu_val, slopes)


def params():
    return pltpu.CompilerParams(vmem_limit_bytes=VMEM_BYTES)


def vmem():
    return pl.BlockSpec(memory_space=pltpu.VMEM)


def smem():
    return pl.BlockSpec(memory_space=pltpu.SMEM)


def pack_rows(ids, signals, cotangent):
    rows = signals.shape[0]

    def body(ids_ref, sig_ref, cot_ref, out_ref, perm_ref):
        ids_row = ids_ref[...].astype(jnp.float32)
        lane_ids = jnp.broadcast_to(ids_row, (rows, rows))
        same = lane_ids == lane_ids.T
        count = jnp.sum(same.astype(jnp.float32), axis=0, keepdims=True)
        full = jnp.max(jnp.where(count == CAP, ids_row, -1.0), axis=1, keepdims=True)
        chosen = ids_row == full
        from_row = lax.broadcasted_iota(jnp.int32, (rows, rows), 0)
        to_lane = lax.broadcasted_iota(jnp.int32, (rows, rows), 1)
        upto = (from_row <= to_lane).astype(jnp.bfloat16)
        ahead = jnp.dot(
            jnp.broadcast_to(chosen.astype(jnp.float32), (8, rows)).astype(jnp.bfloat16),
            upto,
            preferred_element_type=jnp.float32,
        )[:1].astype(jnp.int32)
        place = jnp.where(chosen, ahead - 1, CAP + to_lane[:1] - ahead)
        perm = (from_row == place).astype(jnp.float32).astype(jnp.bfloat16)
        perm_ref[...] = perm
        out_ref[:rows] = jnp.dot(perm, sig_ref[...], preferred_element_type=jnp.float32).astype(
            jnp.bfloat16
        )
        out_ref[rows : 2 * rows] = jnp.dot(
            perm, cot_ref[...], preferred_element_type=jnp.float32
        ).astype(jnp.bfloat16)
        sorted_ids = lax.dot_general(
            jnp.broadcast_to(ids_row, (ID_ROWS, rows)).astype(jnp.bfloat16),
            perm,
            (((1,), (1,)), ((), ())),
            preferred_element_type=jnp.float32,
        ).astype(jnp.bfloat16)
        out_ref[2 * rows :, :rows] = sorted_ids
        out_ref[2 * rows :, rows:] = jnp.zeros((ID_ROWS, SITES - rows), jnp.bfloat16)

    return pl.pallas_call(
        body,
        out_shape=(
            jax.ShapeDtypeStruct((2 * rows + ID_ROWS, SITES), jnp.bfloat16),
            jax.ShapeDtypeStruct((rows, rows), jnp.bfloat16),
        ),
        in_specs=[vmem(), vmem(), vmem()],
        out_specs=(vmem(), vmem()),
        compiler_params=params(),
        name="pack_rows",
    )(ids, signals, cotangent)


def local_grads(pos, touched, slot_map, mine, other, blocks, sizes, piece, width):
    planes = mine.shape[0]
    rows = (mine.shape[1] - ID_ROWS) // 2
    touch = touched.shape[1]
    n_own = len(blocks)
    half = sum(sizes)
    aligned = piece % 16 == 0
    starts = [sum(sizes[:i]) for i in range(len(sizes))]
    n_blocks = n_own if aligned else 1
    n_grads = len(sizes) * n_blocks

    def body(pos_ref, touched_ref, slot_ref, mine_ref, other_ref, *rest):
        block_refs = rest[:n_blocks]
        pred_refs = rest[n_blocks : n_blocks + 2]
        grad_refs = rest[n_blocks + 2 : n_blocks + 2 + n_grads]
        acc, id_cols, held, sorted_rows, pred, full_of, tasks, sems = rest[n_blocks + 2 + n_grads :]
        own_at = pos_ref[1]
        core = lax.rem(own_at, 2)
        partner = own_at + 1 - 2 * core
        row_copies = [
            pltpu.make_async_copy(
                ref, sorted_rows.at[pl.ds(which * planes, planes)], sems.at[which]
            )
            for which, ref in enumerate((mine_ref, other_ref))
        ]
        if aligned:
            block_copies = [
                pltpu.make_async_copy(
                    ref,
                    held.at[
                        :, :, pl.ds(pl.multiple_of((own_at ^ j) * piece, 16), piece), :
                    ],
                    sems.at[2 + j],
                )
                for j, ref in enumerate(block_refs)
            ]
        else:
            block_copies = [pltpu.make_async_copy(block_refs[0], held, sems.at[2])]
        for copy in row_copies + block_copies:
            copy.start()

        def clear(e, _):
            acc[e] = jnp.zeros(acc.shape[1:], jnp.float32)
            return 0

        lax.fori_loop(0, half, clear, 0)
        pred[...] = jnp.zeros_like(pred)
        for copy in row_copies:
            copy.wait()
        for source in range(2 * planes):
            ids_row = sorted_rows[source, 2 * rows :, :rows][:1].astype(jnp.float32)
            id_cols[source] = jnp.broadcast_to(ids_row, (128, rows)).T
            full_of[source] = jnp.max(ids_row[:, :128]).astype(jnp.int32)

        def listing(t, count):
            source = t // (touch + 1)
            j = t - source * (touch + 1)
            which = source // planes
            device = (source - which * planes) * n_own + jnp.where(which == 0, own_at, partner)
            full = full_of[source]
            insertion = jnp.where(j == 0, full, touched_ref[device, jnp.maximum(j - 1, 0)])
            stored = slot_ref[insertion]
            here = (stored // half == core) & ((j == 0) | (insertion != full))
            tasks[0, count] = source
            tasks[1, count] = jnp.where(j == 0, 0, CAP)
            tasks[2, count] = insertion
            tasks[3, count] = stored - core * half
            return count + here.astype(jnp.int32)

        count = lax.fori_loop(0, 2 * planes * (touch + 1), listing, 0)
        tasks[0, count] = 0
        tasks[1, count] = 0
        tasks[2, count] = -1
        tasks[3, count] = 0
        for copy in block_copies:
            copy.wait()

        def pair(i, _):
            loaded = []
            for u in range(2):
                source, insertion, e = tasks[0, 2 * i + u], tasks[2, 2 * i + u], tasks[3, 2 * i + u]
                first = pl.multiple_of(tasks[1, 2 * i + u], CAP)
                keep = (
                    (id_cols[source, pl.ds(first, CAP), :] == insertion.astype(jnp.float32))
                    .astype(jnp.float32)
                    .astype(jnp.bfloat16)
                )
                keep = jnp.concatenate([keep] * (SITES // 128), axis=1)
                sig = sorted_rows[source, pl.ds(first, CAP), :] * keep
                cot = sorted_rows[source, pl.ds(rows + first, CAP), :] * keep
                loaded.append((source, first, e, sig, cot))
            found = []
            for source, first, e, sig, cot in loaded:
                read_out = held[e, 1]
                preact = jnp.dot(sig, held[e, 0], preferred_element_type=jnp.float32)
                back_hidden = jnp.dot(cot, read_out, preferred_element_type=jnp.float32)
                gelu_val, slopes = gelu_parts(preact)
                hidden = gelu_val.astype(jnp.bfloat16)
                back_pre = (back_hidden * slopes).astype(jnp.bfloat16)
                part = lax.dot_general(
                    hidden, read_out, (((1,), (1,)), ((), ())), preferred_element_type=jnp.float32
                ).astype(jnp.bfloat16)
                grad_in = lax.dot_general(
                    sig, back_pre, (((0,), (0,)), ((), ())), preferred_element_type=jnp.float32
                )
                grad_out = lax.dot_general(
                    cot, hidden, (((0,), (0,)), ((), ())), preferred_element_type=jnp.float32
                )
                found.append((part, grad_in, grad_out))
            for (source, first, e, _, _), (part, grad_in, grad_out) in zip(loaded, found):
                pred[source, pl.ds(first, CAP), :] += part
                acc[e, 0] += grad_in
                acc[e, 1] += grad_out
            return 0

        lax.fori_loop(0, (count + 1) // 2, pair, 0)
        for which, ref in enumerate(pred_refs):
            ref[...] = pred[which * planes : (which + 1) * planes]
        for chunk, (start, size) in enumerate(zip(starts, sizes)):
            for j in range(n_blocks):
                ref = grad_refs[chunk * n_blocks + j]

                def write(e, _, start=start, ref=ref, j=j):
                    if aligned:
                        ref[e] = acc[
                            start + e,
                            :,
                            pl.ds(pl.multiple_of((own_at ^ j) * piece, 16), piece),
                            :,
                        ].astype(jnp.bfloat16)
                    else:
                        ref[e] = acc[start + e].astype(jnp.bfloat16)
                    return 0

                lax.fori_loop(0, size, write, 0)

    pred_shape = jax.ShapeDtypeStruct((planes, rows, SITES), jnp.bfloat16)
    grad_rows = piece if aligned else SITES
    grad_shapes = [
        jax.ShapeDtypeStruct((size, 2, grad_rows, width), jnp.bfloat16)
        for size in sizes
        for _ in range(n_blocks)
    ]
    most = 2 * planes * (touch + 1)
    scratch = [
        pltpu.VMEM((half, 2, SITES, width), jnp.float32),
        pltpu.VMEM((2 * planes, rows, 128), jnp.float32),
        pltpu.VMEM((half, 2, SITES, width), jnp.bfloat16),
        pltpu.VMEM((2 * planes,) + mine.shape[1:], jnp.bfloat16),
        pltpu.VMEM((2 * planes, rows, SITES), jnp.bfloat16),
        pltpu.SMEM((2 * planes,), jnp.int32),
        pltpu.SMEM((4, most + 1), jnp.int32),
        pltpu.SemaphoreType.DMA((2 + n_blocks,)),
    ]
    own_at = pos[1]
    if not aligned:
        order = own_at ^ jnp.arange(n_own, dtype=jnp.int32)
        stacked = jnp.take(jnp.stack(blocks), order, axis=0)
        blocks = [stacked.transpose(1, 2, 0, 3, 4).reshape(half, 2, SITES, width)]
    anywhere = pl.BlockSpec(memory_space=pl.ANY)
    found = pl.pallas_call(
        body,
        out_shape=[pred_shape, pred_shape] + grad_shapes,
        in_specs=[smem(), smem(), smem()] + [anywhere] * (2 + n_blocks),
        out_specs=[vmem()] * (2 + n_grads),
        scratch_shapes=scratch,
        compiler_params=params(),
        name="local_grads",
    )(pos, touched, slot_map, mine, other, *blocks)
    grads = []
    for chunk in range(len(sizes)):
        outs = found[2 + chunk * n_blocks : 2 + (chunk + 1) * n_blocks]
        if not aligned:
            outs = [
                lax.dynamic_slice_in_dim(outs[0], (own_at ^ j) * piece, piece, 2)
                for j in range(n_own)
            ]
        grads.append(list(outs))
    return found[0], found[1], grads


def adam(pos, arrived, weights, moment1, moment2, start, before):
    n_own = len(arrived)
    size, _, piece, width = arrived[0].shape
    number = weights.shape[0]
    half = number // 2
    correct_one = 1.0 - 0.9**10
    correct_two = 1.0 - 0.999**10

    def body(pos_ref, *refs):
        grad_refs = refs[:n_own]
        w_ref, m1_ref, m2_ref = refs[n_own : n_own + 3]
        new_w, new_m1, new_m2 = refs[-3:]

        def step(chosen):
            gradient = chosen[0][...].astype(jnp.float32)
            for ref in chosen[1:]:
                gradient = gradient + ref[...].astype(jnp.float32)
            one = 0.9 * m1_ref[...] + 0.1 * gradient
            two = 0.999 * m2_ref[...] + 0.001 * gradient * gradient
            new_m1[...] = one
            new_m2[...] = two
            updated = w_ref[...].astype(jnp.float32) - learn_rate * (one / correct_one) / (
                jnp.sqrt(two / correct_two) + 1e-08
            )
            new_w[0] = updated.astype(jnp.bfloat16)

        pl.when(pl.program_id(0) == 0)(lambda: step(grad_refs[0::2]))
        pl.when(pl.program_id(0) == 1)(lambda: step(grad_refs[1::2]))

    def which(g, pos_ref):
        return lax.rem(pos_ref[1] + g, 2)

    per = math.gcd(size, start) if start else size
    per = math.gcd(per, half)

    def place(g, i, pos_ref):
        return (which(g, pos_ref) * (half // per) + start // per + i, 0, 0, 0)

    small = pl.BlockSpec((per, 2, piece, width), place)
    grad = pl.BlockSpec((per, 2, piece, width), lambda g, i, pos_ref: (i, 0, 0, 0))
    anywhere = pl.BlockSpec(memory_space=pl.ANY)
    grid_spec = pltpu.PrefetchScalarGridSpec(
        num_scalar_prefetch=1,
        grid=(2, size // per),
        in_specs=[grad] * n_own
        + [
            pl.BlockSpec(
                (per, 2, piece, width),
                lambda g, i, pos_ref: place(g, i, pos_ref)[:3] + (pos_ref[0],),
            ),
            small,
            small,
        ]
        + [anywhere] * len(before),
        out_specs=[
            pl.BlockSpec(
                (1, per, 2, piece, width),
                lambda g, i, pos_ref: (which(g, pos_ref), i, 0, 0, 0),
            ),
            small,
            small,
        ],
    )
    return pl.pallas_call(
        body,
        out_shape=[
            jax.ShapeDtypeStruct((2, size, 2, piece, width), jnp.bfloat16),
            jax.ShapeDtypeStruct(moment1.shape, jnp.float32),
            jax.ShapeDtypeStruct(moment1.shape, jnp.float32),
        ],
        grid_spec=grid_spec,
        input_output_aliases={1 + n_own + 3 + i: 1 + i for i in range(len(before))},
        compiler_params=params(),
        name="adam_step",
    )(pos, *arrived, weights, moment1, moment2, *before)


def place_weights(chunk, start, half, before):
    _, size, _, piece, full = chunk.shape

    def body(chunk_ref, *refs):
        out_ref, sems = refs[-2:]
        copies = [
            pltpu.make_async_copy(
                chunk_ref.at[h], out_ref.at[pl.ds(h * half + start, size)], sems.at[h]
            )
            for h in range(2)
        ]
        for copy in copies:
            copy.start()
        for copy in copies:
            copy.wait()

    anywhere = pl.BlockSpec(memory_space=pl.ANY)
    return pl.pallas_call(
        body,
        out_shape=jax.ShapeDtypeStruct((2 * half, 2, piece, full), jnp.bfloat16),
        in_specs=[anywhere] * (1 + len(before)),
        out_specs=anywhere,
        scratch_shapes=[pltpu.SemaphoreType.DMA((2,))],
        input_output_aliases={1: 0} if before else {},
        compiler_params=params(),
        name="place_weights",
    )(chunk, *before)


def finish_predicted(perm, parts):
    def body(perm_ref, *refs):
        total = refs[0][...].astype(jnp.float32)
        for ref in refs[1:-1]:
            total = total + ref[...].astype(jnp.float32)
        refs[-1][...] = lax.dot_general(
            perm_ref[...],
            total.astype(jnp.bfloat16),
            (((0,), (0,)), ((), ())),
            preferred_element_type=jnp.float32,
        ).astype(jnp.bfloat16)

    return pl.pallas_call(
        body,
        out_shape=jax.ShapeDtypeStruct(parts[0].shape, jnp.bfloat16),
        in_specs=[vmem()] * (1 + len(parts)),
        out_specs=vmem(),
        compiler_params=params(),
        name="finish_predicted",
    )(perm, *parts)


def shards(signals, cotangent, row_insertion, touched, slot_map, weights, moment1, moment2):
    n_own = lax.axis_size("own")
    n_dp = lax.axis_size("dp")
    dp_at = lax.axis_index("dp")
    own_at = lax.axis_index("own")
    number, _, piece, _ = weights.shape
    width = moment1.shape[3]
    half = number // 2
    rows = signals.shape[0]
    pos = jnp.stack([dp_at, own_at]).astype(jnp.int32)
    core = lax.rem(own_at, 2)
    parts_of_half = sum(CHUNK_PARTS)
    sizes = [half * part // parts_of_half for part in CHUNK_PARTS]

    def across(value, j):
        return lax.ppermute(value, "own", [(o, o ^ j) for o in range(n_own)])

    packed, perm = pack_rows(row_insertion.reshape(1, rows), signals, cotangent)
    mine = lax.all_gather(packed, "dp", axis=0)

    def column(which):
        return lax.dynamic_slice(
            weights, (which * half, 0, 0, dp_at * width), (half, 2, piece, width)
        )

    outgoing = (column(core), column(1 - core))
    blocks = [outgoing[0]] + [across(outgoing[j % 2], j) for j in range(1, n_own)]
    other = across(mine, 1)

    pred_mine, pred_other, grads = local_grads(
        pos, touched, slot_map, mine, other, blocks, sizes, piece, width
    )
    moments = []
    new_weights = []
    start = 0
    for size, chunk in zip(sizes, grads):
        arrived = [chunk[0]] + [across(chunk[j], j) for j in range(1, n_own)]
        fresh, *moments = adam(pos, arrived, weights, moment1, moment2, start, moments)
        whole = lax.all_gather(fresh, "dp", axis=4, tiled=True)
        new_weights = [place_weights(whole, start, half, new_weights)]
        start += size
    new_weights = new_weights[0]
    new_moment1, new_moment2 = moments

    pred_part = pred_mine + across(pred_other, 1)
    parts = [lax.dynamic_index_in_dim(pred_part, dp_at, 0, keepdims=False)]
    for shift in range(1, n_dp):
        block = lax.dynamic_index_in_dim(pred_part, lax.rem(dp_at + shift, n_dp), 0, keepdims=False)
        parts.append(lax.ppermute(block, "dp", [(d, (d + shift) % n_dp) for d in range(n_dp)]))
    predicted = finish_predicted(perm, parts)
    return (predicted, new_weights, new_moment1, new_moment2)


def solution(mesh):
    in_specs = (
        P(("dp", "own"), None),
        P(("dp", "own"), None),
        P(("dp", "own")),
        P(),
        P(),
        P(None, None, "own", None),
        P(None, None, "own", "dp"),
        P(None, None, "own", "dp"),
    )
    out_specs = (
        P(("dp", "own"), None),
        P(None, None, "own", None),
        P(None, None, "own", "dp"),
        P(None, None, "own", "dp"),
    )
    return jax.shard_map(shards, mesh=mesh, in_specs=in_specs, out_specs=out_specs, check_vma=False)
```

```python
import math

import jax
import jax.numpy as jnp
from jax import lax
from jax.experimental import pallas as pl
from jax.experimental.pallas import tpu as pltpu
from jax.sharding import PartitionSpec as P

SITES = 384
CAP = 128
CHUNK_PARTS = (2, 2, 2, 2)
ID_ROWS = 16
VMEM_BYTES = 56 * 2**20

gelu_coef = math.sqrt(2.0 / math.pi)
cubic_coef = 0.044715
learn_rate = 0.01


def gelu_parts(preact):
    tanh_input = gelu_coef * (preact + cubic_coef * preact * preact * preact)
    tangent = jnp.tanh(tanh_input)
    gelu_val = 0.5 * preact * (1.0 + tangent)
    slopes = 0.5 * (1.0 + tangent) + 0.5 * preact * (1.0 - tangent * tangent) * gelu_coef * (
        1.0 + 3.0 * cubic_coef * preact * preact
    )
    return (gelu_val, slopes)


def params():
    return pltpu.CompilerParams(vmem_limit_bytes=VMEM_BYTES)


def vmem():
    return pl.BlockSpec(memory_space=pltpu.VMEM)


def smem():
    return pl.BlockSpec(memory_space=pltpu.SMEM)


def pack_rows(ids, signals, cotangent):
    rows = signals.shape[0]

    def body(ids_ref, sig_ref, cot_ref, out_ref, perm_ref):
        ids_row = ids_ref[...].astype(jnp.float32)
        lane_ids = jnp.broadcast_to(ids_row, (rows, rows))
        same = lane_ids == lane_ids.T
        count = jnp.sum(same.astype(jnp.float32), axis=0, keepdims=True)
        full = jnp.max(jnp.where(count == CAP, ids_row, -1.0), axis=1, keepdims=True)
        chosen = ids_row == full
        from_row = lax.broadcasted_iota(jnp.int32, (rows, rows), 0)
        to_lane = lax.broadcasted_iota(jnp.int32, (rows, rows), 1)
        upto = (from_row <= to_lane).astype(jnp.bfloat16)
        ahead = jnp.dot(
            jnp.broadcast_to(chosen.astype(jnp.float32), (8, rows)).astype(jnp.bfloat16),
            upto,
            preferred_element_type=jnp.float32,
        )[:1].astype(jnp.int32)
        place = jnp.where(chosen, ahead - 1, CAP + to_lane[:1] - ahead)
        perm = (from_row == place).astype(jnp.float32).astype(jnp.bfloat16)
        perm_ref[...] = perm
        out_ref[:rows] = jnp.dot(perm, sig_ref[...], preferred_element_type=jnp.float32).astype(
            jnp.bfloat16
        )
        out_ref[rows : 2 * rows] = jnp.dot(
            perm, cot_ref[...], preferred_element_type=jnp.float32
        ).astype(jnp.bfloat16)
        sorted_ids = lax.dot_general(
            jnp.broadcast_to(ids_row, (ID_ROWS, rows)).astype(jnp.bfloat16),
            perm,
            (((1,), (1,)), ((), ())),
            preferred_element_type=jnp.float32,
        ).astype(jnp.bfloat16)
        out_ref[2 * rows :, :rows] = sorted_ids
        out_ref[2 * rows :, rows:] = jnp.zeros((ID_ROWS, SITES - rows), jnp.bfloat16)

    return pl.pallas_call(
        body,
        out_shape=(
            jax.ShapeDtypeStruct((2 * rows + ID_ROWS, SITES), jnp.bfloat16),
            jax.ShapeDtypeStruct((rows, rows), jnp.bfloat16),
        ),
        in_specs=[vmem(), vmem(), vmem()],
        out_specs=(vmem(), vmem()),
        compiler_params=params(),
        name="pack_rows",
    )(ids, signals, cotangent)


def local_grads(pos, touched, slot_map, mine, other, blocks, sizes, piece, width):
    planes = mine.shape[0]
    rows = (mine.shape[1] - ID_ROWS) // 2
    touch = touched.shape[1]
    n_own = blocks.shape[0]
    half = sum(sizes)
    aligned = piece % 16 == 0
    starts = [sum(sizes[:i]) for i in range(len(sizes))]
    n_blocks = n_own if aligned else 1
    n_grads = len(sizes) * n_blocks

    def body(pos_ref, touched_ref, slot_ref, mine_ref, other_ref, *rest):
        blocks_ref = rest[0]
        pred_refs = rest[1:3]
        grad_refs = rest[3 : 3 + n_grads]
        acc, id_cols, held, sorted_rows, pred, full_of, tasks, sems = rest[3 + n_grads :]
        own_at = pos_ref[1]
        core = lax.rem(own_at, 2)
        partner = own_at + 1 - 2 * core
        row_copies = [
            pltpu.make_async_copy(
                ref, sorted_rows.at[pl.ds(which * planes, planes)], sems.at[which]
            )
            for which, ref in enumerate((mine_ref, other_ref))
        ]
        if aligned:
            block_copies = [
                pltpu.make_async_copy(
                    blocks_ref.at[s], held.at[:, :, pl.ds(s * piece, piece), :], sems.at[2 + s]
                )
                for s in range(n_own)
            ]
        else:
            block_copies = [pltpu.make_async_copy(blocks_ref, held, sems.at[2])]
        for copy in row_copies + block_copies:
            copy.start()

        def clear(e, _):
            acc[e] = jnp.zeros(acc.shape[1:], jnp.float32)
            return 0

        lax.fori_loop(0, half, clear, 0)
        pred[...] = jnp.zeros_like(pred)
        for copy in row_copies:
            copy.wait()
        for source in range(2 * planes):
            ids_row = sorted_rows[source, 2 * rows :, :rows][:1].astype(jnp.float32)
            id_cols[source] = jnp.broadcast_to(ids_row, (128, rows)).T
            full_of[source] = jnp.max(ids_row[:, :128]).astype(jnp.int32)

        def listing(t, count):
            source = t // (touch + 1)
            j = t - source * (touch + 1)
            which = source // planes
            device = (source - which * planes) * n_own + jnp.where(which == 0, own_at, partner)
            full = full_of[source]
            insertion = jnp.where(j == 0, full, touched_ref[device, jnp.maximum(j - 1, 0)])
            stored = slot_ref[insertion]
            here = (stored // half == core) & ((j == 0) | (insertion != full))
            tasks[0, count] = source
            tasks[1, count] = jnp.where(j == 0, 0, CAP)
            tasks[2, count] = insertion
            tasks[3, count] = stored - core * half
            return count + here.astype(jnp.int32)

        count = lax.fori_loop(0, 2 * planes * (touch + 1), listing, 0)
        tasks[0, count] = 0
        tasks[1, count] = 0
        tasks[2, count] = -1
        tasks[3, count] = 0
        for copy in block_copies:
            copy.wait()

        def pair(i, _):
            loaded = []
            for u in range(2):
                source, insertion, e = tasks[0, 2 * i + u], tasks[2, 2 * i + u], tasks[3, 2 * i + u]
                first = pl.multiple_of(tasks[1, 2 * i + u], CAP)
                keep = (
                    (id_cols[source, pl.ds(first, CAP), :] == insertion.astype(jnp.float32))
                    .astype(jnp.float32)
                    .astype(jnp.bfloat16)
                )
                keep = jnp.concatenate([keep] * (SITES // 128), axis=1)
                sig = sorted_rows[source, pl.ds(first, CAP), :] * keep
                cot = sorted_rows[source, pl.ds(rows + first, CAP), :] * keep
                loaded.append((source, first, e, sig, cot))
            found = []
            for source, first, e, sig, cot in loaded:
                read_out = held[e, 1]
                preact = jnp.dot(sig, held[e, 0], preferred_element_type=jnp.float32)
                back_hidden = jnp.dot(cot, read_out, preferred_element_type=jnp.float32)
                gelu_val, slopes = gelu_parts(preact)
                hidden = gelu_val.astype(jnp.bfloat16)
                back_pre = (back_hidden * slopes).astype(jnp.bfloat16)
                part = lax.dot_general(
                    hidden, read_out, (((1,), (1,)), ((), ())), preferred_element_type=jnp.float32
                ).astype(jnp.bfloat16)
                grad_in = lax.dot_general(
                    sig, back_pre, (((0,), (0,)), ((), ())), preferred_element_type=jnp.float32
                )
                grad_out = lax.dot_general(
                    cot, hidden, (((0,), (0,)), ((), ())), preferred_element_type=jnp.float32
                )
                found.append((part, grad_in, grad_out))
            for (source, first, e, _, _), (part, grad_in, grad_out) in zip(loaded, found):
                pred[source, pl.ds(first, CAP), :] += part
                acc[e, 0] += grad_in
                acc[e, 1] += grad_out
            return 0

        lax.fori_loop(0, (count + 1) // 2, pair, 0)
        for which, ref in enumerate(pred_refs):
            ref[...] = pred[which * planes : (which + 1) * planes]
        for chunk, (start, size) in enumerate(zip(starts, sizes)):
            for j in range(n_blocks):
                ref = grad_refs[chunk * n_blocks + j]

                def write(e, _, start=start, ref=ref, j=j):
                    if aligned:
                        ref[e] = acc[
                            start + e,
                            :,
                            pl.ds(pl.multiple_of((own_at ^ j) * piece, 16), piece),
                            :,
                        ].astype(jnp.bfloat16)
                    else:
                        ref[e] = acc[start + e].astype(jnp.bfloat16)
                    return 0

                lax.fori_loop(0, size, write, 0)

    pred_shape = jax.ShapeDtypeStruct((planes, rows, SITES), jnp.bfloat16)
    grad_rows = piece if aligned else SITES
    grad_shapes = [
        jax.ShapeDtypeStruct((size, 2, grad_rows, width), jnp.bfloat16)
        for size in sizes
        for _ in range(n_blocks)
    ]
    most = 2 * planes * (touch + 1)
    scratch = [
        pltpu.VMEM((half, 2, SITES, width), jnp.float32),
        pltpu.VMEM((2 * planes, rows, 128), jnp.float32),
        pltpu.VMEM((half, 2, SITES, width), jnp.bfloat16),
        pltpu.VMEM((2 * planes,) + mine.shape[1:], jnp.bfloat16),
        pltpu.VMEM((2 * planes, rows, SITES), jnp.bfloat16),
        pltpu.SMEM((2 * planes,), jnp.int32),
        pltpu.SMEM((4, most + 1), jnp.int32),
        pltpu.SemaphoreType.DMA((2 + n_blocks,)),
    ]
    own_at = pos[1]
    if not aligned:
        blocks = blocks.transpose(1, 2, 0, 3, 4).reshape(half, 2, SITES, width)
    anywhere = pl.BlockSpec(memory_space=pl.ANY)
    found = pl.pallas_call(
        body,
        out_shape=[pred_shape, pred_shape] + grad_shapes,
        in_specs=[smem(), smem(), smem()] + [anywhere] * 3,
        out_specs=[vmem()] * (2 + n_grads),
        scratch_shapes=scratch,
        compiler_params=params(),
        name="local_grads",
    )(pos, touched, slot_map, mine, other, blocks)
    grads = []
    for chunk in range(len(sizes)):
        outs = found[2 + chunk * n_blocks : 2 + (chunk + 1) * n_blocks]
        if not aligned:
            outs = [
                lax.dynamic_slice_in_dim(outs[0], (own_at ^ j) * piece, piece, 2)
                for j in range(n_own)
            ]
        grads.append(list(outs))
    return found[0], found[1], grads


def adam(pos, arrived, weights, moment1, moment2, start, before):
    n_own = len(arrived)
    size, _, piece, width = arrived[0].shape
    number = weights.shape[0]
    half = number // 2
    correct_one = 1.0 - 0.9**10
    correct_two = 1.0 - 0.999**10

    def body(pos_ref, *refs):
        grad_refs = refs[:n_own]
        w_ref, m1_ref, m2_ref = refs[n_own : n_own + 3]
        new_w, new_m1, new_m2 = refs[-3:]

        def step(chosen):
            gradient = chosen[0][...].astype(jnp.float32)
            for ref in chosen[1:]:
                gradient = gradient + ref[...].astype(jnp.float32)
            one = 0.9 * m1_ref[...] + 0.1 * gradient
            two = 0.999 * m2_ref[...] + 0.001 * gradient * gradient
            new_m1[...] = one
            new_m2[...] = two
            updated = w_ref[...].astype(jnp.float32) - learn_rate * (one / correct_one) / (
                jnp.sqrt(two / correct_two) + 1e-08
            )
            new_w[0] = updated.astype(jnp.bfloat16)

        pl.when(pl.program_id(0) == 0)(lambda: step(grad_refs[0::2]))
        pl.when(pl.program_id(0) == 1)(lambda: step(grad_refs[1::2]))

    def which(g, pos_ref):
        return lax.rem(pos_ref[1] + g, 2)

    per = math.gcd(size, start) if start else size
    per = math.gcd(per, half)

    def place(g, i, pos_ref):
        return (which(g, pos_ref) * (half // per) + start // per + i, 0, 0, 0)

    small = pl.BlockSpec((per, 2, piece, width), place)
    grad = pl.BlockSpec((per, 2, piece, width), lambda g, i, pos_ref: (i, 0, 0, 0))
    anywhere = pl.BlockSpec(memory_space=pl.ANY)
    grid_spec = pltpu.PrefetchScalarGridSpec(
        num_scalar_prefetch=1,
        grid=(2, size // per),
        in_specs=[grad] * n_own
        + [
            pl.BlockSpec(
                (per, 2, piece, width),
                lambda g, i, pos_ref: place(g, i, pos_ref)[:3] + (pos_ref[0],),
            ),
            small,
            small,
        ]
        + [anywhere] * len(before),
        out_specs=[
            pl.BlockSpec(
                (1, per, 2, piece, width),
                lambda g, i, pos_ref: (which(g, pos_ref), i, 0, 0, 0),
            ),
            small,
            small,
        ],
    )
    return pl.pallas_call(
        body,
        out_shape=[
            jax.ShapeDtypeStruct((2, size, 2, piece, width), jnp.bfloat16),
            jax.ShapeDtypeStruct(moment1.shape, jnp.float32),
            jax.ShapeDtypeStruct(moment1.shape, jnp.float32),
        ],
        grid_spec=grid_spec,
        input_output_aliases={1 + n_own + 3 + i: 1 + i for i in range(len(before))},
        compiler_params=params(),
        name="adam_step",
    )(pos, *arrived, weights, moment1, moment2, *before)


def place_weights(pos, pieces, start, half, before):
    n_dp = len(pieces)
    _, size, _, piece, width = pieces[0].shape
    per = math.gcd(math.gcd(size, start), half)
    pieces = list(pieces)
    far = isinstance(pieces[-1], tuple)
    if far:
        pieces[-1:] = pieces[-1]
    n_in = len(pieces)

    def body(pos_ref, *refs):
        out_ref = refs[-1]
        for k in range(n_dp):

            @pl.when(pos_ref[0] == k)
            def _(k=k):
                for j in range(n_dp):
                    first = (k ^ j) * width
                    i = n_dp if far and j == n_dp - 1 and k in (0, n_dp - 1) else j
                    out_ref[:, :, :, first : first + width] = refs[i][0]

    def place(h, i, pos_ref):
        return (h * (half // per) + start // per + i, 0, 0, 0)

    grid_spec = pltpu.PrefetchScalarGridSpec(
        num_scalar_prefetch=1,
        grid=(2, size // per),
        in_specs=[
            pl.BlockSpec((1, per, 2, piece, width), lambda h, i, pos_ref: (h, i, 0, 0, 0))
        ]
        * n_in
        + [pl.BlockSpec(memory_space=pl.ANY)] * len(before),
        out_specs=pl.BlockSpec((per, 2, piece, n_dp * width), place),
    )
    return pl.pallas_call(
        body,
        out_shape=jax.ShapeDtypeStruct((2 * half, 2, piece, n_dp * width), jnp.bfloat16),
        grid_spec=grid_spec,
        input_output_aliases={1 + n_in: 0} if before else {},
        compiler_params=params(),
        name="place_weights",
    )(pos, *pieces, *before)


def gather_planes(fresh, dp_at, n_dp):
    if n_dp != 4:
        whole = lax.all_gather(fresh, "dp", axis=0)
        return [
            lax.dynamic_index_in_dim(whole, dp_at ^ j, 0, keepdims=False) for j in range(n_dp)
        ]
    two = lax.ppermute(fresh, "dp", [(0, 2), (1, 3), (2, 0), (3, 1)])
    one = lax.ppermute(fresh, "dp", [(0, 1), (1, 0), (2, 3), (3, 2)])
    middle = lax.ppermute(fresh, "dp", [(1, 2), (2, 1)])
    outer = lax.ppermute(two, "dp", [(2, 3), (1, 0)])
    return [fresh, one, two, (middle, outer)]


def finish_predicted(perm, parts):
    def body(perm_ref, *refs):
        total = refs[0][...].astype(jnp.float32)
        for ref in refs[1:-1]:
            total = total + ref[...].astype(jnp.float32)
        refs[-1][...] = lax.dot_general(
            perm_ref[...],
            total.astype(jnp.bfloat16),
            (((0,), (0,)), ((), ())),
            preferred_element_type=jnp.float32,
        ).astype(jnp.bfloat16)

    return pl.pallas_call(
        body,
        out_shape=jax.ShapeDtypeStruct(parts[0].shape, jnp.bfloat16),
        in_specs=[vmem()] * (1 + len(parts)),
        out_specs=vmem(),
        compiler_params=params(),
        name="finish_predicted",
    )(perm, *parts)


def shards(signals, cotangent, row_insertion, touched, slot_map, weights, moment1, moment2):
    n_own = lax.axis_size("own")
    n_dp = lax.axis_size("dp")
    dp_at = lax.axis_index("dp")
    own_at = lax.axis_index("own")
    number, _, piece, _ = weights.shape
    width = moment1.shape[3]
    half = number // 2
    rows = signals.shape[0]
    pos = jnp.stack([dp_at, own_at]).astype(jnp.int32)
    core = lax.rem(own_at, 2)
    parts_of_half = sum(CHUNK_PARTS)
    sizes = [half * part // parts_of_half for part in CHUNK_PARTS]

    def across(value, j):
        return lax.ppermute(value, "own", [(o, o ^ j) for o in range(n_own)])

    packed, perm = pack_rows(row_insertion.reshape(1, rows), signals, cotangent)
    mine = lax.all_gather(packed, "dp", axis=0)

    column = lax.dynamic_slice_in_dim(weights, dp_at * width, width, 3)
    outgoing = jnp.broadcast_to(
        column.reshape(1, 2, half, 2, piece, width), (n_own // 2, 2, half, 2, piece, width)
    ).reshape(n_own, half, 2, piece, width)
    blocks = lax.all_to_all(outgoing, "own", split_axis=0, concat_axis=0, tiled=True)
    other = across(mine, 1)

    pred_mine, pred_other, grads = local_grads(
        pos, touched, slot_map, mine, other, blocks, sizes, piece, width
    )
    moments = []
    new_weights = []
    start = 0
    arrived = None
    for size, chunk in zip(sizes, grads):
        if arrived:
            for j in range(1, n_own):
                before = arrived[j] if j < n_own // 2 else fresh
                chunk[j], _ = lax.optimization_barrier((chunk[j], before))
        arrived = [chunk[0]] + [across(chunk[j], j) for j in range(1, n_own)]
        fresh, *moments = adam(pos, arrived, weights, moment1, moment2, start, moments)
        pieces = gather_planes(fresh, dp_at, n_dp)
        new_weights = [place_weights(pos, pieces, start, half, new_weights)]
        start += size
    new_weights = new_weights[0]
    new_moment1, new_moment2 = moments

    pred_part = pred_mine + across(pred_other, 1)
    parts = [lax.dynamic_index_in_dim(pred_part, dp_at, 0, keepdims=False)]
    for shift in range(1, n_dp):
        block = lax.dynamic_index_in_dim(pred_part, lax.rem(dp_at + shift, n_dp), 0, keepdims=False)
        parts.append(lax.ppermute(block, "dp", [(d, (d + shift) % n_dp) for d in range(n_dp)]))
    predicted = finish_predicted(perm, parts)
    return (predicted, new_weights, new_moment1, new_moment2)


def solution(mesh):
    in_specs = (
        P(("dp", "own"), None),
        P(("dp", "own"), None),
        P(("dp", "own")),
        P(),
        P(),
        P(None, None, "own", None),
        P(None, None, "own", "dp"),
        P(None, None, "own", "dp"),
    )
    out_specs = (
        P(("dp", "own"), None),
        P(None, None, "own", None),
        P(None, None, "own", "dp"),
        P(None, None, "own", "dp"),
    )
    return jax.shard_map(shards, mesh=mesh, in_specs=in_specs, out_specs=out_specs, check_vma=False)
```

```python
import math

import jax
import jax.numpy as jnp
from jax import lax
from jax.experimental import pallas as pl
from jax.experimental.pallas import tpu as pltpu
from jax.sharding import PartitionSpec as P

SITES = 384
CAP = 128
CHUNK_PARTS = (3, 5)
ID_ROWS = 16
VMEM_BYTES = 56 * 2**20

gelu_coef = math.sqrt(2.0 / math.pi)
cubic_coef = 0.044715
learn_rate = 0.01


def gelu_parts(preact):
    tanh_input = gelu_coef * (preact + cubic_coef * preact * preact * preact)
    tangent = jnp.tanh(tanh_input)
    gelu_val = 0.5 * preact * (1.0 + tangent)
    slopes = 0.5 * (1.0 + tangent) + 0.5 * preact * (1.0 - tangent * tangent) * gelu_coef * (
        1.0 + 3.0 * cubic_coef * preact * preact
    )
    return (gelu_val, slopes)


def params():
    return pltpu.CompilerParams(vmem_limit_bytes=VMEM_BYTES)


def vmem():
    return pl.BlockSpec(memory_space=pltpu.VMEM)


def smem():
    return pl.BlockSpec(memory_space=pltpu.SMEM)


def pack_rows(ids, signals, cotangent):
    rows = signals.shape[0]

    def body(ids_ref, sig_ref, cot_ref, out_ref, perm_ref):
        ids_row = ids_ref[...].astype(jnp.float32)
        lane_ids = jnp.broadcast_to(ids_row, (rows, rows))
        same = lane_ids == lane_ids.T
        count = jnp.sum(same.astype(jnp.float32), axis=0, keepdims=True)
        full = jnp.max(jnp.where(count == CAP, ids_row, -1.0), axis=1, keepdims=True)
        chosen = ids_row == full
        from_row = lax.broadcasted_iota(jnp.int32, (rows, rows), 0)
        to_lane = lax.broadcasted_iota(jnp.int32, (rows, rows), 1)
        upto = (from_row <= to_lane).astype(jnp.bfloat16)
        ahead = jnp.dot(
            jnp.broadcast_to(chosen.astype(jnp.float32), (8, rows)).astype(jnp.bfloat16),
            upto,
            preferred_element_type=jnp.float32,
        )[:1].astype(jnp.int32)
        place = jnp.where(chosen, ahead - 1, CAP + to_lane[:1] - ahead)
        perm = (from_row == place).astype(jnp.float32).astype(jnp.bfloat16)
        perm_ref[...] = perm
        out_ref[:rows] = jnp.dot(perm, sig_ref[...], preferred_element_type=jnp.float32).astype(
            jnp.bfloat16
        )
        out_ref[rows : 2 * rows] = jnp.dot(
            perm, cot_ref[...], preferred_element_type=jnp.float32
        ).astype(jnp.bfloat16)
        sorted_ids = lax.dot_general(
            jnp.broadcast_to(ids_row, (ID_ROWS, rows)).astype(jnp.bfloat16),
            perm,
            (((1,), (1,)), ((), ())),
            preferred_element_type=jnp.float32,
        ).astype(jnp.bfloat16)
        out_ref[2 * rows :, :rows] = sorted_ids
        out_ref[2 * rows :, rows:] = jnp.zeros((ID_ROWS, SITES - rows), jnp.bfloat16)

    return pl.pallas_call(
        body,
        out_shape=(
            jax.ShapeDtypeStruct((2 * rows + ID_ROWS, SITES), jnp.bfloat16),
            jax.ShapeDtypeStruct((rows, rows), jnp.bfloat16),
        ),
        in_specs=[vmem(), vmem(), vmem()],
        out_specs=(vmem(), vmem()),
        compiler_params=params(),
        name="pack_rows",
    )(ids, signals, cotangent)


def local_grads(pos, touched, slot_map, rows_in, blocks, sizes, piece, width):
    planes = rows_in[0].shape[0]
    rows = (rows_in[0].shape[1] - ID_ROWS) // 2
    touch = touched.shape[1]
    chips = len(blocks)
    n_own = 2 * chips
    half = blocks[0].shape[1]
    aligned = piece % 16 == 0
    n_in = chips if aligned else 1
    n_out = n_own if aligned else 1
    starts = [sum(sizes[:i]) for i in range(len(sizes))]

    def body(pos_ref, touched_ref, slot_ref, *rest):
        row_refs = rest[:2]
        block_refs = rest[2 : 2 + n_in]
        rest = rest[2 + n_in :]
        pred_refs = rest[:2]
        grad_refs = rest[2:-8]
        acc, id_cols, held, sorted_rows, pred, full_of, tasks, sems = rest[-8:]
        dp_at, own_at = pos_ref[0], pos_ref[1]
        core = lax.rem(own_at, 2)

        def sites(j):
            return pl.ds(pl.multiple_of((own_at ^ j) * piece, 16), piece)

        row_copies = [
            pltpu.make_async_copy(ref, sorted_rows.at[pl.ds(i * planes, planes)], sems.at[i])
            for i, ref in enumerate(row_refs)
        ]
        if aligned:
            block_copies = [
                pltpu.make_async_copy(
                    ref.at[u],
                    held.at[:, :, sites(2 * q + u), :],
                    sems.at[2 + 2 * q + u],
                )
                for q, ref in enumerate(block_refs)
                for u in range(2)
            ]
        else:
            block_copies = [pltpu.make_async_copy(block_refs[0], held, sems.at[2])]
        for copy in row_copies + block_copies:
            copy.start()

        def clear(e, _):
            acc[e] = jnp.zeros(acc.shape[1:], jnp.float32)
            return 0

        lax.fori_loop(0, half, clear, 0)
        pred[...] = jnp.zeros_like(pred)
        for copy in row_copies:
            copy.wait()
        for source in range(2 * planes):
            ids_row = sorted_rows[source, 2 * rows :, :rows][:1].astype(jnp.float32)
            id_cols[source] = jnp.broadcast_to(ids_row, (128, rows)).T
            full_of[source] = jnp.max(ids_row[:, :128]).astype(jnp.int32)

        def listing(t, count):
            source = t // (touch + 1)
            j = t - source * (touch + 1)
            which = source // planes
            device = (dp_at ^ (source - which * planes)) * n_own + (own_at ^ which)
            full = full_of[source]
            insertion = jnp.where(j == 0, full, touched_ref[device, jnp.maximum(j - 1, 0)])
            e = slot_ref[insertion] - core * half
            here = (e >= 0) & (e < half) & ((j == 0) | (insertion != full))
            tasks[0, count] = source
            tasks[1, count] = jnp.where(j == 0, 0, CAP)
            tasks[2, count] = insertion
            tasks[3, count] = e
            return count + here.astype(jnp.int32)

        count = lax.fori_loop(0, 2 * planes * (touch + 1), listing, 0)
        tasks[0, count] = 0
        tasks[1, count] = 0
        tasks[2, count] = -1
        tasks[3, count] = 0
        for copy in block_copies:
            copy.wait()

        def pair(i, _):
            loaded = []
            for u in range(2):
                source, insertion, e = tasks[0, 2 * i + u], tasks[2, 2 * i + u], tasks[3, 2 * i + u]
                first = pl.multiple_of(tasks[1, 2 * i + u], CAP)
                keep = (
                    (id_cols[source, pl.ds(first, CAP), :] == insertion.astype(jnp.float32))
                    .astype(jnp.float32)
                    .astype(jnp.bfloat16)
                )
                keep = jnp.concatenate([keep] * (SITES // 128), axis=1)
                sig = sorted_rows[source, pl.ds(first, CAP), :] * keep
                cot = sorted_rows[source, pl.ds(rows + first, CAP), :] * keep
                loaded.append((source, first, e, sig, cot))
            found = []
            for source, first, e, sig, cot in loaded:
                read_out = held[e, 1]
                preact = jnp.dot(sig, held[e, 0], preferred_element_type=jnp.float32)
                back_hidden = jnp.dot(cot, read_out, preferred_element_type=jnp.float32)
                gelu_val, slopes = gelu_parts(preact)
                hidden = gelu_val.astype(jnp.bfloat16)
                back_pre = (back_hidden * slopes).astype(jnp.bfloat16)
                part = lax.dot_general(
                    hidden, read_out, (((1,), (1,)), ((), ())), preferred_element_type=jnp.float32
                ).astype(jnp.bfloat16)
                grad_in = lax.dot_general(
                    sig, back_pre, (((0,), (0,)), ((), ())), preferred_element_type=jnp.float32
                )
                grad_out = lax.dot_general(
                    cot, hidden, (((0,), (0,)), ((), ())), preferred_element_type=jnp.float32
                )
                found.append((part, grad_in, grad_out))
            for (source, first, e, _, _), (part, grad_in, grad_out) in zip(loaded, found):
                pred[source, pl.ds(first, CAP), :] += part
                acc[e, 0] += grad_in
                acc[e, 1] += grad_out
            return 0

        lax.fori_loop(0, (count + 1) // 2, pair, 0)
        for which, ref in enumerate(pred_refs):
            ref[...] = pred[which * planes : (which + 1) * planes]
        for chunk, (start, size) in enumerate(zip(starts, sizes)):
            for j in range(n_out):
                ref = grad_refs[chunk * n_out + j]

                def write(e, _, start=start, ref=ref, j=j):
                    if aligned:
                        ref[e] = acc[start + e, :, sites(j), :].astype(jnp.bfloat16)
                    else:
                        ref[e] = acc[start + e].astype(jnp.bfloat16)
                    return 0

                lax.fori_loop(0, size, write, 0)

    pred_shape = jax.ShapeDtypeStruct((planes, rows, SITES), jnp.bfloat16)
    grad_shapes = [
        jax.ShapeDtypeStruct((size, 2, piece if aligned else SITES, width), jnp.bfloat16)
        for size in sizes
        for _ in range(n_out)
    ]
    most = 2 * planes * (touch + 1)
    scratch = [
        pltpu.VMEM((half, 2, SITES, width), jnp.float32),
        pltpu.VMEM((2 * planes, rows, 128), jnp.float32),
        pltpu.VMEM((half, 2, SITES, width), jnp.bfloat16),
        pltpu.VMEM((2 * planes,) + rows_in[0].shape[1:], jnp.bfloat16),
        pltpu.VMEM((2 * planes, rows, SITES), jnp.bfloat16),
        pltpu.SMEM((2 * planes,), jnp.int32),
        pltpu.SMEM((4, most + 1), jnp.int32),
        pltpu.SemaphoreType.DMA((2 + n_own,)),
    ]
    own_at = pos[1]
    if not aligned:
        order = own_at ^ jnp.arange(n_own, dtype=jnp.int32)
        stacked = jnp.take(jnp.concatenate(blocks), order, axis=0)
        blocks = [stacked.transpose(1, 2, 0, 3, 4).reshape(half, 2, SITES, width)]
    found = pl.pallas_call(
        body,
        out_shape=[pred_shape, pred_shape] + grad_shapes,
        in_specs=[smem(), smem(), smem()] + [pl.BlockSpec(memory_space=pl.ANY)] * (2 + n_in),
        out_specs=[vmem()] * (2 + len(grad_shapes)),
        scratch_shapes=scratch,
        compiler_params=params(),
        name="local_grads",
    )(pos, touched, slot_map, *rows_in, *blocks)
    grads = []
    for chunk in range(len(sizes)):
        outs = list(found[2 + chunk * n_out : 2 + (chunk + 1) * n_out])
        if not aligned:
            outs = [
                lax.dynamic_slice_in_dim(outs[0], (own_at ^ j) * piece, piece, 2)
                for j in range(n_own)
            ]
        grads.append(outs)
    return found[0], found[1], grads


def adam(pos, arrived, weights, moment1, moment2, start, before):
    n_own = len(arrived)
    size, _, piece, width = arrived[0].shape
    number = weights.shape[0]
    half = number // 2
    correct_one = 1.0 - 0.9**10
    correct_two = 1.0 - 0.999**10

    def body(pos_ref, *refs):
        grad_refs = refs[:n_own]
        w_ref, m1_ref, m2_ref = refs[n_own : n_own + 3]
        new_w, new_m1, new_m2 = refs[-3:]

        def step(chosen):
            gradient = chosen[0][...].astype(jnp.float32)
            for ref in chosen[1:]:
                gradient = gradient + ref[...].astype(jnp.float32)
            one = 0.9 * m1_ref[...] + 0.1 * gradient
            two = 0.999 * m2_ref[...] + 0.001 * gradient * gradient
            new_m1[...] = one
            new_m2[...] = two
            spread = two * (1.0 / correct_two)
            updated = w_ref[...].astype(jnp.float32) - one * (learn_rate / correct_one) / (
                spread * lax.rsqrt(spread) + 1e-08
            )
            new_w[0] = updated.astype(jnp.bfloat16)

        pl.when(pl.program_id(0) == 0)(lambda: step(grad_refs[0::2]))
        pl.when(pl.program_id(0) == 1)(lambda: step(grad_refs[1::2]))

    def which(g, pos_ref):
        return lax.rem(pos_ref[1] + g, 2)

    per = math.gcd(size, start) if start else size
    per = math.gcd(per, half)

    def place(g, i, pos_ref):
        return (which(g, pos_ref) * (half // per) + start // per + i, 0, 0, 0)

    small = pl.BlockSpec((per, 2, piece, width), place)
    grad = pl.BlockSpec((per, 2, piece, width), lambda g, i, pos_ref: (i, 0, 0, 0))
    anywhere = pl.BlockSpec(memory_space=pl.ANY)
    grid_spec = pltpu.PrefetchScalarGridSpec(
        num_scalar_prefetch=1,
        grid=(2, size // per),
        in_specs=[grad] * n_own
        + [
            pl.BlockSpec(
                (per, 2, piece, width),
                lambda g, i, pos_ref: place(g, i, pos_ref)[:3] + (pos_ref[0],),
            ),
            small,
            small,
        ]
        + [anywhere] * len(before),
        out_specs=[
            pl.BlockSpec(
                (1, per, 2, piece, width),
                lambda g, i, pos_ref: (which(g, pos_ref), i, 0, 0, 0),
            ),
            small,
            small,
        ],
    )
    return pl.pallas_call(
        body,
        out_shape=[
            jax.ShapeDtypeStruct((2, size, 2, piece, width), jnp.bfloat16),
            jax.ShapeDtypeStruct(moment1.shape, jnp.float32),
            jax.ShapeDtypeStruct(moment1.shape, jnp.float32),
        ],
        grid_spec=grid_spec,
        input_output_aliases={1 + n_own + 3 + i: 1 + i for i in range(len(before))},
        compiler_params=params(),
        name="adam_step",
    )(pos, *arrived, weights, moment1, moment2, *before)


def place_weights(pos, pieces, start, half, before):
    n_dp = len(pieces)
    _, size, _, piece, width = pieces[0].shape
    per = math.gcd(math.gcd(size, start), half)
    pieces = list(pieces)
    far = isinstance(pieces[-1], tuple)
    if far:
        pieces[-1:] = pieces[-1]
    n_in = len(pieces)

    def body(pos_ref, *refs):
        out_ref = refs[-1]
        for k in range(n_dp):

            @pl.when(pos_ref[0] == k)
            def _(k=k):
                for j in range(n_dp):
                    first = (k ^ j) * width
                    i = n_dp if far and j == n_dp - 1 and k in (0, n_dp - 1) else j
                    out_ref[:, :, :, first : first + width] = refs[i][0]

    def place(h, i, pos_ref):
        return (h * (half // per) + start // per + i, 0, 0, 0)

    grid_spec = pltpu.PrefetchScalarGridSpec(
        num_scalar_prefetch=1,
        grid=(2, size // per),
        in_specs=[
            pl.BlockSpec((1, per, 2, piece, width), lambda h, i, pos_ref: (h, i, 0, 0, 0))
        ]
        * n_in
        + [pl.BlockSpec(memory_space=pl.ANY)] * len(before),
        out_specs=pl.BlockSpec((per, 2, piece, n_dp * width), place),
    )
    return pl.pallas_call(
        body,
        out_shape=jax.ShapeDtypeStruct((2 * half, 2, piece, n_dp * width), jnp.bfloat16),
        grid_spec=grid_spec,
        input_output_aliases={1 + n_in: 0} if before else {},
        compiler_params=params(),
        name="place_weights",
    )(pos, *pieces, *before)


def after(value, *others):
    return lax.optimization_barrier((value,) + others)[0]


def gather_planes(fresh, dp_at, n_dp):
    if n_dp != 4:
        whole = lax.all_gather(fresh, "dp", axis=0)
        return [
            lax.dynamic_index_in_dim(whole, dp_at ^ j, 0, keepdims=False) for j in range(n_dp)
        ]
    two = lax.ppermute(fresh, "dp", [(0, 2), (1, 3), (2, 0), (3, 1)])
    one = lax.ppermute(fresh, "dp", [(0, 1), (1, 0), (2, 3), (3, 2)])
    middle = lax.ppermute(fresh, "dp", [(1, 2), (2, 1)])
    outer = lax.ppermute(two, "dp", [(2, 3), (1, 0)])
    return [fresh, one, two, (middle, outer)]


def finish_predicted(perm, parts):
    def body(perm_ref, *refs):
        total = refs[0][...].astype(jnp.float32)
        for ref in refs[1:-1]:
            total = total + ref[...].astype(jnp.float32)
        refs[-1][...] = lax.dot_general(
            perm_ref[...],
            total.astype(jnp.bfloat16),
            (((0,), (0,)), ((), ())),
            preferred_element_type=jnp.float32,
        ).astype(jnp.bfloat16)

    return pl.pallas_call(
        body,
        out_shape=jax.ShapeDtypeStruct(parts[0].shape, jnp.bfloat16),
        in_specs=[vmem()] * (1 + len(parts)),
        out_specs=vmem(),
        compiler_params=params(),
        name="finish_predicted",
    )(perm, *parts)


def shards(signals, cotangent, row_insertion, touched, slot_map, weights, moment1, moment2):
    n_own = lax.axis_size("own")
    n_dp = lax.axis_size("dp")
    dp_at = lax.axis_index("dp")
    own_at = lax.axis_index("own")
    number, _, piece, _ = weights.shape
    width = moment1.shape[3]
    half = number // 2
    rows = signals.shape[0]
    pos = jnp.stack([dp_at, own_at]).astype(jnp.int32)
    core = lax.rem(own_at, 2)
    parts_of_half = sum(CHUNK_PARTS)
    sizes = [half * part // parts_of_half for part in CHUNK_PARTS]

    def across(value, j):
        return lax.ppermute(value, "own", [(o, o ^ j) for o in range(n_own)])

    def column(which):
        return lax.dynamic_slice(
            weights, (which * half, 0, 0, dp_at * width), (half, 2, piece, width)
        )

    packed, perm = pack_rows(row_insertion.reshape(1, rows), signals, cotangent)
    def between(value, j):
        return lax.ppermute(value, "dp", [(d, d ^ j) for d in range(n_dp)])

    planes = jnp.stack([packed] + [between(packed, j) for j in range(1, n_dp)])

    paired = jnp.stack([column(core), across(column(1 - core), 1)])
    blocks = [paired] + [across(paired, 2 * q) for q in range(1, n_own // 2)]
    rows_in = (planes, across(after(planes, *blocks[1:]), 1))

    pred_mine, pred_other, grads = local_grads(
        pos, touched, slot_map, rows_in, blocks, sizes, piece, width
    )
    pred_part = pred_mine + across(pred_other, 1)
    parts = [pred_part[0]] + [between(pred_part[j], j) for j in range(1, n_dp)]

    moments = []
    new_weights = []
    pieces = None
    start = 0
    for size, chunk in zip(sizes, grads):
        if pieces:
            last = pieces[-1][-1] if isinstance(pieces[-1], tuple) else pieces[-1]
            moving = parts[1:4] + [fresh, fresh, pieces[2], pieces[1]]
            for j in range(1, n_own):
                chunk[j] = after(chunk[j], moving[min(j, len(moving)) - 1])
        arrived = [chunk[0]] + [across(chunk[j], j) for j in range(1, n_own)]
        arrived[-1] = after(arrived[-1], last if pieces else pred_part)
        fresh, *moments = adam(pos, arrived, weights, moment1, moment2, start, moments)
        pieces = gather_planes(fresh, dp_at, n_dp)
        new_weights = [place_weights(pos, pieces, start, half, new_weights)]
        start += size
    new_weights = new_weights[0]
    new_moment1, new_moment2 = moments

    predicted = finish_predicted(perm, parts)
    return (predicted, new_weights, new_moment1, new_moment2)


def solution(mesh):
    in_specs = (
        P(("dp", "own"), None),
        P(("dp", "own"), None),
        P(("dp", "own")),
        P(),
        P(),
        P(None, None, "own", None),
        P(None, None, "own", "dp"),
        P(None, None, "own", "dp"),
    )
    out_specs = (
        P(("dp", "own"), None),
        P(None, None, "own", None),
        P(None, None, "own", "dp"),
        P(None, None, "own", "dp"),
    )
    return jax.shard_map(shards, mesh=mesh, in_specs=in_specs, out_specs=out_specs, check_vma=False)
```

```python
import math

import jax
import jax.numpy as jnp
from jax import lax
from jax.experimental import pallas as pl
from jax.experimental.pallas import tpu as pltpu
from jax.sharding import PartitionSpec as P

SITES = 384
CAP = 128
CHUNK_PARTS = (3, 5)
ID_ROWS = 16
VMEM_BYTES = 56 * 2**20

gelu_coef = math.sqrt(2.0 / math.pi)
cubic_coef = 0.044715
learn_rate = 0.01


def gelu_parts(preact):
    tanh_input = gelu_coef * (preact + cubic_coef * preact * preact * preact)
    tangent = jnp.tanh(tanh_input)
    gelu_val = 0.5 * preact * (1.0 + tangent)
    slopes = 0.5 * (1.0 + tangent) + 0.5 * preact * (1.0 - tangent * tangent) * gelu_coef * (
        1.0 + 3.0 * cubic_coef * preact * preact
    )
    return (gelu_val, slopes)


def params():
    return pltpu.CompilerParams(vmem_limit_bytes=VMEM_BYTES)


def vmem():
    return pl.BlockSpec(memory_space=pltpu.VMEM)


def smem():
    return pl.BlockSpec(memory_space=pltpu.SMEM)


def pack_rows(ids, signals, cotangent):
    rows = signals.shape[0]

    def body(ids_ref, sig_ref, cot_ref, out_ref, perm_ref):
        ids_row = ids_ref[...].astype(jnp.float32)
        lane_ids = jnp.broadcast_to(ids_row, (rows, rows))
        same = lane_ids == lane_ids.T
        count = jnp.sum(same.astype(jnp.float32), axis=0, keepdims=True)
        full = jnp.max(jnp.where(count == CAP, ids_row, -1.0), axis=1, keepdims=True)
        chosen = ids_row == full
        from_row = lax.broadcasted_iota(jnp.int32, (rows, rows), 0)
        to_lane = lax.broadcasted_iota(jnp.int32, (rows, rows), 1)
        upto = (from_row <= to_lane).astype(jnp.bfloat16)
        ahead = jnp.dot(
            jnp.broadcast_to(chosen.astype(jnp.float32), (8, rows)).astype(jnp.bfloat16),
            upto,
            preferred_element_type=jnp.float32,
        )[:1].astype(jnp.int32)
        place = jnp.where(chosen, ahead - 1, CAP + to_lane[:1] - ahead)
        perm = (from_row == place).astype(jnp.float32).astype(jnp.bfloat16)
        perm_ref[...] = perm
        out_ref[:rows] = jnp.dot(perm, sig_ref[...], preferred_element_type=jnp.float32).astype(
            jnp.bfloat16
        )
        out_ref[rows : 2 * rows] = jnp.dot(
            perm, cot_ref[...], preferred_element_type=jnp.float32
        ).astype(jnp.bfloat16)
        sorted_ids = lax.dot_general(
            jnp.broadcast_to(ids_row, (ID_ROWS, rows)).astype(jnp.bfloat16),
            perm,
            (((1,), (1,)), ((), ())),
            preferred_element_type=jnp.float32,
        ).astype(jnp.bfloat16)
        out_ref[2 * rows :, :rows] = sorted_ids
        out_ref[2 * rows :, rows:] = jnp.zeros((ID_ROWS, SITES - rows), jnp.bfloat16)

    return pl.pallas_call(
        body,
        out_shape=(
            jax.ShapeDtypeStruct((2 * rows + ID_ROWS, SITES), jnp.bfloat16),
            jax.ShapeDtypeStruct((rows, rows), jnp.bfloat16),
        ),
        in_specs=[vmem(), vmem(), vmem()],
        out_specs=(vmem(), vmem()),
        compiler_params=params(),
        name="pack_rows",
    )(ids, signals, cotangent)


def local_grads(pos, touched, slot_map, rows_in, blocks, sizes, piece, width):
    planes = rows_in[0].shape[0]
    rows = (rows_in[0].shape[1] - ID_ROWS) // 2
    touch = touched.shape[1]
    n_own = blocks.shape[0]
    half = sum(sizes)
    aligned = piece % 16 == 0
    n_out = n_own if aligned else 1
    starts = [sum(sizes[:i]) for i in range(len(sizes))]

    def body(pos_ref, touched_ref, slot_ref, *rest):
        row_refs = rest[:2]
        blocks_ref = rest[2]
        rest = rest[3:]
        pred_refs = rest[:2]
        grad_refs = rest[2:-8]
        acc, id_cols, held, sorted_rows, pred, full_of, tasks, sems = rest[-8:]
        own_at = pos_ref[1]
        core = lax.rem(own_at, 2)

        def sites(j):
            return pl.ds(pl.multiple_of((own_at ^ j) * piece, 16), piece)

        row_copies = [
            pltpu.make_async_copy(ref, sorted_rows.at[pl.ds(i * planes, planes)], sems.at[i])
            for i, ref in enumerate(row_refs)
        ]
        if aligned:
            block_copies = [
                pltpu.make_async_copy(
                    blocks_ref.at[i], held.at[:, :, pl.ds(i * piece, piece), :], sems.at[2 + i]
                )
                for i in range(n_own)
            ]
        else:
            block_copies = [pltpu.make_async_copy(blocks_ref, held, sems.at[2])]
        for copy in row_copies + block_copies:
            copy.start()

        def clear(e, _):
            acc[e] = jnp.zeros(acc.shape[1:], jnp.float32)
            return 0

        lax.fori_loop(0, half, clear, 0)
        pred[...] = jnp.zeros_like(pred)
        for copy in row_copies:
            copy.wait()
        for source in range(2 * planes):
            ids_row = sorted_rows[source, 2 * rows :, :rows][:1].astype(jnp.float32)
            id_cols[source] = jnp.broadcast_to(ids_row, (128, rows)).T
            full_of[source] = jnp.max(ids_row[:, :128]).astype(jnp.int32)

        def listing(t, count):
            source = t // (touch + 1)
            j = t - source * (touch + 1)
            which = source // planes
            device = (source - which * planes) * n_own + (own_at ^ which)
            full = full_of[source]
            insertion = jnp.where(j == 0, full, touched_ref[device, jnp.maximum(j - 1, 0)])
            e = slot_ref[insertion] - core * half
            here = (e >= 0) & (e < half) & ((j == 0) | (insertion != full))
            tasks[0, count] = source
            tasks[1, count] = jnp.where(j == 0, 0, CAP)
            tasks[2, count] = insertion
            tasks[3, count] = e
            return count + here.astype(jnp.int32)

        count = lax.fori_loop(0, 2 * planes * (touch + 1), listing, 0)
        tasks[0, count] = 0
        tasks[1, count] = 0
        tasks[2, count] = -1
        tasks[3, count] = 0
        for copy in block_copies:
            copy.wait()

        def pair(i, _):
            loaded = []
            for u in range(2):
                source, insertion, e = tasks[0, 2 * i + u], tasks[2, 2 * i + u], tasks[3, 2 * i + u]
                first = pl.multiple_of(tasks[1, 2 * i + u], CAP)
                keep = (
                    (id_cols[source, pl.ds(first, CAP), :] == insertion.astype(jnp.float32))
                    .astype(jnp.float32)
                    .astype(jnp.bfloat16)
                )
                keep = jnp.concatenate([keep] * (SITES // 128), axis=1)
                sig = sorted_rows[source, pl.ds(first, CAP), :] * keep
                cot = sorted_rows[source, pl.ds(rows + first, CAP), :] * keep
                loaded.append((source, first, e, sig, cot))
            found = []
            for source, first, e, sig, cot in loaded:
                read_out = held[e, 1]
                preact = jnp.dot(sig, held[e, 0], preferred_element_type=jnp.float32)
                back_hidden = jnp.dot(cot, read_out, preferred_element_type=jnp.float32)
                gelu_val, slopes = gelu_parts(preact)
                hidden = gelu_val.astype(jnp.bfloat16)
                back_pre = (back_hidden * slopes).astype(jnp.bfloat16)
                part = lax.dot_general(
                    hidden, read_out, (((1,), (1,)), ((), ())), preferred_element_type=jnp.float32
                )
                grad_in = lax.dot_general(
                    sig, back_pre, (((0,), (0,)), ((), ())), preferred_element_type=jnp.float32
                )
                grad_out = lax.dot_general(
                    cot, hidden, (((0,), (0,)), ((), ())), preferred_element_type=jnp.float32
                )
                found.append((part, grad_in, grad_out))
            for (source, first, e, _, _), (part, grad_in, grad_out) in zip(loaded, found):
                pred[source, pl.ds(first, CAP), :] += part
                acc[e, 0] += grad_in
                acc[e, 1] += grad_out
            return 0

        lax.fori_loop(0, (count + 1) // 2, pair, 0)
        for which, ref in enumerate(pred_refs):
            ref[...] = pred[which * planes : (which + 1) * planes]
        for chunk, (start, size) in enumerate(zip(starts, sizes)):
            for j in range(n_out):
                ref = grad_refs[chunk * n_out + j]

                def write(e, _, start=start, ref=ref, j=j):
                    if aligned:
                        ref[e] = acc[start + e, :, sites(j), :].astype(jnp.bfloat16)
                    else:
                        ref[e] = acc[start + e].astype(jnp.bfloat16)
                    return 0

                lax.fori_loop(0, size, write, 0)

    pred_shape = jax.ShapeDtypeStruct((planes, rows, SITES), jnp.float32)
    grad_shapes = [
        jax.ShapeDtypeStruct((size, 2, piece if aligned else SITES, width), jnp.bfloat16)
        for size in sizes
        for _ in range(n_out)
    ]
    most = 2 * planes * (touch + 1)
    scratch = [
        pltpu.VMEM((half, 2, SITES, width), jnp.float32),
        pltpu.VMEM((2 * planes, rows, 128), jnp.float32),
        pltpu.VMEM((half, 2, SITES, width), jnp.bfloat16),
        pltpu.VMEM((2 * planes,) + rows_in[0].shape[1:], jnp.bfloat16),
        pltpu.VMEM((2 * planes, rows, SITES), jnp.float32),
        pltpu.SMEM((2 * planes,), jnp.int32),
        pltpu.SMEM((4, most + 1), jnp.int32),
        pltpu.SemaphoreType.DMA((2 + n_own,)),
    ]
    own_at = pos[1]
    if not aligned:
        blocks = blocks.transpose(1, 2, 0, 3, 4).reshape(half, 2, SITES, width)
    found = pl.pallas_call(
        body,
        out_shape=[pred_shape, pred_shape] + grad_shapes,
        in_specs=[smem(), smem(), smem()] + [pl.BlockSpec(memory_space=pl.ANY)] * 3,
        out_specs=[vmem()] * (2 + len(grad_shapes)),
        scratch_shapes=scratch,
        compiler_params=params(),
        name="local_grads",
    )(pos, touched, slot_map, *rows_in, blocks)
    grads = []
    for chunk in range(len(sizes)):
        outs = list(found[2 + chunk * n_out : 2 + (chunk + 1) * n_out])
        if not aligned:
            outs = [
                lax.dynamic_slice_in_dim(outs[0], (own_at ^ j) * piece, piece, 2)
                for j in range(n_own)
            ]
        grads.append(outs)
    return found[0], found[1], grads


def adam(pos, arrived, weights, moment1, moment2, start, before):
    n_own = len(arrived)
    size, _, piece, width = arrived[0].shape
    number = weights.shape[0]
    half = number // 2
    correct_one = 1.0 - 0.9**10
    correct_two = 1.0 - 0.999**10

    def body(pos_ref, *refs):
        grad_refs = refs[:n_own]
        w_ref, m1_ref, m2_ref = refs[n_own : n_own + 3]
        new_w, new_m1, new_m2 = refs[n_own + 3 + len(before) : n_own + 6 + len(before)]
        grads, w_in, m1_in, m2_in, w_out, m1_out, m2_out, sem_in, sem_grad, sem_out = refs[
            n_own + 6 + len(before) :
        ]
        core = lax.rem(pos_ref[1], 2)
        columns = pl.ds(pl.multiple_of(pos_ref[0] * width, 128), width)

        def block_rows(g):
            return pl.ds((core ^ g) * half + start, size)

        copies = []
        for g in range(2):
            copies.append(
                [
                    pltpu.make_async_copy(
                        w_ref.at[block_rows(g), :, :, columns], w_in.at[g], sem_in.at[g, 0]
                    ),
                    pltpu.make_async_copy(m1_ref.at[block_rows(g)], m1_in.at[g], sem_in.at[g, 1]),
                    pltpu.make_async_copy(m2_ref.at[block_rows(g)], m2_in.at[g], sem_in.at[g, 2]),
                ]
                + [
                    pltpu.make_async_copy(grad_refs[j], grads.at[j], sem_grad.at[j])
                    for j in range(g, n_own, 2)
                ]
            )
            for copy in copies[g]:
                copy.start()
        outs = []
        for g in range(2):
            for copy in copies[g]:
                copy.wait()

            def step(i, _, g=g):
                gradient = grads[g, i].astype(jnp.float32)
                for j in range(g + 2, n_own, 2):
                    gradient = gradient + grads[j, i].astype(jnp.float32)
                one = 0.9 * m1_in[g, i] + 0.1 * gradient
                two = 0.999 * m2_in[g, i] + 0.001 * gradient * gradient
                m1_out[g, i] = one
                m2_out[g, i] = two
                spread = two * (1.0 / correct_two)
                updated = w_in[g, i].astype(jnp.float32) - one * (learn_rate / correct_one) / (
                    spread * lax.rsqrt(spread) + 1e-08
                )
                w_out[g, i] = updated.astype(jnp.bfloat16)
                return 0

            lax.fori_loop(0, size, step, 0)
            outs += [
                pltpu.make_async_copy(w_out.at[g], new_w.at[core ^ g], sem_out.at[g, 0]),
                pltpu.make_async_copy(m1_out.at[g], new_m1.at[block_rows(g)], sem_out.at[g, 1]),
                pltpu.make_async_copy(m2_out.at[g], new_m2.at[block_rows(g)], sem_out.at[g, 2]),
            ]
            for copy in outs[-3:]:
                copy.start()
        for copy in outs:
            copy.wait()

    anywhere = pl.BlockSpec(memory_space=pl.ANY)
    blocks = (2, size, 2, piece, width)
    return pl.pallas_call(
        body,
        out_shape=[
            jax.ShapeDtypeStruct(blocks, jnp.bfloat16),
            jax.ShapeDtypeStruct(moment1.shape, jnp.float32),
            jax.ShapeDtypeStruct(moment1.shape, jnp.float32),
        ],
        in_specs=[smem()] + [anywhere] * (n_own + 3 + len(before)),
        out_specs=[anywhere] * 3,
        scratch_shapes=[
            pltpu.VMEM((n_own,) + blocks[1:], jnp.bfloat16),
            pltpu.VMEM(blocks, jnp.bfloat16),
            pltpu.VMEM(blocks, jnp.float32),
            pltpu.VMEM(blocks, jnp.float32),
            pltpu.VMEM(blocks, jnp.bfloat16),
            pltpu.VMEM(blocks, jnp.float32),
            pltpu.VMEM(blocks, jnp.float32),
            pltpu.SemaphoreType.DMA((2, 3)),
            pltpu.SemaphoreType.DMA((n_own,)),
            pltpu.SemaphoreType.DMA((2, 3)),
        ],
        input_output_aliases={1 + n_own + 3 + i: 1 + i for i in range(len(before))},
        compiler_params=params(),
        name="adam_step",
    )(pos, *arrived, weights, moment1, moment2, *before)


def place_weights(pos, pieces, start, half, before):
    n_dp = len(pieces)
    _, size, _, piece, width = pieces[0].shape
    pieces = list(pieces)
    far = isinstance(pieces[-1], tuple)
    if far:
        pieces[-1:] = pieces[-1]
    n_in = len(pieces)

    def body(pos_ref, *refs):
        out_ref, held, sems, sem_out = refs[-4:]
        dp_at = pos_ref[0]
        inner = (dp_at > 0) & (dp_at < n_dp - 1)

        def each(act):
            for j in range(n_dp):
                columns = pl.ds(pl.multiple_of((dp_at ^ j) * width, 128), width)

                def copy(i, j=j, columns=columns):
                    return pltpu.make_async_copy(
                        refs[i], held.at[:, :, :, :, columns], sems.at[j]
                    )

                if far and j == n_dp - 1:
                    pl.when(inner)(lambda: act(copy(j)))
                    pl.when(~inner)(lambda: act(copy(j + 1)))
                else:
                    act(copy(j))

        each(lambda copy: copy.start())
        each(lambda copy: copy.wait())
        outs = [
            pltpu.make_async_copy(
                held.at[h], out_ref.at[pl.ds(h * half + start, size)], sem_out.at[h]
            )
            for h in range(2)
        ]
        for copy in outs:
            copy.start()
        for copy in outs:
            copy.wait()

    anywhere = pl.BlockSpec(memory_space=pl.ANY)
    return pl.pallas_call(
        body,
        out_shape=jax.ShapeDtypeStruct((2 * half, 2, piece, n_dp * width), jnp.bfloat16),
        in_specs=[smem()] + [anywhere] * (n_in + len(before)),
        out_specs=anywhere,
        scratch_shapes=[
            pltpu.VMEM((2, size, 2, piece, n_dp * width), jnp.bfloat16),
            pltpu.SemaphoreType.DMA((n_dp,)),
            pltpu.SemaphoreType.DMA((2,)),
        ],
        input_output_aliases={1 + n_in: 0} if before else {},
        compiler_params=params(),
        name="place_weights",
    )(pos, *pieces, *before)


def after(value, *others):
    return lax.optimization_barrier((value,) + others)[0]


def gather_planes(fresh, dp_at, n_dp):
    if n_dp != 4:
        whole = lax.all_gather(fresh, "dp", axis=0)
        return [
            lax.dynamic_index_in_dim(whole, dp_at ^ j, 0, keepdims=False) for j in range(n_dp)
        ]
    two = lax.ppermute(fresh, "dp", [(0, 2), (1, 3), (2, 0), (3, 1)])
    one = lax.ppermute(fresh, "dp", [(0, 1), (1, 0), (2, 3), (3, 2)])
    middle = lax.ppermute(fresh, "dp", [(1, 2), (2, 1)])
    outer = lax.ppermute(two, "dp", [(2, 3), (1, 0)])
    return [fresh, one, two, (middle, outer)]


def finish_predicted(perm, total):
    def body(perm_ref, total_ref, out_ref):
        out_ref[...] = lax.dot_general(
            perm_ref[...],
            total_ref[...].astype(jnp.bfloat16),
            (((0,), (0,)), ((), ())),
            preferred_element_type=jnp.float32,
        ).astype(jnp.bfloat16)

    return pl.pallas_call(
        body,
        out_shape=jax.ShapeDtypeStruct(total.shape, jnp.bfloat16),
        in_specs=[vmem(), vmem()],
        out_specs=vmem(),
        compiler_params=params(),
        name="finish_predicted",
    )(perm, total)


def shards(signals, cotangent, row_insertion, touched, slot_map, weights, moment1, moment2):
    n_own = lax.axis_size("own")
    n_dp = lax.axis_size("dp")
    dp_at = lax.axis_index("dp")
    own_at = lax.axis_index("own")
    number, _, piece, _ = weights.shape
    width = moment1.shape[3]
    half = number // 2
    rows = signals.shape[0]
    pos = jnp.stack([dp_at, own_at]).astype(jnp.int32)
    core = lax.rem(own_at, 2)
    parts_of_half = sum(CHUNK_PARTS)
    sizes = [half * part // parts_of_half for part in CHUNK_PARTS]

    def across(value, j):
        return lax.ppermute(value, "own", [(o, o ^ j) for o in range(n_own)])

    packed, perm = pack_rows(row_insertion.reshape(1, rows), signals, cotangent)
    planes = lax.all_gather(packed, "dp", axis=0)

    column = lax.dynamic_slice_in_dim(weights, dp_at * width, width, 3)
    outgoing = jnp.broadcast_to(
        column.reshape(1, 2, half, 2, piece, width), (n_own // 2, 2, half, 2, piece, width)
    ).reshape(n_own, half, 2, piece, width)
    blocks = lax.all_to_all(outgoing, "own", split_axis=0, concat_axis=0, tiled=True)

    rows_in = (planes, across(planes, 1))
    pred_mine, pred_other, grads = local_grads(
        pos, touched, slot_map, rows_in, blocks, sizes, piece, width
    )
    pred_part = pred_mine + across(pred_other, 1)
    total = lax.psum_scatter(pred_part, "dp", scatter_dimension=0)

    arrived = []
    for chunk in grads:
        for j in range(1, n_own if arrived else 1):
            chunk[j] = after(chunk[j], arrived[-1][j])
        arrived.append([chunk[0]] + [across(chunk[j], j) for j in range(1, n_own)])
    ready = [list(one) for one in arrived]
    ready[0][-1] = after(ready[0][-1], pred_part, *arrived[-1][1 : n_own // 2])

    moments = []
    new_weights = []
    start = 0
    for size, chunk in zip(sizes, ready):
        if start:
            chunk[-1] = after(chunk[-1], *jax.tree.leaves(pieces[1:]))
        fresh, *moments = adam(pos, chunk, weights, moment1, moment2, start, moments)
        pieces = gather_planes(fresh, dp_at, n_dp)
        new_weights = [place_weights(pos, pieces, start, half, new_weights)]
        start += size
    new_weights = new_weights[0]
    new_moment1, new_moment2 = moments

    predicted = finish_predicted(perm, total)
    return (predicted, new_weights, new_moment1, new_moment2)


def solution(mesh):
    in_specs = (
        P(("dp", "own"), None),
        P(("dp", "own"), None),
        P(("dp", "own")),
        P(),
        P(),
        P(None, None, "own", None),
        P(None, None, "own", "dp"),
        P(None, None, "own", "dp"),
    )
    out_specs = (
        P(("dp", "own"), None),
        P(None, None, "own", None),
        P(None, None, "own", "dp"),
        P(None, None, "own", "dp"),
    )
    return jax.shard_map(shards, mesh=mesh, in_specs=in_specs, out_specs=out_specs, check_vma=False)
```

```python
import math

import jax
import jax.numpy as jnp
from jax import lax
from jax.experimental import pallas as pl
from jax.experimental.pallas import tpu as pltpu
from jax.sharding import PartitionSpec as P

SITES = 384
CAP = 128
CHUNK_PARTS = (3, 5)
ID_ROWS = 16
VMEM_BYTES = 56 * 2**20

gelu_coef = math.sqrt(2.0 / math.pi)
cubic_coef = 0.044715
learn_rate = 0.01


def gelu_parts(preact):
    tanh_input = gelu_coef * (preact + cubic_coef * preact * preact * preact)
    tangent = jnp.tanh(tanh_input)
    gelu_val = 0.5 * preact * (1.0 + tangent)
    slopes = 0.5 * (1.0 + tangent) + 0.5 * preact * (1.0 - tangent * tangent) * gelu_coef * (
        1.0 + 3.0 * cubic_coef * preact * preact
    )
    return (gelu_val, slopes)


def params():
    return pltpu.CompilerParams(vmem_limit_bytes=VMEM_BYTES)


def vmem():
    return pl.BlockSpec(memory_space=pltpu.VMEM)


def smem():
    return pl.BlockSpec(memory_space=pltpu.SMEM)


def pack_rows(ids, signals, cotangent):
    rows = signals.shape[0]

    def body(ids_ref, sig_ref, cot_ref, out_ref, perm_ref):
        ids_row = ids_ref[...].astype(jnp.float32)
        lane_ids = jnp.broadcast_to(ids_row, (rows, rows))
        same = lane_ids == lane_ids.T
        count = jnp.sum(same.astype(jnp.float32), axis=0, keepdims=True)
        full = jnp.max(jnp.where(count == CAP, ids_row, -1.0), axis=1, keepdims=True)
        chosen = ids_row == full
        from_row = lax.broadcasted_iota(jnp.int32, (rows, rows), 0)
        to_lane = lax.broadcasted_iota(jnp.int32, (rows, rows), 1)
        upto = (from_row <= to_lane).astype(jnp.bfloat16)
        ahead = jnp.dot(
            jnp.broadcast_to(chosen.astype(jnp.float32), (8, rows)).astype(jnp.bfloat16),
            upto,
            preferred_element_type=jnp.float32,
        )[:1].astype(jnp.int32)
        place = jnp.where(chosen, ahead - 1, CAP + to_lane[:1] - ahead)
        perm = (from_row == place).astype(jnp.float32).astype(jnp.bfloat16)
        perm_ref[...] = perm
        out_ref[:rows] = jnp.dot(perm, sig_ref[...], preferred_element_type=jnp.float32).astype(
            jnp.bfloat16
        )
        out_ref[rows : 2 * rows] = jnp.dot(
            perm, cot_ref[...], preferred_element_type=jnp.float32
        ).astype(jnp.bfloat16)
        sorted_ids = lax.dot_general(
            jnp.broadcast_to(ids_row, (ID_ROWS, rows)).astype(jnp.bfloat16),
            perm,
            (((1,), (1,)), ((), ())),
            preferred_element_type=jnp.float32,
        ).astype(jnp.bfloat16)
        out_ref[2 * rows :, :rows] = sorted_ids
        out_ref[2 * rows :, rows:] = jnp.zeros((ID_ROWS, SITES - rows), jnp.bfloat16)

    return pl.pallas_call(
        body,
        out_shape=(
            jax.ShapeDtypeStruct((2 * rows + ID_ROWS, SITES), jnp.bfloat16),
            jax.ShapeDtypeStruct((rows, rows), jnp.bfloat16),
        ),
        in_specs=[vmem(), vmem(), vmem()],
        out_specs=(vmem(), vmem()),
        compiler_params=params(),
        name="pack_rows",
    )(ids, signals, cotangent)


def local_grads(pos, touched, slot_map, rows_in, blocks, sizes, piece, width):
    planes = rows_in[0].shape[0]
    rows = (rows_in[0].shape[1] - ID_ROWS) // 2
    touch = touched.shape[1]
    n_own = blocks.shape[0]
    half = sum(sizes)
    aligned = piece % 16 == 0
    n_out = n_own if aligned else 1
    starts = [sum(sizes[:i]) for i in range(len(sizes))]

    def body(pos_ref, touched_ref, slot_ref, *rest):
        row_refs = rest[:2]
        blocks_ref = rest[2]
        rest = rest[3:]
        pred_refs = rest[:2]
        grad_refs = rest[2:-8]
        acc, id_cols, held, sorted_rows, pred, full_of, tasks, sems = rest[-8:]
        own_at = pos_ref[1]
        core = lax.rem(own_at, 2)

        def sites(j):
            return pl.ds(pl.multiple_of((own_at ^ j) * piece, 16), piece)

        row_copies = [
            pltpu.make_async_copy(ref, sorted_rows.at[pl.ds(i * planes, planes)], sems.at[i])
            for i, ref in enumerate(row_refs)
        ]
        if aligned:
            block_copies = [
                pltpu.make_async_copy(
                    blocks_ref.at[i], held.at[:, :, pl.ds(i * piece, piece), :], sems.at[2 + i]
                )
                for i in range(n_own)
            ]
        else:
            block_copies = [pltpu.make_async_copy(blocks_ref, held, sems.at[2])]
        for copy in row_copies + block_copies:
            copy.start()

        def clear(e, _):
            acc[e] = jnp.zeros(acc.shape[1:], jnp.float32)
            return 0

        lax.fori_loop(0, half, clear, 0)
        pred[...] = jnp.zeros_like(pred)
        for copy in row_copies:
            copy.wait()
        for source in range(2 * planes):
            ids_row = sorted_rows[source, 2 * rows :, :rows][:1].astype(jnp.float32)
            id_cols[source] = jnp.broadcast_to(ids_row, (128, rows)).T
            full_of[source] = jnp.max(ids_row[:, :128]).astype(jnp.int32)

        def listing(t, count):
            source = t // (touch + 1)
            j = t - source * (touch + 1)
            which = source // planes
            device = (source - which * planes) * n_own + (own_at ^ which)
            full = full_of[source]
            insertion = jnp.where(j == 0, full, touched_ref[device, jnp.maximum(j - 1, 0)])
            e = slot_ref[insertion] - core * half
            here = (e >= 0) & (e < half) & ((j == 0) | (insertion != full))
            tasks[0, count] = source
            tasks[1, count] = jnp.where(j == 0, 0, CAP)
            tasks[2, count] = insertion
            tasks[3, count] = e
            return count + here.astype(jnp.int32)

        count = lax.fori_loop(0, 2 * planes * (touch + 1), listing, 0)
        tasks[0, count] = 0
        tasks[1, count] = 0
        tasks[2, count] = -1
        tasks[3, count] = 0
        for copy in block_copies:
            copy.wait()

        def pair(i, _):
            loaded = []
            for u in range(2):
                source, insertion, e = tasks[0, 2 * i + u], tasks[2, 2 * i + u], tasks[3, 2 * i + u]
                first = pl.multiple_of(tasks[1, 2 * i + u], CAP)
                keep = (
                    (id_cols[source, pl.ds(first, CAP), :] == insertion.astype(jnp.float32))
                    .astype(jnp.float32)
                    .astype(jnp.bfloat16)
                )
                keep = jnp.concatenate([keep] * (SITES // 128), axis=1)
                sig = sorted_rows[source, pl.ds(first, CAP), :] * keep
                cot = sorted_rows[source, pl.ds(rows + first, CAP), :] * keep
                loaded.append((source, first, e, sig, cot))
            found = []
            for source, first, e, sig, cot in loaded:
                read_out = held[e, 1]
                preact = jnp.dot(sig, held[e, 0], preferred_element_type=jnp.float32)
                back_hidden = jnp.dot(cot, read_out, preferred_element_type=jnp.float32)
                gelu_val, slopes = gelu_parts(preact)
                hidden = gelu_val.astype(jnp.bfloat16)
                back_pre = (back_hidden * slopes).astype(jnp.bfloat16)
                part = lax.dot_general(
                    hidden, read_out, (((1,), (1,)), ((), ())), preferred_element_type=jnp.float32
                ).astype(jnp.bfloat16)
                grad_in = lax.dot_general(
                    sig, back_pre, (((0,), (0,)), ((), ())), preferred_element_type=jnp.float32
                )
                grad_out = lax.dot_general(
                    cot, hidden, (((0,), (0,)), ((), ())), preferred_element_type=jnp.float32
                )
                found.append((part, grad_in, grad_out))
            for (source, first, e, _, _), (part, grad_in, grad_out) in zip(loaded, found):
                pred[source, pl.ds(first, CAP), :] += part
                acc[e, 0] += grad_in
                acc[e, 1] += grad_out
            return 0

        lax.fori_loop(0, (count + 1) // 2, pair, 0)
        for which, ref in enumerate(pred_refs):
            ref[...] = pred[which * planes : (which + 1) * planes]
        for chunk, (start, size) in enumerate(zip(starts, sizes)):
            for j in range(n_out):
                ref = grad_refs[chunk * n_out + j]

                def write(e, _, start=start, ref=ref, j=j):
                    if aligned:
                        ref[e] = acc[start + e, :, sites(j), :].astype(jnp.bfloat16)
                    else:
                        ref[e] = acc[start + e].astype(jnp.bfloat16)
                    return 0

                lax.fori_loop(0, size, write, 0)

    pred_shape = jax.ShapeDtypeStruct((planes, rows, SITES), jnp.bfloat16)
    grad_shapes = [
        jax.ShapeDtypeStruct((size, 2, piece if aligned else SITES, width), jnp.bfloat16)
        for size in sizes
        for _ in range(n_out)
    ]
    most = 2 * planes * (touch + 1)
    scratch = [
        pltpu.VMEM((half, 2, SITES, width), jnp.float32),
        pltpu.VMEM((2 * planes, rows, 128), jnp.float32),
        pltpu.VMEM((half, 2, SITES, width), jnp.bfloat16),
        pltpu.VMEM((2 * planes,) + rows_in[0].shape[1:], jnp.bfloat16),
        pltpu.VMEM((2 * planes, rows, SITES), jnp.bfloat16),
        pltpu.SMEM((2 * planes,), jnp.int32),
        pltpu.SMEM((4, most + 1), jnp.int32),
        pltpu.SemaphoreType.DMA((2 + n_own,)),
    ]
    own_at = pos[1]
    if not aligned:
        blocks = blocks.transpose(1, 2, 0, 3, 4).reshape(half, 2, SITES, width)
    found = pl.pallas_call(
        body,
        out_shape=[pred_shape, pred_shape] + grad_shapes,
        in_specs=[smem(), smem(), smem()] + [pl.BlockSpec(memory_space=pl.ANY)] * 3,
        out_specs=[vmem()] * (2 + len(grad_shapes)),
        scratch_shapes=scratch,
        compiler_params=params(),
        name="local_grads",
    )(pos, touched, slot_map, *rows_in, blocks)
    grads = []
    for chunk in range(len(sizes)):
        outs = list(found[2 + chunk * n_out : 2 + (chunk + 1) * n_out])
        if not aligned:
            outs = [
                lax.dynamic_slice_in_dim(outs[0], (own_at ^ j) * piece, piece, 2)
                for j in range(n_own)
            ]
        grads.append(outs)
    return found[0], found[1], grads


def adam(pos, arrived, weights, moment1, moment2, start, before):
    n_own = len(arrived)
    size, _, piece, width = arrived[0].shape
    number = weights.shape[0]
    half = number // 2
    correct_one = 1.0 - 0.9**10
    correct_two = 1.0 - 0.999**10

    def body(pos_ref, *refs):
        grad_refs = refs[:n_own]
        w_ref, m1_ref, m2_ref = refs[n_own : n_own + 3]
        new_w, new_m1, new_m2 = refs[n_own + 3 + len(before) : n_own + 6 + len(before)]
        grads, w_in, m1_in, m2_in, w_out, m1_out, m2_out, sem_in, sem_grad, sem_out = refs[
            n_own + 6 + len(before) :
        ]
        core = lax.rem(pos_ref[1], 2)
        columns = pl.ds(pl.multiple_of(pos_ref[0] * width, 128), width)

        def block_rows(g):
            return pl.ds((core ^ g) * half + start, size)

        copies = []
        for g in range(2):
            copies.append(
                [
                    pltpu.make_async_copy(
                        w_ref.at[block_rows(g), :, :, columns], w_in.at[g], sem_in.at[g, 0]
                    ),
                    pltpu.make_async_copy(m1_ref.at[block_rows(g)], m1_in.at[g], sem_in.at[g, 1]),
                    pltpu.make_async_copy(m2_ref.at[block_rows(g)], m2_in.at[g], sem_in.at[g, 2]),
                ]
                + [
                    pltpu.make_async_copy(grad_refs[j], grads.at[j], sem_grad.at[j])
                    for j in range(g, n_own, 2)
                ]
            )
            for copy in copies[g]:
                copy.start()
        outs = []
        for g in range(2):
            for copy in copies[g]:
                copy.wait()

            def step(i, _, g=g):
                gradient = grads[g, i].astype(jnp.float32)
                for j in range(g + 2, n_own, 2):
                    gradient = gradient + grads[j, i].astype(jnp.float32)
                one = 0.9 * m1_in[g, i] + 0.1 * gradient
                two = 0.999 * m2_in[g, i] + 0.001 * gradient * gradient
                m1_out[g, i] = one
                m2_out[g, i] = two
                spread = two * (1.0 / correct_two)
                updated = w_in[g, i].astype(jnp.float32) - one * (learn_rate / correct_one) / (
                    spread * lax.rsqrt(spread) + 1e-08
                )
                w_out[g, i] = updated.astype(jnp.bfloat16)
                return 0

            lax.fori_loop(0, size, step, 0)
            outs += [
                pltpu.make_async_copy(w_out.at[g], new_w.at[core ^ g], sem_out.at[g, 0]),
                pltpu.make_async_copy(m1_out.at[g], new_m1.at[block_rows(g)], sem_out.at[g, 1]),
                pltpu.make_async_copy(m2_out.at[g], new_m2.at[block_rows(g)], sem_out.at[g, 2]),
            ]
            for copy in outs[-3:]:
                copy.start()
        for copy in outs:
            copy.wait()

    anywhere = pl.BlockSpec(memory_space=pl.ANY)
    blocks = (2, size, 2, piece, width)
    return pl.pallas_call(
        body,
        out_shape=[
            jax.ShapeDtypeStruct(blocks, jnp.bfloat16),
            jax.ShapeDtypeStruct(moment1.shape, jnp.float32),
            jax.ShapeDtypeStruct(moment1.shape, jnp.float32),
        ],
        in_specs=[smem()] + [anywhere] * (n_own + 3 + len(before)),
        out_specs=[anywhere] * 3,
        scratch_shapes=[
            pltpu.VMEM((n_own,) + blocks[1:], jnp.bfloat16),
            pltpu.VMEM(blocks, jnp.bfloat16),
            pltpu.VMEM(blocks, jnp.float32),
            pltpu.VMEM(blocks, jnp.float32),
            pltpu.VMEM(blocks, jnp.bfloat16),
            pltpu.VMEM(blocks, jnp.float32),
            pltpu.VMEM(blocks, jnp.float32),
            pltpu.SemaphoreType.DMA((2, 3)),
            pltpu.SemaphoreType.DMA((n_own,)),
            pltpu.SemaphoreType.DMA((2, 3)),
        ],
        input_output_aliases={1 + n_own + 3 + i: 1 + i for i in range(len(before))},
        compiler_params=params(),
        name="adam_step",
    )(pos, *arrived, weights, moment1, moment2, *before)


def place_weights(pos, pieces, start, half, before):
    n_dp = len(pieces)
    _, size, _, piece, width = pieces[0].shape
    pieces = list(pieces)
    far = isinstance(pieces[-1], tuple)
    if far:
        pieces[-1:] = pieces[-1]
    n_in = len(pieces)

    def body(pos_ref, *refs):
        out_ref, held, sems, sem_out = refs[-4:]
        dp_at = pos_ref[0]
        inner = (dp_at > 0) & (dp_at < n_dp - 1)

        def each(act):
            for j in range(n_dp):
                columns = pl.ds(pl.multiple_of((dp_at ^ j) * width, 128), width)

                def copy(i, j=j, columns=columns):
                    return pltpu.make_async_copy(
                        refs[i], held.at[:, :, :, :, columns], sems.at[j]
                    )

                if far and j == n_dp - 1:
                    pl.when(inner)(lambda: act(copy(j)))
                    pl.when(~inner)(lambda: act(copy(j + 1)))
                else:
                    act(copy(j))

        each(lambda copy: copy.start())
        each(lambda copy: copy.wait())
        outs = [
            pltpu.make_async_copy(
                held.at[h], out_ref.at[pl.ds(h * half + start, size)], sem_out.at[h]
            )
            for h in range(2)
        ]
        for copy in outs:
            copy.start()
        for copy in outs:
            copy.wait()

    anywhere = pl.BlockSpec(memory_space=pl.ANY)
    return pl.pallas_call(
        body,
        out_shape=jax.ShapeDtypeStruct((2 * half, 2, piece, n_dp * width), jnp.bfloat16),
        in_specs=[smem()] + [anywhere] * (n_in + len(before)),
        out_specs=anywhere,
        scratch_shapes=[
            pltpu.VMEM((2, size, 2, piece, n_dp * width), jnp.bfloat16),
            pltpu.SemaphoreType.DMA((n_dp,)),
            pltpu.SemaphoreType.DMA((2,)),
        ],
        input_output_aliases={1 + n_in: 0} if before else {},
        compiler_params=params(),
        name="place_weights",
    )(pos, *pieces, *before)


def after(value, *others):
    return lax.optimization_barrier((value,) + others)[0]


def gather_planes(fresh, dp_at, n_dp, before):
    if n_dp != 4:
        whole = lax.all_gather(fresh, "dp", axis=0)
        return [
            lax.dynamic_index_in_dim(whole, dp_at ^ j, 0, keepdims=False) for j in range(n_dp)
        ]
    two = lax.ppermute(fresh, "dp", [(0, 2), (1, 3), (2, 0), (3, 1)])
    one = lax.ppermute(fresh, "dp", [(0, 1), (1, 0), (2, 3), (3, 2)])
    middle = lax.ppermute(fresh, "dp", [(1, 2), (2, 1)])
    outer = lax.ppermute(after(two, *before), "dp", [(2, 3), (1, 0)])
    return [fresh, one, two, (middle, outer)]


def finish_predicted(perm, total):
    def body(perm_ref, total_ref, out_ref):
        out_ref[...] = lax.dot_general(
            perm_ref[...],
            total_ref[...].astype(jnp.bfloat16),
            (((0,), (0,)), ((), ())),
            preferred_element_type=jnp.float32,
        ).astype(jnp.bfloat16)

    return pl.pallas_call(
        body,
        out_shape=jax.ShapeDtypeStruct(total.shape, jnp.bfloat16),
        in_specs=[vmem(), vmem()],
        out_specs=vmem(),
        compiler_params=params(),
        name="finish_predicted",
    )(perm, total)


def shards(signals, cotangent, row_insertion, touched, slot_map, weights, moment1, moment2):
    n_own = lax.axis_size("own")
    n_dp = lax.axis_size("dp")
    dp_at = lax.axis_index("dp")
    own_at = lax.axis_index("own")
    number, _, piece, _ = weights.shape
    width = moment1.shape[3]
    half = number // 2
    rows = signals.shape[0]
    pos = jnp.stack([dp_at, own_at]).astype(jnp.int32)
    core = lax.rem(own_at, 2)
    parts_of_half = sum(CHUNK_PARTS)
    sizes = [half * part // parts_of_half for part in CHUNK_PARTS]

    def across(value, j):
        return lax.ppermute(value, "own", [(o, o ^ j) for o in range(n_own)])

    packed, perm = pack_rows(row_insertion.reshape(1, rows), signals, cotangent)
    planes = lax.all_gather(packed, "dp", axis=0)

    column = lax.dynamic_slice_in_dim(weights, dp_at * width, width, 3)
    outgoing = jnp.broadcast_to(
        column.reshape(1, 2, half, 2, piece, width), (n_own // 2, 2, half, 2, piece, width)
    ).reshape(n_own, half, 2, piece, width)
    blocks = lax.all_to_all(outgoing, "own", split_axis=0, concat_axis=0, tiled=True)

    rows_in = (planes, across(planes, 1))
    pred_mine, pred_other, grads = local_grads(
        pos, touched, slot_map, rows_in, blocks, sizes, piece, width
    )
    arrived = []
    for chunk in grads:
        for j in range(1, n_own if arrived else 1):
            chunk[j] = after(chunk[j], arrived[-1][j])
        arrived.append([chunk[0]] + [across(chunk[j], j) for j in range(1, n_own)])
    pred_other = across(after(pred_other, arrived[0][1]), 1)
    pred_part = pred_mine.astype(jnp.float32) + pred_other.astype(jnp.float32)
    total = lax.psum_scatter(pred_part, "dp", scatter_dimension=0)

    moments = []
    new_weights = []
    start = 0
    for i, size in enumerate(sizes):
        ready = list(arrived[i])
        ready[-1] = after(ready[-1], *(jax.tree.leaves(pieces[1:])[:n_dp - 1] if i else [pred_part]))
        fresh, *moments = adam(pos, ready, weights, moment1, moment2, start, moments)
        later = arrived[i + 1][1 : n_own // 2 + 1] if i + 1 < len(sizes) else []
        pieces = gather_planes(fresh, dp_at, n_dp, later)
        new_weights = [place_weights(pos, pieces, start, half, new_weights)]
        start += size
    new_weights = new_weights[0]
    new_moment1, new_moment2 = moments

    predicted = finish_predicted(perm, total)
    return (predicted, new_weights, new_moment1, new_moment2)


def solution(mesh):
    in_specs = (
        P(("dp", "own"), None),
        P(("dp", "own"), None),
        P(("dp", "own")),
        P(),
        P(),
        P(None, None, "own", None),
        P(None, None, "own", "dp"),
        P(None, None, "own", "dp"),
    )
    out_specs = (
        P(("dp", "own"), None),
        P(None, None, "own", None),
        P(None, None, "own", "dp"),
        P(None, None, "own", "dp"),
    )
    return jax.shard_map(shards, mesh=mesh, in_specs=in_specs, out_specs=out_specs, check_vma=False)
```

```python
import math

import jax
import jax.numpy as jnp
from jax import lax
from jax.experimental import pallas as pl
from jax.experimental.pallas import tpu as pltpu
from jax.sharding import PartitionSpec as P

SITES = 384
CAP = 128
CHUNK_PARTS = (3, 5)
ID_ROWS = 16
VMEM_BYTES = 56 * 2**20

gelu_coef = math.sqrt(2.0 / math.pi)
cubic_coef = 0.044715
learn_rate = 0.01


def gelu_parts(preact):
    tanh_input = gelu_coef * (preact + cubic_coef * preact * preact * preact)
    tangent = jnp.tanh(tanh_input)
    gelu_val = 0.5 * preact * (1.0 + tangent)
    slopes = 0.5 * (1.0 + tangent) + 0.5 * preact * (1.0 - tangent * tangent) * gelu_coef * (
        1.0 + 3.0 * cubic_coef * preact * preact
    )
    return (gelu_val, slopes)


def params():
    return pltpu.CompilerParams(vmem_limit_bytes=VMEM_BYTES)


def vmem():
    return pl.BlockSpec(memory_space=pltpu.VMEM)


def smem():
    return pl.BlockSpec(memory_space=pltpu.SMEM)


def pack_rows(ids, signals, cotangent):
    rows = signals.shape[0]

    def body(ids_ref, sig_ref, cot_ref, out_ref, perm_ref):
        ids_row = ids_ref[...].astype(jnp.float32)
        lane_ids = jnp.broadcast_to(ids_row, (rows, rows))
        same = lane_ids == lane_ids.T
        count = jnp.sum(same.astype(jnp.float32), axis=0, keepdims=True)
        full = jnp.max(jnp.where(count == CAP, ids_row, -1.0), axis=1, keepdims=True)
        chosen = ids_row == full
        from_row = lax.broadcasted_iota(jnp.int32, (rows, rows), 0)
        to_lane = lax.broadcasted_iota(jnp.int32, (rows, rows), 1)
        upto = (from_row <= to_lane).astype(jnp.bfloat16)
        ahead = jnp.dot(
            jnp.broadcast_to(chosen.astype(jnp.float32), (8, rows)).astype(jnp.bfloat16),
            upto,
            preferred_element_type=jnp.float32,
        )[:1].astype(jnp.int32)
        place = jnp.where(chosen, ahead - 1, CAP + to_lane[:1] - ahead)
        perm = (from_row == place).astype(jnp.float32).astype(jnp.bfloat16)
        perm_ref[...] = perm
        out_ref[:rows] = jnp.dot(perm, sig_ref[...], preferred_element_type=jnp.float32).astype(
            jnp.bfloat16
        )
        out_ref[rows : 2 * rows] = jnp.dot(
            perm, cot_ref[...], preferred_element_type=jnp.float32
        ).astype(jnp.bfloat16)
        sorted_ids = lax.dot_general(
            jnp.broadcast_to(ids_row, (ID_ROWS, rows)).astype(jnp.bfloat16),
            perm,
            (((1,), (1,)), ((), ())),
            preferred_element_type=jnp.float32,
        ).astype(jnp.bfloat16)
        out_ref[2 * rows :, :rows] = sorted_ids
        out_ref[2 * rows :, rows:] = jnp.zeros((ID_ROWS, SITES - rows), jnp.bfloat16)

    return pl.pallas_call(
        body,
        out_shape=(
            jax.ShapeDtypeStruct((2 * rows + ID_ROWS, SITES), jnp.bfloat16),
            jax.ShapeDtypeStruct((rows, rows), jnp.bfloat16),
        ),
        in_specs=[vmem(), vmem(), vmem()],
        out_specs=(vmem(), vmem()),
        compiler_params=params(),
        name="pack_rows",
    )(ids, signals, cotangent)


def local_grads(pos, touched, slot_map, rows_in, blocks, sizes, piece, width):
    planes = rows_in[0].shape[0]
    rows = (rows_in[0].shape[1] - ID_ROWS) // 2
    touch = touched.shape[1]
    n_own = blocks.shape[0]
    half = sum(sizes)
    aligned = piece % 16 == 0
    n_out = n_own if aligned else 1
    starts = [sum(sizes[:i]) for i in range(len(sizes))]

    def body(pos_ref, touched_ref, slot_ref, *rest):
        row_refs = rest[:2]
        blocks_ref = rest[2]
        rest = rest[3:]
        pred_refs = rest[:2]
        grad_refs = rest[2:-8]
        acc, id_cols, held, sorted_rows, pred, full_of, tasks, sems = rest[-8:]
        own_at = pos_ref[1]
        core = lax.rem(own_at, 2)

        def sites(j):
            return pl.ds(pl.multiple_of((own_at ^ j) * piece, 16), piece)

        row_copies = [
            pltpu.make_async_copy(ref, sorted_rows.at[pl.ds(i * planes, planes)], sems.at[i])
            for i, ref in enumerate(row_refs)
        ]
        if aligned:
            block_copies = [
                pltpu.make_async_copy(
                    blocks_ref.at[i], held.at[:, :, pl.ds(i * piece, piece), :], sems.at[2 + i]
                )
                for i in range(n_own)
            ]
        else:
            block_copies = [pltpu.make_async_copy(blocks_ref, held, sems.at[2])]
        for copy in row_copies + block_copies:
            copy.start()

        def clear(e, _):
            acc[e] = jnp.zeros(acc.shape[1:], jnp.float32)
            return 0

        lax.fori_loop(0, half, clear, 0)
        pred[...] = jnp.zeros_like(pred)
        for copy in row_copies:
            copy.wait()
        for source in range(2 * planes):
            ids_row = sorted_rows[source, 2 * rows :, :rows][:1].astype(jnp.float32)
            id_cols[source] = jnp.broadcast_to(ids_row, (128, rows)).T
            full_of[source] = jnp.max(ids_row[:, :128]).astype(jnp.int32)

        def listing(t, count):
            source = t // (touch + 1)
            j = t - source * (touch + 1)
            which = source // planes
            device = (source - which * planes) * n_own + (own_at ^ which)
            full = full_of[source]
            insertion = jnp.where(j == 0, full, touched_ref[device, jnp.maximum(j - 1, 0)])
            e = slot_ref[insertion] - core * half
            here = (e >= 0) & (e < half) & ((j == 0) | (insertion != full))
            tasks[0, count] = source
            tasks[1, count] = jnp.where(j == 0, 0, CAP)
            tasks[2, count] = insertion
            tasks[3, count] = e
            return count + here.astype(jnp.int32)

        count = lax.fori_loop(0, 2 * planes * (touch + 1), listing, 0)
        tasks[0, count] = 0
        tasks[1, count] = 0
        tasks[2, count] = -1
        tasks[3, count] = 0
        for copy in block_copies:
            copy.wait()

        def pair(i, _):
            loaded = []
            for u in range(2):
                source, insertion, e = tasks[0, 2 * i + u], tasks[2, 2 * i + u], tasks[3, 2 * i + u]
                first = pl.multiple_of(tasks[1, 2 * i + u], CAP)
                keep = (
                    (id_cols[source, pl.ds(first, CAP), :] == insertion.astype(jnp.float32))
                    .astype(jnp.float32)
                    .astype(jnp.bfloat16)
                )
                keep = jnp.concatenate([keep] * (SITES // 128), axis=1)
                sig = sorted_rows[source, pl.ds(first, CAP), :] * keep
                cot = sorted_rows[source, pl.ds(rows + first, CAP), :] * keep
                loaded.append((source, first, e, sig, cot))
            found = []
            for source, first, e, sig, cot in loaded:
                read_out = held[e, 1]
                preact = jnp.dot(sig, held[e, 0], preferred_element_type=jnp.float32)
                back_hidden = jnp.dot(cot, read_out, preferred_element_type=jnp.float32)
                gelu_val, slopes = gelu_parts(preact)
                hidden = gelu_val.astype(jnp.bfloat16)
                back_pre = (back_hidden * slopes).astype(jnp.bfloat16)
                part = lax.dot_general(
                    hidden, read_out, (((1,), (1,)), ((), ())), preferred_element_type=jnp.float32
                ).astype(jnp.bfloat16)
                grad_in = lax.dot_general(
                    sig, back_pre, (((0,), (0,)), ((), ())), preferred_element_type=jnp.float32
                )
                grad_out = lax.dot_general(
                    cot, hidden, (((0,), (0,)), ((), ())), preferred_element_type=jnp.float32
                )
                found.append((part, grad_in, grad_out))
            for (source, first, e, _, _), (part, grad_in, grad_out) in zip(loaded, found):
                pred[source, pl.ds(first, CAP), :] += part
                acc[e, 0] += grad_in
                acc[e, 1] += grad_out
            return 0

        lax.fori_loop(0, (count + 1) // 2, pair, 0)
        for which, ref in enumerate(pred_refs):
            ref[...] = pred[which * planes : (which + 1) * planes]
        for chunk, (start, size) in enumerate(zip(starts, sizes)):
            for j in range(n_out):
                ref = grad_refs[chunk * n_out + j]

                def write(e, _, start=start, ref=ref, j=j):
                    if aligned:
                        ref[e] = acc[start + e, :, sites(j), :].astype(jnp.bfloat16)
                    else:
                        ref[e] = acc[start + e].astype(jnp.bfloat16)
                    return 0

                lax.fori_loop(0, size, write, 0)

    pred_shape = jax.ShapeDtypeStruct((planes, rows, SITES), jnp.bfloat16)
    grad_shapes = [
        jax.ShapeDtypeStruct((size, 2, piece if aligned else SITES, width), jnp.bfloat16)
        for size in sizes
        for _ in range(n_out)
    ]
    most = 2 * planes * (touch + 1)
    scratch = [
        pltpu.VMEM((half, 2, SITES, width), jnp.float32),
        pltpu.VMEM((2 * planes, rows, 128), jnp.float32),
        pltpu.VMEM((half, 2, SITES, width), jnp.bfloat16),
        pltpu.VMEM((2 * planes,) + rows_in[0].shape[1:], jnp.bfloat16),
        pltpu.VMEM((2 * planes, rows, SITES), jnp.bfloat16),
        pltpu.SMEM((2 * planes,), jnp.int32),
        pltpu.SMEM((4, most + 1), jnp.int32),
        pltpu.SemaphoreType.DMA((2 + n_own,)),
    ]
    own_at = pos[1]
    if not aligned:
        blocks = blocks.transpose(1, 2, 0, 3, 4).reshape(half, 2, SITES, width)
    found = pl.pallas_call(
        body,
        out_shape=[pred_shape, pred_shape] + grad_shapes,
        in_specs=[smem(), smem(), smem()] + [pl.BlockSpec(memory_space=pl.ANY)] * 3,
        out_specs=[vmem()] * (2 + len(grad_shapes)),
        scratch_shapes=scratch,
        compiler_params=params(),
        name="local_grads",
    )(pos, touched, slot_map, *rows_in, blocks)
    grads = []
    for chunk in range(len(sizes)):
        outs = list(found[2 + chunk * n_out : 2 + (chunk + 1) * n_out])
        if not aligned:
            outs = [
                lax.dynamic_slice_in_dim(outs[0], (own_at ^ j) * piece, piece, 2)
                for j in range(n_own)
            ]
        grads.append(outs)
    return found[0], found[1], grads


def adam(pos, arrived, weights, moment1, moment2, start, before):
    n_own = len(arrived)
    size, _, piece, width = arrived[0].shape
    number = weights.shape[0]
    half = number // 2
    correct_one = 1.0 - 0.9**10
    correct_two = 1.0 - 0.999**10

    def body(pos_ref, *refs):
        grad_refs = refs[:n_own]
        w_ref, m1_ref, m2_ref = refs[n_own : n_own + 3]
        new_w, new_m1, new_m2 = refs[n_own + 3 + len(before) : n_own + 6 + len(before)]
        grads, w_in, m1_in, m2_in, w_out, m1_out, m2_out, sem_in, sem_grad, sem_out = refs[
            n_own + 6 + len(before) :
        ]
        core = lax.rem(pos_ref[1], 2)
        columns = pl.ds(pl.multiple_of(pos_ref[0] * width, 128), width)

        def block_rows(g):
            return pl.ds((core ^ g) * half + start, size)

        copies = []
        for g in range(2):
            copies.append(
                [
                    pltpu.make_async_copy(
                        w_ref.at[block_rows(g), :, :, columns], w_in.at[g], sem_in.at[g, 0]
                    ),
                    pltpu.make_async_copy(m1_ref.at[block_rows(g)], m1_in.at[g], sem_in.at[g, 1]),
                    pltpu.make_async_copy(m2_ref.at[block_rows(g)], m2_in.at[g], sem_in.at[g, 2]),
                ]
                + [
                    pltpu.make_async_copy(grad_refs[j], grads.at[j], sem_grad.at[j])
                    for j in range(g, n_own, 2)
                ]
            )
            for copy in copies[g]:
                copy.start()
        outs = []
        for g in range(2):
            for copy in copies[g]:
                copy.wait()

            def step(i, _, g=g):
                gradient = grads[g, i].astype(jnp.float32)
                for j in range(g + 2, n_own, 2):
                    gradient = gradient + grads[j, i].astype(jnp.float32)
                one = 0.9 * m1_in[g, i] + 0.1 * gradient
                two = 0.999 * m2_in[g, i] + 0.001 * gradient * gradient
                m1_out[g, i] = one
                m2_out[g, i] = two
                spread = two * (1.0 / correct_two)
                updated = w_in[g, i].astype(jnp.float32) - one * (learn_rate / correct_one) / (
                    spread * lax.rsqrt(spread) + 1e-08
                )
                w_out[g, i] = updated.astype(jnp.bfloat16)
                return 0

            lax.fori_loop(0, size, step, 0)
            outs += [
                pltpu.make_async_copy(w_out.at[g], new_w.at[core ^ g], sem_out.at[g, 0]),
                pltpu.make_async_copy(m1_out.at[g], new_m1.at[block_rows(g)], sem_out.at[g, 1]),
                pltpu.make_async_copy(m2_out.at[g], new_m2.at[block_rows(g)], sem_out.at[g, 2]),
            ]
            for copy in outs[-3:]:
                copy.start()
        for copy in outs:
            copy.wait()

    anywhere = pl.BlockSpec(memory_space=pl.ANY)
    blocks = (2, size, 2, piece, width)
    return pl.pallas_call(
        body,
        out_shape=[
            jax.ShapeDtypeStruct(blocks, jnp.bfloat16),
            jax.ShapeDtypeStruct(moment1.shape, jnp.float32),
            jax.ShapeDtypeStruct(moment1.shape, jnp.float32),
        ],
        in_specs=[smem()] + [anywhere] * (n_own + 3 + len(before)),
        out_specs=[anywhere] * 3,
        scratch_shapes=[
            pltpu.VMEM((n_own,) + blocks[1:], jnp.bfloat16),
            pltpu.VMEM(blocks, jnp.bfloat16),
            pltpu.VMEM(blocks, jnp.float32),
            pltpu.VMEM(blocks, jnp.float32),
            pltpu.VMEM(blocks, jnp.bfloat16),
            pltpu.VMEM(blocks, jnp.float32),
            pltpu.VMEM(blocks, jnp.float32),
            pltpu.SemaphoreType.DMA((2, 3)),
            pltpu.SemaphoreType.DMA((n_own,)),
            pltpu.SemaphoreType.DMA((2, 3)),
        ],
        input_output_aliases={1 + n_own + 3 + i: 1 + i for i in range(len(before))},
        compiler_params=params(),
        name="adam_step",
    )(pos, *arrived, weights, moment1, moment2, *before)


def place_weights(gathered, start, half, before):
    n_dp, _, size, _, piece, width = gathered.shape

    def body(gathered_ref, *refs):
        out_ref, held, sems, sem_out = refs[-4:]
        copies = [
            pltpu.make_async_copy(
                gathered_ref.at[d], held.at[:, :, :, :, pl.ds(d * width, width)], sems.at[d]
            )
            for d in range(n_dp)
        ]
        for copy in copies:
            copy.start()
        for copy in copies:
            copy.wait()
        outs = [
            pltpu.make_async_copy(
                held.at[h], out_ref.at[pl.ds(h * half + start, size)], sem_out.at[h]
            )
            for h in range(2)
        ]
        for copy in outs:
            copy.start()
        for copy in outs:
            copy.wait()

    anywhere = pl.BlockSpec(memory_space=pl.ANY)
    return pl.pallas_call(
        body,
        out_shape=jax.ShapeDtypeStruct((2 * half, 2, piece, n_dp * width), jnp.bfloat16),
        in_specs=[anywhere] * (1 + len(before)),
        out_specs=anywhere,
        scratch_shapes=[
            pltpu.VMEM((2, size, 2, piece, n_dp * width), jnp.bfloat16),
            pltpu.SemaphoreType.DMA((n_dp,)),
            pltpu.SemaphoreType.DMA((2,)),
        ],
        input_output_aliases={1: 0} if before else {},
        compiler_params=params(),
        name="place_weights",
    )(gathered, *before)


def after(value, *others):
    return lax.optimization_barrier((value,) + others)[0]


def finish_predicted(perm, parts):
    def body(perm_ref, *refs):
        total = refs[0][...].astype(jnp.float32)
        for ref in refs[1:-1]:
            total = total + ref[...].astype(jnp.float32)
        refs[-1][...] = lax.dot_general(
            perm_ref[...],
            total.astype(jnp.bfloat16),
            (((0,), (0,)), ((), ())),
            preferred_element_type=jnp.float32,
        ).astype(jnp.bfloat16)

    return pl.pallas_call(
        body,
        out_shape=jax.ShapeDtypeStruct(parts[0].shape, jnp.bfloat16),
        in_specs=[vmem()] * (1 + len(parts)),
        out_specs=vmem(),
        compiler_params=params(),
        name="finish_predicted",
    )(perm, *parts)


def shards(signals, cotangent, row_insertion, touched, slot_map, weights, moment1, moment2):
    n_own = lax.axis_size("own")
    n_dp = lax.axis_size("dp")
    dp_at = lax.axis_index("dp")
    own_at = lax.axis_index("own")
    number, _, piece, _ = weights.shape
    width = moment1.shape[3]
    half = number // 2
    rows = signals.shape[0]
    pos = jnp.stack([dp_at, own_at]).astype(jnp.int32)
    core = lax.rem(own_at, 2)
    parts_of_half = sum(CHUNK_PARTS)
    sizes = [half * part // parts_of_half for part in CHUNK_PARTS]

    def across(value, j):
        return lax.ppermute(value, "own", [(o, o ^ j) for o in range(n_own)])

    packed, perm = pack_rows(row_insertion.reshape(1, rows), signals, cotangent)
    planes = lax.all_gather(packed, "dp", axis=0)

    column = lax.dynamic_slice_in_dim(weights, dp_at * width, width, 3)
    outgoing = jnp.broadcast_to(
        column.reshape(1, 2, half, 2, piece, width), (n_own // 2, 2, half, 2, piece, width)
    ).reshape(n_own, half, 2, piece, width)
    blocks = lax.all_to_all(outgoing, "own", split_axis=0, concat_axis=0, tiled=True)

    rows_in = (planes, across(planes, 1))
    pred_mine, pred_other, grads = local_grads(
        pos, touched, slot_map, rows_in, blocks, sizes, piece, width
    )
    arrived = []
    for chunk in grads:
        for j in range(1, n_own if arrived else 1):
            chunk[j] = after(chunk[j], arrived[-1][j])
        arrived.append([chunk[0]] + [across(chunk[j], j) for j in range(1, n_own)])
    pred_part = pred_mine + across(pred_other, 1)

    def of_plane(j):
        return lax.dynamic_index_in_dim(pred_part, dp_at ^ j, 0, keepdims=False)

    parts = [of_plane(0)] + [
        lax.ppermute(of_plane(j), "dp", [(d, d ^ j) for d in range(n_dp)]) for j in range(1, n_dp)
    ]
    arrived[-1][-1] = after(arrived[-1][-1], *parts[1:])
    arrived[0][-1] = after(arrived[0][-1], pred_part)

    moments = []
    new_weights = []
    start = 0
    for size, ready in zip(sizes, arrived):
        fresh, *moments = adam(pos, ready, weights, moment1, moment2, start, moments)
        gathered = lax.all_gather(fresh, "dp", axis=0)
        new_weights = [place_weights(gathered, start, half, new_weights)]
        start += size
    new_weights = new_weights[0]
    new_moment1, new_moment2 = moments

    predicted = finish_predicted(perm, parts)
    return (predicted, new_weights, new_moment1, new_moment2)


def solution(mesh):
    in_specs = (
        P(("dp", "own"), None),
        P(("dp", "own"), None),
        P(("dp", "own")),
        P(),
        P(),
        P(None, None, "own", None),
        P(None, None, "own", "dp"),
        P(None, None, "own", "dp"),
    )
    out_specs = (
        P(("dp", "own"), None),
        P(None, None, "own", None),
        P(None, None, "own", "dp"),
        P(None, None, "own", "dp"),
    )
    return jax.shard_map(shards, mesh=mesh, in_specs=in_specs, out_specs=out_specs, check_vma=False)
```

```python
import math

import jax
import jax.numpy as jnp
from jax import lax
from jax.experimental import pallas as pl
from jax.experimental.pallas import tpu as pltpu
from jax.sharding import PartitionSpec as P

SITES = 384
CAP = 128
CHUNK_PARTS = (3, 5)
ID_ROWS = 16
VMEM_BYTES = 56 * 2**20

gelu_coef = math.sqrt(2.0 / math.pi)
cubic_coef = 0.044715
learn_rate = 0.01


def gelu_parts(preact):
    tanh_input = gelu_coef * (preact + cubic_coef * preact * preact * preact)
    tangent = jnp.tanh(tanh_input)
    gelu_val = 0.5 * preact * (1.0 + tangent)
    slopes = 0.5 * (1.0 + tangent) + 0.5 * preact * (1.0 - tangent * tangent) * gelu_coef * (
        1.0 + 3.0 * cubic_coef * preact * preact
    )
    return (gelu_val, slopes)


def params():
    return pltpu.CompilerParams(vmem_limit_bytes=VMEM_BYTES)


def vmem():
    return pl.BlockSpec(memory_space=pltpu.VMEM)


def smem():
    return pl.BlockSpec(memory_space=pltpu.SMEM)


def pack_rows(ids, signals, cotangent):
    rows = signals.shape[0]

    def body(ids_ref, sig_ref, cot_ref, out_ref, perm_ref):
        ids_row = ids_ref[...].astype(jnp.float32)
        lane_ids = jnp.broadcast_to(ids_row, (rows, rows))
        same = lane_ids == lane_ids.T
        count = jnp.sum(same.astype(jnp.float32), axis=0, keepdims=True)
        full = jnp.max(jnp.where(count == CAP, ids_row, -1.0), axis=1, keepdims=True)
        chosen = ids_row == full
        from_row = lax.broadcasted_iota(jnp.int32, (rows, rows), 0)
        to_lane = lax.broadcasted_iota(jnp.int32, (rows, rows), 1)
        upto = (from_row <= to_lane).astype(jnp.bfloat16)
        ahead = jnp.dot(
            jnp.broadcast_to(chosen.astype(jnp.float32), (8, rows)).astype(jnp.bfloat16),
            upto,
            preferred_element_type=jnp.float32,
        )[:1].astype(jnp.int32)
        place = jnp.where(chosen, ahead - 1, CAP + to_lane[:1] - ahead)
        perm = (from_row == place).astype(jnp.float32).astype(jnp.bfloat16)
        perm_ref[...] = perm
        out_ref[:rows] = jnp.dot(perm, sig_ref[...], preferred_element_type=jnp.float32).astype(
            jnp.bfloat16
        )
        out_ref[rows : 2 * rows] = jnp.dot(
            perm, cot_ref[...], preferred_element_type=jnp.float32
        ).astype(jnp.bfloat16)
        sorted_ids = lax.dot_general(
            jnp.broadcast_to(ids_row, (ID_ROWS, rows)).astype(jnp.bfloat16),
            perm,
            (((1,), (1,)), ((), ())),
            preferred_element_type=jnp.float32,
        ).astype(jnp.bfloat16)
        out_ref[2 * rows :, :rows] = sorted_ids
        out_ref[2 * rows :, rows:] = jnp.zeros((ID_ROWS, SITES - rows), jnp.bfloat16)

    return pl.pallas_call(
        body,
        out_shape=(
            jax.ShapeDtypeStruct((2 * rows + ID_ROWS, SITES), jnp.bfloat16),
            jax.ShapeDtypeStruct((rows, rows), jnp.bfloat16),
        ),
        in_specs=[vmem(), vmem(), vmem()],
        out_specs=(vmem(), vmem()),
        compiler_params=params(),
        name="pack_rows",
    )(ids, signals, cotangent)


def local_grads(pos, touched, slot_map, rows_in, blocks, sizes, piece, width):
    planes = rows_in[0].shape[0]
    rows = (rows_in[0].shape[1] - ID_ROWS) // 2
    touch = touched.shape[1]
    n_own = blocks.shape[0]
    half = sum(sizes)
    aligned = piece % 16 == 0
    n_out = n_own if aligned else 1
    starts = [sum(sizes[:i]) for i in range(len(sizes))]

    def body(pos_ref, touched_ref, slot_ref, *rest):
        row_refs = rest[:2]
        blocks_ref = rest[2]
        rest = rest[3:]
        pred_refs = rest[:2]
        grad_refs = rest[2:-8]
        acc, id_cols, held, sorted_rows, pred, full_of, tasks, sems = rest[-8:]
        own_at = pos_ref[1]
        core = lax.rem(own_at, 2)

        def sites(j):
            return pl.ds(pl.multiple_of((own_at ^ j) * piece, 16), piece)

        row_copies = [
            pltpu.make_async_copy(ref, sorted_rows.at[pl.ds(i * planes, planes)], sems.at[i])
            for i, ref in enumerate(row_refs)
        ]
        if aligned:
            block_copies = [
                pltpu.make_async_copy(
                    blocks_ref.at[i], held.at[:, :, pl.ds(i * piece, piece), :], sems.at[2 + i]
                )
                for i in range(n_own)
            ]
        else:
            block_copies = [pltpu.make_async_copy(blocks_ref, held, sems.at[2])]
        for copy in row_copies + block_copies:
            copy.start()

        def clear(e, _):
            acc[e] = jnp.zeros(acc.shape[1:], jnp.float32)
            return 0

        lax.fori_loop(0, half, clear, 0)
        pred[...] = jnp.zeros_like(pred)
        for copy in row_copies:
            copy.wait()
        for source in range(2 * planes):
            ids_row = sorted_rows[source, 2 * rows :, :rows][:1].astype(jnp.float32)
            id_cols[source] = jnp.broadcast_to(ids_row, (128, rows)).T
            full_of[source] = jnp.max(ids_row[:, :128]).astype(jnp.int32)

        def listing(t, count):
            source = t // (touch + 1)
            j = t - source * (touch + 1)
            which = source // planes
            device = (source - which * planes) * n_own + (own_at ^ which)
            full = full_of[source]
            insertion = jnp.where(j == 0, full, touched_ref[device, jnp.maximum(j - 1, 0)])
            e = slot_ref[insertion] - core * half
            here = (e >= 0) & (e < half) & ((j == 0) | (insertion != full))
            tasks[0, count] = source
            tasks[1, count] = jnp.where(j == 0, 0, CAP)
            tasks[2, count] = insertion
            tasks[3, count] = e
            return count + here.astype(jnp.int32)

        count = lax.fori_loop(0, 2 * planes * (touch + 1), listing, 0)
        tasks[0, count] = 0
        tasks[1, count] = 0
        tasks[2, count] = -1
        tasks[3, count] = 0
        for copy in block_copies:
            copy.wait()

        def pair(i, _):
            loaded = []
            for u in range(2):
                source, insertion, e = tasks[0, 2 * i + u], tasks[2, 2 * i + u], tasks[3, 2 * i + u]
                first = pl.multiple_of(tasks[1, 2 * i + u], CAP)
                keep = (
                    (id_cols[source, pl.ds(first, CAP), :] == insertion.astype(jnp.float32))
                    .astype(jnp.float32)
                    .astype(jnp.bfloat16)
                )
                keep = jnp.concatenate([keep] * (SITES // 128), axis=1)
                sig = sorted_rows[source, pl.ds(first, CAP), :] * keep
                cot = sorted_rows[source, pl.ds(rows + first, CAP), :] * keep
                loaded.append((source, first, e, sig, cot))
            found = []
            for source, first, e, sig, cot in loaded:
                read_out = held[e, 1]
                preact = jnp.dot(sig, held[e, 0], preferred_element_type=jnp.float32)
                back_hidden = jnp.dot(cot, read_out, preferred_element_type=jnp.float32)
                gelu_val, slopes = gelu_parts(preact)
                hidden = gelu_val.astype(jnp.bfloat16)
                back_pre = (back_hidden * slopes).astype(jnp.bfloat16)
                part = lax.dot_general(
                    hidden, read_out, (((1,), (1,)), ((), ())), preferred_element_type=jnp.float32
                ).astype(jnp.bfloat16)
                grad_in = lax.dot_general(
                    sig, back_pre, (((0,), (0,)), ((), ())), preferred_element_type=jnp.float32
                )
                grad_out = lax.dot_general(
                    cot, hidden, (((0,), (0,)), ((), ())), preferred_element_type=jnp.float32
                )
                found.append((part, grad_in, grad_out))
            for (source, first, e, _, _), (part, grad_in, grad_out) in zip(loaded, found):
                pred[source, pl.ds(first, CAP), :] += part
                acc[e, 0] += grad_in
                acc[e, 1] += grad_out
            return 0

        lax.fori_loop(0, (count + 1) // 2, pair, 0)
        for which, ref in enumerate(pred_refs):
            ref[...] = pred[which * planes : (which + 1) * planes]
        for chunk, (start, size) in enumerate(zip(starts, sizes)):
            for j in range(n_out):
                ref = grad_refs[chunk * n_out + j]

                def write(e, _, start=start, ref=ref, j=j):
                    if aligned:
                        ref[e] = acc[start + e, :, sites(j), :].astype(jnp.bfloat16)
                    else:
                        ref[e] = acc[start + e].astype(jnp.bfloat16)
                    return 0

                lax.fori_loop(0, size, write, 0)

    pred_shape = jax.ShapeDtypeStruct((planes, rows, SITES), jnp.bfloat16)
    grad_shapes = [
        jax.ShapeDtypeStruct((size, 2, piece if aligned else SITES, width), jnp.bfloat16)
        for size in sizes
        for _ in range(n_out)
    ]
    most = 2 * planes * (touch + 1)
    scratch = [
        pltpu.VMEM((half, 2, SITES, width), jnp.float32),
        pltpu.VMEM((2 * planes, rows, 128), jnp.float32),
        pltpu.VMEM((half, 2, SITES, width), jnp.bfloat16),
        pltpu.VMEM((2 * planes,) + rows_in[0].shape[1:], jnp.bfloat16),
        pltpu.VMEM((2 * planes, rows, SITES), jnp.bfloat16),
        pltpu.SMEM((2 * planes,), jnp.int32),
        pltpu.SMEM((4, most + 1), jnp.int32),
        pltpu.SemaphoreType.DMA((2 + n_own,)),
    ]
    own_at = pos[1]
    if not aligned:
        blocks = blocks.transpose(1, 2, 0, 3, 4).reshape(half, 2, SITES, width)
    found = pl.pallas_call(
        body,
        out_shape=[pred_shape, pred_shape] + grad_shapes,
        in_specs=[smem(), smem(), smem()] + [pl.BlockSpec(memory_space=pl.ANY)] * 3,
        out_specs=[vmem()] * (2 + len(grad_shapes)),
        scratch_shapes=scratch,
        compiler_params=params(),
        name="local_grads",
    )(pos, touched, slot_map, *rows_in, blocks)
    grads = []
    for chunk in range(len(sizes)):
        outs = list(found[2 + chunk * n_out : 2 + (chunk + 1) * n_out])
        if not aligned:
            outs = [
                lax.dynamic_slice_in_dim(outs[0], (own_at ^ j) * piece, piece, 2)
                for j in range(n_own)
            ]
        grads.append(outs)
    return found[0], found[1], grads


def adam(pos, arrived, weights, moment1, moment2, start, before):
    n_own = len(arrived)
    size, _, piece, width = arrived[0].shape
    number = weights.shape[0]
    half = number // 2
    correct_one = 1.0 - 0.9**10
    correct_two = 1.0 - 0.999**10

    def body(pos_ref, *refs):
        grad_refs = refs[:n_own]
        w_ref, m1_ref, m2_ref = refs[n_own : n_own + 3]
        new_w, new_m1, new_m2 = refs[n_own + 3 + len(before) : n_own + 6 + len(before)]
        grads, w_in, m1_in, m2_in, w_out, m1_out, m2_out, sem_in, sem_grad, sem_out = refs[
            n_own + 6 + len(before) :
        ]
        core = lax.rem(pos_ref[1], 2)
        columns = pl.ds(pl.multiple_of(pos_ref[0] * width, 128), width)

        def block_rows(g):
            return pl.ds((core ^ g) * half + start, size)

        copies = []
        for g in range(2):
            copies.append(
                [
                    pltpu.make_async_copy(
                        w_ref.at[block_rows(g), :, :, columns], w_in.at[g], sem_in.at[g, 0]
                    ),
                    pltpu.make_async_copy(m1_ref.at[block_rows(g)], m1_in.at[g], sem_in.at[g, 1]),
                    pltpu.make_async_copy(m2_ref.at[block_rows(g)], m2_in.at[g], sem_in.at[g, 2]),
                ]
                + [
                    pltpu.make_async_copy(grad_refs[j], grads.at[j], sem_grad.at[j])
                    for j in range(g, n_own, 2)
                ]
            )
            for copy in copies[g]:
                copy.start()
        outs = []
        for g in range(2):
            for copy in copies[g]:
                copy.wait()

            def step(i, _, g=g):
                gradient = grads[g, i].astype(jnp.float32)
                for j in range(g + 2, n_own, 2):
                    gradient = gradient + grads[j, i].astype(jnp.float32)
                one = 0.9 * m1_in[g, i] + 0.1 * gradient
                two = 0.999 * m2_in[g, i] + 0.001 * gradient * gradient
                m1_out[g, i] = one
                m2_out[g, i] = two
                spread = two * (1.0 / correct_two)
                updated = w_in[g, i].astype(jnp.float32) - one * (learn_rate / correct_one) / (
                    spread * lax.rsqrt(spread) + 1e-08
                )
                w_out[g, i] = updated.astype(jnp.bfloat16)
                return 0

            lax.fori_loop(0, size, step, 0)
            outs += [
                pltpu.make_async_copy(w_out.at[g], new_w.at[core ^ g], sem_out.at[g, 0]),
                pltpu.make_async_copy(m1_out.at[g], new_m1.at[block_rows(g)], sem_out.at[g, 1]),
                pltpu.make_async_copy(m2_out.at[g], new_m2.at[block_rows(g)], sem_out.at[g, 2]),
            ]
            for copy in outs[-3:]:
                copy.start()
        for copy in outs:
            copy.wait()

    anywhere = pl.BlockSpec(memory_space=pl.ANY)
    blocks = (2, size, 2, piece, width)
    return pl.pallas_call(
        body,
        out_shape=[
            jax.ShapeDtypeStruct(blocks, jnp.bfloat16),
            jax.ShapeDtypeStruct(moment1.shape, jnp.float32),
            jax.ShapeDtypeStruct(moment1.shape, jnp.float32),
        ],
        in_specs=[smem()] + [anywhere] * (n_own + 3 + len(before)),
        out_specs=[anywhere] * 3,
        scratch_shapes=[
            pltpu.VMEM((n_own,) + blocks[1:], jnp.bfloat16),
            pltpu.VMEM(blocks, jnp.bfloat16),
            pltpu.VMEM(blocks, jnp.float32),
            pltpu.VMEM(blocks, jnp.float32),
            pltpu.VMEM(blocks, jnp.bfloat16),
            pltpu.VMEM(blocks, jnp.float32),
            pltpu.VMEM(blocks, jnp.float32),
            pltpu.SemaphoreType.DMA((2, 3)),
            pltpu.SemaphoreType.DMA((n_own,)),
            pltpu.SemaphoreType.DMA((2, 3)),
        ],
        input_output_aliases={1 + n_own + 3 + i: 1 + i for i in range(len(before))},
        compiler_params=params(),
        name="adam_step",
    )(pos, *arrived, weights, moment1, moment2, *before)


def place_weights(pos, pieces, start, half, before):
    n_dp = len(pieces)
    _, size, _, piece, width = pieces[0].shape
    pieces = list(pieces)
    far = isinstance(pieces[-1], tuple)
    if far:
        pieces[-1:] = pieces[-1]
    n_in = len(pieces)

    def body(pos_ref, *refs):
        out_ref, held, sems, sem_out = refs[-4:]
        dp_at = pos_ref[0]
        inner = (dp_at > 0) & (dp_at < n_dp - 1)

        def each(act):
            for j in range(n_dp):
                columns = pl.ds(pl.multiple_of((dp_at ^ j) * width, 128), width)

                def copy(i, j=j, columns=columns):
                    return pltpu.make_async_copy(
                        refs[i], held.at[:, :, :, :, columns], sems.at[j]
                    )

                if far and j == n_dp - 1:
                    pl.when(inner)(lambda: act(copy(j)))
                    pl.when(~inner)(lambda: act(copy(j + 1)))
                else:
                    act(copy(j))

        each(lambda copy: copy.start())
        each(lambda copy: copy.wait())
        outs = [
            pltpu.make_async_copy(
                held.at[h], out_ref.at[pl.ds(h * half + start, size)], sem_out.at[h]
            )
            for h in range(2)
        ]
        for copy in outs:
            copy.start()
        for copy in outs:
            copy.wait()

    anywhere = pl.BlockSpec(memory_space=pl.ANY)
    return pl.pallas_call(
        body,
        out_shape=jax.ShapeDtypeStruct((2 * half, 2, piece, n_dp * width), jnp.bfloat16),
        in_specs=[smem()] + [anywhere] * (n_in + len(before)),
        out_specs=anywhere,
        scratch_shapes=[
            pltpu.VMEM((2, size, 2, piece, n_dp * width), jnp.bfloat16),
            pltpu.SemaphoreType.DMA((n_dp,)),
            pltpu.SemaphoreType.DMA((2,)),
        ],
        input_output_aliases={1 + n_in: 0} if before else {},
        compiler_params=params(),
        name="place_weights",
    )(pos, *pieces, *before)


def gather_planes(fresh, dp_at, n_dp):
    if n_dp != 4:
        whole = lax.all_gather(fresh, "dp", axis=0)
        return [
            lax.dynamic_index_in_dim(whole, dp_at ^ j, 0, keepdims=False) for j in range(n_dp)
        ]
    two = lax.ppermute(fresh, "dp", [(0, 2), (1, 3), (2, 0), (3, 1)])
    one = lax.ppermute(fresh, "dp", [(0, 1), (1, 0), (2, 3), (3, 2)])
    outer = lax.ppermute(two, "dp", [(2, 3), (1, 0)])
    middle = lax.ppermute(after(fresh, two), "dp", [(1, 2), (2, 1)])
    return [fresh, one, two, (middle, outer)]


def after(value, *others):
    return lax.optimization_barrier((value,) + others)[0]


def finish_predicted(perm, parts):
    def body(perm_ref, *refs):
        total = refs[0][...].astype(jnp.float32)
        for ref in refs[1:-1]:
            total = total + ref[...].astype(jnp.float32)
        refs[-1][...] = lax.dot_general(
            perm_ref[...],
            total.astype(jnp.bfloat16),
            (((0,), (0,)), ((), ())),
            preferred_element_type=jnp.float32,
        ).astype(jnp.bfloat16)

    return pl.pallas_call(
        body,
        out_shape=jax.ShapeDtypeStruct(parts[0].shape, jnp.bfloat16),
        in_specs=[vmem()] * (1 + len(parts)),
        out_specs=vmem(),
        compiler_params=params(),
        name="finish_predicted",
    )(perm, *parts)


def shards(signals, cotangent, row_insertion, touched, slot_map, weights, moment1, moment2):
    n_own = lax.axis_size("own")
    n_dp = lax.axis_size("dp")
    dp_at = lax.axis_index("dp")
    own_at = lax.axis_index("own")
    number, _, piece, _ = weights.shape
    width = moment1.shape[3]
    half = number // 2
    rows = signals.shape[0]
    pos = jnp.stack([dp_at, own_at]).astype(jnp.int32)
    core = lax.rem(own_at, 2)
    parts_of_half = sum(CHUNK_PARTS)
    sizes = [half * part // parts_of_half for part in CHUNK_PARTS]

    def across(value, j):
        return lax.ppermute(value, "own", [(o, o ^ j) for o in range(n_own)])

    packed, perm = pack_rows(row_insertion.reshape(1, rows), signals, cotangent)
    planes = lax.all_gather(packed, "dp", axis=0)

    column = lax.dynamic_slice_in_dim(weights, dp_at * width, width, 3)
    outgoing = jnp.broadcast_to(
        column.reshape(1, 2, half, 2, piece, width), (n_own // 2, 2, half, 2, piece, width)
    ).reshape(n_own, half, 2, piece, width)
    blocks = lax.all_to_all(outgoing, "own", split_axis=0, concat_axis=0, tiled=True)

    rows_in = (planes, across(planes, 1))
    pred_mine, pred_other, grads = local_grads(
        pos, touched, slot_map, rows_in, blocks, sizes, piece, width
    )
    arrived = []
    for chunk in grads:
        for j in range(1, n_own if arrived else 1):
            chunk[j] = after(chunk[j], arrived[-1][j])
        arrived.append([chunk[0]] + [across(chunk[j], j) for j in range(1, n_own)])
    pred_part = pred_mine + across(pred_other, 1)

    def of_plane(j):
        return lax.dynamic_index_in_dim(pred_part, dp_at ^ j, 0, keepdims=False)

    parts = [of_plane(0)] + [
        lax.ppermute(of_plane(j), "dp", [(d, d ^ j) for d in range(n_dp)]) for j in range(1, n_dp)
    ]
    arrived[0][-1] = after(arrived[0][-1], *parts[1:])

    moments = []
    new_weights = []
    start = 0
    pieces = []
    for size, ready in zip(sizes, arrived):
        ready[-1] = after(ready[-1], *pieces[1:3])
        fresh, *moments = adam(pos, ready, weights, moment1, moment2, start, moments)
        if pieces:
            fresh = after(fresh, *jax.tree.leaves(pieces[3:]))
        pieces = gather_planes(fresh, dp_at, n_dp)
        new_weights = [place_weights(pos, pieces, start, half, new_weights)]
        start += size
    new_weights = new_weights[0]
    new_moment1, new_moment2 = moments

    predicted = finish_predicted(perm, parts)
    return (predicted, new_weights, new_moment1, new_moment2)


def solution(mesh):
    in_specs = (
        P(("dp", "own"), None),
        P(("dp", "own"), None),
        P(("dp", "own")),
        P(),
        P(),
        P(None, None, "own", None),
        P(None, None, "own", "dp"),
        P(None, None, "own", "dp"),
    )
    out_specs = (
        P(("dp", "own"), None),
        P(None, None, "own", None),
        P(None, None, "own", "dp"),
        P(None, None, "own", "dp"),
    )
    return jax.shard_map(shards, mesh=mesh, in_specs=in_specs, out_specs=out_specs, check_vma=False)
```

```python
import math

import jax
import jax.numpy as jnp
from jax import lax
from jax.experimental import pallas as pl
from jax.experimental.pallas import tpu as pltpu
from jax.sharding import PartitionSpec as P

SITES = 384
CAP = 128
ID_ROWS = 16
PARTS = 4
VMEM_BYTES = 56 * 2**20

gelu_coef = math.sqrt(2.0 / math.pi)
cubic_coef = 0.044715
learn_rate = 0.01


def gelu_parts(preact):
    tanh_input = gelu_coef * (preact + cubic_coef * preact * preact * preact)
    tangent = jnp.tanh(tanh_input)
    gelu_val = 0.5 * preact * (1.0 + tangent)
    slopes = 0.5 * (1.0 + tangent) + 0.5 * preact * (1.0 - tangent * tangent) * gelu_coef * (
        1.0 + 3.0 * cubic_coef * preact * preact
    )
    return (gelu_val, slopes)


def params():
    return pltpu.CompilerParams(vmem_limit_bytes=VMEM_BYTES)


def vmem():
    return pl.BlockSpec(memory_space=pltpu.VMEM)


def smem():
    return pl.BlockSpec(memory_space=pltpu.SMEM)


def pack_rows(ids, signals, cotangent):
    rows = signals.shape[0]

    def body(ids_ref, sig_ref, cot_ref, out_ref, perm_ref):
        ids_row = ids_ref[...].astype(jnp.float32)
        lane_ids = jnp.broadcast_to(ids_row, (rows, rows))
        same = lane_ids == lane_ids.T
        count = jnp.sum(same.astype(jnp.float32), axis=0, keepdims=True)
        full = jnp.max(jnp.where(count == CAP, ids_row, -1.0), axis=1, keepdims=True)
        chosen = ids_row == full
        from_row = lax.broadcasted_iota(jnp.int32, (rows, rows), 0)
        to_lane = lax.broadcasted_iota(jnp.int32, (rows, rows), 1)
        upto = (from_row <= to_lane).astype(jnp.bfloat16)
        ahead = jnp.dot(
            jnp.broadcast_to(chosen.astype(jnp.float32), (8, rows)).astype(jnp.bfloat16),
            upto,
            preferred_element_type=jnp.float32,
        )[:1].astype(jnp.int32)
        place = jnp.where(chosen, ahead - 1, CAP + to_lane[:1] - ahead)
        perm = (from_row == place).astype(jnp.float32).astype(jnp.bfloat16)
        perm_ref[...] = perm
        out_ref[:rows] = jnp.dot(perm, sig_ref[...], preferred_element_type=jnp.float32).astype(
            jnp.bfloat16
        )
        out_ref[rows : 2 * rows] = jnp.dot(
            perm, cot_ref[...], preferred_element_type=jnp.float32
        ).astype(jnp.bfloat16)
        sorted_ids = lax.dot_general(
            jnp.broadcast_to(ids_row, (ID_ROWS, rows)).astype(jnp.bfloat16),
            perm,
            (((1,), (1,)), ((), ())),
            preferred_element_type=jnp.float32,
        ).astype(jnp.bfloat16)
        out_ref[2 * rows :, :rows] = sorted_ids
        out_ref[2 * rows :, rows:] = jnp.zeros((ID_ROWS, SITES - rows), jnp.bfloat16)

    return pl.pallas_call(
        body,
        out_shape=(
            jax.ShapeDtypeStruct((2 * rows + ID_ROWS, SITES), jnp.bfloat16),
            jax.ShapeDtypeStruct((rows, rows), jnp.bfloat16),
        ),
        in_specs=[vmem(), vmem(), vmem()],
        out_specs=(vmem(), vmem()),
        compiler_params=params(),
        name="pack_rows",
    )(ids, signals, cotangent)


def local_grads(pos, touched, slot_map, rows_in, blocks, piece, width):
    planes = rows_in[0].shape[0]
    rows = (rows_in[0].shape[1] - ID_ROWS) // 2
    touch = touched.shape[1]
    n_own = blocks.shape[0]
    half = blocks.shape[1]
    aligned = piece % 16 == 0

    def body(pos_ref, touched_ref, slot_ref, *rest):
        row_refs = rest[:2]
        blocks_ref = rest[2]
        rest = rest[3:]
        pred_refs = rest[:2]
        grad_ref = rest[2]
        acc, id_cols, held, sorted_rows, pred, full_of, tasks, sems = rest[-8:]
        own_at = pos_ref[1]
        core = lax.rem(own_at, 2)

        row_copies = [
            pltpu.make_async_copy(ref, sorted_rows.at[pl.ds(i * planes, planes)], sems.at[i])
            for i, ref in enumerate(row_refs)
        ]
        if aligned:
            block_copies = [
                pltpu.make_async_copy(
                    blocks_ref.at[i], held.at[:, :, pl.ds(i * piece, piece), :], sems.at[2 + i]
                )
                for i in range(n_own)
            ]
        else:
            block_copies = [pltpu.make_async_copy(blocks_ref, held, sems.at[2])]
        for copy in row_copies + block_copies:
            copy.start()

        def clear(e, _):
            acc[e] = jnp.zeros(acc.shape[1:], jnp.float32)
            return 0

        lax.fori_loop(0, half, clear, 0)
        pred[...] = jnp.zeros_like(pred)
        for copy in row_copies:
            copy.wait()
        for source in range(2 * planes):
            ids_row = sorted_rows[source, 2 * rows :, :rows][:1].astype(jnp.float32)
            id_cols[source] = jnp.broadcast_to(ids_row, (128, rows)).T
            full_of[source] = jnp.max(ids_row[:, :128]).astype(jnp.int32)

        def listing(t, count):
            source = t // (touch + 1)
            j = t - source * (touch + 1)
            which = source // planes
            device = (source - which * planes) * n_own + (own_at ^ which)
            full = full_of[source]
            insertion = jnp.where(j == 0, full, touched_ref[device, jnp.maximum(j - 1, 0)])
            e = slot_ref[insertion] - core * half
            here = (e >= 0) & (e < half) & ((j == 0) | (insertion != full))
            tasks[0, count] = source
            tasks[1, count] = jnp.where(j == 0, 0, CAP)
            tasks[2, count] = insertion
            tasks[3, count] = e
            return count + here.astype(jnp.int32)

        count = lax.fori_loop(0, 2 * planes * (touch + 1), listing, 0)
        tasks[0, count] = 0
        tasks[1, count] = 0
        tasks[2, count] = -1
        tasks[3, count] = 0
        for copy in block_copies:
            copy.wait()

        def pair(i, _):
            loaded = []
            for u in range(2):
                source, insertion, e = tasks[0, 2 * i + u], tasks[2, 2 * i + u], tasks[3, 2 * i + u]
                first = pl.multiple_of(tasks[1, 2 * i + u], CAP)
                keep = (
                    (id_cols[source, pl.ds(first, CAP), :] == insertion.astype(jnp.float32))
                    .astype(jnp.float32)
                    .astype(jnp.bfloat16)
                )
                keep = jnp.concatenate([keep] * (SITES // 128), axis=1)
                sig = sorted_rows[source, pl.ds(first, CAP), :] * keep
                cot = sorted_rows[source, pl.ds(rows + first, CAP), :] * keep
                loaded.append((source, first, e, sig, cot))
            found = []
            for source, first, e, sig, cot in loaded:
                read_out = held[e, 1]
                preact = jnp.dot(sig, held[e, 0], preferred_element_type=jnp.float32)
                back_hidden = jnp.dot(cot, read_out, preferred_element_type=jnp.float32)
                gelu_val, slopes = gelu_parts(preact)
                hidden = gelu_val.astype(jnp.bfloat16)
                back_pre = (back_hidden * slopes).astype(jnp.bfloat16)
                part = lax.dot_general(
                    hidden, read_out, (((1,), (1,)), ((), ())), preferred_element_type=jnp.float32
                ).astype(jnp.bfloat16)
                grad_in = lax.dot_general(
                    sig, back_pre, (((0,), (0,)), ((), ())), preferred_element_type=jnp.float32
                )
                grad_out = lax.dot_general(
                    cot, hidden, (((0,), (0,)), ((), ())), preferred_element_type=jnp.float32
                )
                found.append((part, grad_in, grad_out))
            for (source, first, e, _, _), (part, grad_in, grad_out) in zip(loaded, found):
                pred[source, pl.ds(first, CAP), :] += part
                acc[e, 0] += grad_in
                acc[e, 1] += grad_out
            return 0

        lax.fori_loop(0, (count + 1) // 2, pair, 0)
        for which, ref in enumerate(pred_refs):
            ref[...] = pred[which * planes : (which + 1) * planes]

        def write(e, _):
            if aligned:
                for i in range(n_own):
                    grad_ref[i, e] = acc[e, :, i * piece : (i + 1) * piece, :].astype(jnp.bfloat16)
            else:
                grad_ref[e] = acc[e].astype(jnp.bfloat16)
            return 0

        lax.fori_loop(0, half, write, 0)

    pred_shape = jax.ShapeDtypeStruct((planes, rows, SITES), jnp.bfloat16)
    grad_shape = (n_own, half, 2, piece, width) if aligned else (half, 2, SITES, width)
    most = 2 * planes * (touch + 1)
    scratch = [
        pltpu.VMEM((half, 2, SITES, width), jnp.float32),
        pltpu.VMEM((2 * planes, rows, 128), jnp.float32),
        pltpu.VMEM((half, 2, SITES, width), jnp.bfloat16),
        pltpu.VMEM((2 * planes,) + rows_in[0].shape[1:], jnp.bfloat16),
        pltpu.VMEM((2 * planes, rows, SITES), jnp.bfloat16),
        pltpu.SMEM((2 * planes,), jnp.int32),
        pltpu.SMEM((4, most + 1), jnp.int32),
        pltpu.SemaphoreType.DMA((2 + n_own,)),
    ]
    if not aligned:
        blocks = blocks.transpose(1, 2, 0, 3, 4).reshape(half, 2, SITES, width)
    found = pl.pallas_call(
        body,
        out_shape=[pred_shape, pred_shape, jax.ShapeDtypeStruct(grad_shape, jnp.bfloat16)],
        in_specs=[smem(), smem(), smem()] + [pl.BlockSpec(memory_space=pl.ANY)] * 3,
        out_specs=[vmem()] * 3,
        scratch_shapes=scratch,
        compiler_params=params(),
        name="local_grads",
    )(pos, touched, slot_map, *rows_in, blocks)
    grads = found[2]
    if not aligned:
        grads = grads.reshape(half, 2, n_own, piece, width).transpose(2, 0, 1, 3, 4)
    return found[0], found[1], grads


def adam(pos, arrived, weights, moment1, moment2):
    n_own, half, _, piece, width = arrived.shape
    correct_one = 1.0 - 0.9**10
    correct_two = 1.0 - 0.999**10

    def body(pos_ref, arrived_ref, w_ref, m1_ref, m2_ref, *refs):
        new_w, new_m1, new_m2, grads, w_in, m1_in, m2_in, w_out, m1_out, m2_out = refs[:10]
        sem_in, sem_out = refs[10:]
        columns = pl.ds(pl.multiple_of(pos_ref[0] * width, 128), width)
        part = half // PARTS
        steps = [(core, i * part) for core in range(2) for i in range(PARTS)]
        copies = []
        for n, (core, first) in enumerate(steps):
            rows = pl.ds(core * half + first, part)
            copies.append(
                [
                    pltpu.make_async_copy(ref, into.at[rows], sem_in.at[n, i])
                    for i, (ref, into) in enumerate(
                        (
                            (w_ref.at[rows, :, :, columns], w_in),
                            (m1_ref.at[rows], m1_in),
                            (m2_ref.at[rows], m2_in),
                        )
                    )
                ]
                + [
                    pltpu.make_async_copy(
                        arrived_ref.at[i, pl.ds(first, part)],
                        grads.at[i, pl.ds(first, part)],
                        sem_in.at[n, 3 + i // 2],
                    )
                    for i in range(core, n_own, 2)
                ]
            )
            for copy in copies[n]:
                copy.start()
        outs = []
        for n, (core, first) in enumerate(steps):
            for copy in copies[n]:
                copy.wait()

            def step(i, _, core=core, first=first):
                gradient = grads[core, first + i].astype(jnp.float32)
                for j in range(core + 2, n_own, 2):
                    gradient = gradient + grads[j, first + i].astype(jnp.float32)
                at = core * half + first + i
                one = 0.9 * m1_in[at] + 0.1 * gradient
                two = 0.999 * m2_in[at] + 0.001 * gradient * gradient
                m1_out[at] = one
                m2_out[at] = two
                spread = two * (1.0 / correct_two)
                updated = w_in[at].astype(jnp.float32) - one * (learn_rate / correct_one) / (
                    spread * lax.rsqrt(spread) + 1e-08
                )
                w_out[at] = updated.astype(jnp.bfloat16)
                return 0

            lax.fori_loop(0, part, step, 0)
            rows = pl.ds(core * half + first, part)
            for i, (held, ref) in enumerate(
                ((w_out, new_w), (m1_out, new_m1), (m2_out, new_m2))
            ):
                outs.append(pltpu.make_async_copy(held.at[rows], ref.at[rows], sem_out.at[n, i]))
                outs[-1].start()
        for copy in outs:
            copy.wait()

    anywhere = pl.BlockSpec(memory_space=pl.ANY)
    return pl.pallas_call(
        body,
        out_shape=[
            jax.ShapeDtypeStruct(moment1.shape, jnp.bfloat16),
            jax.ShapeDtypeStruct(moment1.shape, jnp.float32),
            jax.ShapeDtypeStruct(moment1.shape, jnp.float32),
        ],
        in_specs=[smem()] + [anywhere] * 4,
        out_specs=[anywhere] * 3,
        scratch_shapes=[pltpu.VMEM(arrived.shape, jnp.bfloat16)]
        + [pltpu.VMEM(moment1.shape, kind) for kind in (jnp.bfloat16, jnp.float32, jnp.float32)] * 2
        + [
            pltpu.SemaphoreType.DMA((2 * PARTS, 3 + n_own // 2)),
            pltpu.SemaphoreType.DMA((2 * PARTS, 3)),
        ],
        compiler_params=params(),
        name="adam_step",
    )(pos, arrived, weights, moment1, moment2)


def place_weights(gathered):
    n_dp, number, _, piece, width = gathered.shape
    part = number // PARTS

    def body(gathered_ref, out_ref, held, sems, sem_out):
        def piece_in(i, d):
            rows = pl.ds(i * part, part)
            return pltpu.make_async_copy(
                gathered_ref.at[d, rows],
                held.at[rows, :, :, pl.ds(d * width, width)],
                sems.at[i, d],
            )

        for i in range(PARTS):
            for d in range(n_dp):
                piece_in(i, d).start()
        outs = []
        for i in range(PARTS):
            for d in range(n_dp):
                piece_in(i, d).wait()
            rows = pl.ds(i * part, part)
            outs.append(pltpu.make_async_copy(held.at[rows], out_ref.at[rows], sem_out.at[i]))
            outs[-1].start()
        for copy in outs:
            copy.wait()

    anywhere = pl.BlockSpec(memory_space=pl.ANY)
    shape = (number, 2, piece, n_dp * width)
    return pl.pallas_call(
        body,
        out_shape=jax.ShapeDtypeStruct(shape, jnp.bfloat16),
        in_specs=[anywhere],
        out_specs=anywhere,
        scratch_shapes=[
            pltpu.VMEM(shape, jnp.bfloat16),
            pltpu.SemaphoreType.DMA((PARTS, n_dp)),
            pltpu.SemaphoreType.DMA((PARTS,)),
        ],
        compiler_params=params(),
        name="place_weights",
    )(gathered)


def after(value, *others):
    return lax.optimization_barrier((value,) + others)[0]


def finish_predicted(perm, parts):
    def body(perm_ref, *refs):
        total = refs[0][...].astype(jnp.float32)
        for ref in refs[1:-1]:
            total = total + ref[...].astype(jnp.float32)
        refs[-1][...] = lax.dot_general(
            perm_ref[...],
            total.astype(jnp.bfloat16),
            (((0,), (0,)), ((), ())),
            preferred_element_type=jnp.float32,
        ).astype(jnp.bfloat16)

    return pl.pallas_call(
        body,
        out_shape=jax.ShapeDtypeStruct(parts[0].shape, jnp.bfloat16),
        in_specs=[vmem()] * (1 + len(parts)),
        out_specs=vmem(),
        compiler_params=params(),
        name="finish_predicted",
    )(perm, *parts)


def shards(signals, cotangent, row_insertion, touched, slot_map, weights, moment1, moment2):
    n_own = lax.axis_size("own")
    n_dp = lax.axis_size("dp")
    dp_at = lax.axis_index("dp")
    own_at = lax.axis_index("own")
    number, _, piece, _ = weights.shape
    width = moment1.shape[3]
    half = number // 2
    rows = signals.shape[0]
    pos = jnp.stack([dp_at, own_at]).astype(jnp.int32)

    def across(value, j):
        return lax.ppermute(value, "own", [(o, o ^ j) for o in range(n_own)])

    packed, perm = pack_rows(row_insertion.reshape(1, rows), signals, cotangent)
    planes = lax.all_gather(packed, "dp", axis=0)

    column = lax.dynamic_slice_in_dim(weights, dp_at * width, width, 3)
    outgoing = jnp.broadcast_to(
        column.reshape(1, 2, half, 2, piece, width), (n_own // 2, 2, half, 2, piece, width)
    ).reshape(n_own, half, 2, piece, width)
    blocks = lax.all_to_all(outgoing, "own", split_axis=0, concat_axis=0, tiled=True)

    rows_in = (planes, across(planes, 1))
    pred_mine, pred_other, grads = local_grads(
        pos, touched, slot_map, rows_in, blocks, piece, width
    )
    arrived = lax.all_to_all(grads, "own", split_axis=0, concat_axis=0, tiled=True)

    pred_part = pred_mine + across(pred_other, 1)

    def of_plane(j):
        return lax.dynamic_index_in_dim(pred_part, dp_at ^ j, 0, keepdims=False)

    parts = [of_plane(0)] + [
        lax.ppermute(of_plane(j), "dp", [(d, d ^ j) for d in range(n_dp)]) for j in range(1, n_dp)
    ]
    arrived = after(arrived, *parts[1:])

    fresh, new_moment1, new_moment2 = adam(pos, arrived, weights, moment1, moment2)
    new_weights = place_weights(lax.all_gather(fresh, "dp", axis=0))

    predicted = finish_predicted(perm, parts)
    return (predicted, new_weights, new_moment1, new_moment2)


def solution(mesh):
    in_specs = (
        P(("dp", "own"), None),
        P(("dp", "own"), None),
        P(("dp", "own")),
        P(),
        P(),
        P(None, None, "own", None),
        P(None, None, "own", "dp"),
        P(None, None, "own", "dp"),
    )
    out_specs = (
        P(("dp", "own"), None),
        P(None, None, "own", None),
        P(None, None, "own", "dp"),
        P(None, None, "own", "dp"),
    )
    return jax.shard_map(shards, mesh=mesh, in_specs=in_specs, out_specs=out_specs, check_vma=False)
```

```python
import math

import jax
import jax.numpy as jnp
from jax import lax
from jax.experimental import pallas as pl
from jax.experimental.pallas import tpu as pltpu
from jax.sharding import PartitionSpec as P

SITES = 384
CAP = 128
ID_ROWS = 16
PARTS = 4
VMEM_BYTES = 60 * 2**20
SPARE_BYTES = 6 * 2**20

gelu_coef = math.sqrt(2.0 / math.pi)
cubic_coef = 0.044715
learn_rate = 0.01


def gelu_parts(preact):
    tanh_input = gelu_coef * (preact + cubic_coef * preact * preact * preact)
    tangent = jnp.tanh(tanh_input)
    gelu_val = 0.5 * preact * (1.0 + tangent)
    slopes = 0.5 * (1.0 + tangent) + 0.5 * preact * (1.0 - tangent * tangent) * gelu_coef * (
        1.0 + 3.0 * cubic_coef * preact * preact
    )
    return (gelu_val, slopes)


def params(*held):
    need = 0
    for shape, item in held:
        rows = -(-shape[-2] // 16) * 16
        need += math.prod(shape[:-2]) * rows * max(shape[-1], 128) * item
    return pltpu.CompilerParams(vmem_limit_bytes=min(need + SPARE_BYTES, VMEM_BYTES))


def vmem():
    return pl.BlockSpec(memory_space=pltpu.VMEM)


def smem():
    return pl.BlockSpec(memory_space=pltpu.SMEM)


def pack_rows(ids, signals, cotangent):
    rows = signals.shape[0]

    def body(ids_ref, sig_ref, cot_ref, out_ref, perm_ref):
        ids_row = ids_ref[...].astype(jnp.float32)
        lane_ids = jnp.broadcast_to(ids_row, (rows, rows))
        same = lane_ids == lane_ids.T
        count = jnp.sum(same.astype(jnp.float32), axis=0, keepdims=True)
        full = jnp.max(jnp.where(count == CAP, ids_row, -1.0), axis=1, keepdims=True)
        chosen = ids_row == full
        from_row = lax.broadcasted_iota(jnp.int32, (rows, rows), 0)
        to_lane = lax.broadcasted_iota(jnp.int32, (rows, rows), 1)
        upto = (from_row <= to_lane).astype(jnp.bfloat16)
        ahead = jnp.dot(
            jnp.broadcast_to(chosen.astype(jnp.float32), (8, rows)).astype(jnp.bfloat16),
            upto,
            preferred_element_type=jnp.float32,
        )[:1].astype(jnp.int32)
        place = jnp.where(chosen, ahead - 1, CAP + to_lane[:1] - ahead)
        perm = (from_row == place).astype(jnp.float32).astype(jnp.bfloat16)
        perm_ref[...] = perm
        out_ref[:rows] = jnp.dot(perm, sig_ref[...], preferred_element_type=jnp.float32).astype(
            jnp.bfloat16
        )
        out_ref[rows : 2 * rows] = jnp.dot(
            perm, cot_ref[...], preferred_element_type=jnp.float32
        ).astype(jnp.bfloat16)
        sorted_ids = lax.dot_general(
            jnp.broadcast_to(ids_row, (ID_ROWS, rows)).astype(jnp.bfloat16),
            perm,
            (((1,), (1,)), ((), ())),
            preferred_element_type=jnp.float32,
        ).astype(jnp.bfloat16)
        out_ref[2 * rows :, :rows] = sorted_ids
        out_ref[2 * rows :, rows:] = jnp.zeros((ID_ROWS, SITES - rows), jnp.bfloat16)

    return pl.pallas_call(
        body,
        out_shape=(
            jax.ShapeDtypeStruct((2 * rows + ID_ROWS, SITES), jnp.bfloat16),
            jax.ShapeDtypeStruct((rows, rows), jnp.bfloat16),
        ),
        in_specs=[vmem(), vmem(), vmem()],
        out_specs=(vmem(), vmem()),
        compiler_params=params(),
        name="pack_rows",
    )(ids, signals, cotangent)


def local_grads(pos, touched, slot_map, rows_in, blocks, piece, width):
    planes = rows_in[0].shape[0]
    rows = (rows_in[0].shape[1] - ID_ROWS) // 2
    touch = touched.shape[1]
    n_own = blocks.shape[0]
    half = blocks.shape[1]
    aligned = piece % 16 == 0

    def body(pos_ref, touched_ref, slot_ref, *rest):
        row_refs = rest[:2]
        blocks_ref = rest[2]
        rest = rest[3:]
        pred_refs = rest[:2]
        grad_ref = rest[2]
        acc, id_cols, held, sorted_rows, pred, full_of, tasks, sems = rest[-8:]
        own_at = pos_ref[1]
        core = lax.rem(own_at, 2)

        row_copies = [
            pltpu.make_async_copy(ref, sorted_rows.at[pl.ds(i * planes, planes)], sems.at[i])
            for i, ref in enumerate(row_refs)
        ]
        if aligned:
            block_copies = [
                pltpu.make_async_copy(
                    blocks_ref.at[i], held.at[:, :, pl.ds(i * piece, piece), :], sems.at[2 + i]
                )
                for i in range(n_own)
            ]
        else:
            block_copies = [pltpu.make_async_copy(blocks_ref, held, sems.at[2])]
        for copy in row_copies + block_copies:
            copy.start()

        def clear(e, _):
            acc[e] = jnp.zeros(acc.shape[1:], jnp.float32)
            return 0

        lax.fori_loop(0, half, clear, 0)
        pred[...] = jnp.zeros_like(pred)
        for copy in row_copies:
            copy.wait()
        for source in range(2 * planes):
            ids_row = sorted_rows[source, 2 * rows :, :rows][:1].astype(jnp.float32)
            id_cols[source] = jnp.broadcast_to(ids_row, (128, rows)).T
            full_of[source] = jnp.max(ids_row[:, :128]).astype(jnp.int32)

        def listing(t, count):
            source = t // (touch + 1)
            j = t - source * (touch + 1)
            which = source // planes
            device = (source - which * planes) * n_own + (own_at ^ which)
            full = full_of[source]
            insertion = jnp.where(j == 0, full, touched_ref[device, jnp.maximum(j - 1, 0)])
            e = slot_ref[insertion] - core * half
            here = (e >= 0) & (e < half) & ((j == 0) | (insertion != full))
            tasks[0, count] = source
            tasks[1, count] = jnp.where(j == 0, 0, CAP)
            tasks[2, count] = insertion
            tasks[3, count] = e
            return count + here.astype(jnp.int32)

        count = lax.fori_loop(0, 2 * planes * (touch + 1), listing, 0)
        tasks[0, count] = 0
        tasks[1, count] = 0
        tasks[2, count] = -1
        tasks[3, count] = 0
        for copy in block_copies:
            copy.wait()

        def pair(i, _):
            loaded = []
            for u in range(2):
                source, insertion, e = tasks[0, 2 * i + u], tasks[2, 2 * i + u], tasks[3, 2 * i + u]
                first = pl.multiple_of(tasks[1, 2 * i + u], CAP)
                keep = (
                    (id_cols[source, pl.ds(first, CAP), :] == insertion.astype(jnp.float32))
                    .astype(jnp.float32)
                    .astype(jnp.bfloat16)
                )
                keep = jnp.concatenate([keep] * (SITES // 128), axis=1)
                sig = sorted_rows[source, pl.ds(first, CAP), :] * keep
                cot = sorted_rows[source, pl.ds(rows + first, CAP), :] * keep
                loaded.append((source, first, e, sig, cot))
            found = []
            for source, first, e, sig, cot in loaded:
                read_out = held[e, 1]
                preact = jnp.dot(sig, held[e, 0], preferred_element_type=jnp.float32)
                back_hidden = jnp.dot(cot, read_out, preferred_element_type=jnp.float32)
                gelu_val, slopes = gelu_parts(preact)
                hidden = gelu_val.astype(jnp.bfloat16)
                back_pre = (back_hidden * slopes).astype(jnp.bfloat16)
                part = lax.dot_general(
                    hidden, read_out, (((1,), (1,)), ((), ())), preferred_element_type=jnp.float32
                ).astype(jnp.bfloat16)
                grad_in = lax.dot_general(
                    sig, back_pre, (((0,), (0,)), ((), ())), preferred_element_type=jnp.float32
                )
                grad_out = lax.dot_general(
                    cot, hidden, (((0,), (0,)), ((), ())), preferred_element_type=jnp.float32
                )
                found.append((part, grad_in, grad_out))
            for (source, first, e, _, _), (part, grad_in, grad_out) in zip(loaded, found):
                pred[source, pl.ds(first, CAP), :] += part
                acc[e, 0] += grad_in
                acc[e, 1] += grad_out
            return 0

        lax.fori_loop(0, (count + 1) // 2, pair, 0)
        for which, ref in enumerate(pred_refs):
            ref[...] = pred[which * planes : (which + 1) * planes]

        def write(e, _):
            if aligned:
                for i in range(n_own):
                    grad_ref[i, e] = acc[e, :, i * piece : (i + 1) * piece, :].astype(jnp.bfloat16)
            else:
                grad_ref[e] = acc[e].astype(jnp.bfloat16)
            return 0

        lax.fori_loop(0, half, write, 0)

    pred_shape = jax.ShapeDtypeStruct((planes, rows, SITES), jnp.bfloat16)
    grad_shape = (n_own, half, 2, piece, width) if aligned else (half, 2, SITES, width)
    most = 2 * planes * (touch + 1)
    acc_shape = (half, 2, SITES, width)
    id_shape = (2 * planes, rows, 128)
    row_shape = (2 * planes,) + rows_in[0].shape[1:]
    pred_all = (2 * planes, rows, SITES)
    scratch = [
        pltpu.VMEM(acc_shape, jnp.float32),
        pltpu.VMEM(id_shape, jnp.float32),
        pltpu.VMEM(acc_shape, jnp.bfloat16),
        pltpu.VMEM(row_shape, jnp.bfloat16),
        pltpu.VMEM(pred_all, jnp.bfloat16),
        pltpu.SMEM((2 * planes,), jnp.int32),
        pltpu.SMEM((4, most + 1), jnp.int32),
        pltpu.SemaphoreType.DMA((2 + n_own,)),
    ]
    if not aligned:
        blocks = blocks.transpose(1, 2, 0, 3, 4).reshape(half, 2, SITES, width)
    found = pl.pallas_call(
        body,
        out_shape=[pred_shape, pred_shape, jax.ShapeDtypeStruct(grad_shape, jnp.bfloat16)],
        in_specs=[smem(), smem(), smem()] + [pl.BlockSpec(memory_space=pl.ANY)] * 3,
        out_specs=[vmem()] * 3,
        scratch_shapes=scratch,
        compiler_params=params(
            (acc_shape, 4), (id_shape, 4), (acc_shape, 2), (row_shape, 2), (pred_all, 2), (pred_all, 2),
            (grad_shape, 2), *([] if aligned else [(acc_shape, 2)])
        ),
        name="local_grads",
    )(pos, touched, slot_map, *rows_in, blocks)
    grads = found[2]
    if not aligned:
        grads = grads.reshape(half, 2, n_own, piece, width).transpose(2, 0, 1, 3, 4)
    return found[0], found[1], grads


def adam(pos, arrived, weights, moment1, moment2):
    n_own, half, _, piece, width = arrived.shape
    correct_one = 1.0 - 0.9**10
    correct_two = 1.0 - 0.999**10

    def body(pos_ref, arrived_ref, w_ref, m1_ref, m2_ref, *refs):
        new_w, new_m1, new_m2, grads, w_in, m1_in, m2_in, w_out, m1_out, m2_out = refs[:10]
        sem_in, sem_out = refs[10:]
        columns = pl.ds(pl.multiple_of(pos_ref[0] * width, 128), width)
        part = half // PARTS
        steps = [(core, i * part) for core in range(2) for i in range(PARTS)]
        copies = []
        for n, (core, first) in enumerate(steps):
            rows = pl.ds(core * half + first, part)
            copies.append(
                [
                    pltpu.make_async_copy(ref, into.at[rows], sem_in.at[n, i])
                    for i, (ref, into) in enumerate(
                        (
                            (w_ref.at[rows, :, :, columns], w_in),
                            (m1_ref.at[rows], m1_in),
                            (m2_ref.at[rows], m2_in),
                        )
                    )
                ]
                + [
                    pltpu.make_async_copy(
                        arrived_ref.at[i, pl.ds(first, part)],
                        grads.at[i, pl.ds(first, part)],
                        sem_in.at[n, 3 + i // 2],
                    )
                    for i in range(core, n_own, 2)
                ]
            )
            for copy in copies[n]:
                copy.start()
        outs = []
        for n, (core, first) in enumerate(steps):
            for copy in copies[n]:
                copy.wait()

            def step(i, _, core=core, first=first):
                gradient = grads[core, first + i].astype(jnp.float32)
                for j in range(core + 2, n_own, 2):
                    gradient = gradient + grads[j, first + i].astype(jnp.float32)
                at = core * half + first + i
                one = 0.9 * m1_in[at] + 0.1 * gradient
                two = 0.999 * m2_in[at] + 0.001 * gradient * gradient
                m1_out[at] = one
                m2_out[at] = two
                spread = two * (1.0 / correct_two)
                updated = w_in[at].astype(jnp.float32) - one * (learn_rate / correct_one) / (
                    spread * lax.rsqrt(spread) + 1e-08
                )
                w_out[at] = updated.astype(jnp.bfloat16)
                return 0

            lax.fori_loop(0, part, step, 0)
            rows = pl.ds(core * half + first, part)
            for i, (held, ref) in enumerate(
                ((w_out, new_w), (m1_out, new_m1), (m2_out, new_m2))
            ):
                outs.append(pltpu.make_async_copy(held.at[rows], ref.at[rows], sem_out.at[n, i]))
                outs[-1].start()
        for copy in outs:
            copy.wait()

    anywhere = pl.BlockSpec(memory_space=pl.ANY)
    return pl.pallas_call(
        body,
        out_shape=[
            jax.ShapeDtypeStruct(moment1.shape, jnp.bfloat16),
            jax.ShapeDtypeStruct(moment1.shape, jnp.float32),
            jax.ShapeDtypeStruct(moment1.shape, jnp.float32),
        ],
        in_specs=[smem()] + [anywhere] * 4,
        out_specs=[anywhere] * 3,
        scratch_shapes=[pltpu.VMEM(arrived.shape, jnp.bfloat16)]
        + [pltpu.VMEM(moment1.shape, kind) for kind in (jnp.bfloat16, jnp.float32, jnp.float32)] * 2
        + [
            pltpu.SemaphoreType.DMA((2 * PARTS, 3 + n_own // 2)),
            pltpu.SemaphoreType.DMA((2 * PARTS, 3)),
        ],
        compiler_params=params((arrived.shape, 2), *[(moment1.shape, 4)] * 5),
        name="adam_step",
    )(pos, arrived, weights, moment1, moment2)


def place_weights(pos, pieces, shape, before):
    flat = [(plane, one if isinstance(one, tuple) else (one,)) for plane, one in pieces]
    arrays = [one for _, group in flat for one in group]
    number, _, _, width = arrays[0].shape
    n_dp = shape[3] // width
    part = number // PARTS

    def body(pos_ref, *refs):
        ins = refs[: len(arrays)]
        out_ref, held, sems, sem_out = refs[-4:]
        dp_at = pos_ref[0]
        inner = (dp_at > 0) & (dp_at < n_dp - 1)

        def into(act, i):
            rows = pl.ds(i * part, part)
            at = 0
            for n, (_, group) in enumerate(flat):
                made = [
                    pltpu.make_async_copy(ins[at + k].at[rows], held.at[n, rows], sems.at[i, n])
                    for k in range(len(group))
                ]
                at += len(group)
                if len(made) == 1:
                    act(made[0])
                else:
                    pl.when(inner)(lambda made=made: act(made[0]))
                    pl.when(~inner)(lambda made=made: act(made[1]))

        for i in range(PARTS):
            into(lambda copy: copy.start(), i)
        outs = []
        for i in range(PARTS):
            into(lambda copy: copy.wait(), i)
            rows = pl.ds(i * part, part)
            for n, (plane, _) in enumerate(flat):
                columns = pl.ds(pl.multiple_of((dp_at ^ plane) * width, 128), width)
                outs.append(
                    pltpu.make_async_copy(
                        held.at[n, rows], out_ref.at[rows, :, :, columns], sem_out.at[i, n]
                    )
                )
                outs[-1].start()
        for copy in outs:
            copy.wait()

    anywhere = pl.BlockSpec(memory_space=pl.ANY)
    held = (len(flat),) + arrays[0].shape
    return pl.pallas_call(
        body,
        out_shape=jax.ShapeDtypeStruct(shape, jnp.bfloat16),
        in_specs=[smem()] + [anywhere] * (len(arrays) + len(before)),
        out_specs=anywhere,
        scratch_shapes=[
            pltpu.VMEM(held, jnp.bfloat16),
            pltpu.SemaphoreType.DMA((PARTS, len(flat))),
            pltpu.SemaphoreType.DMA((PARTS, len(flat))),
        ],
        input_output_aliases={1 + len(arrays): 0} if before else {},
        compiler_params=params((held, 2)),
        name="place_weights",
    )(pos, *arrays, *before)


def gather_weights(pos, fresh, dp_at, n_dp):
    shape = fresh.shape[:3] + (n_dp * fresh.shape[3],)
    if n_dp != 4:
        whole = lax.all_gather(fresh, "dp", axis=0)
        pieces = [
            (j, lax.dynamic_index_in_dim(whole, dp_at ^ j, 0, keepdims=False)) for j in range(n_dp)
        ]
        return place_weights(pos, pieces, shape, [])
    two = lax.ppermute(fresh, "dp", [(0, 2), (1, 3), (2, 0), (3, 1)])
    one = lax.ppermute(fresh, "dp", [(0, 1), (1, 0), (2, 3), (3, 2)])
    outer = lax.ppermute(two, "dp", [(2, 3), (1, 0)])
    middle = lax.ppermute(after(fresh, two), "dp", [(1, 2), (2, 1)])
    most = place_weights(pos, [(0, fresh), (1, one), (2, two)], shape, [])
    return place_weights(pos, [(3, (middle, outer))], shape, [most])


def after(value, *others):
    return lax.optimization_barrier((value,) + others)[0]


def finish_predicted(perm, parts):
    def body(perm_ref, *refs):
        total = refs[0][...].astype(jnp.float32)
        for ref in refs[1:-1]:
            total = total + ref[...].astype(jnp.float32)
        refs[-1][...] = lax.dot_general(
            perm_ref[...],
            total.astype(jnp.bfloat16),
            (((0,), (0,)), ((), ())),
            preferred_element_type=jnp.float32,
        ).astype(jnp.bfloat16)

    return pl.pallas_call(
        body,
        out_shape=jax.ShapeDtypeStruct(parts[0].shape, jnp.bfloat16),
        in_specs=[vmem()] * (1 + len(parts)),
        out_specs=vmem(),
        compiler_params=params(),
        name="finish_predicted",
    )(perm, *parts)


def shards(signals, cotangent, row_insertion, touched, slot_map, weights, moment1, moment2):
    n_own = lax.axis_size("own")
    n_dp = lax.axis_size("dp")
    dp_at = lax.axis_index("dp")
    own_at = lax.axis_index("own")
    number, _, piece, _ = weights.shape
    width = moment1.shape[3]
    half = number // 2
    rows = signals.shape[0]
    pos = jnp.stack([dp_at, own_at]).astype(jnp.int32)

    def across(value, j):
        return lax.ppermute(value, "own", [(o, o ^ j) for o in range(n_own)])

    packed, perm = pack_rows(row_insertion.reshape(1, rows), signals, cotangent)
    planes = lax.all_gather(packed, "dp", axis=0)

    column = lax.dynamic_slice_in_dim(weights, dp_at * width, width, 3)
    outgoing = jnp.broadcast_to(
        column.reshape(1, 2, half, 2, piece, width), (n_own // 2, 2, half, 2, piece, width)
    ).reshape(n_own, half, 2, piece, width)
    blocks = lax.all_to_all(outgoing, "own", split_axis=0, concat_axis=0, tiled=True)

    rows_in = (planes, across(planes, 1))
    pred_mine, pred_other, grads = local_grads(
        pos, touched, slot_map, rows_in, blocks, piece, width
    )
    arrived = lax.all_to_all(grads, "own", split_axis=0, concat_axis=0, tiled=True)

    pred_part = pred_mine + across(pred_other, 1)

    def of_plane(j):
        return lax.dynamic_index_in_dim(pred_part, dp_at ^ j, 0, keepdims=False)

    parts = [of_plane(0)] + [
        lax.ppermute(of_plane(j), "dp", [(d, d ^ j) for d in range(n_dp)]) for j in range(1, n_dp)
    ]
    arrived = after(arrived, *parts[1:])

    fresh, new_moment1, new_moment2 = adam(pos, arrived, weights, moment1, moment2)
    new_weights = gather_weights(pos, fresh, dp_at, n_dp)

    predicted = finish_predicted(perm, parts)
    return (predicted, new_weights, new_moment1, new_moment2)


def solution(mesh):
    in_specs = (
        P(("dp", "own"), None),
        P(("dp", "own"), None),
        P(("dp", "own")),
        P(),
        P(),
        P(None, None, "own", None),
        P(None, None, "own", "dp"),
        P(None, None, "own", "dp"),
    )
    out_specs = (
        P(("dp", "own"), None),
        P(None, None, "own", None),
        P(None, None, "own", "dp"),
        P(None, None, "own", "dp"),
    )
    return jax.shard_map(shards, mesh=mesh, in_specs=in_specs, out_specs=out_specs, check_vma=False)
```

```python
import math

import jax
import jax.numpy as jnp
from jax import lax
from jax.experimental import pallas as pl
from jax.experimental.pallas import tpu as pltpu
from jax.sharding import PartitionSpec as P

SITES = 384
CAP = 128
ID_ROWS = 16
PARTS = 4
VMEM_BYTES = 56 * 2**20

gelu_coef = math.sqrt(2.0 / math.pi)
cubic_coef = 0.044715
learn_rate = 0.01


def gelu_parts(preact):
    tanh_input = gelu_coef * (preact + cubic_coef * preact * preact * preact)
    tangent = jnp.tanh(tanh_input)
    gelu_val = 0.5 * preact * (1.0 + tangent)
    slopes = 0.5 * (1.0 + tangent) + 0.5 * preact * (1.0 - tangent * tangent) * gelu_coef * (
        1.0 + 3.0 * cubic_coef * preact * preact
    )
    return (gelu_val, slopes)


def params():
    return pltpu.CompilerParams(vmem_limit_bytes=VMEM_BYTES)


def vmem():
    return pl.BlockSpec(memory_space=pltpu.VMEM)


def smem():
    return pl.BlockSpec(memory_space=pltpu.SMEM)


def pack_rows(ids, signals, cotangent):
    rows = signals.shape[0]

    def body(ids_ref, sig_ref, cot_ref, out_ref, perm_ref):
        ids_row = ids_ref[...].astype(jnp.float32)
        lane_ids = jnp.broadcast_to(ids_row, (rows, rows))
        same = lane_ids == lane_ids.T
        count = jnp.sum(same.astype(jnp.float32), axis=0, keepdims=True)
        full = jnp.max(jnp.where(count == CAP, ids_row, -1.0), axis=1, keepdims=True)
        chosen = ids_row == full
        from_row = lax.broadcasted_iota(jnp.int32, (rows, rows), 0)
        to_lane = lax.broadcasted_iota(jnp.int32, (rows, rows), 1)
        upto = (from_row <= to_lane).astype(jnp.bfloat16)
        ahead = jnp.dot(
            jnp.broadcast_to(chosen.astype(jnp.float32), (8, rows)).astype(jnp.bfloat16),
            upto,
            preferred_element_type=jnp.float32,
        )[:1].astype(jnp.int32)
        place = jnp.where(chosen, ahead - 1, CAP + to_lane[:1] - ahead)
        perm = (from_row == place).astype(jnp.float32).astype(jnp.bfloat16)
        perm_ref[...] = perm
        out_ref[:rows] = jnp.dot(perm, sig_ref[...], preferred_element_type=jnp.float32).astype(
            jnp.bfloat16
        )
        out_ref[rows : 2 * rows] = jnp.dot(
            perm, cot_ref[...], preferred_element_type=jnp.float32
        ).astype(jnp.bfloat16)
        sorted_ids = lax.dot_general(
            jnp.broadcast_to(ids_row, (ID_ROWS, rows)).astype(jnp.bfloat16),
            perm,
            (((1,), (1,)), ((), ())),
            preferred_element_type=jnp.float32,
        ).astype(jnp.bfloat16)
        out_ref[2 * rows :, :rows] = sorted_ids
        out_ref[2 * rows :, rows:] = jnp.zeros((ID_ROWS, SITES - rows), jnp.bfloat16)

    return pl.pallas_call(
        body,
        out_shape=(
            jax.ShapeDtypeStruct((2 * rows + ID_ROWS, SITES), jnp.bfloat16),
            jax.ShapeDtypeStruct((rows, rows), jnp.bfloat16),
        ),
        in_specs=[vmem(), vmem(), vmem()],
        out_specs=(vmem(), vmem()),
        compiler_params=params(),
        name="pack_rows",
    )(ids, signals, cotangent)


def local_grads(pos, touched, slot_map, rows_in, blocks, piece, width):
    planes = rows_in[0].shape[0]
    rows = (rows_in[0].shape[1] - ID_ROWS) // 2
    touch = touched.shape[1]
    n_own = SITES // piece
    aligned = isinstance(blocks, list)
    arrays = []
    for array, _ in blocks if aligned else [(blocks, None)]:
        if not any(array is one for one in arrays):
            arrays.append(array)
    half = arrays[0].shape[-4]

    def body(pos_ref, touched_ref, slot_ref, *rest):
        row_refs = rest[:2]
        block_refs = rest[2 : 2 + len(arrays)]
        rest = rest[2 + len(arrays) :]
        pred_refs = rest[:2]
        grad_ref = rest[2]
        acc, id_cols, held, sorted_rows, pred, full_of, tasks, sems = rest[-8:]
        own_at = pos_ref[1]
        core = lax.rem(own_at, 2)

        row_copies = [
            pltpu.make_async_copy(ref, sorted_rows.at[pl.ds(i * planes, planes)], sems.at[i])
            for i, ref in enumerate(row_refs)
        ]
        if aligned:
            block_copies = []
            for j, (array, at) in enumerate(blocks):
                ref = [one for one, other in zip(block_refs, arrays) if other is array][0]
                sites = pl.ds(pl.multiple_of((own_at ^ j) * piece, 16), piece)
                block_copies.append(
                    pltpu.make_async_copy(
                        ref if at is None else ref.at[at], held.at[:, :, sites, :], sems.at[2 + j]
                    )
                )
        else:
            block_copies = [pltpu.make_async_copy(block_refs[0], held, sems.at[2])]
        for copy in row_copies + block_copies:
            copy.start()

        def clear(e, _):
            acc[e] = jnp.zeros(acc.shape[1:], jnp.float32)
            return 0

        lax.fori_loop(0, half, clear, 0)
        pred[...] = jnp.zeros_like(pred)
        for copy in row_copies:
            copy.wait()
        for source in range(2 * planes):
            ids_row = sorted_rows[source, 2 * rows :, :rows][:1].astype(jnp.float32)
            id_cols[source] = jnp.broadcast_to(ids_row, (128, rows)).T
            full_of[source] = jnp.max(ids_row[:, :128]).astype(jnp.int32)

        def listing(t, count):
            source = t // (touch + 1)
            j = t - source * (touch + 1)
            which = source // planes
            device = (pos_ref[0] ^ (source - which * planes)) * n_own + (own_at ^ which)
            full = full_of[source]
            insertion = jnp.where(j == 0, full, touched_ref[device, jnp.maximum(j - 1, 0)])
            e = slot_ref[insertion] - core * half
            here = (e >= 0) & (e < half) & ((j == 0) | (insertion != full))
            tasks[0, count] = source
            tasks[1, count] = jnp.where(j == 0, 0, CAP)
            tasks[2, count] = insertion
            tasks[3, count] = e
            return count + here.astype(jnp.int32)

        count = lax.fori_loop(0, 2 * planes * (touch + 1), listing, 0)
        tasks[0, count] = 0
        tasks[1, count] = 0
        tasks[2, count] = -1
        tasks[3, count] = 0
        for copy in block_copies:
            copy.wait()

        def pair(i, _):
            loaded = []
            for u in range(2):
                source, insertion, e = tasks[0, 2 * i + u], tasks[2, 2 * i + u], tasks[3, 2 * i + u]
                first = pl.multiple_of(tasks[1, 2 * i + u], CAP)
                keep = (
                    (id_cols[source, pl.ds(first, CAP), :] == insertion.astype(jnp.float32))
                    .astype(jnp.float32)
                    .astype(jnp.bfloat16)
                )
                keep = jnp.concatenate([keep] * (SITES // 128), axis=1)
                sig = sorted_rows[source, pl.ds(first, CAP), :] * keep
                cot = sorted_rows[source, pl.ds(rows + first, CAP), :] * keep
                loaded.append((source, first, e, sig, cot))
            found = []
            for source, first, e, sig, cot in loaded:
                read_out = held[e, 1]
                preact = jnp.dot(sig, held[e, 0], preferred_element_type=jnp.float32)
                back_hidden = jnp.dot(cot, read_out, preferred_element_type=jnp.float32)
                gelu_val, slopes = gelu_parts(preact)
                hidden = gelu_val.astype(jnp.bfloat16)
                back_pre = (back_hidden * slopes).astype(jnp.bfloat16)
                part = lax.dot_general(
                    hidden, read_out, (((1,), (1,)), ((), ())), preferred_element_type=jnp.float32
                ).astype(jnp.bfloat16)
                grad_in = lax.dot_general(
                    sig, back_pre, (((0,), (0,)), ((), ())), preferred_element_type=jnp.float32
                )
                grad_out = lax.dot_general(
                    cot, hidden, (((0,), (0,)), ((), ())), preferred_element_type=jnp.float32
                )
                found.append((part, grad_in, grad_out))
            for (source, first, e, _, _), (part, grad_in, grad_out) in zip(loaded, found):
                pred[source, pl.ds(first, CAP), :] += part
                acc[e, 0] += grad_in
                acc[e, 1] += grad_out
            return 0

        lax.fori_loop(0, (count + 1) // 2, pair, 0)
        for which, ref in enumerate(pred_refs):
            ref[...] = pred[which * planes : (which + 1) * planes]

        def write(e, _):
            if aligned:
                for i in range(n_own):
                    grad_ref[i, e] = acc[e, :, i * piece : (i + 1) * piece, :].astype(jnp.bfloat16)
            else:
                grad_ref[e] = acc[e].astype(jnp.bfloat16)
            return 0

        lax.fori_loop(0, half, write, 0)

    pred_shape = jax.ShapeDtypeStruct((planes, rows, SITES), jnp.bfloat16)
    grad_shape = (n_own, half, 2, piece, width) if aligned else (half, 2, SITES, width)
    most = 2 * planes * (touch + 1)
    acc_shape = (half, 2, SITES, width)
    id_shape = (2 * planes, rows, 128)
    row_shape = (2 * planes,) + rows_in[0].shape[1:]
    pred_all = (2 * planes, rows, SITES)
    scratch = [
        pltpu.VMEM(acc_shape, jnp.float32),
        pltpu.VMEM(id_shape, jnp.float32),
        pltpu.VMEM(acc_shape, jnp.bfloat16),
        pltpu.VMEM(row_shape, jnp.bfloat16),
        pltpu.VMEM(pred_all, jnp.bfloat16),
        pltpu.SMEM((2 * planes,), jnp.int32),
        pltpu.SMEM((4, most + 1), jnp.int32),
        pltpu.SemaphoreType.DMA((2 + n_own,)),
    ]
    found = pl.pallas_call(
        body,
        out_shape=[pred_shape, pred_shape, jax.ShapeDtypeStruct(grad_shape, jnp.bfloat16)],
        in_specs=[smem(), smem(), smem()] + [pl.BlockSpec(memory_space=pl.ANY)] * (2 + len(arrays)),
        out_specs=[vmem()] * 3,
        scratch_shapes=scratch,
        compiler_params=params(),
        name="local_grads",
    )(pos, touched, slot_map, *rows_in, *arrays)
    grads = found[2]
    if not aligned:
        grads = grads.reshape(half, 2, n_own, piece, width).transpose(2, 0, 1, 3, 4)
    return found[0], found[1], grads


def adam(pos, arrived, weights, moment1, moment2):
    n_own, half, _, piece, width = arrived.shape
    correct_one = 1.0 - 0.9**10
    correct_two = 1.0 - 0.999**10

    def body(pos_ref, arrived_ref, w_ref, m1_ref, m2_ref, *refs):
        new_w, new_m1, new_m2, grads, w_in, m1_in, m2_in, w_out, m1_out, m2_out = refs[:10]
        sem_in, sem_out = refs[10:]
        columns = pl.ds(pl.multiple_of(pos_ref[0] * width, 128), width)
        part = half // PARTS
        steps = [(core, i * part) for core in range(2) for i in range(PARTS)]
        copies = []
        for n, (core, first) in enumerate(steps):
            rows = pl.ds(core * half + first, part)
            copies.append(
                [
                    pltpu.make_async_copy(ref, into.at[rows], sem_in.at[n, i])
                    for i, (ref, into) in enumerate(
                        (
                            (w_ref.at[rows, :, :, columns], w_in),
                            (m1_ref.at[rows], m1_in),
                            (m2_ref.at[rows], m2_in),
                        )
                    )
                ]
                + [
                    pltpu.make_async_copy(
                        arrived_ref.at[i, pl.ds(first, part)],
                        grads.at[i, pl.ds(first, part)],
                        sem_in.at[n, 3 + i // 2],
                    )
                    for i in range(core, n_own, 2)
                ]
            )
            for copy in copies[n]:
                copy.start()
        outs = []
        for n, (core, first) in enumerate(steps):
            for copy in copies[n]:
                copy.wait()

            def step(i, _, core=core, first=first):
                gradient = grads[core, first + i].astype(jnp.float32)
                for j in range(core + 2, n_own, 2):
                    gradient = gradient + grads[j, first + i].astype(jnp.float32)
                at = core * half + first + i
                one = 0.9 * m1_in[at] + 0.1 * gradient
                two = 0.999 * m2_in[at] + 0.001 * gradient * gradient
                m1_out[at] = one
                m2_out[at] = two
                spread = two * (1.0 / correct_two)
                updated = w_in[at].astype(jnp.float32) - one * (learn_rate / correct_one) / (
                    spread * lax.rsqrt(spread) + 1e-08
                )
                w_out[at] = updated.astype(jnp.bfloat16)
                return 0

            lax.fori_loop(0, part, step, 0)
            rows = pl.ds(core * half + first, part)
            for i, (held, ref) in enumerate(
                ((w_out, new_w), (m1_out, new_m1), (m2_out, new_m2))
            ):
                outs.append(pltpu.make_async_copy(held.at[rows], ref.at[rows], sem_out.at[n, i]))
                outs[-1].start()
        for copy in outs:
            copy.wait()

    anywhere = pl.BlockSpec(memory_space=pl.ANY)
    return pl.pallas_call(
        body,
        out_shape=[
            jax.ShapeDtypeStruct(moment1.shape, jnp.bfloat16),
            jax.ShapeDtypeStruct(moment1.shape, jnp.float32),
            jax.ShapeDtypeStruct(moment1.shape, jnp.float32),
        ],
        in_specs=[smem()] + [anywhere] * 4,
        out_specs=[anywhere] * 3,
        scratch_shapes=[pltpu.VMEM(arrived.shape, jnp.bfloat16)]
        + [pltpu.VMEM(moment1.shape, kind) for kind in (jnp.bfloat16, jnp.float32, jnp.float32)] * 2
        + [
            pltpu.SemaphoreType.DMA((2 * PARTS, 3 + n_own // 2)),
            pltpu.SemaphoreType.DMA((2 * PARTS, 3)),
        ],
        compiler_params=params(),
        name="adam_step",
    )(pos, arrived, weights, moment1, moment2)


def place_weights(pos, pieces, shape, before):
    flat = [(plane, one if isinstance(one, tuple) else (one,)) for plane, one in pieces]
    arrays = [one for _, group in flat for one in group]
    number, _, _, width = arrays[0].shape
    n_dp = shape[3] // width
    part = number // PARTS

    def body(pos_ref, *refs):
        ins = refs[: len(arrays)]
        out_ref, held, sems, sem_out = refs[-4:]
        dp_at = pos_ref[0]
        inner = (dp_at > 0) & (dp_at < n_dp - 1)

        def into(act, i):
            rows = pl.ds(i * part, part)
            at = 0
            for n, (_, group) in enumerate(flat):
                made = [
                    pltpu.make_async_copy(ins[at + k].at[rows], held.at[n, rows], sems.at[i, n])
                    for k in range(len(group))
                ]
                at += len(group)
                if len(made) == 1:
                    act(made[0])
                else:
                    pl.when(inner)(lambda made=made: act(made[0]))
                    pl.when(~inner)(lambda made=made: act(made[1]))

        for i in range(PARTS):
            into(lambda copy: copy.start(), i)
        outs = []
        for i in range(PARTS):
            into(lambda copy: copy.wait(), i)
            rows = pl.ds(i * part, part)
            for n, (plane, _) in enumerate(flat):
                columns = pl.ds(pl.multiple_of((dp_at ^ plane) * width, 128), width)
                outs.append(
                    pltpu.make_async_copy(
                        held.at[n, rows], out_ref.at[rows, :, :, columns], sem_out.at[i, n]
                    )
                )
                outs[-1].start()
        for copy in outs:
            copy.wait()

    anywhere = pl.BlockSpec(memory_space=pl.ANY)
    held = (len(flat),) + arrays[0].shape
    return pl.pallas_call(
        body,
        out_shape=jax.ShapeDtypeStruct(shape, jnp.bfloat16),
        in_specs=[smem()] + [anywhere] * (len(arrays) + len(before)),
        out_specs=anywhere,
        scratch_shapes=[
            pltpu.VMEM(held, jnp.bfloat16),
            pltpu.SemaphoreType.DMA((PARTS, len(flat))),
            pltpu.SemaphoreType.DMA((PARTS, len(flat))),
        ],
        input_output_aliases={1 + len(arrays): 0} if before else {},
        compiler_params=params(),
        name="place_weights",
    )(pos, *arrays, *before)


def between_planes(value, dp_at, n_dp, first=(), second=()):
    if n_dp != 4:
        whole = lax.all_gather(value, "dp", axis=0)
        return [
            lax.dynamic_index_in_dim(whole, dp_at ^ j, 0, keepdims=False) for j in range(n_dp)
        ]
    two = lax.ppermute(value, "dp", [(0, 2), (1, 3), (2, 0), (3, 1)])
    one = lax.ppermute(after(value, *first), "dp", [(0, 1), (1, 0), (2, 3), (3, 2)])
    outer = lax.ppermute(after(two, one, *second), "dp", [(2, 3), (1, 0)])
    middle = lax.ppermute(after(value, two, one, *second), "dp", [(1, 2), (2, 1)])
    return [value, one, two, (middle, outer)]


def gather_weights(pos, fresh, dp_at, n_dp):
    shape = fresh.shape[:3] + (n_dp * fresh.shape[3],)
    pieces = list(enumerate(between_planes(fresh, dp_at, n_dp)))
    most = place_weights(pos, pieces[:-1], shape, [])
    return place_weights(pos, pieces[-1:], shape, [most])


def after(value, *others):
    return lax.optimization_barrier((value,) + others)[0]


def finish_predicted(perm, parts):
    def body(perm_ref, *refs):
        total = refs[0][...].astype(jnp.float32)
        for ref in refs[1:-1]:
            total = total + ref[...].astype(jnp.float32)
        refs[-1][...] = lax.dot_general(
            perm_ref[...],
            total.astype(jnp.bfloat16),
            (((0,), (0,)), ((), ())),
            preferred_element_type=jnp.float32,
        ).astype(jnp.bfloat16)

    return pl.pallas_call(
        body,
        out_shape=jax.ShapeDtypeStruct(parts[0].shape, jnp.bfloat16),
        in_specs=[vmem()] * (1 + len(parts)),
        out_specs=vmem(),
        compiler_params=params(),
        name="finish_predicted",
    )(perm, *parts)


def shards(signals, cotangent, row_insertion, touched, slot_map, weights, moment1, moment2):
    n_own = lax.axis_size("own")
    n_dp = lax.axis_size("dp")
    dp_at = lax.axis_index("dp")
    own_at = lax.axis_index("own")
    number, _, piece, _ = weights.shape
    width = moment1.shape[3]
    half = number // 2
    rows = signals.shape[0]
    pos = jnp.stack([dp_at, own_at]).astype(jnp.int32)

    def across(value, j):
        return lax.ppermute(value, "own", [(o, o ^ j) for o in range(n_own)])

    packed, perm = pack_rows(row_insertion.reshape(1, rows), signals, cotangent)
    if n_own == 8 and piece % 16 == 0:
        core = lax.rem(own_at, 2)
        columns = [
            lax.dynamic_slice(
                weights, (which * half, 0, 0, dp_at * width), (half, 2, piece, width)
            )
            for which in (core, 1 - core)
        ]
        chip = jnp.stack([columns[0], across(columns[1], 1)])
        beside = [across(chip, 2), across(chip, 4)]
        diagonal = [across(beside[0][0], 4), across(beside[1][1], 2)]
        blocks = [(one, u) for one in [chip] + beside for u in range(2)]
        blocks += [(one, None) for one in diagonal]
        first, second, last = [chip], beside, diagonal
    else:
        column = lax.dynamic_slice_in_dim(weights, dp_at * width, width, 3)
        outgoing = jnp.broadcast_to(
            column.reshape(1, 2, half, 2, piece, width), (n_own // 2, 2, half, 2, piece, width)
        ).reshape(n_own, half, 2, piece, width)
        blocks = lax.all_to_all(outgoing, "own", split_axis=0, concat_axis=0, tiled=True)
        blocks = blocks.transpose(1, 2, 0, 3, 4).reshape(half, 2, SITES, width)
        first, second, last = [], [], []
    *near, far = between_planes(packed, dp_at, n_dp, first, second)
    if isinstance(far, tuple):
        far = far[0] + far[1]
    planes = jnp.stack(near + [far])
    rows_in = (planes, across(after(planes, *last), 1))

    pred_mine, pred_other, grads = local_grads(
        pos, touched, slot_map, rows_in, blocks, piece, width
    )
    arrived = lax.all_to_all(grads, "own", split_axis=0, concat_axis=0, tiled=True)

    pred_part = pred_mine + across(pred_other, 1)

    parts = [pred_part[0]] + [
        lax.ppermute(pred_part[j], "dp", [(d, d ^ j) for d in range(n_dp)]) for j in range(1, n_dp)
    ]
    arrived = after(arrived, *parts[1:])

    fresh, new_moment1, new_moment2 = adam(pos, arrived, weights, moment1, moment2)
    new_weights = gather_weights(pos, fresh, dp_at, n_dp)

    predicted = finish_predicted(perm, parts)
    return (predicted, new_weights, new_moment1, new_moment2)


def solution(mesh):
    in_specs = (
        P(("dp", "own"), None),
        P(("dp", "own"), None),
        P(("dp", "own")),
        P(),
        P(),
        P(None, None, "own", None),
        P(None, None, "own", "dp"),
        P(None, None, "own", "dp"),
    )
    out_specs = (
        P(("dp", "own"), None),
        P(None, None, "own", None),
        P(None, None, "own", "dp"),
        P(None, None, "own", "dp"),
    )
    return jax.shard_map(shards, mesh=mesh, in_specs=in_specs, out_specs=out_specs, check_vma=False)
```

```python
import math

import jax
import jax.numpy as jnp
from jax import lax
from jax.experimental import pallas as pl
from jax.experimental.pallas import tpu as pltpu
from jax.sharding import PartitionSpec as P

SITES = 384
CAP = 128
ID_ROWS = 16
PARTS = 4
VMEM_BYTES = 56 * 2**20

gelu_coef = math.sqrt(2.0 / math.pi)
cubic_coef = 0.044715
learn_rate = 0.01


def gelu_parts(preact):
    tanh_input = gelu_coef * (preact + cubic_coef * preact * preact * preact)
    tangent = jnp.tanh(tanh_input)
    gelu_val = 0.5 * preact * (1.0 + tangent)
    slopes = 0.5 * (1.0 + tangent) + 0.5 * preact * (1.0 - tangent * tangent) * gelu_coef * (
        1.0 + 3.0 * cubic_coef * preact * preact
    )
    return (gelu_val, slopes)


def params():
    return pltpu.CompilerParams(vmem_limit_bytes=VMEM_BYTES)


def vmem():
    return pl.BlockSpec(memory_space=pltpu.VMEM)


def smem():
    return pl.BlockSpec(memory_space=pltpu.SMEM)


def pack_rows(ids, signals, cotangent):
    rows = signals.shape[0]

    def body(ids_ref, sig_ref, cot_ref, out_ref, perm_ref):
        ids_row = ids_ref[...].astype(jnp.float32)
        lane_ids = jnp.broadcast_to(ids_row, (rows, rows))
        same = lane_ids == lane_ids.T
        count = jnp.sum(same.astype(jnp.float32), axis=0, keepdims=True)
        full = jnp.max(jnp.where(count == CAP, ids_row, -1.0), axis=1, keepdims=True)
        chosen = ids_row == full
        from_row = lax.broadcasted_iota(jnp.int32, (rows, rows), 0)
        to_lane = lax.broadcasted_iota(jnp.int32, (rows, rows), 1)
        upto = (from_row <= to_lane).astype(jnp.bfloat16)
        ahead = jnp.dot(
            jnp.broadcast_to(chosen.astype(jnp.float32), (8, rows)).astype(jnp.bfloat16),
            upto,
            preferred_element_type=jnp.float32,
        )[:1].astype(jnp.int32)
        place = jnp.where(chosen, ahead - 1, CAP + to_lane[:1] - ahead)
        perm = (from_row == place).astype(jnp.float32).astype(jnp.bfloat16)
        perm_ref[...] = perm
        out_ref[:rows] = jnp.dot(perm, sig_ref[...], preferred_element_type=jnp.float32).astype(
            jnp.bfloat16
        )
        out_ref[rows : 2 * rows] = jnp.dot(
            perm, cot_ref[...], preferred_element_type=jnp.float32
        ).astype(jnp.bfloat16)
        sorted_ids = lax.dot_general(
            jnp.broadcast_to(ids_row, (ID_ROWS, rows)).astype(jnp.bfloat16),
            perm,
            (((1,), (1,)), ((), ())),
            preferred_element_type=jnp.float32,
        ).astype(jnp.bfloat16)
        out_ref[2 * rows :, :rows] = sorted_ids
        out_ref[2 * rows :, rows:] = jnp.zeros((ID_ROWS, SITES - rows), jnp.bfloat16)

    return pl.pallas_call(
        body,
        out_shape=(
            jax.ShapeDtypeStruct((2 * rows + ID_ROWS, SITES), jnp.bfloat16),
            jax.ShapeDtypeStruct((rows, rows), jnp.bfloat16),
        ),
        in_specs=[vmem(), vmem(), vmem()],
        out_specs=(vmem(), vmem()),
        compiler_params=params(),
        name="pack_rows",
    )(ids, signals, cotangent)


def local_grads(pos, touched, slot_map, rows_in, blocks, sends, piece, width):
    planes = rows_in[0].shape[0]
    rows = (rows_in[0].shape[1] - ID_ROWS) // 2
    touch = touched.shape[1]
    n_own = SITES // piece
    aligned = isinstance(blocks, list)
    arrays = []
    for array, _ in blocks if aligned else [(blocks, None)]:
        if not any(array is one for one in arrays):
            arrays.append(array)
    half = arrays[0].shape[-4]

    def body(pos_ref, touched_ref, slot_ref, *rest):
        row_refs = rest[:2]
        block_refs = rest[2 : 2 + len(arrays)]
        rest = rest[2 + len(arrays) :]
        pred_refs = rest[:2]
        grad_refs = rest[2:-8]
        acc, id_cols, held, sorted_rows, pred, full_of, tasks, sems = rest[-8:]
        own_at = pos_ref[1]
        core = lax.rem(own_at, 2)

        row_copies = [
            pltpu.make_async_copy(ref, sorted_rows.at[pl.ds(i * planes, planes)], sems.at[i])
            for i, ref in enumerate(row_refs)
        ]
        if aligned:
            block_copies = []
            for j, (array, at) in enumerate(blocks):
                ref = [one for one, other in zip(block_refs, arrays) if other is array][0]
                sites = pl.ds(pl.multiple_of((own_at ^ j) * piece, 16), piece)
                block_copies.append(
                    pltpu.make_async_copy(
                        ref if at is None else ref.at[at], held.at[:, :, sites, :], sems.at[2 + j]
                    )
                )
        else:
            block_copies = [pltpu.make_async_copy(block_refs[0], held, sems.at[2])]
        for copy in row_copies + block_copies:
            copy.start()

        def clear(e, _):
            acc[e] = jnp.zeros(acc.shape[1:], jnp.float32)
            return 0

        lax.fori_loop(0, half, clear, 0)
        pred[...] = jnp.zeros_like(pred)
        for copy in row_copies:
            copy.wait()
        for source in range(2 * planes):
            ids_row = sorted_rows[source, 2 * rows :, :rows][:1].astype(jnp.float32)
            id_cols[source] = jnp.broadcast_to(ids_row, (128, rows)).T
            full_of[source] = jnp.max(ids_row[:, :128]).astype(jnp.int32)

        def listing(t, count):
            source = t // (touch + 1)
            j = t - source * (touch + 1)
            which = source // planes
            device = (pos_ref[0] ^ (source - which * planes)) * n_own + (own_at ^ which)
            full = full_of[source]
            insertion = jnp.where(j == 0, full, touched_ref[device, jnp.maximum(j - 1, 0)])
            e = slot_ref[insertion] - core * half
            here = (e >= 0) & (e < half) & ((j == 0) | (insertion != full))
            tasks[0, count] = source
            tasks[1, count] = jnp.where(j == 0, 0, CAP)
            tasks[2, count] = insertion
            tasks[3, count] = e
            return count + here.astype(jnp.int32)

        count = lax.fori_loop(0, 2 * planes * (touch + 1), listing, 0)
        tasks[0, count] = 0
        tasks[1, count] = 0
        tasks[2, count] = -1
        tasks[3, count] = 0
        for copy in block_copies:
            copy.wait()

        def pair(i, _):
            loaded = []
            for u in range(2):
                source, insertion, e = tasks[0, 2 * i + u], tasks[2, 2 * i + u], tasks[3, 2 * i + u]
                first = pl.multiple_of(tasks[1, 2 * i + u], CAP)
                keep = (
                    (id_cols[source, pl.ds(first, CAP), :] == insertion.astype(jnp.float32))
                    .astype(jnp.float32)
                    .astype(jnp.bfloat16)
                )
                keep = jnp.concatenate([keep] * (SITES // 128), axis=1)
                sig = sorted_rows[source, pl.ds(first, CAP), :] * keep
                cot = sorted_rows[source, pl.ds(rows + first, CAP), :] * keep
                loaded.append((source, first, e, sig, cot))
            found = []
            for source, first, e, sig, cot in loaded:
                read_out = held[e, 1]
                preact = jnp.dot(sig, held[e, 0], preferred_element_type=jnp.float32)
                back_hidden = jnp.dot(cot, read_out, preferred_element_type=jnp.float32)
                gelu_val, slopes = gelu_parts(preact)
                hidden = gelu_val.astype(jnp.bfloat16)
                back_pre = (back_hidden * slopes).astype(jnp.bfloat16)
                part = lax.dot_general(
                    hidden, read_out, (((1,), (1,)), ((), ())), preferred_element_type=jnp.float32
                ).astype(jnp.bfloat16)
                grad_in = lax.dot_general(
                    sig, back_pre, (((0,), (0,)), ((), ())), preferred_element_type=jnp.float32
                )
                grad_out = lax.dot_general(
                    cot, hidden, (((0,), (0,)), ((), ())), preferred_element_type=jnp.float32
                )
                found.append((part, grad_in, grad_out))
            for (source, first, e, _, _), (part, grad_in, grad_out) in zip(loaded, found):
                pred[source, pl.ds(first, CAP), :] += part
                acc[e, 0] += grad_in
                acc[e, 1] += grad_out
            return 0

        lax.fori_loop(0, (count + 1) // 2, pair, 0)
        for which, ref in enumerate(pred_refs):
            for i in range(planes):
                ref[pos_ref[0] ^ i] = pred[which * planes + i]

        def write(e, _):
            if aligned:
                for ref, group in zip(grad_refs, sends):
                    for i, j in enumerate(group):
                        first = pl.multiple_of((own_at ^ j) * piece, 16)
                        ref[i, e] = acc[e, :, pl.ds(first, piece), :].astype(jnp.bfloat16)
            else:
                grad_refs[0][e] = acc[e].astype(jnp.bfloat16)
            return 0

        lax.fori_loop(0, half, write, 0)

    pred_shape = jax.ShapeDtypeStruct((planes, rows, SITES), jnp.bfloat16)
    grad_shapes = [
        jax.ShapeDtypeStruct(shape, jnp.bfloat16)
        for shape in (
            [(len(group), half, 2, piece, width) for group in sends]
            if aligned
            else [(half, 2, SITES, width)]
        )
    ]
    most = 2 * planes * (touch + 1)
    acc_shape = (half, 2, SITES, width)
    id_shape = (2 * planes, rows, 128)
    row_shape = (2 * planes,) + rows_in[0].shape[1:]
    pred_all = (2 * planes, rows, SITES)
    scratch = [
        pltpu.VMEM(acc_shape, jnp.float32),
        pltpu.VMEM(id_shape, jnp.float32),
        pltpu.VMEM(acc_shape, jnp.bfloat16),
        pltpu.VMEM(row_shape, jnp.bfloat16),
        pltpu.VMEM(pred_all, jnp.bfloat16),
        pltpu.SMEM((2 * planes,), jnp.int32),
        pltpu.SMEM((4, most + 1), jnp.int32),
        pltpu.SemaphoreType.DMA((2 + n_own,)),
    ]
    found = pl.pallas_call(
        body,
        out_shape=[pred_shape, pred_shape] + grad_shapes,
        in_specs=[smem(), smem(), smem()] + [pl.BlockSpec(memory_space=pl.ANY)] * (2 + len(arrays)),
        out_specs=[vmem()] * (2 + len(grad_shapes)),
        scratch_shapes=scratch,
        compiler_params=params(),
        name="local_grads",
    )(pos, touched, slot_map, *rows_in, *arrays)
    grads = list(found[2:])
    if not aligned:
        grads = grads[0].reshape(half, 2, n_own, piece, width).transpose(2, 0, 1, 3, 4)
    return found[0], found[1], grads


def adam(pos, terms, weights, moment1, moment2):
    number, _, piece, width = moment1.shape
    half = number // 2
    flat = [one if isinstance(one, tuple) else (one, None) for group in terms for one in group]
    arrays = [array for array, _ in flat]
    per = len(terms[0])
    correct_one = 1.0 - 0.9**10
    correct_two = 1.0 - 0.999**10

    def body(pos_ref, *refs):
        term_refs = [
            ref if at is None else ref.at[at] for ref, (_, at) in zip(refs, flat)
        ]
        w_ref, m1_ref, m2_ref = refs[len(flat) : len(flat) + 3]
        refs = refs[len(flat) + 3 :]
        new_w, new_m1, new_m2, grads, w_in, m1_in, m2_in, w_out, m1_out, m2_out = refs[:10]
        sem_in, sem_out = refs[10:]
        columns = pl.ds(pl.multiple_of(pos_ref[0] * width, 128), width)
        part = half // PARTS
        steps = [(g, i * part) for g in range(2) for i in range(PARTS)]
        own_core = lax.rem(pos_ref[1], 2)
        copies = []
        for n, (g, first) in enumerate(steps):
            rows = pl.ds((own_core ^ g) * half + first, part)
            copies.append(
                [
                    pltpu.make_async_copy(ref, into.at[rows], sem_in.at[n, i])
                    for i, (ref, into) in enumerate(
                        (
                            (w_ref.at[rows, :, :, columns], w_in),
                            (m1_ref.at[rows], m1_in),
                            (m2_ref.at[rows], m2_in),
                        )
                    )
                ]
                + [
                    pltpu.make_async_copy(
                        term_refs[g * per + i].at[pl.ds(first, part)],
                        grads.at[g * per + i, pl.ds(first, part)],
                        sem_in.at[n, 3 + i],
                    )
                    for i in range(per)
                ]
            )
            for copy in copies[n]:
                copy.start()
        outs = []
        for n, (g, first) in enumerate(steps):
            for copy in copies[n]:
                copy.wait()

            def step(i, _, g=g, first=first):
                gradient = grads[g * per, first + i].astype(jnp.float32)
                for j in range(1, per):
                    gradient = gradient + grads[g * per + j, first + i].astype(jnp.float32)
                at = (own_core ^ g) * half + first + i
                one = 0.9 * m1_in[at] + 0.1 * gradient
                two = 0.999 * m2_in[at] + 0.001 * gradient * gradient
                m1_out[at] = one
                m2_out[at] = two
                spread = two * (1.0 / correct_two)
                updated = w_in[at].astype(jnp.float32) - one * (learn_rate / correct_one) / (
                    spread * lax.rsqrt(spread) + 1e-08
                )
                w_out[at] = updated.astype(jnp.bfloat16)
                return 0

            lax.fori_loop(0, part, step, 0)
            rows = pl.ds((own_core ^ g) * half + first, part)
            for i, (held, ref) in enumerate(
                ((w_out, new_w), (m1_out, new_m1), (m2_out, new_m2))
            ):
                outs.append(pltpu.make_async_copy(held.at[rows], ref.at[rows], sem_out.at[n, i]))
                outs[-1].start()
        for copy in outs:
            copy.wait()

    anywhere = pl.BlockSpec(memory_space=pl.ANY)
    return pl.pallas_call(
        body,
        out_shape=[
            jax.ShapeDtypeStruct(moment1.shape, jnp.bfloat16),
            jax.ShapeDtypeStruct(moment1.shape, jnp.float32),
            jax.ShapeDtypeStruct(moment1.shape, jnp.float32),
        ],
        in_specs=[smem()] + [anywhere] * (len(flat) + 3),
        out_specs=[anywhere] * 3,
        scratch_shapes=[pltpu.VMEM((len(flat), half, 2, piece, width), jnp.bfloat16)]
        + [pltpu.VMEM(moment1.shape, kind) for kind in (jnp.bfloat16, jnp.float32, jnp.float32)] * 2
        + [
            pltpu.SemaphoreType.DMA((2 * PARTS, 3 + per)),
            pltpu.SemaphoreType.DMA((2 * PARTS, 3)),
        ],
        compiler_params=params(),
        name="adam_step",
    )(pos, *arrays, weights, moment1, moment2)


def place_weights(pos, pieces, shape, before):
    flat = [(plane, one if isinstance(one, tuple) else (one,)) for plane, one in pieces]
    arrays = [one for _, group in flat for one in group]
    number, _, _, width = arrays[0].shape
    n_dp = shape[3] // width
    part = number // PARTS

    def body(pos_ref, *refs):
        ins = refs[: len(arrays)]
        out_ref, held, sems, sem_out = refs[-4:]
        dp_at = pos_ref[0]
        inner = (dp_at > 0) & (dp_at < n_dp - 1)

        def into(act, i):
            rows = pl.ds(i * part, part)
            at = 0
            for n, (_, group) in enumerate(flat):
                made = [
                    pltpu.make_async_copy(ins[at + k].at[rows], held.at[n, rows], sems.at[i, n])
                    for k in range(len(group))
                ]
                at += len(group)
                if len(made) == 1:
                    act(made[0])
                else:
                    pl.when(inner)(lambda made=made: act(made[0]))
                    pl.when(~inner)(lambda made=made: act(made[1]))

        for i in range(PARTS):
            into(lambda copy: copy.start(), i)
        outs = []
        for i in range(PARTS):
            into(lambda copy: copy.wait(), i)
            rows = pl.ds(i * part, part)
            for n, (plane, _) in enumerate(flat):
                columns = pl.ds(pl.multiple_of((dp_at ^ plane) * width, 128), width)
                outs.append(
                    pltpu.make_async_copy(
                        held.at[n, rows], out_ref.at[rows, :, :, columns], sem_out.at[i, n]
                    )
                )
                outs[-1].start()
        for copy in outs:
            copy.wait()

    anywhere = pl.BlockSpec(memory_space=pl.ANY)
    held = (len(flat),) + arrays[0].shape
    return pl.pallas_call(
        body,
        out_shape=jax.ShapeDtypeStruct(shape, jnp.bfloat16),
        in_specs=[smem()] + [anywhere] * (len(arrays) + len(before)),
        out_specs=anywhere,
        scratch_shapes=[
            pltpu.VMEM(held, jnp.bfloat16),
            pltpu.SemaphoreType.DMA((PARTS, len(flat))),
            pltpu.SemaphoreType.DMA((PARTS, len(flat))),
        ],
        input_output_aliases={1 + len(arrays): 0} if before else {},
        compiler_params=params(),
        name="place_weights",
    )(pos, *arrays, *before)


def between_planes(value, dp_at, n_dp, first=(), second=()):
    if n_dp != 4:
        whole = lax.all_gather(value, "dp", axis=0)
        return [
            lax.dynamic_index_in_dim(whole, dp_at ^ j, 0, keepdims=False) for j in range(n_dp)
        ]
    two = lax.ppermute(value, "dp", [(0, 2), (1, 3), (2, 0), (3, 1)])
    one = lax.ppermute(after(value, *first), "dp", [(0, 1), (1, 0), (2, 3), (3, 2)])
    outer = lax.ppermute(after(two, one, *second), "dp", [(2, 3), (1, 0)])
    middle = lax.ppermute(after(value, two, one, *second), "dp", [(1, 2), (2, 1)])
    return [value, one, two, (middle, outer)]


def gather_weights(pos, fresh, dp_at, n_dp):
    shape = fresh.shape[:3] + (n_dp * fresh.shape[3],)
    pieces = list(enumerate(between_planes(fresh, dp_at, n_dp)))
    most = place_weights(pos, pieces[:-1], shape, [])
    return place_weights(pos, pieces[-1:], shape, [most])


def after(value, *others):
    return lax.optimization_barrier((value,) + others)[0]


def finish_predicted(perm, parts):
    def body(perm_ref, parts_ref, out_ref):
        total = jnp.sum(parts_ref[...].astype(jnp.float32), axis=0)
        out_ref[...] = lax.dot_general(
            perm_ref[...],
            total.astype(jnp.bfloat16),
            (((0,), (0,)), ((), ())),
            preferred_element_type=jnp.float32,
        ).astype(jnp.bfloat16)

    return pl.pallas_call(
        body,
        out_shape=jax.ShapeDtypeStruct(parts.shape[1:], jnp.bfloat16),
        in_specs=[vmem(), vmem()],
        out_specs=vmem(),
        compiler_params=params(),
        name="finish_predicted",
    )(perm, parts)


def shards(signals, cotangent, row_insertion, touched, slot_map, weights, moment1, moment2):
    n_own = lax.axis_size("own")
    n_dp = lax.axis_size("dp")
    dp_at = lax.axis_index("dp")
    own_at = lax.axis_index("own")
    number, _, piece, _ = weights.shape
    width = moment1.shape[3]
    half = number // 2
    rows = signals.shape[0]
    pos = jnp.stack([dp_at, own_at]).astype(jnp.int32)

    def across(value, j):
        return lax.ppermute(value, "own", [(o, o ^ j) for o in range(n_own)])

    packed, perm = pack_rows(row_insertion.reshape(1, rows), signals, cotangent)
    if n_own == 8 and piece % 16 == 0:
        core = lax.rem(own_at, 2)
        columns = [
            lax.dynamic_slice(
                weights, (which * half, 0, 0, dp_at * width), (half, 2, piece, width)
            )
            for which in (core, 1 - core)
        ]
        chip = jnp.stack([columns[0], after(across(columns[1], 1), packed)])
        beside = [across(chip, 2), across(chip, 4)]
        diagonal = [across(beside[0][0], 4), across(beside[1][1], 2)]
        blocks = [(one, u) for one in [chip] + beside for u in range(2)]
        blocks += [(one, None) for one in diagonal]
        first, second, last = [chip], beside, diagonal
        sends = [(0,), (1,), (2, 6), (7,), (5,), (3,), (4,)]
    else:
        column = lax.dynamic_slice_in_dim(weights, dp_at * width, width, 3)
        outgoing = jnp.broadcast_to(
            column.reshape(1, 2, half, 2, piece, width), (n_own // 2, 2, half, 2, piece, width)
        ).reshape(n_own, half, 2, piece, width)
        blocks = lax.all_to_all(outgoing, "own", split_axis=0, concat_axis=0, tiled=True)
        blocks = blocks.transpose(1, 2, 0, 3, 4).reshape(half, 2, SITES, width)
        first, second, last = [], [], []
        sends = None
    *near, far = between_planes(packed, dp_at, n_dp, first, second)
    if isinstance(far, tuple):
        far = far[0] + far[1]
    planes = jnp.stack(near + [far])
    rows_in = (planes, across(after(planes, *last), 1))

    pred_mine, pred_other, grads = local_grads(
        pos, touched, slot_map, rows_in, blocks, sends, piece, width
    )
    if sends:
        own, partner, x_same, y_diagonal, y_cross, x_cross, y_same = grads
        x_same = across(x_same, 2)
        y_diagonal = across(y_diagonal, 4)
        y_cross = across(y_cross, 5)
        partner = across(partner, 1)
        x_cross = across(x_cross[0] + y_diagonal[0], 3)
        y_same = across(y_same[0] + x_same[1], 4)
        terms = [[(own, 0), (x_same, 0), y_same], [(partner, 0), (y_cross, 0), x_cross]]
    else:
        arrived = lax.all_to_all(grads, "own", split_axis=0, concat_axis=0, tiled=True)
        arrived = [
            lax.dynamic_index_in_dim(arrived, own_at ^ j, 0, keepdims=False) for j in range(n_own)
        ]
        terms = [arrived[0::2], arrived[1::2]]

    pred_part = pred_mine + across(pred_other, 1)
    parts = lax.all_to_all(pred_part, "dp", split_axis=0, concat_axis=0, tiled=True)
    predicted = finish_predicted(perm, parts)
    terms[0][-1] = after(terms[0][-1], parts)

    fresh, new_moment1, new_moment2 = adam(pos, terms, weights, moment1, moment2)
    new_weights = gather_weights(pos, fresh, dp_at, n_dp)

    return (predicted, new_weights, new_moment1, new_moment2)


def solution(mesh):
    in_specs = (
        P(("dp", "own"), None),
        P(("dp", "own"), None),
        P(("dp", "own")),
        P(),
        P(),
        P(None, None, "own", None),
        P(None, None, "own", "dp"),
        P(None, None, "own", "dp"),
    )
    out_specs = (
        P(("dp", "own"), None),
        P(None, None, "own", None),
        P(None, None, "own", "dp"),
        P(None, None, "own", "dp"),
    )
    return jax.shard_map(shards, mesh=mesh, in_specs=in_specs, out_specs=out_specs, check_vma=False)
```

```python
import math

import jax
import jax.numpy as jnp
from jax import lax
from jax.experimental import pallas as pl
from jax.experimental.pallas import tpu as pltpu
from jax.sharding import PartitionSpec as P

SITES = 384
CAP = 128
ID_ROWS = 16
PARTS = 4
VMEM_BYTES = 56 * 2**20

gelu_coef = math.sqrt(2.0 / math.pi)
cubic_coef = 0.044715
learn_rate = 0.01


def gelu_parts(preact):
    tanh_input = gelu_coef * (preact + cubic_coef * preact * preact * preact)
    tangent = jnp.tanh(tanh_input)
    gelu_val = 0.5 * preact * (1.0 + tangent)
    slopes = 0.5 * (1.0 + tangent) + 0.5 * preact * (1.0 - tangent * tangent) * gelu_coef * (
        1.0 + 3.0 * cubic_coef * preact * preact
    )
    return (gelu_val, slopes)


def params():
    return pltpu.CompilerParams(vmem_limit_bytes=VMEM_BYTES)


def vmem():
    return pl.BlockSpec(memory_space=pltpu.VMEM)


def smem():
    return pl.BlockSpec(memory_space=pltpu.SMEM)


def pack_rows(ids, signals, cotangent):
    rows = signals.shape[0]

    def body(ids_ref, sig_ref, cot_ref, out_ref, perm_ref):
        ids_row = ids_ref[...].astype(jnp.float32)
        lane_ids = jnp.broadcast_to(ids_row, (rows, rows))
        same = lane_ids == lane_ids.T
        count = jnp.sum(same.astype(jnp.float32), axis=0, keepdims=True)
        full = jnp.max(jnp.where(count == CAP, ids_row, -1.0), axis=1, keepdims=True)
        chosen = ids_row == full
        from_row = lax.broadcasted_iota(jnp.int32, (rows, rows), 0)
        to_lane = lax.broadcasted_iota(jnp.int32, (rows, rows), 1)
        upto = (from_row <= to_lane).astype(jnp.bfloat16)
        ahead = jnp.dot(
            jnp.broadcast_to(chosen.astype(jnp.float32), (8, rows)).astype(jnp.bfloat16),
            upto,
            preferred_element_type=jnp.float32,
        )[:1].astype(jnp.int32)
        place = jnp.where(chosen, ahead - 1, CAP + to_lane[:1] - ahead)
        perm = (from_row == place).astype(jnp.float32).astype(jnp.bfloat16)
        perm_ref[...] = perm
        out_ref[:rows] = jnp.dot(perm, sig_ref[...], preferred_element_type=jnp.float32).astype(
            jnp.bfloat16
        )
        out_ref[rows : 2 * rows] = jnp.dot(
            perm, cot_ref[...], preferred_element_type=jnp.float32
        ).astype(jnp.bfloat16)
        sorted_ids = lax.dot_general(
            jnp.broadcast_to(ids_row, (ID_ROWS, rows)).astype(jnp.bfloat16),
            perm,
            (((1,), (1,)), ((), ())),
            preferred_element_type=jnp.float32,
        ).astype(jnp.bfloat16)
        out_ref[2 * rows :, :rows] = sorted_ids
        out_ref[2 * rows :, rows:] = jnp.zeros((ID_ROWS, SITES - rows), jnp.bfloat16)

    return pl.pallas_call(
        body,
        out_shape=(
            jax.ShapeDtypeStruct((2 * rows + ID_ROWS, SITES), jnp.bfloat16),
            jax.ShapeDtypeStruct((rows, rows), jnp.bfloat16),
        ),
        in_specs=[vmem(), vmem(), vmem()],
        out_specs=(vmem(), vmem()),
        compiler_params=params(),
        name="pack_rows",
    )(ids, signals, cotangent)


def local_grads(pos, touched, slot_map, rows_in, blocks, sends, piece, width):
    near = rows_in[0].shape[0]
    planes = near + 1
    rows = (rows_in[0].shape[1] - ID_ROWS) // 2
    touch = touched.shape[1]
    n_own = SITES // piece
    aligned = isinstance(blocks, list)
    arrays = []
    for array, _ in blocks if aligned else [(blocks, None)]:
        if not any(array is one for one in arrays):
            arrays.append(array)
    half = arrays[0].shape[-4]

    def body(pos_ref, touched_ref, slot_ref, *rest):
        row_refs = rest[:4]
        block_refs = rest[4 : 4 + len(arrays)]
        rest = rest[4 + len(arrays) :]
        pred_refs = rest[:2]
        n_out = len(grad_shapes)
        grad_refs = rest[2 : 2 + n_out]
        staged = rest[2 + n_out : 2 + 2 * n_out]
        acc, id_cols, held, sorted_rows, pred, full_of, tasks, sems, sem_out = rest[-9:]
        own_at = pos_ref[1]
        core = lax.rem(own_at, 2)

        row_copies = [
            pltpu.make_async_copy(
                ref, sorted_rows.at[pl.ds(at, near) if i % 2 == 0 else at], sems.at[i]
            )
            for i, (ref, at) in enumerate(zip(row_refs, (0, near, planes, planes + near)))
        ]
        if aligned:
            block_copies = []
            for j, (array, at) in enumerate(blocks):
                ref = [one for one, other in zip(block_refs, arrays) if other is array][0]
                sites = pl.ds(pl.multiple_of((own_at ^ j) * piece, 16), piece)
                block_copies.append(
                    pltpu.make_async_copy(
                        ref if at is None else ref.at[at], held.at[:, :, sites, :], sems.at[4 + j]
                    )
                )
        else:
            block_copies = [pltpu.make_async_copy(block_refs[0], held, sems.at[4])]
        for copy in row_copies + block_copies:
            copy.start()

        def clear(e, _):
            acc[e] = jnp.zeros(acc.shape[1:], jnp.float32)
            return 0

        lax.fori_loop(0, half, clear, 0)
        pred[...] = jnp.zeros_like(pred)
        for copy in row_copies:
            copy.wait()
        for source in range(2 * planes):
            ids_row = sorted_rows[source, 2 * rows :, :rows][:1].astype(jnp.float32)
            id_cols[source] = jnp.broadcast_to(ids_row, (128, rows)).T
            full_of[source] = jnp.max(ids_row[:, :128]).astype(jnp.int32)

        def listing(t, count):
            source = t // (touch + 1)
            j = t - source * (touch + 1)
            which = source // planes
            device = (pos_ref[0] ^ (source - which * planes)) * n_own + (own_at ^ which)
            full = full_of[source]
            insertion = jnp.where(j == 0, full, touched_ref[device, jnp.maximum(j - 1, 0)])
            e = slot_ref[insertion] - core * half
            here = (e >= 0) & (e < half) & ((j == 0) | (insertion != full))
            tasks[0, count] = source
            tasks[1, count] = jnp.where(j == 0, 0, CAP)
            tasks[2, count] = insertion
            tasks[3, count] = e
            return count + here.astype(jnp.int32)

        count = lax.fori_loop(0, 2 * planes * (touch + 1), listing, 0)
        tasks[0, count] = 0
        tasks[1, count] = 0
        tasks[2, count] = -1
        tasks[3, count] = 0
        for copy in block_copies:
            copy.wait()

        def pair(i, _):
            loaded = []
            for u in range(2):
                source, insertion, e = tasks[0, 2 * i + u], tasks[2, 2 * i + u], tasks[3, 2 * i + u]
                first = pl.multiple_of(tasks[1, 2 * i + u], CAP)
                keep = (
                    (id_cols[source, pl.ds(first, CAP), :] == insertion.astype(jnp.float32))
                    .astype(jnp.float32)
                    .astype(jnp.bfloat16)
                )
                keep = jnp.concatenate([keep] * (SITES // 128), axis=1)
                sig = sorted_rows[source, pl.ds(first, CAP), :] * keep
                cot = sorted_rows[source, pl.ds(rows + first, CAP), :] * keep
                loaded.append((source, first, e, sig, cot))
            found = []
            for source, first, e, sig, cot in loaded:
                read_out = held[e, 1]
                preact = jnp.dot(sig, held[e, 0], preferred_element_type=jnp.float32)
                back_hidden = jnp.dot(cot, read_out, preferred_element_type=jnp.float32)
                gelu_val, slopes = gelu_parts(preact)
                hidden = gelu_val.astype(jnp.bfloat16)
                back_pre = (back_hidden * slopes).astype(jnp.bfloat16)
                part = lax.dot_general(
                    hidden, read_out, (((1,), (1,)), ((), ())), preferred_element_type=jnp.float32
                ).astype(jnp.bfloat16)
                grad_in = lax.dot_general(
                    sig, back_pre, (((0,), (0,)), ((), ())), preferred_element_type=jnp.float32
                )
                grad_out = lax.dot_general(
                    cot, hidden, (((0,), (0,)), ((), ())), preferred_element_type=jnp.float32
                )
                found.append((part, grad_in, grad_out))
            for (source, first, e, _, _), (part, grad_in, grad_out) in zip(loaded, found):
                pred[source, pl.ds(first, CAP), :] += part
                acc[e, 0] += grad_in
                acc[e, 1] += grad_out
            return 0

        lax.fori_loop(0, (count + 1) // 2, pair, 0)
        outs = [
            pltpu.make_async_copy(
                pred.at[pl.ds(which * planes, planes)], pred_refs[which], sem_out.at[which]
            )
            for which in (1, 0)
        ]
        for copy in outs:
            copy.start()
        for n, (ref, into) in enumerate(zip(grad_refs, staged)):

            def write(e, _, into=into, n=n):
                if aligned:
                    for i, j in enumerate(sends[n]):
                        first = pl.multiple_of((own_at ^ j) * piece, 16)
                        into[i, e] = acc[e, :, pl.ds(first, piece), :].astype(jnp.bfloat16)
                else:
                    into[e] = acc[e].astype(jnp.bfloat16)
                return 0

            lax.fori_loop(0, half, write, 0)
            outs.append(pltpu.make_async_copy(into, ref, sem_out.at[2 + n]))
            outs[-1].start()
        for copy in outs:
            copy.wait()

    pred_shape = jax.ShapeDtypeStruct((planes, rows, SITES), jnp.bfloat16)
    grad_shapes = [
        jax.ShapeDtypeStruct(shape, jnp.bfloat16)
        for shape in (
            [(len(group), half, 2, piece, width) for group in sends]
            if aligned
            else [(half, 2, SITES, width)]
        )
    ]
    most = 2 * planes * (touch + 1)
    acc_shape = (half, 2, SITES, width)
    id_shape = (2 * planes, rows, 128)
    row_shape = (2 * planes,) + rows_in[0].shape[1:]
    pred_all = (2 * planes, rows, SITES)
    scratch = [pltpu.VMEM(one.shape, jnp.bfloat16) for one in grad_shapes] + [
        pltpu.VMEM(acc_shape, jnp.float32),
        pltpu.VMEM(id_shape, jnp.float32),
        pltpu.VMEM(acc_shape, jnp.bfloat16),
        pltpu.VMEM(row_shape, jnp.bfloat16),
        pltpu.VMEM(pred_all, jnp.bfloat16),
        pltpu.SMEM((2 * planes,), jnp.int32),
        pltpu.SMEM((4, most + 1), jnp.int32),
        pltpu.SemaphoreType.DMA((4 + n_own,)),
        pltpu.SemaphoreType.DMA((2 + len(grad_shapes),)),
    ]
    found = pl.pallas_call(
        body,
        out_shape=[pred_shape, pred_shape] + grad_shapes,
        in_specs=[smem(), smem(), smem()] + [pl.BlockSpec(memory_space=pl.ANY)] * (4 + len(arrays)),
        out_specs=[pl.BlockSpec(memory_space=pl.ANY)] * (2 + len(grad_shapes)),
        scratch_shapes=scratch,
        compiler_params=params(),
        name="local_grads",
    )(pos, touched, slot_map, *rows_in, *arrays)
    grads = list(found[2:])
    if not aligned:
        grads = grads[0].reshape(half, 2, n_own, piece, width).transpose(2, 0, 1, 3, 4)
    return found[0], found[1], grads


def adam(pos, terms, weights, moment1, moment2):
    number, _, piece, width = moment1.shape
    half = number // 2
    flat = [one if isinstance(one, tuple) else (one, None) for group in terms for one in group]
    arrays = [array for array, _ in flat]
    per = len(terms[0])
    correct_one = 1.0 - 0.9**10
    correct_two = 1.0 - 0.999**10

    def body(pos_ref, *refs):
        term_refs = [
            ref if at is None else ref.at[at] for ref, (_, at) in zip(refs, flat)
        ]
        w_ref, m1_ref, m2_ref = refs[len(flat) : len(flat) + 3]
        refs = refs[len(flat) + 3 :]
        new_w, new_m1, new_m2, grads, w_in, m1_in, m2_in, w_out, m1_out, m2_out = refs[:10]
        sem_in, sem_out = refs[10:]
        columns = pl.ds(pl.multiple_of(pos_ref[0] * width, 128), width)
        part = half // PARTS
        steps = [(g, i * part) for g in range(2) for i in range(PARTS)]
        own_core = lax.rem(pos_ref[1], 2)
        copies = []
        for n, (g, first) in enumerate(steps):
            rows = pl.ds((own_core ^ g) * half + first, part)
            copies.append(
                [
                    pltpu.make_async_copy(ref, into.at[rows], sem_in.at[n, i])
                    for i, (ref, into) in enumerate(
                        (
                            (w_ref.at[rows, :, :, columns], w_in),
                            (m1_ref.at[rows], m1_in),
                            (m2_ref.at[rows], m2_in),
                        )
                    )
                ]
                + [
                    pltpu.make_async_copy(
                        term_refs[g * per + i].at[pl.ds(first, part)],
                        grads.at[g * per + i, pl.ds(first, part)],
                        sem_in.at[n, 3 + i],
                    )
                    for i in range(per)
                ]
            )
            for copy in copies[n]:
                copy.start()
        outs = []
        for n, (g, first) in enumerate(steps):
            for copy in copies[n]:
                copy.wait()

            def step(i, _, g=g, first=first):
                gradient = grads[g * per, first + i].astype(jnp.float32)
                for j in range(1, per):
                    gradient = gradient + grads[g * per + j, first + i].astype(jnp.float32)
                at = (own_core ^ g) * half + first + i
                one = 0.9 * m1_in[at] + 0.1 * gradient
                two = 0.999 * m2_in[at] + 0.001 * gradient * gradient
                m1_out[at] = one
                m2_out[at] = two
                spread = two * (1.0 / correct_two)
                updated = w_in[at].astype(jnp.float32) - one * (learn_rate / correct_one) / (
                    spread * lax.rsqrt(spread) + 1e-08
                )
                w_out[at] = updated.astype(jnp.bfloat16)
                return 0

            lax.fori_loop(0, part, step, 0)
            rows = pl.ds((own_core ^ g) * half + first, part)
            for i, (held, ref) in enumerate(
                ((w_out, new_w), (m1_out, new_m1), (m2_out, new_m2))
            ):
                outs.append(pltpu.make_async_copy(held.at[rows], ref.at[rows], sem_out.at[n, i]))
                outs[-1].start()
        for copy in outs:
            copy.wait()

    anywhere = pl.BlockSpec(memory_space=pl.ANY)
    return pl.pallas_call(
        body,
        out_shape=[
            jax.ShapeDtypeStruct(moment1.shape, jnp.bfloat16),
            jax.ShapeDtypeStruct(moment1.shape, jnp.float32),
            jax.ShapeDtypeStruct(moment1.shape, jnp.float32),
        ],
        in_specs=[smem()] + [anywhere] * (len(flat) + 3),
        out_specs=[anywhere] * 3,
        scratch_shapes=[pltpu.VMEM((len(flat), half, 2, piece, width), jnp.bfloat16)]
        + [pltpu.VMEM(moment1.shape, kind) for kind in (jnp.bfloat16, jnp.float32, jnp.float32)] * 2
        + [
            pltpu.SemaphoreType.DMA((2 * PARTS, 3 + per)),
            pltpu.SemaphoreType.DMA((2 * PARTS, 3)),
        ],
        compiler_params=params(),
        name="adam_step",
    )(pos, *arrays, weights, moment1, moment2)


def place_weights(pos, pieces, shape, before):
    flat = [(plane, one if isinstance(one, tuple) else (one,)) for plane, one in pieces]
    arrays = [one for _, group in flat for one in group]
    number, _, _, width = arrays[0].shape
    n_dp = shape[3] // width
    part = number // PARTS

    def body(pos_ref, *refs):
        ins = refs[: len(arrays)]
        out_ref, held, sems, sem_out = refs[-4:]
        dp_at = pos_ref[0]
        inner = (dp_at > 0) & (dp_at < n_dp - 1)

        def into(act, i):
            rows = pl.ds(i * part, part)
            at = 0
            for n, (_, group) in enumerate(flat):
                made = [
                    pltpu.make_async_copy(ins[at + k].at[rows], held.at[n, rows], sems.at[i, n])
                    for k in range(len(group))
                ]
                at += len(group)
                if len(made) == 1:
                    act(made[0])
                else:
                    pl.when(inner)(lambda made=made: act(made[0]))
                    pl.when(~inner)(lambda made=made: act(made[1]))

        for i in range(PARTS):
            into(lambda copy: copy.start(), i)
        outs = []
        for i in range(PARTS):
            into(lambda copy: copy.wait(), i)
            rows = pl.ds(i * part, part)
            for n, (plane, _) in enumerate(flat):
                columns = pl.ds(pl.multiple_of((dp_at ^ plane) * width, 128), width)
                outs.append(
                    pltpu.make_async_copy(
                        held.at[n, rows], out_ref.at[rows, :, :, columns], sem_out.at[i, n]
                    )
                )
                outs[-1].start()
        for copy in outs:
            copy.wait()

    anywhere = pl.BlockSpec(memory_space=pl.ANY)
    held = (len(flat),) + arrays[0].shape
    return pl.pallas_call(
        body,
        out_shape=jax.ShapeDtypeStruct(shape, jnp.bfloat16),
        in_specs=[smem()] + [anywhere] * (len(arrays) + len(before)),
        out_specs=anywhere,
        scratch_shapes=[
            pltpu.VMEM(held, jnp.bfloat16),
            pltpu.SemaphoreType.DMA((PARTS, len(flat))),
            pltpu.SemaphoreType.DMA((PARTS, len(flat))),
        ],
        input_output_aliases={1 + len(arrays): 0} if before else {},
        compiler_params=params(),
        name="place_weights",
    )(pos, *arrays, *before)


def between_planes(value, dp_at, n_dp, first=(), second=()):
    if n_dp != 4:
        whole = lax.all_gather(value, "dp", axis=0)
        return [
            lax.dynamic_index_in_dim(whole, dp_at ^ j, 0, keepdims=False) for j in range(n_dp)
        ]
    two = lax.ppermute(value, "dp", [(0, 2), (1, 3), (2, 0), (3, 1)])
    one = lax.ppermute(after(value, *first), "dp", [(0, 1), (1, 0), (2, 3), (3, 2)])
    outer = lax.ppermute(after(two, one, *second), "dp", [(2, 3), (1, 0)])
    middle = lax.ppermute(after(value, two, one, *second), "dp", [(1, 2), (2, 1)])
    return [value, one, two, (middle, outer)]


def gather_weights(pos, fresh, dp_at, n_dp):
    shape = fresh.shape[:3] + (n_dp * fresh.shape[3],)
    pieces = list(enumerate(between_planes(fresh, dp_at, n_dp)))
    most = place_weights(pos, pieces[:-1], shape, [])
    return place_weights(pos, pieces[-1:], shape, [most])


def after(value, *others):
    return lax.optimization_barrier((value,) + others)[0]


def finish_predicted(perm, parts):
    def body(perm_ref, *refs):
        total = refs[0][...].astype(jnp.float32)
        for ref in refs[1:-1]:
            total = total + ref[...].astype(jnp.float32)
        refs[-1][...] = lax.dot_general(
            perm_ref[...],
            total.astype(jnp.bfloat16),
            (((0,), (0,)), ((), ())),
            preferred_element_type=jnp.float32,
        ).astype(jnp.bfloat16)

    return pl.pallas_call(
        body,
        out_shape=jax.ShapeDtypeStruct(parts[0].shape, jnp.bfloat16),
        in_specs=[vmem()] * (1 + len(parts)),
        out_specs=vmem(),
        compiler_params=params(),
        name="finish_predicted",
    )(perm, *parts)


def shards(signals, cotangent, row_insertion, touched, slot_map, weights, moment1, moment2):
    n_own = lax.axis_size("own")
    n_dp = lax.axis_size("dp")
    dp_at = lax.axis_index("dp")
    own_at = lax.axis_index("own")
    number, _, piece, _ = weights.shape
    width = moment1.shape[3]
    half = number // 2
    rows = signals.shape[0]
    pos = jnp.stack([dp_at, own_at]).astype(jnp.int32)

    def across(value, j):
        return lax.ppermute(value, "own", [(o, o ^ j) for o in range(n_own)])

    packed, perm = pack_rows(row_insertion.reshape(1, rows), signals, cotangent)
    if n_own == 8 and piece % 16 == 0:
        core = lax.rem(own_at, 2)
        columns = [
            lax.dynamic_slice(
                weights, (which * half, 0, 0, dp_at * width), (half, 2, piece, width)
            )
            for which in (core, 1 - core)
        ]
        chip = jnp.stack([columns[0], after(across(columns[1], 1), packed)])
        beside = [across(chip, 2), across(chip, 4)]
        diagonal = [across(beside[0][0], 4), across(beside[1][1], 2)]
        blocks = [(one, u) for one in [chip] + beside for u in range(2)]
        blocks += [(one, None) for one in diagonal]
        first, second, last = [chip], beside, diagonal
        sends = [(2, 6), (7,), (5,), (1,), (3,), (4,), (0,)]
    else:
        column = lax.dynamic_slice_in_dim(weights, dp_at * width, width, 3)
        outgoing = jnp.broadcast_to(
            column.reshape(1, 2, half, 2, piece, width), (n_own // 2, 2, half, 2, piece, width)
        ).reshape(n_own, half, 2, piece, width)
        blocks = lax.all_to_all(outgoing, "own", split_axis=0, concat_axis=0, tiled=True)
        blocks = blocks.transpose(1, 2, 0, 3, 4).reshape(half, 2, SITES, width)
        first, second, last = [], [], []
        sends = None
    *near, far = between_planes(packed, dp_at, n_dp, first, second)
    if isinstance(far, tuple):
        far = far[0] + far[1]
    near = jnp.stack(near)
    rows_in = (near, far, across(near, 1), across(after(far, *last), 1))

    pred_mine, pred_other, grads = local_grads(
        pos, touched, slot_map, rows_in, blocks, sends, piece, width
    )
    if sends:
        x_same, y_diagonal, y_cross, partner, x_cross, y_same, own = grads
        x_same = across(x_same, 2)
        y_diagonal = across(y_diagonal, 4)
        y_cross = across(y_cross, 5)
        partner = across(partner, 1)
        first = (x_same, y_diagonal, y_cross, partner)
        x_cross = across(after(x_cross[0] + y_diagonal[0], *first), 3)
        y_same = across(after(y_same[0] + x_same[1], *first), 4)
        terms = [[(own, 0), (x_same, 0), y_same], [(partner, 0), (y_cross, 0), x_cross]]
    else:
        arrived = lax.all_to_all(grads, "own", split_axis=0, concat_axis=0, tiled=True)
        arrived = [
            lax.dynamic_index_in_dim(arrived, own_at ^ j, 0, keepdims=False) for j in range(n_own)
        ]
        terms = [arrived[0::2], arrived[1::2]]

    pred_part = pred_mine + across(pred_other, 1)
    parts = [pred_part[0]] + [
        lax.ppermute(pred_part[j], "dp", [(d, d ^ j) for d in range(n_dp)]) for j in range(1, n_dp)
    ]
    predicted = finish_predicted(perm, parts)
    terms[0][-1] = after(terms[0][-1], *parts[1:])

    fresh, new_moment1, new_moment2 = adam(pos, terms, weights, moment1, moment2)
    new_weights = gather_weights(pos, fresh, dp_at, n_dp)

    return (predicted, new_weights, new_moment1, new_moment2)


def solution(mesh):
    in_specs = (
        P(("dp", "own"), None),
        P(("dp", "own"), None),
        P(("dp", "own")),
        P(),
        P(),
        P(None, None, "own", None),
        P(None, None, "own", "dp"),
        P(None, None, "own", "dp"),
    )
    out_specs = (
        P(("dp", "own"), None),
        P(None, None, "own", None),
        P(None, None, "own", "dp"),
        P(None, None, "own", "dp"),
    )
    return jax.shard_map(shards, mesh=mesh, in_specs=in_specs, out_specs=out_specs, check_vma=False)
```

```python
import math

import jax
import jax.numpy as jnp
from jax import lax
from jax.experimental import pallas as pl
from jax.experimental.pallas import tpu as pltpu
from jax.sharding import PartitionSpec as P

SITES = 384
CAP = 128
ID_ROWS = 16
PARTS = 4
VMEM_BYTES = 56 * 2**20
LAST_VMEM_BYTES = 8 * 2**20

gelu_coef = math.sqrt(2.0 / math.pi)
cubic_coef = 0.044715
learn_rate = 0.01


def gelu_parts(preact):
    tanh_input = gelu_coef * (preact + cubic_coef * preact * preact * preact)
    tangent = jnp.tanh(tanh_input)
    gelu_val = 0.5 * preact * (1.0 + tangent)
    slopes = 0.5 * (1.0 + tangent) + 0.5 * preact * (1.0 - tangent * tangent) * gelu_coef * (
        1.0 + 3.0 * cubic_coef * preact * preact
    )
    return (gelu_val, slopes)


def params(limit=VMEM_BYTES):
    return pltpu.CompilerParams(vmem_limit_bytes=limit)


def vmem():
    return pl.BlockSpec(memory_space=pltpu.VMEM)


def smem():
    return pl.BlockSpec(memory_space=pltpu.SMEM)


def pack_rows(ids, signals, cotangent):
    rows = signals.shape[0]

    def body(ids_ref, sig_ref, cot_ref, out_ref, perm_ref):
        ids_row = ids_ref[...].astype(jnp.float32)
        lane_ids = jnp.broadcast_to(ids_row, (rows, rows))
        same = lane_ids == lane_ids.T
        count = jnp.sum(same.astype(jnp.float32), axis=0, keepdims=True)
        full = jnp.max(jnp.where(count == CAP, ids_row, -1.0), axis=1, keepdims=True)
        chosen = ids_row == full
        from_row = lax.broadcasted_iota(jnp.int32, (rows, rows), 0)
        to_lane = lax.broadcasted_iota(jnp.int32, (rows, rows), 1)
        upto = (from_row <= to_lane).astype(jnp.bfloat16)
        ahead = jnp.dot(
            jnp.broadcast_to(chosen.astype(jnp.float32), (8, rows)).astype(jnp.bfloat16),
            upto,
            preferred_element_type=jnp.float32,
        )[:1].astype(jnp.int32)
        place = jnp.where(chosen, ahead - 1, CAP + to_lane[:1] - ahead)
        perm = (from_row == place).astype(jnp.float32).astype(jnp.bfloat16)
        perm_ref[...] = perm
        out_ref[:rows] = jnp.dot(perm, sig_ref[...], preferred_element_type=jnp.float32).astype(
            jnp.bfloat16
        )
        out_ref[rows : 2 * rows] = jnp.dot(
            perm, cot_ref[...], preferred_element_type=jnp.float32
        ).astype(jnp.bfloat16)
        sorted_ids = lax.dot_general(
            jnp.broadcast_to(ids_row, (ID_ROWS, rows)).astype(jnp.bfloat16),
            perm,
            (((1,), (1,)), ((), ())),
            preferred_element_type=jnp.float32,
        ).astype(jnp.bfloat16)
        out_ref[2 * rows :, :rows] = sorted_ids
        out_ref[2 * rows :, rows:] = jnp.zeros((ID_ROWS, SITES - rows), jnp.bfloat16)

    return pl.pallas_call(
        body,
        out_shape=(
            jax.ShapeDtypeStruct((2 * rows + ID_ROWS, SITES), jnp.bfloat16),
            jax.ShapeDtypeStruct((rows, rows), jnp.bfloat16),
        ),
        in_specs=[vmem(), vmem(), vmem()],
        out_specs=(vmem(), vmem()),
        compiler_params=params(),
        name="pack_rows",
    )(ids, signals, cotangent)


def local_grads(pos, touched, slot_map, rows_in, blocks, sends, piece, width):
    near = rows_in[0].shape[0]
    planes = near + 1
    rows = (rows_in[0].shape[1] - ID_ROWS) // 2
    touch = touched.shape[1]
    n_own = SITES // piece
    aligned = isinstance(blocks, list)
    arrays = []
    for array, _ in blocks if aligned else [(blocks, None)]:
        if not any(array is one for one in arrays):
            arrays.append(array)
    half = arrays[0].shape[-4]

    def body(pos_ref, touched_ref, slot_ref, *rest):
        row_refs = rest[:4]
        block_refs = rest[4 : 4 + len(arrays)]
        rest = rest[4 + len(arrays) :]
        pred_refs = rest[:2]
        n_out = len(grad_shapes)
        grad_refs = rest[2 : 2 + n_out]
        staged = rest[2 + n_out : 2 + 2 * n_out]
        acc, id_cols, held, sorted_rows, pred, full_of, tasks, sems, sem_out = rest[-9:]
        own_at = pos_ref[1]
        core = lax.rem(own_at, 2)

        row_copies = [
            pltpu.make_async_copy(
                ref, sorted_rows.at[pl.ds(at, near) if i % 2 == 0 else at], sems.at[i]
            )
            for i, (ref, at) in enumerate(zip(row_refs, (0, near, planes, planes + near)))
        ]
        if aligned:
            block_copies = []
            for j, (array, at) in enumerate(blocks):
                ref = [one for one, other in zip(block_refs, arrays) if other is array][0]
                sites = pl.ds(pl.multiple_of((own_at ^ j) * piece, 16), piece)
                block_copies.append(
                    pltpu.make_async_copy(
                        ref if at is None else ref.at[at], held.at[:, :, sites, :], sems.at[4 + j]
                    )
                )
        else:
            block_copies = [pltpu.make_async_copy(block_refs[0], held, sems.at[4])]
        for copy in row_copies + block_copies:
            copy.start()

        def clear(e, _):
            acc[e] = jnp.zeros(acc.shape[1:], jnp.float32)
            return 0

        lax.fori_loop(0, half, clear, 0)
        pred[...] = jnp.zeros_like(pred)
        for copy in row_copies:
            copy.wait()
        for source in range(2 * planes):
            ids_row = sorted_rows[source, 2 * rows :, :rows][:1].astype(jnp.float32)
            id_cols[source] = jnp.broadcast_to(ids_row, (128, rows)).T
            full_of[source] = jnp.max(ids_row[:, :128]).astype(jnp.int32)

        def listing(t, count):
            source = t // (touch + 1)
            j = t - source * (touch + 1)
            which = source // planes
            device = (pos_ref[0] ^ (source - which * planes)) * n_own + (own_at ^ which)
            full = full_of[source]
            insertion = jnp.where(j == 0, full, touched_ref[device, jnp.maximum(j - 1, 0)])
            e = slot_ref[insertion] - core * half
            here = (e >= 0) & (e < half) & ((j == 0) | (insertion != full))
            tasks[0, count] = source
            tasks[1, count] = jnp.where(j == 0, 0, CAP)
            tasks[2, count] = insertion
            tasks[3, count] = e
            return count + here.astype(jnp.int32)

        count = lax.fori_loop(0, 2 * planes * (touch + 1), listing, 0)
        tasks[0, count] = 0
        tasks[1, count] = 0
        tasks[2, count] = -1
        tasks[3, count] = 0
        for copy in block_copies:
            copy.wait()

        def pair(i, _):
            loaded = []
            for u in range(2):
                source, insertion, e = tasks[0, 2 * i + u], tasks[2, 2 * i + u], tasks[3, 2 * i + u]
                first = pl.multiple_of(tasks[1, 2 * i + u], CAP)
                keep = (
                    (id_cols[source, pl.ds(first, CAP), :] == insertion.astype(jnp.float32))
                    .astype(jnp.float32)
                    .astype(jnp.bfloat16)
                )
                keep = jnp.concatenate([keep] * (SITES // 128), axis=1)
                sig = sorted_rows[source, pl.ds(first, CAP), :] * keep
                cot = sorted_rows[source, pl.ds(rows + first, CAP), :] * keep
                loaded.append((source, first, e, sig, cot))
            found = []
            for source, first, e, sig, cot in loaded:
                read_out = held[e, 1]
                preact = jnp.dot(sig, held[e, 0], preferred_element_type=jnp.float32)
                back_hidden = jnp.dot(cot, read_out, preferred_element_type=jnp.float32)
                gelu_val, slopes = gelu_parts(preact)
                hidden = gelu_val.astype(jnp.bfloat16)
                back_pre = (back_hidden * slopes).astype(jnp.bfloat16)
                part = lax.dot_general(
                    hidden, read_out, (((1,), (1,)), ((), ())), preferred_element_type=jnp.float32
                ).astype(jnp.bfloat16)
                grad_in = lax.dot_general(
                    sig, back_pre, (((0,), (0,)), ((), ())), preferred_element_type=jnp.float32
                )
                grad_out = lax.dot_general(
                    cot, hidden, (((0,), (0,)), ((), ())), preferred_element_type=jnp.float32
                )
                found.append((part, grad_in, grad_out))
            for (source, first, e, _, _), (part, grad_in, grad_out) in zip(loaded, found):
                pred[source, pl.ds(first, CAP), :] += part
                acc[e, 0] += grad_in
                acc[e, 1] += grad_out
            return 0

        lax.fori_loop(0, (count + 1) // 2, pair, 0)
        outs = [
            pltpu.make_async_copy(
                pred.at[which * planes + i], pred_refs[which].at[pos_ref[0] ^ i], sem_out.at[which, i]
            )
            for which in (1, 0)
            for i in range(planes)
        ]
        for copy in outs:
            copy.start()
        for n, (ref, into) in enumerate(zip(grad_refs, staged)):

            def write(e, _, into=into, n=n):
                if aligned:
                    for i, j in enumerate(sends[n]):
                        first = pl.multiple_of((own_at ^ j) * piece, 16)
                        into[i, e] = acc[e, :, pl.ds(first, piece), :].astype(jnp.bfloat16)
                else:
                    into[e] = acc[e].astype(jnp.bfloat16)
                return 0

            lax.fori_loop(0, half, write, 0)
            outs.append(pltpu.make_async_copy(into, ref, sem_out.at[2 + n, 0]))
            outs[-1].start()
        for copy in outs:
            copy.wait()

    pred_shape = jax.ShapeDtypeStruct((planes, rows, SITES), jnp.bfloat16)
    grad_shapes = [
        jax.ShapeDtypeStruct(shape, jnp.bfloat16)
        for shape in (
            [(len(group), half, 2, piece, width) for group in sends]
            if aligned
            else [(half, 2, SITES, width)]
        )
    ]
    most = 2 * planes * (touch + 1)
    acc_shape = (half, 2, SITES, width)
    id_shape = (2 * planes, rows, 128)
    row_shape = (2 * planes,) + rows_in[0].shape[1:]
    pred_all = (2 * planes, rows, SITES)
    scratch = [pltpu.VMEM(one.shape, jnp.bfloat16) for one in grad_shapes] + [
        pltpu.VMEM(acc_shape, jnp.float32),
        pltpu.VMEM(id_shape, jnp.float32),
        pltpu.VMEM(acc_shape, jnp.bfloat16),
        pltpu.VMEM(row_shape, jnp.bfloat16),
        pltpu.VMEM(pred_all, jnp.bfloat16),
        pltpu.SMEM((2 * planes,), jnp.int32),
        pltpu.SMEM((4, most + 1), jnp.int32),
        pltpu.SemaphoreType.DMA((4 + n_own,)),
        pltpu.SemaphoreType.DMA((2 + len(grad_shapes), planes)),
    ]
    found = pl.pallas_call(
        body,
        out_shape=[pred_shape, pred_shape] + grad_shapes,
        in_specs=[smem(), smem(), smem()] + [pl.BlockSpec(memory_space=pl.ANY)] * (4 + len(arrays)),
        out_specs=[pl.BlockSpec(memory_space=pl.ANY)] * (2 + len(grad_shapes)),
        scratch_shapes=scratch,
        compiler_params=params(),
        name="local_grads",
    )(pos, touched, slot_map, *rows_in, *arrays)
    grads = list(found[2:])
    if not aligned:
        grads = grads[0].reshape(half, 2, n_own, piece, width).transpose(2, 0, 1, 3, 4)
    return found[0], found[1], grads


def adam(pos, terms, weights, moment1, moment2):
    number, _, piece, width = moment1.shape
    half = number // 2
    flat = [one if isinstance(one, tuple) else (one, None) for group in terms for one in group]
    arrays = [array for array, _ in flat]
    per = len(terms[0])
    correct_one = 1.0 - 0.9**10
    correct_two = 1.0 - 0.999**10

    def body(pos_ref, *refs):
        term_refs = [
            ref if at is None else ref.at[at] for ref, (_, at) in zip(refs, flat)
        ]
        w_ref, m1_ref, m2_ref = refs[len(flat) : len(flat) + 3]
        refs = refs[len(flat) + 3 :]
        new_w, new_m1, new_m2, grads, w_in, m1_in, m2_in, w_out, m1_out, m2_out = refs[:10]
        sem_in, sem_out = refs[10:]
        columns = pl.ds(pl.multiple_of(pos_ref[0] * width, 128), width)
        part = half // PARTS
        steps = [(g, i * part) for g in range(2) for i in range(PARTS)]
        own_core = lax.rem(pos_ref[1], 2)
        copies = []
        for n, (g, first) in enumerate(steps):
            rows = pl.ds((own_core ^ g) * half + first, part)
            copies.append(
                [
                    pltpu.make_async_copy(ref, into.at[rows], sem_in.at[n, i])
                    for i, (ref, into) in enumerate(
                        (
                            (w_ref.at[rows, :, :, columns], w_in),
                            (m1_ref.at[rows], m1_in),
                            (m2_ref.at[rows], m2_in),
                        )
                    )
                ]
                + [
                    pltpu.make_async_copy(
                        term_refs[g * per + i].at[pl.ds(first, part)],
                        grads.at[g * per + i, pl.ds(first, part)],
                        sem_in.at[n, 3 + i],
                    )
                    for i in range(per)
                ]
            )
            for copy in copies[n]:
                copy.start()
        outs = []
        for n, (g, first) in enumerate(steps):
            for copy in copies[n]:
                copy.wait()

            def step(i, _, g=g, first=first):
                gradient = grads[g * per, first + i].astype(jnp.float32)
                for j in range(1, per):
                    gradient = gradient + grads[g * per + j, first + i].astype(jnp.float32)
                at = (own_core ^ g) * half + first + i
                one = 0.9 * m1_in[at] + 0.1 * gradient
                two = 0.999 * m2_in[at] + 0.001 * gradient * gradient
                m1_out[at] = one
                m2_out[at] = two
                spread = two * (1.0 / correct_two)
                updated = w_in[at].astype(jnp.float32) - one * (learn_rate / correct_one) / (
                    spread * lax.rsqrt(spread) + 1e-08
                )
                w_out[at] = updated.astype(jnp.bfloat16)
                return 0

            lax.fori_loop(0, part, step, 0)
            rows = pl.ds((own_core ^ g) * half + first, part)
            for i, (held, ref) in enumerate(
                ((w_out, new_w), (m1_out, new_m1), (m2_out, new_m2))
            ):
                outs.append(pltpu.make_async_copy(held.at[rows], ref.at[rows], sem_out.at[n, i]))
                outs[-1].start()
        for copy in outs:
            copy.wait()

    anywhere = pl.BlockSpec(memory_space=pl.ANY)
    return pl.pallas_call(
        body,
        out_shape=[
            jax.ShapeDtypeStruct(moment1.shape, jnp.bfloat16),
            jax.ShapeDtypeStruct(moment1.shape, jnp.float32),
            jax.ShapeDtypeStruct(moment1.shape, jnp.float32),
        ],
        in_specs=[smem()] + [anywhere] * (len(flat) + 3),
        out_specs=[anywhere] * 3,
        scratch_shapes=[pltpu.VMEM((len(flat), half, 2, piece, width), jnp.bfloat16)]
        + [pltpu.VMEM(moment1.shape, kind) for kind in (jnp.bfloat16, jnp.float32, jnp.float32)] * 2
        + [
            pltpu.SemaphoreType.DMA((2 * PARTS, 3 + per)),
            pltpu.SemaphoreType.DMA((2 * PARTS, 3)),
        ],
        compiler_params=params(),
        name="adam_step",
    )(pos, *arrays, weights, moment1, moment2)


def place_weights(pos, pieces, shape, before):
    flat = [(plane, one if isinstance(one, tuple) else (one,)) for plane, one in pieces]
    arrays = [one for _, group in flat for one in group]
    number, _, _, width = arrays[0].shape
    n_dp = shape[3] // width
    part = number // PARTS

    def body(pos_ref, *refs):
        ins = refs[: len(arrays)]
        out_ref, held, sems, sem_out = refs[-4:]
        dp_at = pos_ref[0]
        inner = (dp_at > 0) & (dp_at < n_dp - 1)

        def into(act, i):
            rows = pl.ds(i * part, part)
            at = 0
            for n, (_, group) in enumerate(flat):
                made = [
                    pltpu.make_async_copy(ins[at + k].at[rows], held.at[n, rows], sems.at[i, n])
                    for k in range(len(group))
                ]
                at += len(group)
                if len(made) == 1:
                    act(made[0])
                else:
                    pl.when(inner)(lambda made=made: act(made[0]))
                    pl.when(~inner)(lambda made=made: act(made[1]))

        for i in range(PARTS):
            into(lambda copy: copy.start(), i)
        outs = []
        for i in range(PARTS):
            into(lambda copy: copy.wait(), i)
            rows = pl.ds(i * part, part)
            for n, (plane, _) in enumerate(flat):
                columns = pl.ds(pl.multiple_of((dp_at ^ plane) * width, 128), width)
                outs.append(
                    pltpu.make_async_copy(
                        held.at[n, rows], out_ref.at[rows, :, :, columns], sem_out.at[i, n]
                    )
                )
                outs[-1].start()
        for copy in outs:
            copy.wait()

    anywhere = pl.BlockSpec(memory_space=pl.ANY)
    held = (len(flat),) + arrays[0].shape
    return pl.pallas_call(
        body,
        out_shape=jax.ShapeDtypeStruct(shape, jnp.bfloat16),
        in_specs=[smem()] + [anywhere] * (len(arrays) + len(before)),
        out_specs=anywhere,
        scratch_shapes=[
            pltpu.VMEM(held, jnp.bfloat16),
            pltpu.SemaphoreType.DMA((PARTS, len(flat))),
            pltpu.SemaphoreType.DMA((PARTS, len(flat))),
        ],
        input_output_aliases={1 + len(arrays): 0} if before else {},
        compiler_params=params(LAST_VMEM_BYTES if before else VMEM_BYTES),
        name="place_weights",
    )(pos, *arrays, *before)


def between_planes(value, dp_at, n_dp, first=(), second=()):
    if n_dp != 4:
        whole = lax.all_gather(value, "dp", axis=0)
        return [
            lax.dynamic_index_in_dim(whole, dp_at ^ j, 0, keepdims=False) for j in range(n_dp)
        ]
    two = lax.ppermute(value, "dp", [(0, 2), (1, 3), (2, 0), (3, 1)])
    one = lax.ppermute(after(value, *first), "dp", [(0, 1), (1, 0), (2, 3), (3, 2)])
    outer = lax.ppermute(after(two, one, *second), "dp", [(2, 3), (1, 0)])
    middle = lax.ppermute(after(value, two, one, *second), "dp", [(1, 2), (2, 1)])
    return [value, one, two, (middle, outer)]


def gather_weights(pos, fresh, dp_at, n_dp):
    shape = fresh.shape[:3] + (n_dp * fresh.shape[3],)
    pieces = list(enumerate(between_planes(fresh, dp_at, n_dp)))
    most = place_weights(pos, pieces[:-1], shape, [])
    return place_weights(pos, pieces[-1:], shape, [most])


def after(value, *others):
    return lax.optimization_barrier((value,) + others)[0]


def finish_predicted(perm, parts):
    def body(perm_ref, parts_ref, out_ref):
        total = jnp.sum(parts_ref[...].astype(jnp.float32), axis=0)
        out_ref[...] = lax.dot_general(
            perm_ref[...],
            total.astype(jnp.bfloat16),
            (((0,), (0,)), ((), ())),
            preferred_element_type=jnp.float32,
        ).astype(jnp.bfloat16)

    return pl.pallas_call(
        body,
        out_shape=jax.ShapeDtypeStruct(parts.shape[1:], jnp.bfloat16),
        in_specs=[vmem(), vmem()],
        out_specs=vmem(),
        compiler_params=params(),
        name="finish_predicted",
    )(perm, parts)


def shards(signals, cotangent, row_insertion, touched, slot_map, weights, moment1, moment2):
    n_own = lax.axis_size("own")
    n_dp = lax.axis_size("dp")
    dp_at = lax.axis_index("dp")
    own_at = lax.axis_index("own")
    number, _, piece, _ = weights.shape
    width = moment1.shape[3]
    half = number // 2
    rows = signals.shape[0]
    pos = jnp.stack([dp_at, own_at]).astype(jnp.int32)

    def across(value, j):
        return lax.ppermute(value, "own", [(o, o ^ j) for o in range(n_own)])

    packed, perm = pack_rows(row_insertion.reshape(1, rows), signals, cotangent)
    if n_own == 8 and piece % 16 == 0:
        core = lax.rem(own_at, 2)
        columns = [
            lax.dynamic_slice(
                weights, (which * half, 0, 0, dp_at * width), (half, 2, piece, width)
            )
            for which in (core, 1 - core)
        ]
        chip = jnp.stack([columns[0], after(across(columns[1], 1), packed)])
        beside = [across(chip, 2), across(chip, 4)]
        diagonal = [across(beside[0][0], 4), across(beside[1][1], 2)]
        blocks = [(one, u) for one in [chip] + beside for u in range(2)]
        blocks += [(one, None) for one in diagonal]
        first, second, last = [chip], beside, diagonal
        sends = [(2, 6), (7,), (5,), (1,), (3,), (4,), (0,)]
    else:
        column = lax.dynamic_slice_in_dim(weights, dp_at * width, width, 3)
        outgoing = jnp.broadcast_to(
            column.reshape(1, 2, half, 2, piece, width), (n_own // 2, 2, half, 2, piece, width)
        ).reshape(n_own, half, 2, piece, width)
        blocks = lax.all_to_all(outgoing, "own", split_axis=0, concat_axis=0, tiled=True)
        blocks = blocks.transpose(1, 2, 0, 3, 4).reshape(half, 2, SITES, width)
        first, second, last = [], [], []
        sends = None
    *near, far = between_planes(packed, dp_at, n_dp, first, second)
    if isinstance(far, tuple):
        far = far[0] + far[1]
    near = jnp.stack(near)
    rows_in = (near, far, across(near, 1), across(after(far, *last), 1))

    pred_mine, pred_other, grads = local_grads(
        pos, touched, slot_map, rows_in, blocks, sends, piece, width
    )
    pred_part = pred_mine + across(pred_other, 1)
    parts = lax.all_to_all(pred_part, "dp", split_axis=0, concat_axis=0, tiled=True)
    if sends:
        x_same, y_diagonal, y_cross, partner, x_cross, y_same, own = grads
        x_same = across(x_same, 2)
        y_diagonal = across(y_diagonal, 4)
        y_cross = across(after(y_cross, pred_part), 5)
        partner = across(after(partner, pred_part), 1)
        first = (x_same, y_diagonal, y_cross, partner)
        x_cross = across(after(x_cross[0] + y_diagonal[0], *first), 3)
        y_same = across(after(y_same[0] + x_same[1], *first), 4)
        terms = [[(own, 0), (x_same, 0), y_same], [(partner, 0), (y_cross, 0), x_cross]]
    else:
        arrived = lax.all_to_all(grads, "own", split_axis=0, concat_axis=0, tiled=True)
        arrived = [
            lax.dynamic_index_in_dim(arrived, own_at ^ j, 0, keepdims=False) for j in range(n_own)
        ]
        terms = [arrived[0::2], arrived[1::2]]

    predicted = finish_predicted(perm, parts)
    terms[0][-1] = after(terms[0][-1], parts)

    fresh, new_moment1, new_moment2 = adam(pos, terms, weights, moment1, moment2)
    new_weights = gather_weights(pos, fresh, dp_at, n_dp)

    return (predicted, new_weights, new_moment1, new_moment2)


def solution(mesh):
    in_specs = (
        P(("dp", "own"), None),
        P(("dp", "own"), None),
        P(("dp", "own")),
        P(),
        P(),
        P(None, None, "own", None),
        P(None, None, "own", "dp"),
        P(None, None, "own", "dp"),
    )
    out_specs = (
        P(("dp", "own"), None),
        P(None, None, "own", None),
        P(None, None, "own", "dp"),
        P(None, None, "own", "dp"),
    )
    return jax.shard_map(shards, mesh=mesh, in_specs=in_specs, out_specs=out_specs, check_vma=False)
```

```python
import math

import jax
import jax.numpy as jnp
from jax import lax
from jax.experimental import pallas as pl
from jax.experimental.pallas import tpu as pltpu
from jax.sharding import PartitionSpec as P

SITES = 384
CAP = 128
ID_ROWS = 16
CHUNKS = 2
PARTS = 2
VMEM_BYTES = 56 * 2**20
LAST_VMEM_BYTES = 8 * 2**20

gelu_coef = math.sqrt(2.0 / math.pi)
cubic_coef = 0.044715
learn_rate = 0.01


def gelu_parts(preact):
    tanh_input = gelu_coef * (preact + cubic_coef * preact * preact * preact)
    tangent = jnp.tanh(tanh_input)
    gelu_val = 0.5 * preact * (1.0 + tangent)
    slopes = 0.5 * (1.0 + tangent) + 0.5 * preact * (1.0 - tangent * tangent) * gelu_coef * (
        1.0 + 3.0 * cubic_coef * preact * preact
    )
    return (gelu_val, slopes)


def params(limit=VMEM_BYTES):
    return pltpu.CompilerParams(vmem_limit_bytes=limit)


def vmem():
    return pl.BlockSpec(memory_space=pltpu.VMEM)


def smem():
    return pl.BlockSpec(memory_space=pltpu.SMEM)


def pack_rows(ids, signals, cotangent):
    rows = signals.shape[0]

    def body(ids_ref, sig_ref, cot_ref, out_ref, perm_ref):
        ids_row = ids_ref[...].astype(jnp.float32)
        lane_ids = jnp.broadcast_to(ids_row, (rows, rows))
        same = lane_ids == lane_ids.T
        count = jnp.sum(same.astype(jnp.float32), axis=0, keepdims=True)
        full = jnp.max(jnp.where(count == CAP, ids_row, -1.0), axis=1, keepdims=True)
        chosen = ids_row == full
        from_row = lax.broadcasted_iota(jnp.int32, (rows, rows), 0)
        to_lane = lax.broadcasted_iota(jnp.int32, (rows, rows), 1)
        upto = (from_row <= to_lane).astype(jnp.bfloat16)
        ahead = jnp.dot(
            jnp.broadcast_to(chosen.astype(jnp.float32), (8, rows)).astype(jnp.bfloat16),
            upto,
            preferred_element_type=jnp.float32,
        )[:1].astype(jnp.int32)
        place = jnp.where(chosen, ahead - 1, CAP + to_lane[:1] - ahead)
        perm = (from_row == place).astype(jnp.float32).astype(jnp.bfloat16)
        perm_ref[...] = perm
        out_ref[:rows] = jnp.dot(perm, sig_ref[...], preferred_element_type=jnp.float32).astype(
            jnp.bfloat16
        )
        out_ref[rows : 2 * rows] = jnp.dot(
            perm, cot_ref[...], preferred_element_type=jnp.float32
        ).astype(jnp.bfloat16)
        sorted_ids = lax.dot_general(
            jnp.broadcast_to(ids_row, (ID_ROWS, rows)).astype(jnp.bfloat16),
            perm,
            (((1,), (1,)), ((), ())),
            preferred_element_type=jnp.float32,
        ).astype(jnp.bfloat16)
        out_ref[2 * rows :, :rows] = sorted_ids
        out_ref[2 * rows :, rows:] = jnp.zeros((ID_ROWS, SITES - rows), jnp.bfloat16)

    return pl.pallas_call(
        body,
        out_shape=(
            jax.ShapeDtypeStruct((2 * rows + ID_ROWS, SITES), jnp.bfloat16),
            jax.ShapeDtypeStruct((rows, rows), jnp.bfloat16),
        ),
        in_specs=[vmem(), vmem(), vmem()],
        out_specs=(vmem(), vmem()),
        compiler_params=params(),
        name="pack_rows",
    )(ids, signals, cotangent)


def local_grads(pos, touched, slot_map, rows_in, blocks, sends, piece, width):
    near = rows_in[0].shape[0]
    planes = near + 1
    rows = (rows_in[0].shape[1] - ID_ROWS) // 2
    touch = touched.shape[1]
    n_own = SITES // piece
    aligned = isinstance(blocks, list)
    arrays = []
    for array, _ in blocks if aligned else [(blocks, None)]:
        if not any(array is one for one in arrays):
            arrays.append(array)
    half = arrays[0].shape[-4]

    def body(pos_ref, touched_ref, slot_ref, *rest):
        row_refs = rest[:4]
        block_refs = rest[4 : 4 + len(arrays)]
        rest = rest[4 + len(arrays) :]
        pred_refs = rest[:2]
        n_out = len(grad_shapes)
        grad_refs = rest[2 : 2 + n_out]
        staged = rest[2 + n_out : 2 + 2 * n_out]
        acc, id_cols, held, sorted_rows, pred, full_of, tasks, sems, sem_out = rest[-9:]
        own_at = pos_ref[1]
        core = lax.rem(own_at, 2)

        row_copies = [
            pltpu.make_async_copy(
                ref, sorted_rows.at[pl.ds(at, near) if i % 2 == 0 else at], sems.at[i]
            )
            for i, (ref, at) in enumerate(zip(row_refs, (0, near, planes, planes + near)))
        ]
        if aligned:
            block_copies = []
            for j, (array, at) in enumerate(blocks):
                ref = [one for one, other in zip(block_refs, arrays) if other is array][0]
                sites = pl.ds(pl.multiple_of((own_at ^ j) * piece, 16), piece)
                block_copies.append(
                    pltpu.make_async_copy(
                        ref if at is None else ref.at[at], held.at[:, :, sites, :], sems.at[4 + j]
                    )
                )
        else:
            block_copies = [pltpu.make_async_copy(block_refs[0], held, sems.at[4])]
        for copy in row_copies + block_copies:
            copy.start()

        def clear(e, _):
            acc[e] = jnp.zeros(acc.shape[1:], jnp.float32)
            return 0

        lax.fori_loop(0, half, clear, 0)
        pred[...] = jnp.zeros_like(pred)
        for copy in row_copies:
            copy.wait()
        for source in range(2 * planes):
            ids_row = sorted_rows[source, 2 * rows :, :rows][:1].astype(jnp.float32)
            id_cols[source] = jnp.broadcast_to(ids_row, (128, rows)).T
            full_of[source] = jnp.max(ids_row[:, :128]).astype(jnp.int32)

        def listing(t, count):
            source = t // (touch + 1)
            j = t - source * (touch + 1)
            which = source // planes
            device = (pos_ref[0] ^ (source - which * planes)) * n_own + (own_at ^ which)
            full = full_of[source]
            insertion = jnp.where(j == 0, full, touched_ref[device, jnp.maximum(j - 1, 0)])
            e = slot_ref[insertion] - core * half
            here = (e >= 0) & (e < half) & ((j == 0) | (insertion != full))
            tasks[0, count] = source
            tasks[1, count] = jnp.where(j == 0, 0, CAP)
            tasks[2, count] = insertion
            tasks[3, count] = e
            return count + here.astype(jnp.int32)

        count = lax.fori_loop(0, 2 * planes * (touch + 1), listing, 0)
        tasks[0, count] = 0
        tasks[1, count] = 0
        tasks[2, count] = -1
        tasks[3, count] = 0
        for copy in block_copies:
            copy.wait()

        def pair(i, _):
            loaded = []
            for u in range(2):
                source, insertion, e = tasks[0, 2 * i + u], tasks[2, 2 * i + u], tasks[3, 2 * i + u]
                first = pl.multiple_of(tasks[1, 2 * i + u], CAP)
                keep = (
                    (id_cols[source, pl.ds(first, CAP), :] == insertion.astype(jnp.float32))
                    .astype(jnp.float32)
                    .astype(jnp.bfloat16)
                )
                keep = jnp.concatenate([keep] * (SITES // 128), axis=1)
                sig = sorted_rows[source, pl.ds(first, CAP), :] * keep
                cot = sorted_rows[source, pl.ds(rows + first, CAP), :] * keep
                loaded.append((source, first, e, sig, cot))
            found = []
            for source, first, e, sig, cot in loaded:
                read_out = held[e, 1]
                preact = jnp.dot(sig, held[e, 0], preferred_element_type=jnp.float32)
                back_hidden = jnp.dot(cot, read_out, preferred_element_type=jnp.float32)
                gelu_val, slopes = gelu_parts(preact)
                hidden = gelu_val.astype(jnp.bfloat16)
                back_pre = (back_hidden * slopes).astype(jnp.bfloat16)
                part = lax.dot_general(
                    hidden, read_out, (((1,), (1,)), ((), ())), preferred_element_type=jnp.float32
                ).astype(jnp.bfloat16)
                grad_in = lax.dot_general(
                    sig, back_pre, (((0,), (0,)), ((), ())), preferred_element_type=jnp.float32
                )
                grad_out = lax.dot_general(
                    cot, hidden, (((0,), (0,)), ((), ())), preferred_element_type=jnp.float32
                )
                found.append((part, grad_in, grad_out))
            for (source, first, e, _, _), (part, grad_in, grad_out) in zip(loaded, found):
                pred[source, pl.ds(first, CAP), :] += part
                acc[e, 0] += grad_in
                acc[e, 1] += grad_out
            return 0

        lax.fori_loop(0, (count + 1) // 2, pair, 0)
        outs = [
            pltpu.make_async_copy(
                pred.at[which * planes + i], pred_refs[which].at[pos_ref[0] ^ i], sem_out.at[which, i]
            )
            for which in (1, 0)
            for i in range(planes)
        ]
        for copy in outs:
            copy.start()
        for n, (ref, into) in enumerate(zip(grad_refs, staged)):

            def write(e, _, into=into, n=n):
                if aligned:
                    for i, j in enumerate(sends[n]):
                        first = pl.multiple_of((own_at ^ j) * piece, 16)
                        into[i, e] = acc[e, :, pl.ds(first, piece), :].astype(jnp.bfloat16)
                else:
                    into[e] = acc[e].astype(jnp.bfloat16)
                return 0

            lax.fori_loop(0, half, write, 0)
            outs.append(pltpu.make_async_copy(into, ref, sem_out.at[2 + n, 0]))
            outs[-1].start()
        for copy in outs:
            copy.wait()

    pred_shape = jax.ShapeDtypeStruct((planes, rows, SITES), jnp.bfloat16)
    grad_shapes = [
        jax.ShapeDtypeStruct(shape, jnp.bfloat16)
        for shape in (
            [(len(group), half, 2, piece, width) for group in sends]
            if aligned
            else [(half, 2, SITES, width)]
        )
    ]
    most = 2 * planes * (touch + 1)
    acc_shape = (half, 2, SITES, width)
    id_shape = (2 * planes, rows, 128)
    row_shape = (2 * planes,) + rows_in[0].shape[1:]
    pred_all = (2 * planes, rows, SITES)
    scratch = [pltpu.VMEM(one.shape, jnp.bfloat16) for one in grad_shapes] + [
        pltpu.VMEM(acc_shape, jnp.float32),
        pltpu.VMEM(id_shape, jnp.float32),
        pltpu.VMEM(acc_shape, jnp.bfloat16),
        pltpu.VMEM(row_shape, jnp.bfloat16),
        pltpu.VMEM(pred_all, jnp.bfloat16),
        pltpu.SMEM((2 * planes,), jnp.int32),
        pltpu.SMEM((4, most + 1), jnp.int32),
        pltpu.SemaphoreType.DMA((4 + n_own,)),
        pltpu.SemaphoreType.DMA((2 + len(grad_shapes), planes)),
    ]
    found = pl.pallas_call(
        body,
        out_shape=[pred_shape, pred_shape] + grad_shapes,
        in_specs=[smem(), smem(), smem()] + [pl.BlockSpec(memory_space=pl.ANY)] * (4 + len(arrays)),
        out_specs=[pl.BlockSpec(memory_space=pl.ANY)] * (2 + len(grad_shapes)),
        scratch_shapes=scratch,
        compiler_params=params(),
        name="local_grads",
    )(pos, touched, slot_map, *rows_in, *arrays)
    grads = list(found[2:])
    if not aligned:
        grads = grads[0].reshape(half, 2, n_own, piece, width).transpose(2, 0, 1, 3, 4)
    return found[0], found[1], grads


def adam(pos, terms, weights, moment1, moment2, chunk, before):
    number, _, piece, width = moment1.shape
    half = number // 2
    flat = [one if isinstance(one, tuple) else (one, None) for group in terms for one in group]
    arrays = [array for array, _ in flat]
    per = len(terms[0])
    size = half // CHUNKS
    held = (2, size, 2, piece, width)
    correct_one = 1.0 - 0.9**10
    correct_two = 1.0 - 0.999**10

    def body(pos_ref, *refs):
        term_refs = [
            ref if at is None else ref.at[at] for ref, (_, at) in zip(refs, flat)
        ]
        w_ref, m1_ref, m2_ref = refs[len(flat) : len(flat) + 3]
        refs = refs[len(flat) + 3 + len(before) :]
        new_w, new_m1, new_m2, grads, w_in, m1_in, m2_in, w_out, m1_out, m2_out = refs[:10]
        sem_in, sem_out = refs[10:]
        columns = pl.ds(pl.multiple_of(pos_ref[0] * width, 128), width)
        part = size // PARTS
        steps = [(g, i * part) for g in range(2) for i in range(PARTS)]
        own_core = lax.rem(pos_ref[1], 2)
        copies = []
        for n, (g, first) in enumerate(steps):
            rows = pl.ds((own_core ^ g) * half + chunk * size + first, part)
            local = pl.ds(first, part)
            copies.append(
                [
                    pltpu.make_async_copy(ref, into.at[g, local], sem_in.at[n, i])
                    for i, (ref, into) in enumerate(
                        (
                            (w_ref.at[rows, :, :, columns], w_in),
                            (m1_ref.at[rows], m1_in),
                            (m2_ref.at[rows], m2_in),
                        )
                    )
                ]
                + [
                    pltpu.make_async_copy(
                        term_refs[g * per + i].at[pl.ds(chunk * size + first, part)],
                        grads.at[g * per + i, local],
                        sem_in.at[n, 3 + i],
                    )
                    for i in range(per)
                ]
            )
            for copy in copies[n]:
                copy.start()
        outs = []
        for n, (g, first) in enumerate(steps):
            for copy in copies[n]:
                copy.wait()

            def step(i, _, g=g, first=first):
                at = first + i
                gradient = grads[g * per, at].astype(jnp.float32)
                for j in range(1, per):
                    gradient = gradient + grads[g * per + j, at].astype(jnp.float32)
                one = 0.9 * m1_in[g, at] + 0.1 * gradient
                two = 0.999 * m2_in[g, at] + 0.001 * gradient * gradient
                m1_out[g, at] = one
                m2_out[g, at] = two
                spread = two * (1.0 / correct_two)
                updated = w_in[g, at].astype(jnp.float32) - one * (learn_rate / correct_one) / (
                    spread * lax.rsqrt(spread) + 1e-08
                )
                w_out[g, at] = updated.astype(jnp.bfloat16)
                return 0

            lax.fori_loop(0, part, step, 0)
            half_at = own_core ^ g
            local = pl.ds(first, part)
            rows = pl.ds(half_at * half + chunk * size + first, part)
            for i, (source, ref) in enumerate(
                (
                    (w_out, new_w.at[pl.ds(half_at * size + first, part)]),
                    (m1_out, new_m1.at[rows]),
                    (m2_out, new_m2.at[rows]),
                )
            ):
                outs.append(pltpu.make_async_copy(source.at[g, local], ref, sem_out.at[n, i]))
                outs[-1].start()
        for copy in outs:
            copy.wait()

    anywhere = pl.BlockSpec(memory_space=pl.ANY)
    return pl.pallas_call(
        body,
        out_shape=[
            jax.ShapeDtypeStruct((2 * size, 2, piece, width), jnp.bfloat16),
            jax.ShapeDtypeStruct(moment1.shape, jnp.float32),
            jax.ShapeDtypeStruct(moment1.shape, jnp.float32),
        ],
        in_specs=[smem()] + [anywhere] * (len(flat) + 3 + len(before)),
        out_specs=[anywhere] * 3,
        scratch_shapes=[pltpu.VMEM((len(flat), size, 2, piece, width), jnp.bfloat16)]
        + [pltpu.VMEM(held, kind) for kind in (jnp.bfloat16, jnp.float32, jnp.float32)] * 2
        + [
            pltpu.SemaphoreType.DMA((2 * PARTS, 3 + per)),
            pltpu.SemaphoreType.DMA((2 * PARTS, 3)),
        ],
        input_output_aliases={1 + len(flat) + 3 + i: 1 + i for i in range(len(before))},
        compiler_params=params(),
        name="adam_step",
    )(pos, *arrays, weights, moment1, moment2, *before)


def place_weights(pos, pieces, shape, chunk, before):
    flat = [(plane, one if isinstance(one, tuple) else (one,)) for plane, one in pieces]
    arrays = [one for _, group in flat for one in group]
    number, _, _, width = arrays[0].shape
    n_dp = shape[3] // width
    part = number // 2

    def body(pos_ref, *refs):
        ins = refs[: len(arrays)]
        out_ref, held, sems, sem_out = refs[-4:]
        dp_at = pos_ref[0]
        inner = (dp_at > 0) & (dp_at < n_dp - 1)

        def into(act, i):
            rows = pl.ds(i * part, part)
            at = 0
            for n, (_, group) in enumerate(flat):
                made = [
                    pltpu.make_async_copy(ins[at + k].at[rows], held.at[n, rows], sems.at[i, n])
                    for k in range(len(group))
                ]
                at += len(group)
                if len(made) == 1:
                    act(made[0])
                else:
                    pl.when(inner)(lambda made=made: act(made[0]))
                    pl.when(~inner)(lambda made=made: act(made[1]))

        for i in range(2):
            into(lambda copy: copy.start(), i)
        outs = []
        for i in range(2):
            into(lambda copy: copy.wait(), i)
            rows = pl.ds(i * part, part)
            to = pl.ds((i * CHUNKS + chunk) * part, part)
            for n, (plane, _) in enumerate(flat):
                columns = pl.ds(pl.multiple_of((dp_at ^ plane) * width, 128), width)
                outs.append(
                    pltpu.make_async_copy(
                        held.at[n, rows], out_ref.at[to, :, :, columns], sem_out.at[i, n]
                    )
                )
                outs[-1].start()
        for copy in outs:
            copy.wait()

    anywhere = pl.BlockSpec(memory_space=pl.ANY)
    held = (len(flat),) + arrays[0].shape
    return pl.pallas_call(
        body,
        out_shape=jax.ShapeDtypeStruct(shape, jnp.bfloat16),
        in_specs=[smem()] + [anywhere] * (len(arrays) + len(before)),
        out_specs=anywhere,
        scratch_shapes=[
            pltpu.VMEM(held, jnp.bfloat16),
            pltpu.SemaphoreType.DMA((2, len(flat))),
            pltpu.SemaphoreType.DMA((2, len(flat))),
        ],
        input_output_aliases={1 + len(arrays): 0} if before else {},
        compiler_params=params(LAST_VMEM_BYTES if len(flat) == 1 else VMEM_BYTES),
        name="place_weights",
    )(pos, *arrays, *before)


def between_planes(value, dp_at, n_dp, first=(), second=()):
    if n_dp != 4:
        whole = lax.all_gather(value, "dp", axis=0)
        return [
            lax.dynamic_index_in_dim(whole, dp_at ^ j, 0, keepdims=False) for j in range(n_dp)
        ]
    two = lax.ppermute(value, "dp", [(0, 2), (1, 3), (2, 0), (3, 1)])
    one = lax.ppermute(after(value, *first), "dp", [(0, 1), (1, 0), (2, 3), (3, 2)])
    outer = lax.ppermute(after(two, one, *second), "dp", [(2, 3), (1, 0)])
    middle = lax.ppermute(after(value, two, one, *second), "dp", [(1, 2), (2, 1)])
    return [value, one, two, (middle, outer)]


def gather_weights(pos, fresh, dp_at, n_dp, chunk, before, moving):
    number, _, piece, width = fresh.shape
    shape = (CHUNKS * number, 2, piece, n_dp * width)
    pieces = between_planes(fresh, dp_at, n_dp, (), jax.tree.leaves(moving[3:]))
    most = place_weights(pos, list(enumerate(pieces))[:-1], shape, chunk, before)
    return [place_weights(pos, [(n_dp - 1, pieces[-1])], shape, chunk, [most])], pieces


def after(value, *others):
    return lax.optimization_barrier((value,) + others)[0]


def finish_predicted(perm, parts):
    def body(perm_ref, parts_ref, out_ref):
        total = jnp.sum(parts_ref[...].astype(jnp.float32), axis=0)
        out_ref[...] = lax.dot_general(
            perm_ref[...],
            total.astype(jnp.bfloat16),
            (((0,), (0,)), ((), ())),
            preferred_element_type=jnp.float32,
        ).astype(jnp.bfloat16)

    return pl.pallas_call(
        body,
        out_shape=jax.ShapeDtypeStruct(parts.shape[1:], jnp.bfloat16),
        in_specs=[vmem(), vmem()],
        out_specs=vmem(),
        compiler_params=params(),
        name="finish_predicted",
    )(perm, parts)


def shards(signals, cotangent, row_insertion, touched, slot_map, weights, moment1, moment2):
    n_own = lax.axis_size("own")
    n_dp = lax.axis_size("dp")
    dp_at = lax.axis_index("dp")
    own_at = lax.axis_index("own")
    number, _, piece, _ = weights.shape
    width = moment1.shape[3]
    half = number // 2
    rows = signals.shape[0]
    pos = jnp.stack([dp_at, own_at]).astype(jnp.int32)

    def across(value, j):
        return lax.ppermute(value, "own", [(o, o ^ j) for o in range(n_own)])

    packed, perm = pack_rows(row_insertion.reshape(1, rows), signals, cotangent)
    if n_own == 8 and piece % 16 == 0:
        core = lax.rem(own_at, 2)
        columns = [
            lax.dynamic_slice(
                weights, (which * half, 0, 0, dp_at * width), (half, 2, piece, width)
            )
            for which in (core, 1 - core)
        ]
        chip = jnp.stack([columns[0], after(across(columns[1], 1), packed)])
        beside = [across(chip, 2), across(chip, 4)]
        diagonal = [across(beside[0][0], 4), across(beside[1][1], 2)]
        blocks = [(one, u) for one in [chip] + beside for u in range(2)]
        blocks += [(one, None) for one in diagonal]
        first, second, last = [chip], beside, diagonal
        sends = [(2, 6), (7,), (5,), (1,), (3,), (4,), (0,)]
    else:
        column = lax.dynamic_slice_in_dim(weights, dp_at * width, width, 3)
        outgoing = jnp.broadcast_to(
            column.reshape(1, 2, half, 2, piece, width), (n_own // 2, 2, half, 2, piece, width)
        ).reshape(n_own, half, 2, piece, width)
        blocks = lax.all_to_all(outgoing, "own", split_axis=0, concat_axis=0, tiled=True)
        blocks = blocks.transpose(1, 2, 0, 3, 4).reshape(half, 2, SITES, width)
        first, second, last = [], [], []
        sends = None
    *near, far = between_planes(packed, dp_at, n_dp, first, second)
    if isinstance(far, tuple):
        far = far[0] + far[1]
    near = jnp.stack(near)
    rows_in = (near, far, across(near, 1), across(after(far, *last), 1))

    pred_mine, pred_other, grads = local_grads(
        pos, touched, slot_map, rows_in, blocks, sends, piece, width
    )
    pred_part = pred_mine + across(pred_other, 1)
    parts = lax.all_to_all(pred_part, "dp", split_axis=0, concat_axis=0, tiled=True)
    if sends:
        x_same, y_diagonal, y_cross, partner, x_cross, y_same, own = grads
        x_same = across(x_same, 2)
        y_diagonal = across(y_diagonal, 4)
        y_cross = across(after(y_cross, pred_part), 5)
        partner = across(after(partner, pred_part), 1)
        first = (x_same, y_diagonal, y_cross, partner)
        x_cross = across(after(x_cross[0] + y_diagonal[0], *first), 3)
        y_same = across(after(y_same[0] + x_same[1], *first), 4)
        terms = [[(own, 0), (x_same, 0), y_same], [(partner, 0), (y_cross, 0), x_cross]]
    else:
        arrived = lax.all_to_all(grads, "own", split_axis=0, concat_axis=0, tiled=True)
        arrived = [
            lax.dynamic_index_in_dim(arrived, own_at ^ j, 0, keepdims=False) for j in range(n_own)
        ]
        terms = [arrived[0::2], arrived[1::2]]

    predicted = finish_predicted(perm, parts)
    terms[0][-1] = after(terms[0][-1], parts)

    moments = []
    new_weights = []
    pieces = []
    for chunk in range(CHUNKS):
        terms[0][-1] = after(terms[0][-1], *pieces[1:2])
        fresh, *moments = adam(pos, terms, weights, moment1, moment2, chunk, moments)
        new_weights, pieces = gather_weights(
            pos, fresh, dp_at, n_dp, chunk, new_weights, pieces
        )
    new_weights = new_weights[0]
    new_moment1, new_moment2 = moments

    return (predicted, new_weights, new_moment1, new_moment2)


def solution(mesh):
    in_specs = (
        P(("dp", "own"), None),
        P(("dp", "own"), None),
        P(("dp", "own")),
        P(),
        P(),
        P(None, None, "own", None),
        P(None, None, "own", "dp"),
        P(None, None, "own", "dp"),
    )
    out_specs = (
        P(("dp", "own"), None),
        P(None, None, "own", None),
        P(None, None, "own", "dp"),
        P(None, None, "own", "dp"),
    )
    return jax.shard_map(shards, mesh=mesh, in_specs=in_specs, out_specs=out_specs, check_vma=False)
```

```python
import math

import jax
import jax.numpy as jnp
from jax import lax
from jax.experimental import pallas as pl
from jax.experimental.pallas import tpu as pltpu
from jax.sharding import PartitionSpec as P

SITES = 384
CAP = 128
ID_ROWS = 16
PARTS = 4
TOGETHER = 4
VMEM_BYTES = 56 * 2**20
LAST_VMEM_BYTES = 8 * 2**20

gelu_coef = math.sqrt(2.0 / math.pi)
cubic_coef = 0.044715
learn_rate = 0.01


def gelu_parts(preact):
    tanh_input = gelu_coef * (preact + cubic_coef * preact * preact * preact)
    tangent = jnp.tanh(tanh_input)
    gelu_val = 0.5 * preact * (1.0 + tangent)
    slopes = 0.5 * (1.0 + tangent) + 0.5 * preact * (1.0 - tangent * tangent) * gelu_coef * (
        1.0 + 3.0 * cubic_coef * preact * preact
    )
    return (gelu_val, slopes)


def params(limit=VMEM_BYTES):
    return pltpu.CompilerParams(vmem_limit_bytes=limit)


def vmem():
    return pl.BlockSpec(memory_space=pltpu.VMEM)


def smem():
    return pl.BlockSpec(memory_space=pltpu.SMEM)


def pack_rows(ids, signals, cotangent):
    rows = signals.shape[0]

    def body(ids_ref, sig_ref, cot_ref, out_ref, perm_ref):
        ids_row = ids_ref[...].astype(jnp.float32)
        lane_ids = jnp.broadcast_to(ids_row, (rows, rows))
        same = lane_ids == lane_ids.T
        count = jnp.sum(same.astype(jnp.float32), axis=0, keepdims=True)
        full = jnp.max(jnp.where(count == CAP, ids_row, -1.0), axis=1, keepdims=True)
        chosen = ids_row == full
        from_row = lax.broadcasted_iota(jnp.int32, (rows, rows), 0)
        to_lane = lax.broadcasted_iota(jnp.int32, (rows, rows), 1)
        upto = (from_row <= to_lane).astype(jnp.bfloat16)
        ahead = jnp.dot(
            jnp.broadcast_to(chosen.astype(jnp.float32), (8, rows)).astype(jnp.bfloat16),
            upto,
            preferred_element_type=jnp.float32,
        )[:1].astype(jnp.int32)
        place = jnp.where(chosen, ahead - 1, CAP + to_lane[:1] - ahead)
        perm = (from_row == place).astype(jnp.float32).astype(jnp.bfloat16)
        perm_ref[...] = perm
        out_ref[:rows] = jnp.dot(perm, sig_ref[...], preferred_element_type=jnp.float32).astype(
            jnp.bfloat16
        )
        out_ref[rows : 2 * rows] = jnp.dot(
            perm, cot_ref[...], preferred_element_type=jnp.float32
        ).astype(jnp.bfloat16)
        sorted_ids = lax.dot_general(
            jnp.broadcast_to(ids_row, (ID_ROWS, rows)).astype(jnp.bfloat16),
            perm,
            (((1,), (1,)), ((), ())),
            preferred_element_type=jnp.float32,
        ).astype(jnp.bfloat16)
        out_ref[2 * rows :, :rows] = sorted_ids
        out_ref[2 * rows :, rows:] = jnp.zeros((ID_ROWS, SITES - rows), jnp.bfloat16)

    return pl.pallas_call(
        body,
        out_shape=(
            jax.ShapeDtypeStruct((2 * rows + ID_ROWS, SITES), jnp.bfloat16),
            jax.ShapeDtypeStruct((rows, rows), jnp.bfloat16),
        ),
        in_specs=[vmem(), vmem(), vmem()],
        out_specs=(vmem(), vmem()),
        compiler_params=params(),
        name="pack_rows",
    )(ids, signals, cotangent)


def local_grads(pos, touched, slot_map, rows_in, blocks, sends, piece, width):
    near = rows_in[0].shape[0]
    planes = near + 1
    rows = (rows_in[0].shape[1] - ID_ROWS) // 2
    touch = touched.shape[1]
    n_own = SITES // piece
    aligned = isinstance(blocks, list)
    arrays = []
    for array, _ in blocks if aligned else [(blocks, None)]:
        if not any(array is one for one in arrays):
            arrays.append(array)
    half = arrays[0].shape[-4]

    def body(pos_ref, touched_ref, slot_ref, *rest):
        row_refs = rest[:4]
        block_refs = rest[4 : 4 + len(arrays)]
        rest = rest[4 + len(arrays) :]
        pred_refs = rest[:2]
        n_out = len(grad_shapes)
        grad_refs = rest[2 : 2 + n_out]
        staged = rest[2 + n_out : 2 + 2 * n_out]
        acc, id_cols, held, sorted_rows, pred, full_of, tasks, sems, sem_out = rest[-9:]
        own_at = pos_ref[1]
        core = lax.rem(own_at, 2)

        row_copies = [
            pltpu.make_async_copy(
                ref, sorted_rows.at[pl.ds(at, near) if i % 2 == 0 else at], sems.at[i]
            )
            for i, (ref, at) in enumerate(zip(row_refs, (0, near, planes, planes + near)))
        ]
        if aligned:
            block_copies = []
            for j, (array, at) in enumerate(blocks):
                ref = [one for one, other in zip(block_refs, arrays) if other is array][0]
                sites = pl.ds(pl.multiple_of((own_at ^ j) * piece, 16), piece)
                block_copies.append(
                    pltpu.make_async_copy(
                        ref if at is None else ref.at[at], held.at[:, :, sites, :], sems.at[4 + j]
                    )
                )
        else:
            block_copies = [pltpu.make_async_copy(block_refs[0], held, sems.at[4])]
        for copy in row_copies + block_copies:
            copy.start()

        def clear(e, _):
            acc[e] = jnp.zeros(acc.shape[1:], jnp.float32)
            return 0

        lax.fori_loop(0, half, clear, 0)
        pred[...] = jnp.zeros_like(pred)
        for copy in row_copies:
            copy.wait()
        for source in range(2 * planes):
            ids_row = sorted_rows[source, 2 * rows :, :rows][:1].astype(jnp.float32)
            id_cols[source] = jnp.broadcast_to(ids_row[:, CAP:], (128, rows - CAP)).T
            full_of[source] = jnp.max(ids_row[:, :CAP]).astype(jnp.int32)

        count = jnp.int32(0)
        for source in range(2 * planes):
            which, plane = divmod(source, planes)
            device = (pos_ref[0] ^ plane) * n_own + (own_at ^ which)
            full = full_of[source]
            for j in range(touch + 1):
                insertion = full if j == 0 else touched_ref[device, j - 1]
                e = slot_ref[insertion] - core * half
                here = (e >= 0) & (e < half)
                if j:
                    here = here & (insertion != full)
                tasks[0, count] = jnp.int32(source)
                tasks[1, count] = jnp.int32(0 if j == 0 else CAP)
                tasks[2, count] = insertion
                tasks[3, count] = e
                count = count + here.astype(jnp.int32)
        for u in range(TOGETHER - 1):
            tasks[0, count + u] = jnp.int32(0)
            tasks[1, count + u] = jnp.int32(CAP)
            tasks[2, count + u] = jnp.int32(-1)
            tasks[3, count + u] = jnp.int32(0)
        for copy in block_copies:
            copy.wait()

        def together(i, _):
            loaded = []
            for u in range(TOGETHER):
                source, offset, insertion, e = [tasks[k, TOGETHER * i + u] for k in range(4)]
                first = pl.multiple_of(offset, CAP)
                wanted = jnp.where(offset == 0, -1, insertion).astype(jnp.float32)
                every = (offset == 0).astype(jnp.float32)
                keep = (id_cols[source] == wanted).astype(jnp.float32)
                keep = jnp.maximum(keep, every).astype(jnp.bfloat16)
                keep = jnp.concatenate([keep] * (SITES // 128), axis=1)
                sig = sorted_rows[source, pl.ds(first, CAP), :] * keep
                cot = sorted_rows[source, pl.ds(rows + first, CAP), :] * keep
                loaded.append((source, first, e, sig, cot))
            found = []
            for source, first, e, sig, cot in loaded:
                read_out = held[e, 1]
                preact = jnp.dot(sig, held[e, 0], preferred_element_type=jnp.float32)
                back_hidden = jnp.dot(cot, read_out, preferred_element_type=jnp.float32)
                gelu_val, slopes = gelu_parts(preact)
                hidden = gelu_val.astype(jnp.bfloat16)
                back_pre = (back_hidden * slopes).astype(jnp.bfloat16)
                part = lax.dot_general(
                    hidden, read_out, (((1,), (1,)), ((), ())), preferred_element_type=jnp.float32
                ).astype(jnp.bfloat16)
                grad_in = lax.dot_general(
                    sig, back_pre, (((0,), (0,)), ((), ())), preferred_element_type=jnp.float32
                )
                grad_out = lax.dot_general(
                    cot, hidden, (((0,), (0,)), ((), ())), preferred_element_type=jnp.float32
                )
                found.append((part, grad_in, grad_out))
            for (source, first, e, _, _), (part, grad_in, grad_out) in zip(loaded, found):
                pred[source, pl.ds(first, CAP), :] += part
                acc[e, 0] += grad_in
                acc[e, 1] += grad_out
            return 0

        lax.fori_loop(0, (count + TOGETHER - 1) // TOGETHER, together, 0)
        outs = [
            pltpu.make_async_copy(
                pred.at[which * planes + i], pred_refs[which].at[pos_ref[0] ^ i], sem_out.at[which, i]
            )
            for which in (1, 0)
            for i in range(planes)
        ]
        for copy in outs:
            copy.start()
        for n, (ref, into) in enumerate(zip(grad_refs, staged)):

            def write(e, _, into=into, n=n):
                if aligned:
                    for i, j in enumerate(sends[n]):
                        first = pl.multiple_of((own_at ^ j) * piece, 16)
                        into[i, e] = acc[e, :, pl.ds(first, piece), :].astype(jnp.bfloat16)
                else:
                    into[e] = acc[e].astype(jnp.bfloat16)
                return 0

            lax.fori_loop(0, half, write, 0)
            outs.append(pltpu.make_async_copy(into, ref, sem_out.at[2 + n, 0]))
            outs[-1].start()
        for copy in outs:
            copy.wait()

    pred_shape = jax.ShapeDtypeStruct((planes, rows, SITES), jnp.bfloat16)
    grad_shapes = [
        jax.ShapeDtypeStruct(shape, jnp.bfloat16)
        for shape in (
            [(len(group), half, 2, piece, width) for group in sends]
            if aligned
            else [(half, 2, SITES, width)]
        )
    ]
    most = 2 * planes * (touch + 1)
    acc_shape = (half, 2, SITES, width)
    id_shape = (2 * planes, rows - CAP, 128)
    row_shape = (2 * planes,) + rows_in[0].shape[1:]
    pred_all = (2 * planes, rows, SITES)
    scratch = [pltpu.VMEM(one.shape, jnp.bfloat16) for one in grad_shapes] + [
        pltpu.VMEM(acc_shape, jnp.float32),
        pltpu.VMEM(id_shape, jnp.float32),
        pltpu.VMEM(acc_shape, jnp.bfloat16),
        pltpu.VMEM(row_shape, jnp.bfloat16),
        pltpu.VMEM(pred_all, jnp.bfloat16),
        pltpu.SMEM((2 * planes,), jnp.int32),
        pltpu.SMEM((4, most + TOGETHER), jnp.int32),
        pltpu.SemaphoreType.DMA((4 + n_own,)),
        pltpu.SemaphoreType.DMA((2 + len(grad_shapes), planes)),
    ]
    found = pl.pallas_call(
        body,
        out_shape=[pred_shape, pred_shape] + grad_shapes,
        in_specs=[smem(), smem(), smem()] + [pl.BlockSpec(memory_space=pl.ANY)] * (4 + len(arrays)),
        out_specs=[pl.BlockSpec(memory_space=pl.ANY)] * (2 + len(grad_shapes)),
        scratch_shapes=scratch,
        compiler_params=params(),
        name="local_grads",
    )(pos, touched, slot_map, *rows_in, *arrays)
    grads = list(found[2:])
    if not aligned:
        grads = grads[0].reshape(half, 2, n_own, piece, width).transpose(2, 0, 1, 3, 4)
    return found[0], found[1], grads


def adam(pos, terms, weights, moment1, moment2):
    number, _, piece, width = moment1.shape
    half = number // 2
    flat = [one if isinstance(one, tuple) else (one, None) for group in terms for one in group]
    arrays = [array for array, _ in flat]
    per = len(terms[0])
    correct_one = 1.0 - 0.9**10
    correct_two = 1.0 - 0.999**10

    def body(pos_ref, *refs):
        term_refs = [
            ref if at is None else ref.at[at] for ref, (_, at) in zip(refs, flat)
        ]
        w_ref, m1_ref, m2_ref = refs[len(flat) : len(flat) + 3]
        refs = refs[len(flat) + 3 :]
        new_w, new_m1, new_m2, grads, w_in, m1_in, m2_in, w_out, m1_out, m2_out = refs[:10]
        sem_in, sem_out = refs[10:]
        columns = pl.ds(pl.multiple_of(pos_ref[0] * width, 128), width)
        part = half // PARTS
        steps = [(g, i * part) for g in range(2) for i in range(PARTS)]
        own_core = lax.rem(pos_ref[1], 2)
        copies = []
        for n, (g, first) in enumerate(steps):
            rows = pl.ds((own_core ^ g) * half + first, part)
            copies.append(
                [
                    pltpu.make_async_copy(ref, into.at[rows], sem_in.at[n, i])
                    for i, (ref, into) in enumerate(
                        (
                            (w_ref.at[rows, :, :, columns], w_in),
                            (m1_ref.at[rows], m1_in),
                            (m2_ref.at[rows], m2_in),
                        )
                    )
                ]
                + [
                    pltpu.make_async_copy(
                        term_refs[g * per + i].at[pl.ds(first, part)],
                        grads.at[g * per + i, pl.ds(first, part)],
                        sem_in.at[n, 3 + i],
                    )
                    for i in range(per)
                ]
            )
            for copy in copies[n]:
                copy.start()
        outs = []
        for n, (g, first) in enumerate(steps):
            for copy in copies[n]:
                copy.wait()

            def step(i, _, g=g, first=first):
                gradient = grads[g * per, first + i].astype(jnp.float32)
                for j in range(1, per):
                    gradient = gradient + grads[g * per + j, first + i].astype(jnp.float32)
                at = (own_core ^ g) * half + first + i
                one = 0.9 * m1_in[at] + 0.1 * gradient
                two = 0.999 * m2_in[at] + 0.001 * gradient * gradient
                m1_out[at] = one
                m2_out[at] = two
                spread = two * (1.0 / correct_two)
                updated = w_in[at].astype(jnp.float32) - one * (learn_rate / correct_one) / (
                    spread * lax.rsqrt(spread) + 1e-08
                )
                w_out[at] = updated.astype(jnp.bfloat16)
                return 0

            lax.fori_loop(0, part, step, 0)
            rows = pl.ds((own_core ^ g) * half + first, part)
            for i, (held, ref) in enumerate(
                ((w_out, new_w), (m1_out, new_m1), (m2_out, new_m2))
            ):
                outs.append(pltpu.make_async_copy(held.at[rows], ref.at[rows], sem_out.at[n, i]))
                outs[-1].start()
        for copy in outs:
            copy.wait()

    anywhere = pl.BlockSpec(memory_space=pl.ANY)
    return pl.pallas_call(
        body,
        out_shape=[
            jax.ShapeDtypeStruct(moment1.shape, jnp.bfloat16),
            jax.ShapeDtypeStruct(moment1.shape, jnp.float32),
            jax.ShapeDtypeStruct(moment1.shape, jnp.float32),
        ],
        in_specs=[smem()] + [anywhere] * (len(flat) + 3),
        out_specs=[anywhere] * 3,
        scratch_shapes=[pltpu.VMEM((len(flat), half, 2, piece, width), jnp.bfloat16)]
        + [pltpu.VMEM(moment1.shape, kind) for kind in (jnp.bfloat16, jnp.float32, jnp.float32)] * 2
        + [
            pltpu.SemaphoreType.DMA((2 * PARTS, 3 + per)),
            pltpu.SemaphoreType.DMA((2 * PARTS, 3)),
        ],
        compiler_params=params(),
        name="adam_step",
    )(pos, *arrays, weights, moment1, moment2)


def place_weights(pos, pieces, shape, before):
    flat = [(plane, one if isinstance(one, tuple) else (one,)) for plane, one in pieces]
    arrays = [one for _, group in flat for one in group]
    number, _, _, width = arrays[0].shape
    n_dp = shape[3] // width
    part = number // PARTS

    def body(pos_ref, *refs):
        ins = refs[: len(arrays)]
        out_ref, held, sems, sem_out = refs[-4:]
        dp_at = pos_ref[0]
        inner = (dp_at > 0) & (dp_at < n_dp - 1)

        def into(act, i):
            rows = pl.ds(i * part, part)
            at = 0
            for n, (_, group) in enumerate(flat):
                made = [
                    pltpu.make_async_copy(ins[at + k].at[rows], held.at[n, rows], sems.at[i, n])
                    for k in range(len(group))
                ]
                at += len(group)
                if len(made) == 1:
                    act(made[0])
                else:
                    pl.when(inner)(lambda made=made: act(made[0]))
                    pl.when(~inner)(lambda made=made: act(made[1]))

        for i in range(PARTS):
            into(lambda copy: copy.start(), i)
        outs = []
        for i in range(PARTS):
            into(lambda copy: copy.wait(), i)
            rows = pl.ds(i * part, part)
            for n, (plane, _) in enumerate(flat):
                columns = pl.ds(pl.multiple_of((dp_at ^ plane) * width, 128), width)
                outs.append(
                    pltpu.make_async_copy(
                        held.at[n, rows], out_ref.at[rows, :, :, columns], sem_out.at[i, n]
                    )
                )
                outs[-1].start()
        for copy in outs:
            copy.wait()

    anywhere = pl.BlockSpec(memory_space=pl.ANY)
    held = (len(flat),) + arrays[0].shape
    return pl.pallas_call(
        body,
        out_shape=jax.ShapeDtypeStruct(shape, jnp.bfloat16),
        in_specs=[smem()] + [anywhere] * (len(arrays) + len(before)),
        out_specs=anywhere,
        scratch_shapes=[
            pltpu.VMEM(held, jnp.bfloat16),
            pltpu.SemaphoreType.DMA((PARTS, len(flat))),
            pltpu.SemaphoreType.DMA((PARTS, len(flat))),
        ],
        input_output_aliases={1 + len(arrays): 0} if before else {},
        compiler_params=params(LAST_VMEM_BYTES if before else VMEM_BYTES),
        name="place_weights",
    )(pos, *arrays, *before)


def between_planes(value, dp_at, n_dp, first=(), second=()):
    if n_dp != 4:
        whole = lax.all_gather(value, "dp", axis=0)
        return [
            lax.dynamic_index_in_dim(whole, dp_at ^ j, 0, keepdims=False) for j in range(n_dp)
        ]
    two = lax.ppermute(value, "dp", [(0, 2), (1, 3), (2, 0), (3, 1)])
    one = lax.ppermute(after(value, *first), "dp", [(0, 1), (1, 0), (2, 3), (3, 2)])
    outer = lax.ppermute(after(two, one, *second), "dp", [(2, 3), (1, 0)])
    middle = lax.ppermute(after(value, two, one, *second), "dp", [(1, 2), (2, 1)])
    return [value, one, two, (middle, outer)]


def gather_weights(pos, fresh, dp_at, n_dp):
    shape = fresh.shape[:3] + (n_dp * fresh.shape[3],)
    pieces = list(enumerate(between_planes(fresh, dp_at, n_dp)))
    most = place_weights(pos, pieces[:-1], shape, [])
    return place_weights(pos, pieces[-1:], shape, [most])


def after(value, *others):
    return lax.optimization_barrier((value,) + others)[0]


def finish_predicted(perm, parts):
    def body(perm_ref, parts_ref, out_ref):
        total = jnp.sum(parts_ref[...].astype(jnp.float32), axis=0)
        out_ref[...] = lax.dot_general(
            perm_ref[...],
            total.astype(jnp.bfloat16),
            (((0,), (0,)), ((), ())),
            preferred_element_type=jnp.float32,
        ).astype(jnp.bfloat16)

    return pl.pallas_call(
        body,
        out_shape=jax.ShapeDtypeStruct(parts.shape[1:], jnp.bfloat16),
        in_specs=[vmem(), vmem()],
        out_specs=vmem(),
        compiler_params=params(),
        name="finish_predicted",
    )(perm, parts)


def shards(signals, cotangent, row_insertion, touched, slot_map, weights, moment1, moment2):
    n_own = lax.axis_size("own")
    n_dp = lax.axis_size("dp")
    dp_at = lax.axis_index("dp")
    own_at = lax.axis_index("own")
    number, _, piece, _ = weights.shape
    width = moment1.shape[3]
    half = number // 2
    rows = signals.shape[0]
    pos = jnp.stack([dp_at, own_at]).astype(jnp.int32)

    def across(value, j):
        return lax.ppermute(value, "own", [(o, o ^ j) for o in range(n_own)])

    packed, perm = pack_rows(row_insertion.reshape(1, rows), signals, cotangent)
    if n_own == 8 and piece % 16 == 0:
        core = lax.rem(own_at, 2)
        columns = [
            lax.dynamic_slice(
                weights, (which * half, 0, 0, dp_at * width), (half, 2, piece, width)
            )
            for which in (core, 1 - core)
        ]
        chip = jnp.stack([columns[0], after(across(columns[1], 1), packed)])
        beside = [across(chip, 2), across(chip, 4)]
        diagonal = [across(beside[0][0], 4), across(beside[1][1], 2)]
        blocks = [(one, u) for one in [chip] + beside for u in range(2)]
        blocks += [(one, None) for one in diagonal]
        first, second, last = [chip], beside, diagonal
        sends = [(2, 6), (7,), (5,), (1,), (3,), (4,), (0,)]
    else:
        column = lax.dynamic_slice_in_dim(weights, dp_at * width, width, 3)
        outgoing = jnp.broadcast_to(
            column.reshape(1, 2, half, 2, piece, width), (n_own // 2, 2, half, 2, piece, width)
        ).reshape(n_own, half, 2, piece, width)
        blocks = lax.all_to_all(outgoing, "own", split_axis=0, concat_axis=0, tiled=True)
        blocks = blocks.transpose(1, 2, 0, 3, 4).reshape(half, 2, SITES, width)
        first, second, last = [], [], []
        sends = None
    *near, far = between_planes(packed, dp_at, n_dp, first, second)
    if isinstance(far, tuple):
        far = far[0] + far[1]
    near = jnp.stack(near)
    rows_in = (near, far, across(near, 1), across(after(far, *last), 1))

    pred_mine, pred_other, grads = local_grads(
        pos, touched, slot_map, rows_in, blocks, sends, piece, width
    )
    pred_part = pred_mine + across(pred_other, 1)
    parts = lax.all_to_all(pred_part, "dp", split_axis=0, concat_axis=0, tiled=True)
    if sends:
        x_same, y_diagonal, y_cross, partner, x_cross, y_same, own = grads
        x_same = across(x_same, 2)
        y_diagonal = across(y_diagonal, 4)
        y_cross = across(after(y_cross, pred_part), 5)
        partner = across(after(partner, pred_part), 1)
        first = (x_same, y_diagonal, y_cross, partner)
        x_cross = across(after(x_cross[0] + y_diagonal[0], *first), 3)
        y_same = across(after(y_same[0] + x_same[1], *first), 4)
        terms = [[(own, 0), (x_same, 0), y_same], [(partner, 0), (y_cross, 0), x_cross]]
    else:
        arrived = lax.all_to_all(grads, "own", split_axis=0, concat_axis=0, tiled=True)
        arrived = [
            lax.dynamic_index_in_dim(arrived, own_at ^ j, 0, keepdims=False) for j in range(n_own)
        ]
        terms = [arrived[0::2], arrived[1::2]]

    predicted = finish_predicted(perm, parts)
    terms[0][-1] = after(terms[0][-1], parts)

    fresh, new_moment1, new_moment2 = adam(pos, terms, weights, moment1, moment2)
    new_weights = gather_weights(pos, fresh, dp_at, n_dp)

    return (predicted, new_weights, new_moment1, new_moment2)


def solution(mesh):
    in_specs = (
        P(("dp", "own"), None),
        P(("dp", "own"), None),
        P(("dp", "own")),
        P(),
        P(),
        P(None, None, "own", None),
        P(None, None, "own", "dp"),
        P(None, None, "own", "dp"),
    )
    out_specs = (
        P(("dp", "own"), None),
        P(None, None, "own", None),
        P(None, None, "own", "dp"),
        P(None, None, "own", "dp"),
    )
    return jax.shard_map(shards, mesh=mesh, in_specs=in_specs, out_specs=out_specs, check_vma=False)
```

```python
import math

import jax
import jax.numpy as jnp
from jax import lax
from jax.experimental import pallas as pl
from jax.experimental.pallas import tpu as pltpu
from jax.sharding import PartitionSpec as P

SITES = 384
CAP = 128
ID_ROWS = 16
PARTS = 4
TOGETHER = 4
VMEM_BYTES = 56 * 2**20
LAST_VMEM_BYTES = 4 * 2**20

gelu_coef = math.sqrt(2.0 / math.pi)
cubic_coef = 0.044715
learn_rate = 0.01


def gelu_parts(preact):
    tanh_input = gelu_coef * (preact + cubic_coef * preact * preact * preact)
    tangent = jnp.tanh(tanh_input)
    gelu_val = 0.5 * preact * (1.0 + tangent)
    slopes = 0.5 * (1.0 + tangent) + 0.5 * preact * (1.0 - tangent * tangent) * gelu_coef * (
        1.0 + 3.0 * cubic_coef * preact * preact
    )
    return (gelu_val, slopes)


def params(limit=VMEM_BYTES):
    return pltpu.CompilerParams(vmem_limit_bytes=limit)


def vmem():
    return pl.BlockSpec(memory_space=pltpu.VMEM)


def smem():
    return pl.BlockSpec(memory_space=pltpu.SMEM)


def pack_rows(ids, signals, cotangent):
    rows = signals.shape[0]

    def body(ids_ref, sig_ref, cot_ref, out_ref, perm_ref):
        ids_row = ids_ref[...].astype(jnp.float32)
        lane_ids = jnp.broadcast_to(ids_row, (rows, rows))
        same = lane_ids == lane_ids.T
        count = jnp.sum(same.astype(jnp.float32), axis=0, keepdims=True)
        full = jnp.max(jnp.where(count == CAP, ids_row, -1.0), axis=1, keepdims=True)
        chosen = ids_row == full
        from_row = lax.broadcasted_iota(jnp.int32, (rows, rows), 0)
        to_lane = lax.broadcasted_iota(jnp.int32, (rows, rows), 1)
        upto = (from_row <= to_lane).astype(jnp.bfloat16)
        ahead = jnp.dot(
            jnp.broadcast_to(chosen.astype(jnp.float32), (8, rows)).astype(jnp.bfloat16),
            upto,
            preferred_element_type=jnp.float32,
        )[:1].astype(jnp.int32)
        place = jnp.where(chosen, ahead - 1, CAP + to_lane[:1] - ahead)
        perm = (from_row == place).astype(jnp.float32).astype(jnp.bfloat16)
        perm_ref[...] = perm
        out_ref[:rows] = jnp.dot(perm, sig_ref[...], preferred_element_type=jnp.float32).astype(
            jnp.bfloat16
        )
        out_ref[rows : 2 * rows] = jnp.dot(
            perm, cot_ref[...], preferred_element_type=jnp.float32
        ).astype(jnp.bfloat16)
        sorted_ids = lax.dot_general(
            jnp.broadcast_to(ids_row, (ID_ROWS, rows)).astype(jnp.bfloat16),
            perm,
            (((1,), (1,)), ((), ())),
            preferred_element_type=jnp.float32,
        ).astype(jnp.bfloat16)
        out_ref[2 * rows :, :rows] = sorted_ids
        out_ref[2 * rows :, rows:] = jnp.zeros((ID_ROWS, SITES - rows), jnp.bfloat16)

    return pl.pallas_call(
        body,
        out_shape=(
            jax.ShapeDtypeStruct((2 * rows + ID_ROWS, SITES), jnp.bfloat16),
            jax.ShapeDtypeStruct((rows, rows), jnp.bfloat16),
        ),
        in_specs=[vmem(), vmem(), vmem()],
        out_specs=(vmem(), vmem()),
        compiler_params=params(),
        name="pack_rows",
    )(ids, signals, cotangent)


def local_grads(pos, touched, slot_map, rows_in, blocks, sends, piece, width):
    near = rows_in[0].shape[0]
    planes = near + 1
    rows = (rows_in[0].shape[1] - ID_ROWS) // 2
    touch = touched.shape[1]
    n_own = SITES // piece
    aligned = isinstance(blocks, list)
    arrays = []
    for array, _ in blocks if aligned else [(blocks, None)]:
        if not any(array is one for one in arrays):
            arrays.append(array)
    half = arrays[0].shape[-4]

    def body(pos_ref, touched_ref, slot_ref, *rest):
        row_refs = rest[:4]
        block_refs = rest[4 : 4 + len(arrays)]
        rest = rest[4 + len(arrays) :]
        pred_refs = rest[:2]
        n_out = len(grad_shapes)
        grad_refs = rest[2 : 2 + n_out]
        staged = rest[2 + n_out : 2 + 2 * n_out]
        acc, id_cols, held, sorted_rows, pred, full_of, tasks, sems, sem_out = rest[-9:]
        own_at = pos_ref[1]
        core = lax.rem(own_at, 2)

        row_copies = [
            pltpu.make_async_copy(
                ref, sorted_rows.at[pl.ds(at, near) if i % 2 == 0 else at], sems.at[i]
            )
            for i, (ref, at) in enumerate(zip(row_refs, (0, near, planes, planes + near)))
        ]
        if aligned:
            block_copies = []
            for j, (array, at) in enumerate(blocks):
                ref = [one for one, other in zip(block_refs, arrays) if other is array][0]
                sites = pl.ds(pl.multiple_of((own_at ^ j) * piece, 16), piece)
                block_copies.append(
                    pltpu.make_async_copy(
                        ref if at is None else ref.at[at], held.at[:, :, sites, :], sems.at[4 + j]
                    )
                )
        else:
            block_copies = [pltpu.make_async_copy(block_refs[0], held, sems.at[4])]
        for copy in row_copies + block_copies:
            copy.start()

        def clear(e, _):
            acc[e] = jnp.zeros(acc.shape[1:], jnp.float32)
            return 0

        lax.fori_loop(0, half, clear, 0)
        pred[...] = jnp.zeros_like(pred)
        for copy in row_copies:
            copy.wait()
        for source in range(2 * planes):
            ids_row = sorted_rows[source, 2 * rows :, :rows][:1].astype(jnp.float32)
            id_cols[source] = jnp.broadcast_to(ids_row[:, CAP:], (128, rows - CAP)).T
            full_of[source] = jnp.max(ids_row[:, :CAP]).astype(jnp.int32)

        count = jnp.int32(0)
        for source in range(2 * planes):
            which, plane = divmod(source, planes)
            device = (pos_ref[0] ^ plane) * n_own + (own_at ^ which)
            full = full_of[source]
            for j in range(touch + 1):
                insertion = full if j == 0 else touched_ref[device, j - 1]
                e = slot_ref[insertion] - core * half
                here = (e >= 0) & (e < half)
                if j:
                    here = here & (insertion != full)
                tasks[0, count] = jnp.int32(source)
                tasks[1, count] = jnp.int32(0 if j == 0 else CAP)
                tasks[2, count] = insertion
                tasks[3, count] = e
                count = count + here.astype(jnp.int32)
        for u in range(TOGETHER - 1):
            tasks[0, count + u] = jnp.int32(0)
            tasks[1, count + u] = jnp.int32(CAP)
            tasks[2, count + u] = jnp.int32(-1)
            tasks[3, count + u] = jnp.int32(0)
        for copy in block_copies:
            copy.wait()

        def together(i, _):
            loaded = []
            for u in range(TOGETHER):
                source, offset, insertion, e = [tasks[k, TOGETHER * i + u] for k in range(4)]
                first = pl.multiple_of(offset, CAP)
                wanted = jnp.where(offset == 0, -1, insertion).astype(jnp.float32)
                every = (offset == 0).astype(jnp.float32)
                keep = (id_cols[source] == wanted).astype(jnp.float32)
                keep = jnp.maximum(keep, every).astype(jnp.bfloat16)
                keep = jnp.concatenate([keep] * (SITES // 128), axis=1)
                sig = sorted_rows[source, pl.ds(first, CAP), :] * keep
                cot = sorted_rows[source, pl.ds(rows + first, CAP), :] * keep
                loaded.append((source, first, e, sig, cot))
            found = []
            for source, first, e, sig, cot in loaded:
                read_out = held[e, 1]
                preact = jnp.dot(sig, held[e, 0], preferred_element_type=jnp.float32)
                back_hidden = jnp.dot(cot, read_out, preferred_element_type=jnp.float32)
                gelu_val, slopes = gelu_parts(preact)
                hidden = gelu_val.astype(jnp.bfloat16)
                back_pre = (back_hidden * slopes).astype(jnp.bfloat16)
                part = lax.dot_general(
                    hidden, read_out, (((1,), (1,)), ((), ())), preferred_element_type=jnp.float32
                ).astype(jnp.bfloat16)
                grad_in = lax.dot_general(
                    sig, back_pre, (((0,), (0,)), ((), ())), preferred_element_type=jnp.float32
                )
                grad_out = lax.dot_general(
                    cot, hidden, (((0,), (0,)), ((), ())), preferred_element_type=jnp.float32
                )
                found.append((part, grad_in, grad_out))
            for (source, first, e, _, _), (part, grad_in, grad_out) in zip(loaded, found):
                pred[source, pl.ds(first, CAP), :] += part
                acc[e, 0] += grad_in
                acc[e, 1] += grad_out
            return 0

        lax.fori_loop(0, (count + TOGETHER - 1) // TOGETHER, together, 0)
        outs = [
            pltpu.make_async_copy(
                pred.at[which * planes + i], pred_refs[which].at[pos_ref[0] ^ i], sem_out.at[which, i]
            )
            for which in (1, 0)
            for i in range(planes)
        ]
        for copy in outs:
            copy.start()
        for n, (ref, into) in enumerate(zip(grad_refs, staged)):

            def write(e, _, into=into, n=n):
                if aligned:
                    for i, j in enumerate(sends[n]):
                        first = pl.multiple_of((own_at ^ j) * piece, 16)
                        into[i, e] = acc[e, :, pl.ds(first, piece), :].astype(jnp.bfloat16)
                else:
                    into[e] = acc[e].astype(jnp.bfloat16)
                return 0

            lax.fori_loop(0, half, write, 0)
            outs.append(pltpu.make_async_copy(into, ref, sem_out.at[2 + n, 0]))
            outs[-1].start()
        for copy in outs:
            copy.wait()

    pred_shape = jax.ShapeDtypeStruct((planes, rows, SITES), jnp.bfloat16)
    grad_shapes = [
        jax.ShapeDtypeStruct(shape, jnp.bfloat16)
        for shape in (
            [(len(group), half, 2, piece, width) for group in sends]
            if aligned
            else [(half, 2, SITES, width)]
        )
    ]
    most = 2 * planes * (touch + 1)
    acc_shape = (half, 2, SITES, width)
    id_shape = (2 * planes, rows - CAP, 128)
    row_shape = (2 * planes,) + rows_in[0].shape[1:]
    pred_all = (2 * planes, rows, SITES)
    scratch = [pltpu.VMEM(one.shape, jnp.bfloat16) for one in grad_shapes] + [
        pltpu.VMEM(acc_shape, jnp.float32),
        pltpu.VMEM(id_shape, jnp.float32),
        pltpu.VMEM(acc_shape, jnp.bfloat16),
        pltpu.VMEM(row_shape, jnp.bfloat16),
        pltpu.VMEM(pred_all, jnp.bfloat16),
        pltpu.SMEM((2 * planes,), jnp.int32),
        pltpu.SMEM((4, most + TOGETHER), jnp.int32),
        pltpu.SemaphoreType.DMA((4 + n_own,)),
        pltpu.SemaphoreType.DMA((2 + len(grad_shapes), planes)),
    ]
    found = pl.pallas_call(
        body,
        out_shape=[pred_shape, pred_shape] + grad_shapes,
        in_specs=[smem(), smem(), smem()] + [pl.BlockSpec(memory_space=pl.ANY)] * (4 + len(arrays)),
        out_specs=[pl.BlockSpec(memory_space=pl.ANY)] * (2 + len(grad_shapes)),
        scratch_shapes=scratch,
        compiler_params=params(),
        name="local_grads",
    )(pos, touched, slot_map, *rows_in, *arrays)
    grads = list(found[2:])
    if not aligned:
        grads = grads[0].reshape(half, 2, n_own, piece, width).transpose(2, 0, 1, 3, 4)
    return found[0], found[1], grads


def adam(pos, terms, weights, moment1, moment2):
    number, _, piece, width = moment1.shape
    half = number // 2
    flat = [one if isinstance(one, tuple) else (one, None) for group in terms for one in group]
    arrays = [array for array, _ in flat]
    per = len(terms[0])
    correct_one = 1.0 - 0.9**10
    correct_two = 1.0 - 0.999**10

    def body(pos_ref, *refs):
        term_refs = [
            ref if at is None else ref.at[at] for ref, (_, at) in zip(refs, flat)
        ]
        w_ref, m1_ref, m2_ref = refs[len(flat) : len(flat) + 3]
        refs = refs[len(flat) + 3 :]
        new_w, new_m1, new_m2, grads, w_in, m1_in, m2_in, w_out, m1_out, m2_out = refs[:10]
        sem_in, sem_out = refs[10:]
        columns = pl.ds(pl.multiple_of(pos_ref[0] * width, 128), width)
        part = half // PARTS
        steps = [(g, i * part) for g in range(2) for i in range(PARTS)]
        own_core = lax.rem(pos_ref[1], 2)
        copies = []
        for n, (g, first) in enumerate(steps):
            rows = pl.ds((own_core ^ g) * half + first, part)
            copies.append(
                [
                    pltpu.make_async_copy(ref, into.at[rows], sem_in.at[n, i])
                    for i, (ref, into) in enumerate(
                        (
                            (w_ref.at[rows, :, :, columns], w_in),
                            (m1_ref.at[rows], m1_in),
                            (m2_ref.at[rows], m2_in),
                        )
                    )
                ]
                + [
                    pltpu.make_async_copy(
                        term_refs[g * per + i].at[pl.ds(first, part)],
                        grads.at[g * per + i, pl.ds(first, part)],
                        sem_in.at[n, 3 + i],
                    )
                    for i in range(per)
                ]
            )
            for copy in copies[n]:
                copy.start()
        outs = []
        for n, (g, first) in enumerate(steps):
            for copy in copies[n]:
                copy.wait()

            def step(i, _, g=g, first=first):
                gradient = grads[g * per, first + i].astype(jnp.float32)
                for j in range(1, per):
                    gradient = gradient + grads[g * per + j, first + i].astype(jnp.float32)
                at = (own_core ^ g) * half + first + i
                one = 0.9 * m1_in[at] + 0.1 * gradient
                two = 0.999 * m2_in[at] + 0.001 * gradient * gradient
                m1_out[at] = one
                m2_out[at] = two
                spread = two * (1.0 / correct_two)
                updated = w_in[at].astype(jnp.float32) - one * (learn_rate / correct_one) / (
                    spread * lax.rsqrt(spread) + 1e-08
                )
                w_out[at] = updated.astype(jnp.bfloat16)
                return 0

            lax.fori_loop(0, part, step, 0)
            rows = pl.ds((own_core ^ g) * half + first, part)
            for i, (held, ref) in enumerate(
                ((w_out, new_w), (m1_out, new_m1), (m2_out, new_m2))
            ):
                outs.append(pltpu.make_async_copy(held.at[rows], ref.at[rows], sem_out.at[n, i]))
                outs[-1].start()
        for copy in outs:
            copy.wait()

    anywhere = pl.BlockSpec(memory_space=pl.ANY)
    return pl.pallas_call(
        body,
        out_shape=[
            jax.ShapeDtypeStruct(moment1.shape, jnp.bfloat16),
            jax.ShapeDtypeStruct(moment1.shape, jnp.float32),
            jax.ShapeDtypeStruct(moment1.shape, jnp.float32),
        ],
        in_specs=[smem()] + [anywhere] * (len(flat) + 3),
        out_specs=[anywhere] * 3,
        scratch_shapes=[pltpu.VMEM((len(flat), half, 2, piece, width), jnp.bfloat16)]
        + [pltpu.VMEM(moment1.shape, kind) for kind in (jnp.bfloat16, jnp.float32, jnp.float32)] * 2
        + [
            pltpu.SemaphoreType.DMA((2 * PARTS, 3 + per)),
            pltpu.SemaphoreType.DMA((2 * PARTS, 3)),
        ],
        compiler_params=params(),
        name="adam_step",
    )(pos, *arrays, weights, moment1, moment2)


def place_weights(pos, pieces, shape, before):
    flat = [(plane, one if isinstance(one, tuple) else (one,)) for plane, one in pieces]
    arrays = [one for _, group in flat for one in group]
    number, _, _, width = arrays[0].shape
    n_dp = shape[3] // width
    part = number // PARTS
    last = bool(before)

    def body(pos_ref, *refs):
        ins = refs[: len(arrays)]
        out_ref, held, sems, sem_out = refs[-4:]
        dp_at = pos_ref[0]
        inner = (dp_at > 0) & (dp_at < n_dp - 1)

        def into(act, i):
            rows = pl.ds(i * part, part)
            at = 0
            for n, (_, group) in enumerate(flat):
                made = [
                    pltpu.make_async_copy(ins[at + k].at[rows], held.at[n, rows], sems.at[i, n])
                    for k in range(len(group))
                ]
                at += len(group)
                if len(made) == 1:
                    act(made[0])
                else:
                    pl.when(inner)(lambda made=made: act(made[0]))
                    pl.when(~inner)(lambda made=made: act(made[1]))

        def onto(n, source, rows, sem):
            columns = pl.ds(pl.multiple_of((dp_at ^ flat[n][0]) * width, 128), width)
            return pltpu.make_async_copy(source, out_ref.at[rows, :, :, columns], sem)

        if last:
            every = pl.ds(0, number)
            copies = [onto(0, ref, every, sem_out.at[0, 0]) for ref in ins]
            for act in (lambda copy: copy.start(), lambda copy: copy.wait()):
                if len(copies) == 1:
                    act(copies[0])
                else:
                    pl.when(inner)(lambda act=act: act(copies[0]))
                    pl.when(~inner)(lambda act=act: act(copies[1]))
            return

        for i in range(PARTS):
            into(lambda copy: copy.start(), i)
        outs = []
        for i in range(PARTS):
            into(lambda copy: copy.wait(), i)
            rows = pl.ds(i * part, part)
            for n in range(len(flat)):
                outs.append(onto(n, held.at[n, rows], rows, sem_out.at[i, n]))
                outs[-1].start()
        for copy in outs:
            copy.wait()

    anywhere = pl.BlockSpec(memory_space=pl.ANY)
    held = (1, 16, 128) if last else (len(flat),) + arrays[0].shape
    return pl.pallas_call(
        body,
        out_shape=jax.ShapeDtypeStruct(shape, jnp.bfloat16),
        in_specs=[smem()] + [anywhere] * (len(arrays) + len(before)),
        out_specs=anywhere,
        scratch_shapes=[
            pltpu.VMEM(held, jnp.bfloat16),
            pltpu.SemaphoreType.DMA((PARTS, len(flat))),
            pltpu.SemaphoreType.DMA((PARTS, len(flat))),
        ],
        input_output_aliases={1 + len(arrays): 0} if before else {},
        compiler_params=params(LAST_VMEM_BYTES if before else VMEM_BYTES),
        name="place_weights",
    )(pos, *arrays, *before)


def between_planes(value, dp_at, n_dp, first=(), second=()):
    if n_dp != 4:
        whole = lax.all_gather(value, "dp", axis=0)
        return [
            lax.dynamic_index_in_dim(whole, dp_at ^ j, 0, keepdims=False) for j in range(n_dp)
        ]
    two = lax.ppermute(value, "dp", [(0, 2), (1, 3), (2, 0), (3, 1)])
    one = lax.ppermute(after(value, *first), "dp", [(0, 1), (1, 0), (2, 3), (3, 2)])
    outer = lax.ppermute(after(two, one, *second), "dp", [(2, 3), (1, 0)])
    middle = lax.ppermute(after(value, two, one, *second), "dp", [(1, 2), (2, 1)])
    return [value, one, two, (middle, outer)]


def gather_weights(pos, fresh, dp_at, n_dp, first):
    shape = fresh.shape[:3] + (n_dp * fresh.shape[3],)
    pieces = list(enumerate(between_planes(fresh, dp_at, n_dp, first)))
    most = place_weights(pos, pieces[:-1], shape, [])
    return place_weights(pos, pieces[-1:], shape, [most])


def after(value, *others):
    return lax.optimization_barrier((value,) + others)[0] if others else value


def finish_predicted(perm, parts):
    def body(perm_ref, parts_ref, out_ref):
        total = jnp.sum(parts_ref[...].astype(jnp.float32), axis=0)
        out_ref[...] = lax.dot_general(
            perm_ref[...],
            total.astype(jnp.bfloat16),
            (((0,), (0,)), ((), ())),
            preferred_element_type=jnp.float32,
        ).astype(jnp.bfloat16)

    return pl.pallas_call(
        body,
        out_shape=jax.ShapeDtypeStruct(parts.shape[1:], jnp.bfloat16),
        in_specs=[vmem(), vmem()],
        out_specs=vmem(),
        compiler_params=params(),
        name="finish_predicted",
    )(perm, parts)


def shards(signals, cotangent, row_insertion, touched, slot_map, weights, moment1, moment2):
    n_own = lax.axis_size("own")
    n_dp = lax.axis_size("dp")
    dp_at = lax.axis_index("dp")
    own_at = lax.axis_index("own")
    number, _, piece, _ = weights.shape
    width = moment1.shape[3]
    half = number // 2
    rows = signals.shape[0]
    pos = jnp.stack([dp_at, own_at]).astype(jnp.int32)

    def across(value, j):
        return lax.ppermute(value, "own", [(o, o ^ j) for o in range(n_own)])

    packed, perm = pack_rows(row_insertion.reshape(1, rows), signals, cotangent)
    if n_own == 8 and piece % 16 == 0:
        core = lax.rem(own_at, 2)
        columns = [
            lax.dynamic_slice(
                weights, (which * half, 0, 0, dp_at * width), (half, 2, piece, width)
            )
            for which in (core, 1 - core)
        ]
        chip = jnp.stack([columns[0], after(across(columns[1], 1), packed)])
        beside = [across(chip, 2), across(chip, 4)]
        diagonal = [across(beside[0][0], 4), across(beside[1][1], 2)]
        blocks = [(one, u) for one in [chip] + beside for u in range(2)]
        blocks += [(one, None) for one in diagonal]
        first, second, last = [chip], beside, diagonal
        sends = [(2, 6), (7,), (5,), (1,), (3,), (4,), (0,)]
    else:
        column = lax.dynamic_slice_in_dim(weights, dp_at * width, width, 3)
        outgoing = jnp.broadcast_to(
            column.reshape(1, 2, half, 2, piece, width), (n_own // 2, 2, half, 2, piece, width)
        ).reshape(n_own, half, 2, piece, width)
        blocks = lax.all_to_all(outgoing, "own", split_axis=0, concat_axis=0, tiled=True)
        blocks = blocks.transpose(1, 2, 0, 3, 4).reshape(half, 2, SITES, width)
        first, second, last = [], [], []
        sends = None
    *near, far = between_planes(packed, dp_at, n_dp, first, second)
    if isinstance(far, tuple):
        far = far[0] + far[1]
    near = jnp.stack(near)
    rows_in = (near, far, across(near, 1), across(after(far, *last), 1))

    pred_mine, pred_other, grads = local_grads(
        pos, touched, slot_map, rows_in, blocks, sends, piece, width
    )
    pred_part = pred_mine + across(pred_other, 1)
    parts = lax.all_to_all(pred_part, "dp", split_axis=0, concat_axis=0, tiled=True)
    if sends:
        x_same, y_diagonal, y_cross, partner, x_cross, y_same, own = grads
        x_same = across(x_same, 2)
        y_diagonal = across(y_diagonal, 4)
        y_cross = across(after(y_cross, pred_part), 5)
        partner = across(after(partner, pred_part), 1)
        first = (x_same, y_diagonal, y_cross, partner)
        x_cross = across(after(x_cross[0] + y_diagonal[0], *first), 3)
        y_same = across(after(y_same[0] + x_same[1], *first), 4)
        terms = [[(own, 0), (x_same, 0), y_same], [(partner, 0), (y_cross, 0), x_cross]]
    else:
        arrived = lax.all_to_all(grads, "own", split_axis=0, concat_axis=0, tiled=True)
        arrived = [
            lax.dynamic_index_in_dim(arrived, own_at ^ j, 0, keepdims=False) for j in range(n_own)
        ]
        terms = [arrived[0::2], arrived[1::2]]

    terms[0][-1] = after(terms[0][-1], parts)

    fresh, new_moment1, new_moment2 = adam(pos, terms, weights, moment1, moment2)
    predicted = finish_predicted(perm, after(parts, fresh))
    new_weights = gather_weights(pos, fresh, dp_at, n_dp, [predicted])

    return (predicted, new_weights, new_moment1, new_moment2)


def solution(mesh):
    in_specs = (
        P(("dp", "own"), None),
        P(("dp", "own"), None),
        P(("dp", "own")),
        P(),
        P(),
        P(None, None, "own", None),
        P(None, None, "own", "dp"),
        P(None, None, "own", "dp"),
    )
    out_specs = (
        P(("dp", "own"), None),
        P(None, None, "own", None),
        P(None, None, "own", "dp"),
        P(None, None, "own", "dp"),
    )
    return jax.shard_map(shards, mesh=mesh, in_specs=in_specs, out_specs=out_specs, check_vma=False)
```

```python
import math

import jax
import jax.numpy as jnp
from jax import lax
from jax.experimental import pallas as pl
from jax.experimental.pallas import tpu as pltpu
from jax.sharding import PartitionSpec as P

SITES = 384
CAP = 128
ID_ROWS = 16
PARTS = 2
TOGETHER = 4
VMEM_BYTES = 56 * 2**20
LAST_VMEM_BYTES = 4 * 2**20

gelu_coef = math.sqrt(2.0 / math.pi)
cubic_coef = 0.044715
learn_rate = 0.01


def gelu_parts(preact):
    tanh_input = gelu_coef * (preact + cubic_coef * preact * preact * preact)
    tangent = jnp.tanh(tanh_input)
    gelu_val = 0.5 * preact * (1.0 + tangent)
    slopes = 0.5 * (1.0 + tangent) + 0.5 * preact * (1.0 - tangent * tangent) * gelu_coef * (
        1.0 + 3.0 * cubic_coef * preact * preact
    )
    return (gelu_val, slopes)


def params(limit=VMEM_BYTES):
    return pltpu.CompilerParams(vmem_limit_bytes=limit)


def vmem():
    return pl.BlockSpec(memory_space=pltpu.VMEM)


def smem():
    return pl.BlockSpec(memory_space=pltpu.SMEM)


def pack_rows(ids, signals, cotangent):
    rows = signals.shape[0]

    def body(ids_ref, sig_ref, cot_ref, out_ref, perm_ref):
        ids_row = ids_ref[...].astype(jnp.float32)
        lane_ids = jnp.broadcast_to(ids_row, (rows, rows))
        same = lane_ids == lane_ids.T
        count = jnp.sum(same.astype(jnp.float32), axis=0, keepdims=True)
        full = jnp.max(jnp.where(count == CAP, ids_row, -1.0), axis=1, keepdims=True)
        chosen = ids_row == full
        from_row = lax.broadcasted_iota(jnp.int32, (rows, rows), 0)
        to_lane = lax.broadcasted_iota(jnp.int32, (rows, rows), 1)
        upto = (from_row <= to_lane).astype(jnp.bfloat16)
        ahead = jnp.dot(
            jnp.broadcast_to(chosen.astype(jnp.float32), (8, rows)).astype(jnp.bfloat16),
            upto,
            preferred_element_type=jnp.float32,
        )[:1].astype(jnp.int32)
        place = jnp.where(chosen, ahead - 1, CAP + to_lane[:1] - ahead)
        perm = (from_row == place).astype(jnp.float32).astype(jnp.bfloat16)
        perm_ref[...] = perm
        out_ref[:rows] = jnp.dot(perm, sig_ref[...], preferred_element_type=jnp.float32).astype(
            jnp.bfloat16
        )
        out_ref[rows : 2 * rows] = jnp.dot(
            perm, cot_ref[...], preferred_element_type=jnp.float32
        ).astype(jnp.bfloat16)
        sorted_ids = lax.dot_general(
            jnp.broadcast_to(ids_row, (ID_ROWS, rows)).astype(jnp.bfloat16),
            perm,
            (((1,), (1,)), ((), ())),
            preferred_element_type=jnp.float32,
        ).astype(jnp.bfloat16)
        out_ref[2 * rows :, :rows] = sorted_ids
        out_ref[2 * rows :, rows:] = jnp.zeros((ID_ROWS, SITES - rows), jnp.bfloat16)

    return pl.pallas_call(
        body,
        out_shape=(
            jax.ShapeDtypeStruct((2 * rows + ID_ROWS, SITES), jnp.bfloat16),
            jax.ShapeDtypeStruct((rows, rows), jnp.bfloat16),
        ),
        in_specs=[vmem(), vmem(), vmem()],
        out_specs=(vmem(), vmem()),
        compiler_params=params(),
        name="pack_rows",
    )(ids, signals, cotangent)


def local_grads(pos, touched, slot_map, rows_in, blocks, sends, piece, width):
    near = rows_in[0].shape[0]
    planes = near + 1
    rows = (rows_in[0].shape[1] - ID_ROWS) // 2
    touch = touched.shape[1]
    n_own = SITES // piece
    aligned = isinstance(blocks, list)
    arrays = []
    for array, _ in blocks if aligned else [(blocks, None)]:
        if not any(array is one for one in arrays):
            arrays.append(array)
    half = arrays[0].shape[-4]

    def body(pos_ref, touched_ref, slot_ref, *rest):
        row_refs = rest[:4]
        block_refs = rest[4 : 4 + len(arrays)]
        rest = rest[4 + len(arrays) :]
        pred_refs = rest[:2]
        n_out = len(grad_shapes)
        grad_refs = rest[2 : 2 + n_out]
        staged = rest[2 + n_out : 2 + 2 * n_out]
        acc, id_cols, held, sorted_rows, pred, full_of, tasks, sems, sem_out = rest[-9:]
        own_at = pos_ref[1]
        core = lax.rem(own_at, 2)

        row_copies = [
            pltpu.make_async_copy(
                ref, sorted_rows.at[pl.ds(at, near) if i % 2 == 0 else at], sems.at[i]
            )
            for i, (ref, at) in enumerate(zip(row_refs, (0, near, planes, planes + near)))
        ]
        if aligned:
            block_copies = []
            for j, (array, at) in enumerate(blocks):
                ref = [one for one, other in zip(block_refs, arrays) if other is array][0]
                sites = pl.ds(pl.multiple_of((own_at ^ j) * piece, 16), piece)
                block_copies.append(
                    pltpu.make_async_copy(
                        ref if at is None else ref.at[at], held.at[:, :, sites, :], sems.at[4 + j]
                    )
                )
        else:
            block_copies = [pltpu.make_async_copy(block_refs[0], held, sems.at[4])]
        for copy in row_copies + block_copies:
            copy.start()

        def clear(e, _):
            acc[e] = jnp.zeros(acc.shape[1:], jnp.float32)
            return 0

        lax.fori_loop(0, half, clear, 0)
        pred[...] = jnp.zeros_like(pred)
        for copy in row_copies:
            copy.wait()
        for source in range(2 * planes):
            ids_row = sorted_rows[source, 2 * rows :, :rows][:1].astype(jnp.float32)
            id_cols[source] = jnp.broadcast_to(ids_row[:, CAP:], (128, rows - CAP)).T
            full_of[source] = jnp.max(ids_row[:, :CAP]).astype(jnp.int32)

        count = jnp.int32(0)
        for source in range(2 * planes):
            which, plane = divmod(source, planes)
            device = (pos_ref[0] ^ plane) * n_own + (own_at ^ which)
            full = full_of[source]
            for j in range(touch + 1):
                insertion = full if j == 0 else touched_ref[device, j - 1]
                e = slot_ref[insertion] - core * half
                here = (e >= 0) & (e < half)
                if j:
                    here = here & (insertion != full)
                tasks[0, count] = jnp.int32(source)
                tasks[1, count] = jnp.int32(0 if j == 0 else CAP)
                tasks[2, count] = insertion
                tasks[3, count] = e
                count = count + here.astype(jnp.int32)
        for u in range(TOGETHER - 1):
            tasks[0, count + u] = jnp.int32(0)
            tasks[1, count + u] = jnp.int32(CAP)
            tasks[2, count + u] = jnp.int32(-1)
            tasks[3, count + u] = jnp.int32(0)
        for copy in block_copies:
            copy.wait()

        def together(i, _):
            loaded = []
            for u in range(TOGETHER):
                source, offset, insertion, e = [tasks[k, TOGETHER * i + u] for k in range(4)]
                first = pl.multiple_of(offset, CAP)
                wanted = jnp.where(offset == 0, -1, insertion).astype(jnp.float32)
                every = (offset == 0).astype(jnp.float32)
                keep = (id_cols[source] == wanted).astype(jnp.float32)
                keep = jnp.maximum(keep, every).astype(jnp.bfloat16)
                keep = jnp.concatenate([keep] * (SITES // 128), axis=1)
                sig = sorted_rows[source, pl.ds(first, CAP), :] * keep
                cot = sorted_rows[source, pl.ds(rows + first, CAP), :] * keep
                loaded.append((source, first, e, sig, cot))
            found = []
            for source, first, e, sig, cot in loaded:
                read_out = held[e, 1]
                preact = jnp.dot(sig, held[e, 0], preferred_element_type=jnp.float32)
                back_hidden = jnp.dot(cot, read_out, preferred_element_type=jnp.float32)
                gelu_val, slopes = gelu_parts(preact)
                hidden = gelu_val.astype(jnp.bfloat16)
                back_pre = (back_hidden * slopes).astype(jnp.bfloat16)
                part = lax.dot_general(
                    hidden, read_out, (((1,), (1,)), ((), ())), preferred_element_type=jnp.float32
                ).astype(jnp.bfloat16)
                grad_in = lax.dot_general(
                    sig, back_pre, (((0,), (0,)), ((), ())), preferred_element_type=jnp.float32
                )
                grad_out = lax.dot_general(
                    cot, hidden, (((0,), (0,)), ((), ())), preferred_element_type=jnp.float32
                )
                found.append((part, grad_in, grad_out))
            for (source, first, e, _, _), (part, grad_in, grad_out) in zip(loaded, found):
                pred[source, pl.ds(first, CAP), :] += part
                acc[e, 0] += grad_in
                acc[e, 1] += grad_out
            return 0

        lax.fori_loop(0, (count + TOGETHER - 1) // TOGETHER, together, 0)
        outs = [
            pltpu.make_async_copy(
                pred.at[which * planes + i], pred_refs[which].at[pos_ref[0] ^ i], sem_out.at[which, i]
            )
            for which in (1, 0)
            for i in range(planes)
        ]
        for copy in outs:
            copy.start()
        for n, (ref, into) in enumerate(zip(grad_refs, staged)):

            def write(e, _, into=into, n=n):
                if aligned:
                    for i, j in enumerate(sends[n]):
                        first = pl.multiple_of((own_at ^ j) * piece, 16)
                        into[i, e] = acc[e, :, pl.ds(first, piece), :].astype(jnp.bfloat16)
                else:
                    into[e] = acc[e].astype(jnp.bfloat16)
                return 0

            lax.fori_loop(0, half, write, 0)
            outs.append(pltpu.make_async_copy(into, ref, sem_out.at[2 + n, 0]))
            outs[-1].start()
        for copy in outs:
            copy.wait()

    pred_shape = jax.ShapeDtypeStruct((planes, rows, SITES), jnp.bfloat16)
    grad_shapes = [
        jax.ShapeDtypeStruct(shape, jnp.bfloat16)
        for shape in (
            [(len(group), half, 2, piece, width) for group in sends]
            if aligned
            else [(half, 2, SITES, width)]
        )
    ]
    most = 2 * planes * (touch + 1)
    acc_shape = (half, 2, SITES, width)
    id_shape = (2 * planes, rows - CAP, 128)
    row_shape = (2 * planes,) + rows_in[0].shape[1:]
    pred_all = (2 * planes, rows, SITES)
    scratch = [pltpu.VMEM(one.shape, jnp.bfloat16) for one in grad_shapes] + [
        pltpu.VMEM(acc_shape, jnp.float32),
        pltpu.VMEM(id_shape, jnp.float32),
        pltpu.VMEM(acc_shape, jnp.bfloat16),
        pltpu.VMEM(row_shape, jnp.bfloat16),
        pltpu.VMEM(pred_all, jnp.bfloat16),
        pltpu.SMEM((2 * planes,), jnp.int32),
        pltpu.SMEM((4, most + TOGETHER), jnp.int32),
        pltpu.SemaphoreType.DMA((4 + n_own,)),
        pltpu.SemaphoreType.DMA((2 + len(grad_shapes), planes)),
    ]
    found = pl.pallas_call(
        body,
        out_shape=[pred_shape, pred_shape] + grad_shapes,
        in_specs=[smem(), smem(), smem()] + [pl.BlockSpec(memory_space=pl.ANY)] * (4 + len(arrays)),
        out_specs=[pl.BlockSpec(memory_space=pl.ANY)] * (2 + len(grad_shapes)),
        scratch_shapes=scratch,
        compiler_params=params(),
        name="local_grads",
    )(pos, touched, slot_map, *rows_in, *arrays)
    grads = list(found[2:])
    if not aligned:
        grads = grads[0].reshape(half, 2, n_own, piece, width).transpose(2, 0, 1, 3, 4)
    return found[0], found[1], grads


def adam(pos, terms, weights, moment1, moment2):
    number, _, piece, width = moment1.shape
    half = number // 2
    flat = [one if isinstance(one, tuple) else (one, None) for group in terms for one in group]
    arrays = [array for array, _ in flat]
    per = len(terms[0])
    correct_one = 1.0 - 0.9**10
    correct_two = 1.0 - 0.999**10

    def body(pos_ref, *refs):
        term_refs = [
            ref if at is None else ref.at[at] for ref, (_, at) in zip(refs, flat)
        ]
        w_ref, m1_ref, m2_ref = refs[len(flat) : len(flat) + 3]
        refs = refs[len(flat) + 3 :]
        new_w, new_m1, new_m2, grads, w_in, m1_in, m2_in, w_out, m1_out, m2_out = refs[:10]
        sem_in, sem_out = refs[10:]
        columns = pl.ds(pl.multiple_of(pos_ref[0] * width, 128), width)
        part = half // PARTS
        steps = [(g, i * part) for g in range(2) for i in range(PARTS)]
        own_core = lax.rem(pos_ref[1], 2)
        copies = []
        for n, (g, first) in enumerate(steps):
            rows = pl.ds((own_core ^ g) * half + first, part)
            copies.append(
                [
                    pltpu.make_async_copy(ref, into.at[rows], sem_in.at[n, i])
                    for i, (ref, into) in enumerate(
                        (
                            (w_ref.at[rows, :, :, columns], w_in),
                            (m1_ref.at[rows], m1_in),
                            (m2_ref.at[rows], m2_in),
                        )
                    )
                ]
                + [
                    pltpu.make_async_copy(
                        term_refs[g * per + i].at[pl.ds(first, part)],
                        grads.at[g * per + i, pl.ds(first, part)],
                        sem_in.at[n, 3 + i],
                    )
                    for i in range(per)
                ]
            )
            for copy in copies[n]:
                copy.start()
        outs = []
        for n, (g, first) in enumerate(steps):
            for copy in copies[n]:
                copy.wait()

            def step(i, _, g=g, first=first):
                gradient = grads[g * per, first + i].astype(jnp.float32)
                for j in range(1, per):
                    gradient = gradient + grads[g * per + j, first + i].astype(jnp.float32)
                at = (own_core ^ g) * half + first + i
                one = 0.9 * m1_in[at] + 0.1 * gradient
                two = 0.999 * m2_in[at] + 0.001 * gradient * gradient
                m1_out[at] = one
                m2_out[at] = two
                spread = two * (1.0 / correct_two)
                updated = w_in[at].astype(jnp.float32) - one * (learn_rate / correct_one) / (
                    spread * lax.rsqrt(spread) + 1e-08
                )
                w_out[at] = updated.astype(jnp.bfloat16)
                return 0

            lax.fori_loop(0, part, step, 0)
            rows = pl.ds((own_core ^ g) * half + first, part)
            for i, (held, ref) in enumerate(
                ((w_out, new_w), (m1_out, new_m1), (m2_out, new_m2))
            ):
                outs.append(pltpu.make_async_copy(held.at[rows], ref.at[rows], sem_out.at[n, i]))
                outs[-1].start()
        for copy in outs:
            copy.wait()

    anywhere = pl.BlockSpec(memory_space=pl.ANY)
    return pl.pallas_call(
        body,
        out_shape=[
            jax.ShapeDtypeStruct(moment1.shape, jnp.bfloat16),
            jax.ShapeDtypeStruct(moment1.shape, jnp.float32),
            jax.ShapeDtypeStruct(moment1.shape, jnp.float32),
        ],
        in_specs=[smem()] + [anywhere] * (len(flat) + 3),
        out_specs=[anywhere] * 3,
        scratch_shapes=[pltpu.VMEM((len(flat), half, 2, piece, width), jnp.bfloat16)]
        + [pltpu.VMEM(moment1.shape, kind) for kind in (jnp.bfloat16, jnp.float32, jnp.float32)] * 2
        + [
            pltpu.SemaphoreType.DMA((2 * PARTS, 3 + per)),
            pltpu.SemaphoreType.DMA((2 * PARTS, 3)),
        ],
        compiler_params=params(),
        name="adam_step",
    )(pos, *arrays, weights, moment1, moment2)


def place_weights(pos, pieces, shape, before):
    flat = [(plane, one if isinstance(one, tuple) else (one,)) for plane, one in pieces]
    arrays = [one for _, group in flat for one in group]
    number, _, _, width = arrays[0].shape
    n_dp = shape[3] // width
    part = number // PARTS
    last = bool(before)

    def body(pos_ref, *refs):
        ins = refs[: len(arrays)]
        out_ref, held, sems, sem_out = refs[-4:]
        dp_at = pos_ref[0]
        inner = (dp_at > 0) & (dp_at < n_dp - 1)

        def into(act, i):
            rows = pl.ds(i * part, part)
            at = 0
            for n, (_, group) in enumerate(flat):
                made = [
                    pltpu.make_async_copy(ins[at + k].at[rows], held.at[n, rows], sems.at[i, n])
                    for k in range(len(group))
                ]
                at += len(group)
                if len(made) == 1:
                    act(made[0])
                else:
                    pl.when(inner)(lambda made=made: act(made[0]))
                    pl.when(~inner)(lambda made=made: act(made[1]))

        def onto(n, source, rows, sem):
            columns = pl.ds(pl.multiple_of((dp_at ^ flat[n][0]) * width, 128), width)
            return pltpu.make_async_copy(source, out_ref.at[rows, :, :, columns], sem)

        if last:
            every = pl.ds(0, number)
            copies = [onto(0, ref, every, sem_out.at[0, 0]) for ref in ins]
            for act in (lambda copy: copy.start(), lambda copy: copy.wait()):
                if len(copies) == 1:
                    act(copies[0])
                else:
                    pl.when(inner)(lambda act=act: act(copies[0]))
                    pl.when(~inner)(lambda act=act: act(copies[1]))
            return

        for i in range(PARTS):
            into(lambda copy: copy.start(), i)
        outs = []
        for i in range(PARTS):
            into(lambda copy: copy.wait(), i)
            rows = pl.ds(i * part, part)
            for n in range(len(flat)):
                outs.append(onto(n, held.at[n, rows], rows, sem_out.at[i, n]))
                outs[-1].start()
        for copy in outs:
            copy.wait()

    anywhere = pl.BlockSpec(memory_space=pl.ANY)
    held = (1, 16, 128) if last else (len(flat),) + arrays[0].shape
    return pl.pallas_call(
        body,
        out_shape=jax.ShapeDtypeStruct(shape, jnp.bfloat16),
        in_specs=[smem()] + [anywhere] * (len(arrays) + len(before)),
        out_specs=anywhere,
        scratch_shapes=[
            pltpu.VMEM(held, jnp.bfloat16),
            pltpu.SemaphoreType.DMA((PARTS, len(flat))),
            pltpu.SemaphoreType.DMA((PARTS, len(flat))),
        ],
        input_output_aliases={1 + len(arrays): 0} if before else {},
        compiler_params=params(LAST_VMEM_BYTES if before else VMEM_BYTES),
        name="place_weights",
    )(pos, *arrays, *before)


def between_planes(value, dp_at, n_dp, first=(), second=()):
    if n_dp != 4:
        whole = lax.all_gather(value, "dp", axis=0)
        return [
            lax.dynamic_index_in_dim(whole, dp_at ^ j, 0, keepdims=False) for j in range(n_dp)
        ]
    two = lax.ppermute(value, "dp", [(0, 2), (1, 3), (2, 0), (3, 1)])
    one = lax.ppermute(after(value, *first), "dp", [(0, 1), (1, 0), (2, 3), (3, 2)])
    outer = lax.ppermute(after(two, one, *second), "dp", [(2, 3), (1, 0)])
    middle = lax.ppermute(after(value, two, one, *second), "dp", [(1, 2), (2, 1)])
    return [value, one, two, (middle, outer)]


def gather_weights(pos, fresh, dp_at, n_dp):
    shape = fresh.shape[:3] + (n_dp * fresh.shape[3],)
    pieces = list(enumerate(between_planes(fresh, dp_at, n_dp)))
    most = place_weights(pos, pieces[:-1], shape, [])
    return place_weights(pos, pieces[-1:], shape, [most])


def after(value, *others):
    return lax.optimization_barrier((value,) + others)[0] if others else value


def finish_predicted(perm, parts):
    def body(perm_ref, parts_ref, out_ref):
        total = jnp.sum(parts_ref[...].astype(jnp.float32), axis=0)
        out_ref[...] = lax.dot_general(
            perm_ref[...],
            total.astype(jnp.bfloat16),
            (((0,), (0,)), ((), ())),
            preferred_element_type=jnp.float32,
        ).astype(jnp.bfloat16)

    return pl.pallas_call(
        body,
        out_shape=jax.ShapeDtypeStruct(parts.shape[1:], jnp.bfloat16),
        in_specs=[vmem(), vmem()],
        out_specs=vmem(),
        compiler_params=params(),
        name="finish_predicted",
    )(perm, parts)


def shards(signals, cotangent, row_insertion, touched, slot_map, weights, moment1, moment2):
    n_own = lax.axis_size("own")
    n_dp = lax.axis_size("dp")
    dp_at = lax.axis_index("dp")
    own_at = lax.axis_index("own")
    number, _, piece, _ = weights.shape
    width = moment1.shape[3]
    half = number // 2
    rows = signals.shape[0]
    pos = jnp.stack([dp_at, own_at]).astype(jnp.int32)

    def across(value, j):
        return lax.ppermute(value, "own", [(o, o ^ j) for o in range(n_own)])

    packed, perm = pack_rows(row_insertion.reshape(1, rows), signals, cotangent)
    if n_own == 8 and piece % 16 == 0:
        core = lax.rem(own_at, 2)
        columns = [
            lax.dynamic_slice(
                weights, (which * half, 0, 0, dp_at * width), (half, 2, piece, width)
            )
            for which in (core, 1 - core)
        ]
        chip = jnp.stack([columns[0], after(across(columns[1], 1), packed)])
        beside = [across(chip, 2), across(chip, 4)]
        diagonal = [across(beside[0][0], 4), across(beside[1][1], 2)]
        blocks = [(one, u) for one in [chip] + beside for u in range(2)]
        blocks += [(one, None) for one in diagonal]
        first, second, last = [chip], beside, diagonal
        sends = [(2, 6), (7,), (5,), (1,), (3,), (4,), (0,)]
    else:
        column = lax.dynamic_slice_in_dim(weights, dp_at * width, width, 3)
        outgoing = jnp.broadcast_to(
            column.reshape(1, 2, half, 2, piece, width), (n_own // 2, 2, half, 2, piece, width)
        ).reshape(n_own, half, 2, piece, width)
        blocks = lax.all_to_all(outgoing, "own", split_axis=0, concat_axis=0, tiled=True)
        blocks = blocks.transpose(1, 2, 0, 3, 4).reshape(half, 2, SITES, width)
        first, second, last = [], [], []
        sends = None
    *near, far = between_planes(packed, dp_at, n_dp, first, second)
    if isinstance(far, tuple):
        far = far[0] + far[1]
    near = jnp.stack(near)
    rows_in = (near, far, across(near, 1), across(after(far, *last), 1))

    pred_mine, pred_other, grads = local_grads(
        pos, touched, slot_map, rows_in, blocks, sends, piece, width
    )
    pred_part = pred_mine + across(pred_other, 1)
    parts = lax.all_to_all(pred_part, "dp", split_axis=0, concat_axis=0, tiled=True)
    if sends:
        x_same, y_diagonal, y_cross, partner, x_cross, y_same, own = grads
        x_same = across(x_same, 2)
        y_diagonal = across(y_diagonal, 4)
        y_cross = across(after(y_cross, pred_part), 5)
        partner = across(after(partner, pred_part), 1)
        first = (x_same, y_diagonal, y_cross, partner)
        x_cross = across(after(x_cross[0] + y_diagonal[0], *first), 3)
        y_same = across(after(y_same[0] + x_same[1], *first), 4)
        terms = [[(own, 0), (x_same, 0), y_same], [(partner, 0), (y_cross, 0), x_cross]]
    else:
        arrived = lax.all_to_all(grads, "own", split_axis=0, concat_axis=0, tiled=True)
        arrived = [
            lax.dynamic_index_in_dim(arrived, own_at ^ j, 0, keepdims=False) for j in range(n_own)
        ]
        terms = [arrived[0::2], arrived[1::2]]

    predicted = finish_predicted(perm, parts)
    terms[0][-1] = after(terms[0][-1], parts)

    fresh, new_moment1, new_moment2 = adam(pos, terms, weights, moment1, moment2)
    new_weights = gather_weights(pos, fresh, dp_at, n_dp)

    return (predicted, new_weights, new_moment1, new_moment2)


def solution(mesh):
    in_specs = (
        P(("dp", "own"), None),
        P(("dp", "own"), None),
        P(("dp", "own")),
        P(),
        P(),
        P(None, None, "own", None),
        P(None, None, "own", "dp"),
        P(None, None, "own", "dp"),
    )
    out_specs = (
        P(("dp", "own"), None),
        P(None, None, "own", None),
        P(None, None, "own", "dp"),
        P(None, None, "own", "dp"),
    )
    return jax.shard_map(shards, mesh=mesh, in_specs=in_specs, out_specs=out_specs, check_vma=False)
```

```python
import math

import jax
import jax.numpy as jnp
from jax import lax
from jax.experimental import pallas as pl
from jax.experimental.pallas import tpu as pltpu
from jax.sharding import PartitionSpec as P

SITES = 384
CAP = 128
ID_ROWS = 16
PARTS = 2
TOGETHER = 4
VMEM_BYTES = 56 * 2**20
LAST_VMEM_BYTES = 4 * 2**20

gelu_coef = math.sqrt(2.0 / math.pi)
cubic_coef = 0.044715
learn_rate = 0.01


def gelu_parts(preact):
    tanh_input = gelu_coef * (preact + cubic_coef * preact * preact * preact)
    tangent = jnp.tanh(tanh_input)
    gelu_val = 0.5 * preact * (1.0 + tangent)
    slopes = 0.5 * (1.0 + tangent) + 0.5 * preact * (1.0 - tangent * tangent) * gelu_coef * (
        1.0 + 3.0 * cubic_coef * preact * preact
    )
    return (gelu_val, slopes)


def params(limit=VMEM_BYTES):
    return pltpu.CompilerParams(vmem_limit_bytes=limit)


def vmem():
    return pl.BlockSpec(memory_space=pltpu.VMEM)


def smem():
    return pl.BlockSpec(memory_space=pltpu.SMEM)


def pack_rows(ids, signals, cotangent):
    rows = signals.shape[0]

    def body(ids_ref, sig_ref, cot_ref, out_ref, perm_ref):
        ids_row = ids_ref[...].astype(jnp.float32)
        lane_ids = jnp.broadcast_to(ids_row, (rows, rows))
        same = lane_ids == lane_ids.T
        count = jnp.sum(same.astype(jnp.float32), axis=0, keepdims=True)
        full = jnp.max(jnp.where(count == CAP, ids_row, -1.0), axis=1, keepdims=True)
        chosen = ids_row == full
        from_row = lax.broadcasted_iota(jnp.int32, (rows, rows), 0)
        to_lane = lax.broadcasted_iota(jnp.int32, (rows, rows), 1)
        upto = (from_row <= to_lane).astype(jnp.bfloat16)
        ahead = jnp.dot(
            jnp.broadcast_to(chosen.astype(jnp.float32), (8, rows)).astype(jnp.bfloat16),
            upto,
            preferred_element_type=jnp.float32,
        )[:1].astype(jnp.int32)
        place = jnp.where(chosen, ahead - 1, CAP + to_lane[:1] - ahead)
        perm = (from_row == place).astype(jnp.float32).astype(jnp.bfloat16)
        perm_ref[...] = perm
        out_ref[:rows] = jnp.dot(perm, sig_ref[...], preferred_element_type=jnp.float32).astype(
            jnp.bfloat16
        )
        out_ref[rows : 2 * rows] = jnp.dot(
            perm, cot_ref[...], preferred_element_type=jnp.float32
        ).astype(jnp.bfloat16)
        sorted_ids = lax.dot_general(
            jnp.broadcast_to(ids_row, (ID_ROWS, rows)).astype(jnp.bfloat16),
            perm,
            (((1,), (1,)), ((), ())),
            preferred_element_type=jnp.float32,
        ).astype(jnp.bfloat16)
        out_ref[2 * rows :, :rows] = sorted_ids
        out_ref[2 * rows :, rows:] = jnp.zeros((ID_ROWS, SITES - rows), jnp.bfloat16)

    return pl.pallas_call(
        body,
        out_shape=(
            jax.ShapeDtypeStruct((2 * rows + ID_ROWS, SITES), jnp.bfloat16),
            jax.ShapeDtypeStruct((rows, rows), jnp.bfloat16),
        ),
        in_specs=[vmem(), vmem(), vmem()],
        out_specs=(vmem(), vmem()),
        compiler_params=params(),
        name="pack_rows",
    )(ids, signals, cotangent)


def local_grads(pos, touched, slot_map, rows_in, blocks, sends, piece, width):
    near = rows_in[0].shape[0]
    planes = near + 1
    rows = (rows_in[0].shape[1] - ID_ROWS) // 2
    touch = touched.shape[1]
    n_own = SITES // piece
    aligned = isinstance(blocks, list)
    arrays = []
    for array, _ in blocks if aligned else [(blocks, None)]:
        if not any(array is one for one in arrays):
            arrays.append(array)
    half = arrays[0].shape[-4]

    def body(pos_ref, touched_ref, slot_ref, *rest):
        row_refs = rest[:4]
        block_refs = rest[4 : 4 + len(arrays)]
        rest = rest[4 + len(arrays) :]
        pred_refs = rest[:2]
        n_out = len(grad_shapes)
        grad_refs = rest[2 : 2 + n_out]
        staged = rest[2 + n_out : 2 + 2 * n_out]
        acc, id_cols, held, sorted_rows, pred, full_of, tasks, sems, sem_out = rest[-9:]
        own_at = pos_ref[1]
        core = lax.rem(own_at, 2)

        row_copies = [
            pltpu.make_async_copy(
                ref, sorted_rows.at[pl.ds(at, near) if i % 2 == 0 else at], sems.at[i]
            )
            for i, (ref, at) in enumerate(zip(row_refs, (0, near, planes, planes + near)))
        ]
        if aligned:
            block_copies = []
            for j, (array, at) in enumerate(blocks):
                ref = [one for one, other in zip(block_refs, arrays) if other is array][0]
                sites = pl.ds(pl.multiple_of((own_at ^ j) * piece, 16), piece)
                block_copies.append(
                    pltpu.make_async_copy(
                        ref if at is None else ref.at[at], held.at[:, :, sites, :], sems.at[4 + j]
                    )
                )
        else:
            block_copies = [pltpu.make_async_copy(block_refs[0], held, sems.at[4])]
        for copy in row_copies + block_copies:
            copy.start()

        def clear(e, _):
            acc[e] = jnp.zeros(acc.shape[1:], jnp.float32)
            return 0

        lax.fori_loop(0, half, clear, 0)
        pred[...] = jnp.zeros_like(pred)
        for copy in row_copies:
            copy.wait()
        for source in range(2 * planes):
            ids_row = sorted_rows[source, 2 * rows :, :rows][:1].astype(jnp.float32)
            id_cols[source] = jnp.broadcast_to(ids_row[:, CAP:], (128, rows - CAP)).T
            full_of[source] = jnp.max(ids_row[:, :CAP]).astype(jnp.int32)

        count = jnp.int32(0)
        for source in range(2 * planes):
            which, plane = divmod(source, planes)
            device = (pos_ref[0] ^ plane) * n_own + (own_at ^ which)
            full = full_of[source]
            for j in range(touch + 1):
                insertion = full if j == 0 else touched_ref[device, j - 1]
                e = slot_ref[insertion] - core * half
                here = (e >= 0) & (e < half)
                if j:
                    here = here & (insertion != full)
                tasks[0, count] = jnp.int32(source)
                tasks[1, count] = jnp.int32(0 if j == 0 else CAP)
                tasks[2, count] = insertion
                tasks[3, count] = e
                count = count + here.astype(jnp.int32)
        for u in range(TOGETHER - 1):
            tasks[0, count + u] = jnp.int32(0)
            tasks[1, count + u] = jnp.int32(CAP)
            tasks[2, count + u] = jnp.int32(-1)
            tasks[3, count + u] = jnp.int32(0)
        for copy in block_copies:
            copy.wait()

        def together(i, _):
            loaded = []
            for u in range(TOGETHER):
                source, offset, insertion, e = [tasks[k, TOGETHER * i + u] for k in range(4)]
                first = pl.multiple_of(offset, CAP)
                wanted = jnp.where(offset == 0, -1, insertion).astype(jnp.float32)
                every = (offset == 0).astype(jnp.float32)
                keep = (id_cols[source] == wanted).astype(jnp.float32)
                keep = jnp.maximum(keep, every).astype(jnp.bfloat16)
                keep = jnp.concatenate([keep] * (SITES // 128), axis=1)
                sig = sorted_rows[source, pl.ds(first, CAP), :] * keep
                cot = sorted_rows[source, pl.ds(rows + first, CAP), :] * keep
                loaded.append((source, first, e, sig, cot))
            found = []
            for source, first, e, sig, cot in loaded:
                read_out = held[e, 1]
                preact = jnp.dot(sig, held[e, 0], preferred_element_type=jnp.float32)
                back_hidden = jnp.dot(cot, read_out, preferred_element_type=jnp.float32)
                gelu_val, slopes = gelu_parts(preact)
                hidden = gelu_val.astype(jnp.bfloat16)
                back_pre = (back_hidden * slopes).astype(jnp.bfloat16)
                part = lax.dot_general(
                    hidden, read_out, (((1,), (1,)), ((), ())), preferred_element_type=jnp.float32
                ).astype(jnp.bfloat16)
                grad_in = lax.dot_general(
                    sig, back_pre, (((0,), (0,)), ((), ())), preferred_element_type=jnp.float32
                )
                grad_out = lax.dot_general(
                    cot, hidden, (((0,), (0,)), ((), ())), preferred_element_type=jnp.float32
                )
                found.append((part, grad_in, grad_out))
            for (source, first, e, _, _), (part, grad_in, grad_out) in zip(loaded, found):
                pred[source, pl.ds(first, CAP), :] += part
                acc[e, 0] += grad_in
                acc[e, 1] += grad_out
            return 0

        lax.fori_loop(0, (count + TOGETHER - 1) // TOGETHER, together, 0)
        outs = [
            pltpu.make_async_copy(
                pred.at[which * planes + i], pred_refs[which].at[pos_ref[0] ^ i], sem_out.at[which, i]
            )
            for which in (1, 0)
            for i in range(planes)
        ]
        for copy in outs:
            copy.start()
        for n, (ref, into) in enumerate(zip(grad_refs, staged)):

            def write(e, _, into=into, n=n):
                if aligned:
                    for i, j in enumerate(sends[n]):
                        first = pl.multiple_of((own_at ^ j) * piece, 16)
                        into[i, e] = acc[e, :, pl.ds(first, piece), :].astype(jnp.bfloat16)
                else:
                    into[e] = acc[e].astype(jnp.bfloat16)
                return 0

            lax.fori_loop(0, half, write, 0)
            outs.append(pltpu.make_async_copy(into, ref, sem_out.at[2 + n, 0]))
            outs[-1].start()
        for copy in outs:
            copy.wait()

    pred_shape = jax.ShapeDtypeStruct((planes, rows, SITES), jnp.bfloat16)
    grad_shapes = [
        jax.ShapeDtypeStruct(shape, jnp.bfloat16)
        for shape in (
            [(len(group), half, 2, piece, width) for group in sends]
            if aligned
            else [(half, 2, SITES, width)]
        )
    ]
    most = 2 * planes * (touch + 1)
    acc_shape = (half, 2, SITES, width)
    id_shape = (2 * planes, rows - CAP, 128)
    row_shape = (2 * planes,) + rows_in[0].shape[1:]
    pred_all = (2 * planes, rows, SITES)
    scratch = [pltpu.VMEM(one.shape, jnp.bfloat16) for one in grad_shapes] + [
        pltpu.VMEM(acc_shape, jnp.float32),
        pltpu.VMEM(id_shape, jnp.float32),
        pltpu.VMEM(acc_shape, jnp.bfloat16),
        pltpu.VMEM(row_shape, jnp.bfloat16),
        pltpu.VMEM(pred_all, jnp.bfloat16),
        pltpu.SMEM((2 * planes,), jnp.int32),
        pltpu.SMEM((4, most + TOGETHER), jnp.int32),
        pltpu.SemaphoreType.DMA((4 + n_own,)),
        pltpu.SemaphoreType.DMA((2 + len(grad_shapes), planes)),
    ]
    found = pl.pallas_call(
        body,
        out_shape=[pred_shape, pred_shape] + grad_shapes,
        in_specs=[smem(), smem(), smem()] + [pl.BlockSpec(memory_space=pl.ANY)] * (4 + len(arrays)),
        out_specs=[pl.BlockSpec(memory_space=pl.ANY)] * (2 + len(grad_shapes)),
        scratch_shapes=scratch,
        compiler_params=params(),
        name="local_grads",
    )(pos, touched, slot_map, *rows_in, *arrays)
    grads = list(found[2:])
    if not aligned:
        grads = grads[0].reshape(half, 2, n_own, piece, width).transpose(2, 0, 1, 3, 4)
    return found[0], found[1], grads


def adam(pos, terms, weights, moment1, moment2):
    number, _, piece, width = moment1.shape
    half = number // 2
    flat = [one if isinstance(one, tuple) else (one, None) for group in terms for one in group]
    arrays = [array for array, _ in flat]
    per = len(terms[0])
    correct_one = 1.0 - 0.9**10
    correct_two = 1.0 - 0.999**10

    def body(pos_ref, *refs):
        term_refs = [
            ref if at is None else ref.at[at] for ref, (_, at) in zip(refs, flat)
        ]
        w_ref, m1_ref, m2_ref = refs[len(flat) : len(flat) + 3]
        refs = refs[len(flat) + 3 :]
        new_w, new_m1, new_m2, grads, w_in, m1_in, m2_in, w_out, m1_out, m2_out = refs[:10]
        sem_in, sem_out = refs[10:]
        columns = pl.ds(pl.multiple_of(pos_ref[0] * width, 128), width)
        part = half // PARTS
        steps = [(g, i * part) for g in range(2) for i in range(PARTS)]
        own_core = lax.rem(pos_ref[1], 2)
        copies = []
        for n, (g, first) in enumerate(steps):
            rows = pl.ds((own_core ^ g) * half + first, part)
            copies.append(
                [
                    pltpu.make_async_copy(ref, into.at[rows], sem_in.at[n, i])
                    for i, (ref, into) in enumerate(
                        (
                            (w_ref.at[rows, :, :, columns], w_in),
                            (m1_ref.at[rows], m1_in),
                            (m2_ref.at[rows], m2_in),
                        )
                    )
                ]
                + [
                    pltpu.make_async_copy(
                        term_refs[g * per + i].at[pl.ds(first, part)],
                        grads.at[g * per + i, pl.ds(first, part)],
                        sem_in.at[n, 3 + i],
                    )
                    for i in range(per)
                ]
            )
            for copy in copies[n]:
                copy.start()
        outs = []
        for n, (g, first) in enumerate(steps):
            for copy in copies[n]:
                copy.wait()

            def step(i, _, g=g, first=first):
                gradient = grads[g * per, first + i].astype(jnp.float32)
                for j in range(1, per):
                    gradient = gradient + grads[g * per + j, first + i].astype(jnp.float32)
                at = (own_core ^ g) * half + first + i
                one = 0.9 * m1_in[at] + 0.1 * gradient
                two = 0.999 * m2_in[at] + 0.001 * gradient * gradient
                m1_out[at] = one
                m2_out[at] = two
                spread = two * (1.0 / correct_two)
                updated = w_in[at].astype(jnp.float32) - one * (learn_rate / correct_one) / (
                    spread * lax.rsqrt(spread) + 1e-08
                )
                w_out[at] = updated.astype(jnp.bfloat16)
                return 0

            lax.fori_loop(0, part, step, 0)
            rows = pl.ds((own_core ^ g) * half + first, part)
            for i, (held, ref) in enumerate(
                ((w_out, new_w), (m1_out, new_m1), (m2_out, new_m2))
            ):
                outs.append(pltpu.make_async_copy(held.at[rows], ref.at[rows], sem_out.at[n, i]))
                outs[-1].start()
        for copy in outs:
            copy.wait()

    anywhere = pl.BlockSpec(memory_space=pl.ANY)
    return pl.pallas_call(
        body,
        out_shape=[
            jax.ShapeDtypeStruct(moment1.shape, jnp.bfloat16),
            jax.ShapeDtypeStruct(moment1.shape, jnp.float32),
            jax.ShapeDtypeStruct(moment1.shape, jnp.float32),
        ],
        in_specs=[smem()] + [anywhere] * (len(flat) + 3),
        out_specs=[anywhere] * 3,
        scratch_shapes=[pltpu.VMEM((len(flat), half, 2, piece, width), jnp.bfloat16)]
        + [pltpu.VMEM(moment1.shape, kind) for kind in (jnp.bfloat16, jnp.float32, jnp.float32)] * 2
        + [
            pltpu.SemaphoreType.DMA((2 * PARTS, 3 + per)),
            pltpu.SemaphoreType.DMA((2 * PARTS, 3)),
        ],
        compiler_params=params(),
        name="adam_step",
    )(pos, *arrays, weights, moment1, moment2)


def place_weights(pos, pieces, shape, before):
    flat = [(plane, one if isinstance(one, tuple) else (one,)) for plane, one in pieces]
    arrays = [one for _, group in flat for one in group]
    number, _, _, width = arrays[0].shape
    n_dp = shape[3] // width
    part = number // PARTS
    last = bool(before)

    def body(pos_ref, *refs):
        ins = refs[: len(arrays)]
        out_ref, held, sems, sem_out = refs[-4:]
        dp_at = pos_ref[0]
        inner = (dp_at > 0) & (dp_at < n_dp - 1)

        def into(act, i):
            rows = pl.ds(i * part, part)
            at = 0
            for n, (_, group) in enumerate(flat):
                made = [
                    pltpu.make_async_copy(ins[at + k].at[rows], held.at[n, rows], sems.at[i, n])
                    for k in range(len(group))
                ]
                at += len(group)
                if len(made) == 1:
                    act(made[0])
                else:
                    pl.when(inner)(lambda made=made: act(made[0]))
                    pl.when(~inner)(lambda made=made: act(made[1]))

        def onto(n, source, rows, sem):
            columns = pl.ds(pl.multiple_of((dp_at ^ flat[n][0]) * width, 128), width)
            return pltpu.make_async_copy(source, out_ref.at[rows, :, :, columns], sem)

        if last:
            every = pl.ds(0, number)
            copies = [onto(0, ref, every, sem_out.at[0, 0]) for ref in ins]
            for act in (lambda copy: copy.start(), lambda copy: copy.wait()):
                if len(copies) == 1:
                    act(copies[0])
                else:
                    pl.when(inner)(lambda act=act: act(copies[0]))
                    pl.when(~inner)(lambda act=act: act(copies[1]))
            return

        for i in range(PARTS):
            into(lambda copy: copy.start(), i)
        outs = []
        for i in range(PARTS):
            into(lambda copy: copy.wait(), i)
            rows = pl.ds(i * part, part)
            for n in range(len(flat)):
                outs.append(onto(n, held.at[n, rows], rows, sem_out.at[i, n]))
                outs[-1].start()
        for copy in outs:
            copy.wait()

    anywhere = pl.BlockSpec(memory_space=pl.ANY)
    held = (1, 16, 128) if last else (len(flat),) + arrays[0].shape
    return pl.pallas_call(
        body,
        out_shape=jax.ShapeDtypeStruct(shape, jnp.bfloat16),
        in_specs=[smem()] + [anywhere] * (len(arrays) + len(before)),
        out_specs=anywhere,
        scratch_shapes=[
            pltpu.VMEM(held, jnp.bfloat16),
            pltpu.SemaphoreType.DMA((PARTS, len(flat))),
            pltpu.SemaphoreType.DMA((PARTS, len(flat))),
        ],
        input_output_aliases={1 + len(arrays): 0} if before else {},
        compiler_params=params(LAST_VMEM_BYTES if before else VMEM_BYTES),
        name="place_weights",
    )(pos, *arrays, *before)


def between_planes(value, dp_at, n_dp, first=(), second=()):
    if n_dp != 4:
        whole = lax.all_gather(value, "dp", axis=0)
        return [
            lax.dynamic_index_in_dim(whole, dp_at ^ j, 0, keepdims=False) for j in range(n_dp)
        ]
    two = lax.ppermute(value, "dp", [(0, 2), (1, 3), (2, 0), (3, 1)])
    one = lax.ppermute(after(value, *first), "dp", [(0, 1), (1, 0), (2, 3), (3, 2)])
    outer = lax.ppermute(after(two, one, *second), "dp", [(2, 3), (1, 0)])
    middle = lax.ppermute(after(value, two, one, *second), "dp", [(1, 2), (2, 1)])
    return [value, one, two, (middle, outer)]


def gather_weights(pos, fresh, dp_at, n_dp):
    shape = fresh.shape[:3] + (n_dp * fresh.shape[3],)
    pieces = list(enumerate(between_planes(fresh, dp_at, n_dp)))
    most = place_weights(pos, pieces[:-1], shape, [])
    return place_weights(pos, pieces[-1:], shape, [most])


def after(value, *others):
    return lax.optimization_barrier((value,) + others)[0] if others else value


def finish_predicted(perm, parts):
    def body(perm_ref, parts_ref, out_ref):
        total = jnp.sum(parts_ref[...].astype(jnp.float32), axis=0)
        out_ref[...] = lax.dot_general(
            perm_ref[...],
            total.astype(jnp.bfloat16),
            (((0,), (0,)), ((), ())),
            preferred_element_type=jnp.float32,
        ).astype(jnp.bfloat16)

    return pl.pallas_call(
        body,
        out_shape=jax.ShapeDtypeStruct(parts.shape[1:], jnp.bfloat16),
        in_specs=[vmem(), vmem()],
        out_specs=vmem(),
        compiler_params=params(),
        name="finish_predicted",
    )(perm, parts)


def shards(signals, cotangent, row_insertion, touched, slot_map, weights, moment1, moment2):
    n_own = lax.axis_size("own")
    n_dp = lax.axis_size("dp")
    dp_at = lax.axis_index("dp")
    own_at = lax.axis_index("own")
    number, _, piece, _ = weights.shape
    width = moment1.shape[3]
    half = number // 2
    rows = signals.shape[0]
    pos = jnp.stack([dp_at, own_at]).astype(jnp.int32)

    def across(value, j):
        return lax.ppermute(value, "own", [(o, o ^ j) for o in range(n_own)])

    packed, perm = pack_rows(row_insertion.reshape(1, rows), signals, cotangent)
    if n_own == 8 and piece % 16 == 0:
        core = lax.rem(own_at, 2)
        columns = [
            lax.dynamic_slice(
                weights, (which * half, 0, 0, dp_at * width), (half, 2, piece, width)
            )
            for which in (core, 1 - core)
        ]
        chip = jnp.stack([columns[0], after(across(columns[1], 1), packed)])
        beside = [across(chip, 2), across(chip, 4)]
        diagonal = [across(beside[0][0], 4), across(beside[1][1], 2)]
        blocks = [(one, u) for one in [chip] + beside for u in range(2)]
        blocks += [(one, None) for one in diagonal]
        first, second, last = [chip], beside, diagonal
        sends = [(2, 6), (7,), (5,), (1,), (3,), (4,), (0,)]
    else:
        column = lax.dynamic_slice_in_dim(weights, dp_at * width, width, 3)
        outgoing = jnp.broadcast_to(
            column.reshape(1, 2, half, 2, piece, width), (n_own // 2, 2, half, 2, piece, width)
        ).reshape(n_own, half, 2, piece, width)
        blocks = lax.all_to_all(outgoing, "own", split_axis=0, concat_axis=0, tiled=True)
        blocks = blocks.transpose(1, 2, 0, 3, 4).reshape(half, 2, SITES, width)
        first, second, last = [], [], []
        sends = None
    *near, far = between_planes(packed, dp_at, n_dp, first, second)
    if isinstance(far, tuple):
        far = far[0] + far[1]
    near = jnp.stack(near)
    rows_in = (near, far, across(near, 1), across(after(far, *last), 1))

    pred_mine, pred_other, grads = local_grads(
        pos, touched, slot_map, rows_in, blocks, sends, piece, width
    )
    pred_swapped = across(pred_other, 1)
    pred_part = pred_mine + pred_swapped
    parts = lax.all_to_all(pred_part, "dp", split_axis=0, concat_axis=0, tiled=True)
    if sends:
        x_same, y_diagonal, y_cross, partner, x_cross, y_same, own = grads
        x_same = across(x_same, 2)
        y_diagonal = across(y_diagonal, 4)
        y_cross = across(after(y_cross, pred_swapped), 5)
        partner = across(after(partner, pred_part), 1)
        first = (x_same, y_diagonal, y_cross, partner)
        x_cross = across(after(x_cross[0] + y_diagonal[0], *first), 3)
        y_same = across(after(y_same[0] + x_same[1], *first), 4)
        terms = [[(own, 0), (x_same, 0), y_same], [(partner, 0), (y_cross, 0), x_cross]]
    else:
        arrived = lax.all_to_all(grads, "own", split_axis=0, concat_axis=0, tiled=True)
        arrived = [
            lax.dynamic_index_in_dim(arrived, own_at ^ j, 0, keepdims=False) for j in range(n_own)
        ]
        terms = [arrived[0::2], arrived[1::2]]

    predicted = finish_predicted(perm, parts)
    terms[0][-1] = after(terms[0][-1], parts)

    fresh, new_moment1, new_moment2 = adam(pos, terms, weights, moment1, moment2)
    new_weights = gather_weights(pos, fresh, dp_at, n_dp)

    return (predicted, new_weights, new_moment1, new_moment2)


def solution(mesh):
    in_specs = (
        P(("dp", "own"), None),
        P(("dp", "own"), None),
        P(("dp", "own")),
        P(),
        P(),
        P(None, None, "own", None),
        P(None, None, "own", "dp"),
        P(None, None, "own", "dp"),
    )
    out_specs = (
        P(("dp", "own"), None),
        P(None, None, "own", None),
        P(None, None, "own", "dp"),
        P(None, None, "own", "dp"),
    )
    return jax.shard_map(shards, mesh=mesh, in_specs=in_specs, out_specs=out_specs, check_vma=False)
```
